32 devices in a mesh: chan: 8 (over z, y), state: 4 (over x, core).
Axes of the slice: x: 2, y: 2, z: 4, core: 2. Of those that a mesh axis runs over, the one named last changes fastest.
Arguments:
- hidden_in: float32 [2048, 2048], P('chan'), may hold values from -6 to 6
- norm_gain: float32 [2048], replicated, may hold values from 0.25 to 1.75
- in_weight: bfloat16 [2048, 2, 4096], P(None, None, 'chan'), may hold values from -0.125 to 0.125
- conv_kernel: float32 [4, 4096], P(None, 'chan'), may hold values from -3 to 3
- conv_offset: float32 [4096], P('chan'), may hold values from -3 to 3
- select_rank: bfloat16 [4096, 128], P('chan'), may hold values from -0.09375 to 0.09375
- select_entry: bfloat16 [4096, 16], P('chan', 'state'), may hold values from -0.1875 to 0.1875
- select_read: bfloat16 [4096, 16], P('chan', 'state'), may hold values from -0.1875 to 0.1875
- delta_weight: bfloat16 [128, 4096], P(None, 'chan'), may hold values from -0.5 to 0.5
- step_bias: float32 [4096], P('chan'), as said below
- decay_log: float32 [16, 4096], P('state', 'chan'), may hold values from 0 to 2.77
- skip_weight: float32 [4096], P('chan'), may hold values from 0.5 to 1.5
- out_weight: bfloat16 [4096, 2048], P('chan'), may hold values from -0.375 to 0.375
- lengths: int32 [8], replicated, may hold values from 1 to 1024, 2048 in all
- pad_mask: int32 [2048], replicated, may hold values 0 or 1
- cotangent: float32 [2048, 2048], P('chan'), may hold values from -6 to 6
Outputs:
- result: float32 [2048, 2048], P('chan')
- input_grad: float32 [2048, 2048], P('chan')
- gain_grad: float32 [2048], replicated
- in_grad: float32 [2048, 2, 4096], P(None, None, 'chan')
- kernel_grad: float32 [4, 4096], P(None, 'chan')
- offset_grad: float32 [4096], P('chan')
- rank_grad: float32 [4096, 128], P('chan')
- entry_grad: float32 [4096, 16], P('chan', 'state')
- read_grad: float32 [4096, 16], P('chan', 'state')
- delta_grad: float32 [128, 4096], P(None, 'chan')
- bias_grad: float32 [4096], P('chan')
- decay_grad: float32 [16, 4096], P('state', 'chan')
- skip_grad: float32 [4096], P('chan')
- out_grad: float32 [4096, 2048], P('chan')
The draws below stay inside these ranges and needn't reach their ends.
Inputs may be any that keep to these rules, and one draw needn't show every extreme that they name: lengths of the 8 sequences packed in order into all 2048 tokens; they sum to 2048 and the longest has exactly 1024. `pad_mask`: 1 marks a real token, 0 padding. `step_bias`: the step-size bias of each inner channel.
All inputs are finite; a program needn't handle non-finite values.
Results may differ from the reference program's by a relative error of at most 0.011.
Values may be sent and summed in bfloat16 or wider, within the bound.
No kernel may reach another device: no remote copies, remote signals or barrier semaphores. Data moves between devices by JAX's collectives and lax.ppermute only.
A program may use at most 384 MiB of HBM per device.

```python
import math
import jax
import jax.numpy as jnp
import numpy as np
from jax import lax

D = 2048
DI = 4096
NS = 16
RANK = 128
KCONV = 4
SEQS = 8
TOKENS = 2048
LONGEST = 1024


def draw_step_bias(key, part):
    key = jax.random.fold_in(key, 11)
    pick_key, slow_key, fast_key = jax.random.split(key, 3)
    share = 0.5
    lower = 0.3
    upper = 2.0
    pick = jax.random.uniform(pick_key, (DI,), jnp.float32)
    level = jax.random.uniform(slow_key, (DI,), jnp.float32, math.log(lower), math.log(upper))
    slow_bias = level - math.log(LONGEST)
    fast_bias = jax.random.uniform(fast_key, (DI,), jnp.float32, -4.5, -1.0)
    return jnp.where(pick < share, slow_bias, fast_bias).astype(jnp.float32)


def plant(array, rng, low, largest):
    dims = array.shape
    spot = [jax.random.randint(jax.random.fold_in(rng, axis), (), 0, dims[axis]) for axis in range(len(dims))]
    array = array.at[tuple(spot)].set(low)
    longest = dims.index(max(dims))
    spot[longest] = (spot[longest] + 1) % dims[longest]
    return array.at[tuple(spot)].set(largest)


def block_scale(own_key, extent, shards, least, largest):
    def one(dim, parts):
        steps = jax.random.uniform(jax.random.fold_in(jax.random.fold_in(own_key, 6), dim), (parts,), jnp.float32, least / len(shards), largest / len(shards))
        return jnp.repeat(jnp.exp(steps), extent[dim] // parts).reshape((-1,) + (1,) * (len(extent) - dim - 1))

    factor_of = one(*shards[0])
    for cut in shards[1:]:
        factor_of = factor_of * one(*cut)
    return factor_of


def profile(count, total, bound, skew):
    weights = [(1 << 20) // math.isqrt(rank ** skew) + 1 for rank in range(2, count + 1)]
    rest, counts = total - bound - (count - 1), [1] * (count - 1)
    while rest > 0:
        movable = [i for i in range(count - 1) if counts[i] < bound]
        pool, budget = sum([weights[i] for i in movable]), rest
        for i in movable:
            extra = min(bound - counts[i], max(1, budget * weights[i] // pool), rest)
            counts[i] = counts[i] + extra
            rest = rest - extra
    return np.array([bound] + counts)


def ragged(stream_key, count, total, bound, lean):
    if count == 2:
        one = jax.random.randint(stream_key, (), max(1, total - bound), min(bound, total - 1) + 1)
        return jnp.stack([one, total - one])
    tallies = jnp.asarray(profile(count, total, bound, lean), jnp.int32)
    couples = (count - 1) // 2
    giver, taker = tallies[1:1 + 2 * couples:2], tallies[2:2 + 2 * couples:2]
    slack = jnp.minimum(giver - 1, bound - taker)
    passed = jax.random.randint(jax.random.fold_in(stream_key, 1), (couples,), 0, 1 << 20) % (slack + 1)
    tallies = tallies.at[1:1 + 2 * couples:2].set(giver - passed).at[2:2 + 2 * couples:2].set(taker + passed)
    return tallies[jax.random.permutation(jax.random.fold_in(stream_key, 2), count)]


def centred(stream_key, extent, spread, reach, cuts=(), kind=jnp.bfloat16):
    drawn = spread * jax.random.normal(stream_key, extent, jnp.float32)
    if cuts:
        drawn = drawn * block_scale(stream_key, extent, cuts, -0.22, 0.18)
    return jnp.clip(drawn, -reach, reach).astype(kind)


def setup_inputs(seed: int = 0) -> dict:
    keys = jax.random.split(jax.random.key(seed), 17)
    hidden_in = centred(keys[0], (TOKENS, D), 1.0, 6.0, ((0, 8),), jnp.float32)
    norm_gain = jnp.clip(1.0 + 0.15 * jax.random.normal(keys[1], (D,), jnp.float32), 0.25, 1.75)
    in_weight = centred(keys[2], (D, 2, DI), D ** -0.5, 0.125, ((2, 8),))
    conv_kernel = centred(keys[3], (KCONV, DI), KCONV ** -0.5, 3.0, ((1, 8),), jnp.float32)
    conv_offset = centred(keys[4], (DI,), 0.5, 3.0, ((0, 8),), jnp.float32)
    select_rank = centred(keys[5], (DI, RANK), DI ** -0.5, 0.09375, ((0, 8),))
    select_entry = centred(keys[6], (DI, NS), (DI // 4) ** -0.5, 0.1875, ((0, 8), (1, 4)))
    select_read = centred(keys[7], (DI, NS), (DI // 4) ** -0.5, 0.1875, ((0, 8), (1, 4)))
    delta_weight = centred(keys[8], (RANK, DI), RANK ** -0.5, 0.5, ((1, 8),))
    step_bias = draw_step_bias(jax.random.fold_in(keys[16], 71), 0)
    decay_log = jnp.clip(2.77 * jax.random.uniform(keys[10], (NS, DI), jnp.float32) ** block_scale(keys[10], (NS, DI), ((0, 4), (1, 8)), -0.2, 0.2), 0.0, 2.77)
    skip_weight = jnp.clip(0.5 + 1.0 * jax.random.uniform(keys[11], (DI,), jnp.float32) ** block_scale(keys[11], (DI,), ((0, 8),), -0.2, 0.2), 0.5, 1.5)
    out_weight = centred(keys[12], (DI, D), (DI // 16) ** -0.5, 0.375, ((0, 8),))
    lengths = ragged(keys[13], SEQS, TOKENS, LONGEST, 2).astype(jnp.int32)
    pad_mask = plant((jax.random.randint(keys[14], (TOKENS,), 0, 8) < 7).astype(jnp.int32), jax.random.fold_in(keys[14], 1), 0, 1)
    cotangent = centred(keys[15], (TOKENS, D), 1.0, 6.0, ((0, 8),), jnp.float32)
    return dict(hidden_in=hidden_in, norm_gain=norm_gain, in_weight=in_weight, conv_kernel=conv_kernel, conv_offset=conv_offset, select_rank=select_rank, select_entry=select_entry, select_read=select_read, delta_weight=delta_weight, step_bias=step_bias, decay_log=decay_log, skip_weight=skip_weight, out_weight=out_weight, lengths=lengths, pad_mask=pad_mask, cotangent=cotangent)


epsilon = 1e-05
highest = lax.Precision.HIGHEST

@jax.custom_vjp
def low(v):
    return lax.optimization_barrier(v.astype(jnp.bfloat16)).astype(jnp.float32)

@jax.custom_vjp
def low_back(v):
    return v

def low_keep(v):
    return (low(v), None)

def low_pass(kept, grad):
    return (grad,)

def back_keep(v):
    return (v, None)

def back_low(kept, grad):
    return (low(grad),)
low.defvjp(low_keep, low_pass)
low_back.defvjp(back_keep, back_low)

def positions(lengths):
    ends = jnp.cumsum(lengths).astype(jnp.int32)
    begins = ends - lengths
    places = jnp.arange(TOKENS, dtype=jnp.int32)
    opening = lax.optimization_barrier(jnp.max(jnp.where(begins[:, None] <= places[None, :], begins[:, None], 0), axis=0))
    return (places - opening).astype(jnp.int32)

def delayed(values, amount):
    if amount == 0:
        return values
    padding = jnp.zeros((amount,) + values.shape[1:], jnp.float32)
    return jnp.concatenate([padding, values[:values.shape[0] - amount]], axis=0)

def selective(delta, act, entry, readout, coeff, fresh):
    blocks = TOKENS // 16

    def shape_up(values):
        return values.reshape((blocks, 16) + values.shape[1:])

    def block_step(state, packed):

        def advance(inner_state, item):
            delta_now, act_now, entry_now, read_now, fresh_now = item
            decays = jnp.exp(delta_now[None, :] * coeff) * fresh_now
            inner_state = decays * inner_state + (delta_now * act_now)[None, :] * entry_now[:, None]
            return (inner_state, lax.optimization_barrier(jnp.sum(read_now[:, None] * inner_state, axis=0)))
        return lax.scan(advance, state, packed)
    initial = jnp.zeros((NS, DI), jnp.float32)
    packed = (shape_up(delta), shape_up(act), shape_up(entry), shape_up(readout), shape_up(fresh))
    final_state, outputs = lax.scan(jax.checkpoint(block_step), initial, packed)
    return outputs.reshape(TOKENS, DI)

def reference(hidden_in, norm_gain, in_weight, conv_kernel, conv_offset, select_rank, select_entry, select_read, delta_weight, step_bias, decay_log, skip_weight, out_weight, lengths, pad_mask, cotangent):
    place = positions(lengths)
    fresh = (place > 0).astype(jnp.float32)
    maskf = pad_mask.astype(jnp.float32)[:, None]

    def forward(hidden_in, norm_gain, in_weight, conv_kernel, conv_offset, select_rank, select_entry, select_read, delta_weight, step_bias, decay_log, skip_weight, out_weight):
        square = lax.optimization_barrier(jnp.mean(hidden_in * hidden_in, axis=1, keepdims=True))
        scaled = hidden_in * lax.rsqrt(square + epsilon)
        normed = low(scaled * norm_gain[None, :])
        both = low_back(jnp.einsum('tk,kjc->tjc', normed, in_weight, precision=highest))
        inner = both[:, 0, :] * maskf
        gate_in = both[:, 1, :]
        conv = jnp.zeros((TOKENS, DI), jnp.float32) + conv_offset[None, :]
        for index in range(KCONV):
            lag = KCONV - 1 - index
            valid = (place >= lag).astype(jnp.float32)[:, None]
            conv = conv + conv_kernel[index][None, :] * delayed(inner, lag) * valid
        act = low(jax.nn.silu(conv) * maskf)
        lowrank = low_back(low(jnp.dot(act, select_rank, precision=highest)))
        entry = low_back(jnp.dot(act, select_entry, precision=highest))
        readout = low_back(jnp.dot(act, select_read, precision=highest))
        dpre = low_back(jnp.dot(lowrank, delta_weight, precision=highest) + step_bias[None, :])
        delta = jax.nn.softplus(dpre)
        coeff = -jnp.exp(decay_log)
        scanned = selective(delta, act, entry, readout, coeff, fresh)
        mixed = scanned + skip_weight[None, :] * act
        gated = low(mixed * jax.nn.silu(gate_in))
        branch = low_back(jnp.dot(gated, out_weight, precision=highest))
        return hidden_in + branch
    floats = tuple((value.astype(jnp.float32) for value in (hidden_in, norm_gain, in_weight, conv_kernel, conv_offset, select_rank, select_entry, select_read, delta_weight, step_bias, decay_log, skip_weight, out_weight)))
    result, pullback = jax.vjp(forward, *floats)
    grads = pullback(cotangent.astype(jnp.float32))
    return (result, grads[0], grads[1], grads[2], grads[3], grads[4], grads[5], grads[6], grads[7], grads[8], grads[9], grads[10], grads[11], grads[12])
```

```python
import functools
import math

import jax
import jax.numpy as jnp
from jax import lax
from jax.experimental import pallas as pl
from jax.experimental.pallas import tpu as pltpu
from jax.sharding import PartitionSpec as P

epsilon = 1e-05
GROUP = 16
CHUNK = 256
HALO = 4
FAR = 1e30
wide = jnp.float32
low = jnp.bfloat16


def positions(lengths, tokens_all):
    ends = jnp.cumsum(lengths)
    begins = ends - lengths
    places = jnp.arange(tokens_all, dtype=jnp.int32)
    opening = jnp.max(jnp.where(begins[:, None] <= places[None, :], begins[:, None], 0), axis=0)
    return places - opening


def silu_slope(values):
    logistic = jax.nn.sigmoid(values)
    return logistic * (1.0 + values * (1.0 - logistic))


def own_block(states):
    row = lax.broadcasted_iota(jnp.int32, (GROUP, GROUP * states), 0)
    col = lax.broadcasted_iota(jnp.int32, (GROUP, GROUP * states), 1)
    return jnp.logical_and(col >= row * states, col < (row + 1) * states)


def forward_body(step_ref, drive_ref, coeff_ref, entry_ref, read_ref, y_ref, state_ref, carry):
    @pl.when(pl.program_id(0) == 0)
    def _():
        carry[...] = jnp.zeros_like(carry)

    coeff = coeff_ref[...]
    states = coeff.shape[0]
    chosen = own_block(states)

    def group(index, state):
        base = pl.multiple_of(index * GROUP, GROUP)
        entry = entry_ref[index]
        kept = []
        for i in range(GROUP):
            decay = jnp.exp2(step_ref[pl.ds(base + i, 1), :] * coeff)
            state = decay * state + drive_ref[pl.ds(base + i, 1), :] * entry[:, i : i + 1]
            kept.append(state)
        rows = pl.multiple_of(base * states, GROUP * states)
        block = jnp.concatenate(kept, axis=0).astype(low)
        state_ref[pl.ds(rows, GROUP * states), :] = block
        weights = jnp.where(chosen, read_ref[index], 0.0).astype(low)
        y_ref[pl.ds(base, GROUP), :] = jnp.dot(weights, block, preferred_element_type=wide)
        return state

    carry[...] = lax.fori_loop(0, step_ref.shape[0] // GROUP, group, carry[...])


def backward_body(
    step_ref,
    delta_ref,
    drive_ref,
    dmix_ref,
    coeff_ref,
    entry_ref,
    read_ref,
    state_ref,
    before_ref,
    lam_ref,
    flow_ref,
    dentry_ref,
    dread_ref,
    decay_ref,
    carry,
    total,
):
    turn = pl.program_id(0)

    @pl.when(turn == 0)
    def _():
        carry[...] = jnp.zeros_like(carry)
        total[...] = jnp.zeros_like(total)

    coeff = coeff_ref[...]
    states = coeff.shape[0]
    chosen = own_block(states)
    groups = step_ref.shape[0] // GROUP
    first = jnp.where(turn == pl.num_programs(0) - 1, 0.0, before_ref[...].astype(wide))
    across = (((1,), (1,)), ((), ()))

    def group(turned, totals):
        pulled, summed = totals
        index = groups - 1 - turned
        base = pl.multiple_of(index * GROUP, GROUP)
        rows = pl.multiple_of(base * states, GROUP * states)
        read = read_ref[index]
        block = state_ref[pl.ds(rows, GROUP * states), :]
        block_wide = block.astype(wide)
        prior = pl.multiple_of(jnp.maximum(rows - states, 0), states)
        edge = jnp.where(index == 0, first, state_ref[pl.ds(prior, states), :].astype(wide))
        lams = [None] * GROUP
        flows = [None] * GROUP
        for i in range(GROUP - 1, -1, -1):
            lam = read[:, i : i + 1] * dmix_ref[pl.ds(base + i, 1), :] + pulled
            pulled = jnp.exp2(step_ref[pl.ds(base + i, 1), :] * coeff) * lam
            earlier = block_wide[(i - 1) * states : i * states] if i else edge
            flow = pulled * earlier
            summed = summed + flow * delta_ref[pl.ds(base + i, 1), :]
            lams[i] = lam
            flows[i] = flow * coeff
        lam_block = jnp.concatenate(lams, axis=0).astype(low)
        flow_block = jnp.concatenate(flows, axis=0).astype(low)
        here = pl.ds(base, GROUP)
        weights = jnp.where(chosen, entry_ref[index], 0.0).astype(low)
        lam_ref[here, :] = jnp.dot(weights, lam_block, preferred_element_type=wide)
        ones = jnp.where(chosen, 1.0, 0.0).astype(low)
        flow_ref[here, :] = jnp.dot(ones, flow_block, preferred_element_type=wide)
        cross = lax.dot_general(
            drive_ref[here, :].astype(low), lam_block, across, preferred_element_type=wide
        )
        dentry_ref[index] = jnp.sum(jnp.where(chosen, cross, 0.0), axis=0, keepdims=True)
        cross = lax.dot_general(
            dmix_ref[here, :].astype(low), block, across, preferred_element_type=wide
        )
        dread_ref[index] = jnp.sum(jnp.where(chosen, cross, 0.0), axis=0, keepdims=True)
        return pulled, summed

    pulled, summed = lax.fori_loop(0, groups, group, (carry[...], total[...]))
    carry[...] = pulled
    total[...] = summed
    decay_ref[...] = summed


def per_group(values):
    tokens, states = values.shape
    return jnp.swapaxes(values.reshape(tokens // GROUP, GROUP, states), 1, 2)


def forward_scan(step, drive, coeff, entry, readout):
    tokens, width = step.shape
    states = coeff.shape[0]
    many = CHUNK // GROUP
    row = pl.BlockSpec((CHUNK, width), lambda t: (t, 0))
    return pl.pallas_call(
        forward_body,
        grid=(tokens // CHUNK,),
        in_specs=[
            row,
            row,
            pl.BlockSpec((states, width), lambda t: (0, 0)),
            pl.BlockSpec((many, states, GROUP), lambda t: (t, 0, 0)),
            pl.BlockSpec((many, 1, GROUP * states), lambda t: (t, 0, 0)),
        ],
        out_specs=[row, pl.BlockSpec((CHUNK * states, width), lambda t: (t, 0))],
        out_shape=[
            jax.ShapeDtypeStruct((tokens, width), wide),
            jax.ShapeDtypeStruct((tokens * states, width), low),
        ],
        scratch_shapes=[pltpu.VMEM((states, width), wide)],
        compiler_params=pltpu.CompilerParams(vmem_limit_bytes=24 * 1024 * 1024),
        name="forward_scan",
    )(step, drive, coeff, per_group(entry), readout.reshape(tokens // GROUP, 1, GROUP * states))


def backward_scan(step, delta, drive, dmix, coeff, entry, readout, kept):
    tokens, width = step.shape
    states = coeff.shape[0]
    many = CHUNK // GROUP
    last = tokens // CHUNK - 1
    row = pl.BlockSpec((CHUNK, width), lambda t: (last - t, 0))
    flat = pl.BlockSpec((many, 1, GROUP * states), lambda t: (last - t, 0, 0))
    fixed = pl.BlockSpec((states, width), lambda t: (0, 0))
    return pl.pallas_call(
        backward_body,
        grid=(tokens // CHUNK,),
        in_specs=[
            row,
            row,
            row,
            row,
            fixed,
            flat,
            pl.BlockSpec((many, states, GROUP), lambda t: (last - t, 0, 0)),
            pl.BlockSpec((CHUNK * states, width), lambda t: (last - t, 0)),
            pl.BlockSpec(
                (states, width), lambda t: (jnp.maximum((last - t) * CHUNK - 1, 0), 0)
            ),
        ],
        out_specs=[row, row, flat, flat, fixed],
        out_shape=[
            jax.ShapeDtypeStruct((tokens, width), wide),
            jax.ShapeDtypeStruct((tokens, width), wide),
            jax.ShapeDtypeStruct((tokens // GROUP, 1, GROUP * states), wide),
            jax.ShapeDtypeStruct((tokens // GROUP, 1, GROUP * states), wide),
            jax.ShapeDtypeStruct((states, width), wide),
        ],
        scratch_shapes=[pltpu.VMEM((states, width), wide), pltpu.VMEM((states, width), wide)],
        compiler_params=pltpu.CompilerParams(vmem_limit_bytes=24 * 1024 * 1024),
        name="backward_scan",
    )(
        step,
        delta,
        drive,
        dmix,
        coeff,
        entry.reshape(tokens // GROUP, 1, GROUP * states),
        per_group(readout),
        kept,
        kept,
    )


def shards(
    n_chan,
    n_state,
    hidden_in,
    norm_gain,
    in_weight,
    conv_kernel,
    conv_offset,
    select_rank,
    select_entry,
    select_read,
    delta_weight,
    step_bias,
    decay_log,
    skip_weight,
    out_weight,
    lengths,
    pad_mask,
    cotangent,
):
    rows_dev, width = hidden_in.shape
    tokens = pad_mask.shape[0]
    chans = in_weight.shape[2]
    taps = conv_kernel.shape[0]
    rank = select_rank.shape[1]
    per_state = select_entry.shape[1]
    states = per_state * n_state
    small = rank + 2 * states
    quarter = rows_dev // n_state
    own = chans // n_state
    part = lax.axis_index("state")
    contract_rows = (((0,), (0,)), ((), ()))
    contract_cols = (((1,), (1,)), ((), ()))

    def gather_chan(values):
        return lax.all_gather(values, "chan", axis=0)

    def gather_state(values):
        return lax.all_gather(values, "state", axis=0)

    def swap_state(values):
        return lax.all_to_all(values, "state", 0, 0, tiled=True)

    def sum_chan(parts):
        moved = lax.all_to_all(parts, "chan", 0, 0, tiled=True)
        return jnp.sum(moved.astype(wide), axis=0)

    def mine(values, axis=0):
        return lax.dynamic_slice_in_dim(values, part * own, own, axis)

    def windows(values, before, after):
        tail = values.shape[1:]
        groups = values.reshape((n_chan * n_state, quarter) + tail)
        pieces = [groups]
        if before:
            pad = jnp.zeros((1, before) + tail, values.dtype)
            pieces.insert(0, jnp.concatenate([pad, groups[:-1, quarter - before :]], axis=0))
        if after:
            pad = jnp.zeros((1, after) + tail, values.dtype)
            pieces.append(jnp.concatenate([groups[1:, :after], pad], axis=0))
        joined = jnp.concatenate(pieces, axis=1)
        return joined.reshape((n_chan, n_state) + joined.shape[1:])

    def window_of(values, before, after):
        found = windows(values, before, after)
        return lax.dynamic_index_in_dim(found, part, axis=1, keepdims=False)

    def to_tokens(values):
        return jnp.swapaxes(values, 0, 1).reshape((tokens,) + values.shape[3:])

    def split_own(values):
        lead = values.shape[:-1]
        cut = values.reshape(lead + (n_state, own))
        return jnp.moveaxis(cut, -2, 0)

    def join_own(values):
        moved = jnp.moveaxis(values, 0, -2)
        return moved.reshape(moved.shape[:-2] + (chans,))

    place = positions(lengths, tokens)
    maskf = pad_mask.astype(wide)
    place_win = window_of(place, HALO, HALO)
    mask_win = window_of(maskf, HALO, HALO)[:, :, None]

    start = part * quarter
    hidden_q = lax.dynamic_slice_in_dim(hidden_in, start, quarter, 0)
    ahead = lax.rem(start + rows_dev - HALO, rows_dev)
    behind = lax.rem(start + quarter, rows_dev)
    local = jnp.concatenate(
        [
            hidden_q,
            lax.dynamic_slice_in_dim(hidden_in, ahead, HALO, 0),
            lax.dynamic_slice_in_dim(hidden_in, behind, HALO, 0),
        ],
        axis=0,
    )
    inv_all = lax.rsqrt(jnp.mean(local * local, axis=1, keepdims=True) + epsilon)
    scaled_all = local * inv_all
    normed_all = (scaled_all * norm_gain[None, :]).astype(low)
    inv_rms = inv_all[:quarter]
    scaled = scaled_all[:quarter]
    gathered = gather_chan(normed_all)
    normed_q = gathered[:, :quarter].reshape(n_chan * quarter, width)

    cot_q = lax.dynamic_slice_in_dim(cotangent, start, quarter, 0)
    grad_q = gather_chan(cot_q.astype(low)).reshape(n_chan * quarter, width)

    columns = jnp.concatenate([select_entry, select_read], axis=1)
    columns = gather_state(columns).reshape(n_state, chans, 2, per_state)
    columns = jnp.transpose(columns, (1, 2, 0, 3)).reshape(chans, 2 * states)
    select = jnp.concatenate([select_rank, columns], axis=1)
    decay_own = swap_state(jnp.swapaxes(decay_log.reshape(per_state, n_state, own), 0, 1))
    coeff = -jnp.exp(decay_own.reshape(states, own))

    in_flat = in_weight.reshape(width, 2 * chans)
    both = jnp.dot(
        gathered.reshape(-1, width), in_flat, preferred_element_type=wide
    ).reshape(n_chan, quarter + 2 * HALO, 2 * chans)
    gate_q = both[:, :quarter, chans:].astype(low)
    raw = both[:, :, :chans].astype(low)
    nothing = jnp.zeros((1, HALO, chans), low)
    before = raw[:, quarter : quarter + HALO]
    before = jnp.where(part == 0, jnp.concatenate([nothing, before[:-1]], axis=0), before)
    after = raw[:, quarter + HALO :]
    after = jnp.where(
        part == n_state - 1, jnp.concatenate([after[1:], nothing], axis=0), after
    )
    inner_win = jnp.concatenate([before, raw[:, :quarter], after], axis=1) * mask_win

    def convolve(values, places, span):
        total = conv_offset
        for index in range(taps):
            lag = taps - 1 - index
            valid = (places >= lag).astype(wide)[..., None]
            first = taps - 1 - lag
            total = total + conv_kernel[index] * values[:, first : first + span] * valid
        return total

    span = quarter + HALO
    conv_win = convolve(inner_win[:, HALO - taps + 1 :], place_win[:, HALO:], span)
    act_q = (jax.nn.silu(conv_win[:, :quarter]) * mask_win[:, HALO : HALO + quarter]).astype(low)
    act_q = act_q.reshape(n_chan * quarter, chans)

    partial = jnp.dot(act_q, select, preferred_element_type=wide)
    summed = sum_chan(partial.reshape(n_chan, quarter, small))
    picked = lax.all_gather(summed.astype(low), ("chan", "state"), axis=0, tiled=True)
    lowrank = picked[:, :rank]
    entry = picked[:, rank : rank + states].astype(wide)
    readout = picked[:, rank + states :].astype(wide)

    sent = jnp.stack([raw[:, :quarter], gate_q], axis=2)
    moved = to_tokens(swap_state(split_own(sent)))
    inner_own = moved[:, 0].astype(wide) * maskf[:, None]
    gate_own = moved[:, 1].astype(wide)
    kernel_own = mine(conv_kernel, 1)
    offset_own = mine(conv_offset)
    conv_own = offset_own[None, :]
    for index in range(taps):
        lag = taps - 1 - index
        valid = (place >= lag).astype(wide)[:, None]
        shifted = jnp.pad(inner_own, ((lag, 0), (0, 0)))[:tokens]
        conv_own = conv_own + kernel_own[index][None, :] * shifted * valid
    act_own = (jax.nn.silu(conv_own) * maskf[:, None]).astype(low)
    act_wide = act_own.astype(wide)
    weight_own = mine(delta_weight, 1)
    dpre = jnp.dot(lowrank, weight_own, preferred_element_type=wide) + mine(step_bias)[None, :]
    delta = jax.nn.softplus(dpre)
    drive = delta * act_wide
    step = jnp.where((place > 0)[:, None], delta, FAR)
    coeff_two = coeff * math.log2(math.e)
    scanned, kept = forward_scan(step, drive, coeff_two, entry, readout)
    skip_own = mine(skip_weight)
    mixed = scanned + skip_own[None, :] * act_wide
    gate_act = jax.nn.silu(gate_own)
    gated = (mixed * gate_act).astype(low)

    dgated_q = lax.dot_general(grad_q, out_weight, contract_cols, preferred_element_type=wide)
    dgated_q = dgated_q.astype(low).reshape(n_chan, quarter, chans)
    dgated = to_tokens(swap_state(split_own(dgated_q))).astype(wide)
    dmix = dgated * gate_act
    dgate = (dgated * mixed * silu_slope(gate_own)).astype(low)
    skip_grad_own = jnp.sum(dmix * act_wide, axis=0)

    lam_sum, flow_sum, dentry, dread, flow_total = backward_scan(
        step, delta, drive, dmix, coeff_two, entry, readout, kept
    )
    scale = 1.0 / math.log2(math.e)
    decay_grad_own = coeff * flow_total
    ddelta = flow_sum * scale + lam_sum * act_wide
    ddpre = (ddelta * jax.nn.sigmoid(dpre)).astype(low)
    bias_grad_own = jnp.sum(ddpre.astype(wide), axis=0)
    delta_grad_own = lax.dot_general(lowrank, ddpre, contract_rows, preferred_element_type=wide)
    dlow = lax.dot_general(ddpre, weight_own, contract_cols, preferred_element_type=wide)
    partial = jnp.concatenate(
        [dlow, dentry.reshape(tokens, states), dread.reshape(tokens, states)], axis=1
    )
    parts = windows(partial.astype(low), 0, HALO)
    parts = lax.all_to_all(
        parts.reshape((n_chan * n_state,) + parts.shape[2:]),
        ("chan", "state"),
        0,
        0,
        tiled=True,
    )
    dsmall = gather_chan(jnp.sum(parts.astype(wide), axis=0).astype(low))

    gated_all = gather_state(jnp.moveaxis(gated.reshape(n_chan, n_state, quarter, own), 1, 0))
    gated_all = jnp.moveaxis(gated_all, 0, 3).reshape(n_state, n_chan * quarter, chans)
    gated_q = lax.dynamic_index_in_dim(gated_all, part, axis=0, keepdims=False)
    branch = jnp.dot(gated_q, out_weight, preferred_element_type=wide).astype(low)
    branch = sum_chan(branch.reshape(n_chan, quarter, width))
    branch = gather_state(branch.astype(low)).reshape(rows_dev, width)
    result = hidden_in + branch
    grad_all = gather_state(grad_q).reshape(tokens, width)
    out_grad = lax.dot_general(
        gated_all.reshape(tokens, chans), grad_all, contract_rows, preferred_element_type=wide
    )

    reach = quarter + HALO
    dscan = lam_sum * delta + dmix * skip_own[None, :]
    dscan = jnp.swapaxes(windows(dscan.astype(low), 0, HALO), 0, 1)
    dscan_win = join_own(swap_state(dscan)).astype(wide)
    dact = dscan_win + lax.dot_general(
        dsmall.reshape(-1, small), select, contract_cols, preferred_element_type=wide
    ).reshape(n_chan, reach, chans)
    dconv = dact * mask_win[:, HALO:] * silu_slope(conv_win)
    dinner = jnp.zeros((n_chan, quarter, chans), wide)
    kernel_rows = []
    for index in range(taps):
        lag = taps - 1 - index
        valid = (place_win[:, HALO:] >= lag).astype(wide)[..., None]
        masked = dconv * valid
        kernel_rows.append(
            jnp.sum(
                masked[:, :quarter] * inner_win[:, HALO - lag : HALO - lag + quarter], axis=(0, 1)
            )
        )
        dinner = dinner + masked[:, lag : lag + quarter] * conv_kernel[index]
    kernel_rows.append(jnp.sum(dconv[:, :quarter], axis=(0, 1)))
    dinner = (dinner * mask_win[:, HALO : HALO + quarter]).astype(low)
    dgate_q = jnp.swapaxes(dgate.reshape(n_chan, n_state, quarter, own), 0, 1)
    dgate_q = join_own(swap_state(dgate_q))
    dboth = jnp.concatenate([dinner, dgate_q], axis=2).reshape(n_chan * quarter, 2 * chans)

    dnormed = lax.dot_general(dboth, in_flat, contract_cols, preferred_element_type=wide)
    gain_part = jnp.sum(dnormed * normed_q.astype(wide), axis=0)
    dnormed = sum_chan(dnormed.astype(low).reshape(n_chan, quarter, width))
    gain_grad = lax.psum(gain_part, ("chan", "state")) / norm_gain
    dscaled = dnormed * norm_gain[None, :]
    change = inv_rms * (dscaled - scaled * jnp.mean(dscaled * scaled, axis=1, keepdims=True))
    input_grad = cotangent + gather_state(change.astype(low)).reshape(rows_dev, width)

    dboth_all = gather_state(dboth).reshape(tokens, 2 * chans)
    normed_rows = gather_state(normed_q).reshape(tokens, width)
    in_grad = lax.dot_general(
        normed_rows, dboth_all, contract_rows, preferred_element_type=wide
    ).reshape(width, 2, chans)

    dsmall_q = dsmall[:, :quarter].reshape(n_chan * quarter, small)
    select_grad = lax.dot_general(act_q, dsmall_q, contract_rows, preferred_element_type=wide)
    rest = lax.psum((select_grad, jnp.stack(kernel_rows)), "state")
    select_grad, kernel_rows = rest
    rank_grad = select_grad[:, :rank]
    first = rank + part * per_state
    entry_grad = lax.dynamic_slice_in_dim(select_grad, first, per_state, 1)
    read_grad = lax.dynamic_slice_in_dim(select_grad, first + states, per_state, 1)
    kernel_grad = kernel_rows[:taps]
    offset_grad = kernel_rows[taps]
    packed = jnp.concatenate(
        [delta_grad_own, decay_grad_own, bias_grad_own[None], skip_grad_own[None]], axis=0
    )
    packed = jnp.swapaxes(gather_state(packed), 0, 1).reshape(-1, chans)
    delta_grad = packed[:rank]
    decay_grad = lax.dynamic_slice_in_dim(packed, rank + part * per_state, per_state, 0)
    bias_grad = packed[rank + states]
    skip_grad = packed[rank + states + 1]
    return (
        result,
        input_grad,
        gain_grad,
        in_grad,
        kernel_grad,
        offset_grad,
        rank_grad,
        entry_grad,
        read_grad,
        delta_grad,
        bias_grad,
        decay_grad,
        skip_grad,
        out_grad,
    )


def solution(mesh):
    sizes = dict(mesh.shape)
    return jax.shard_map(
        functools.partial(shards, sizes["chan"], sizes["state"]),
        mesh=mesh,
        in_specs=(
            P("chan", None),
            P(),
            P(None, None, "chan"),
            P(None, "chan"),
            P("chan"),
            P("chan", None),
            P("chan", "state"),
            P("chan", "state"),
            P(None, "chan"),
            P("chan"),
            P("state", "chan"),
            P("chan"),
            P("chan", None),
            P(),
            P(),
            P("chan", None),
        ),
        out_specs=(
            P("chan", None),
            P("chan", None),
            P(),
            P(None, None, "chan"),
            P(None, "chan"),
            P("chan"),
            P("chan", None),
            P("chan", "state"),
            P("chan", "state"),
            P(None, "chan"),
            P("chan"),
            P("state", "chan"),
            P("chan"),
            P("chan", None),
        ),
        check_vma=False,
    )
```

```python
import functools
import math

import jax
import jax.numpy as jnp
from jax import lax
from jax.experimental import pallas as pl
from jax.experimental.pallas import tpu as pltpu
from jax.sharding import PartitionSpec as P

epsilon = 1e-05
GROUP = 16
HALO = 4
TAIL = 16
FAR = 1e30
wide = jnp.float32
low = jnp.bfloat16


def positions(lengths, tokens_all):
    ends = jnp.cumsum(lengths)
    begins = ends - lengths
    places = jnp.arange(tokens_all, dtype=jnp.int32)
    opening = jnp.max(jnp.where(begins[:, None] <= places[None, :], begins[:, None], 0), axis=0)
    return places - opening


def silu_slope(values):
    logistic = jax.nn.sigmoid(values)
    return logistic * (1.0 + values * (1.0 - logistic))


def own_block(states):
    row = lax.broadcasted_iota(jnp.int32, (GROUP, GROUP * states), 0)
    col = lax.broadcasted_iota(jnp.int32, (GROUP, GROUP * states), 1)
    return jnp.logical_and(col >= row * states, col < (row + 1) * states)


def spreading(states):
    eye = jnp.eye(states, dtype=low)
    tiled = jnp.tile(eye, (1, GROUP))
    nothing = jnp.zeros_like(tiled)
    return jnp.concatenate(
        [
            jnp.concatenate([tiled, nothing], axis=1),
            jnp.concatenate([nothing, tiled], axis=1),
        ],
        axis=0,
    )


def transposed(values):
    count = values.shape[1]
    row = lax.broadcasted_iota(jnp.int32, (count, count), 0)
    col = lax.broadcasted_iota(jnp.int32, (count, count), 1)
    eye = jnp.where(row == col, 1.0, 0.0).astype(low)
    return lax.dot_general(eye, values, (((1,), (1,)), ((), ())), preferred_element_type=wide)


def forward_body(
    order_ref,
    small_ref,
    pair_ref,
    fresh_ref,
    weight_ref,
    bias_ref,
    skip_ref,
    coeff_ref,
    spread_ref,
    kept_ref,
    mixed_ref,
    gated_ref,
    dpre_ref,
    carry,
    step_all,
    drive_all,
):
    @pl.when(pl.program_id(0) == 0)
    def _():
        carry[...] = jnp.zeros_like(carry)

    coeff = coeff_ref[...]
    states = coeff.shape[0]
    rank = weight_ref.shape[0]
    parts = small_ref.shape[0]
    length = mixed_ref.shape[0]
    quarter = length // parts
    chosen = own_block(states)
    part = order_ref[order_ref.shape[0] - 1]
    small = jnp.concatenate([small_ref[part ^ j, 0] for j in range(parts)], axis=0)
    act = jnp.concatenate([pair_ref[j, 0, 0] for j in range(parts)], axis=0).astype(wide)
    gate = jnp.concatenate([pair_ref[j, 1, 0] for j in range(parts)], axis=0).astype(wide)
    dpre = jnp.dot(small[:, :rank], weight_ref[...], preferred_element_type=wide) + bias_ref[...]
    dpre_ref[...] = dpre
    delta = jax.nn.softplus(dpre)
    step_all[...] = jnp.where(fresh_ref[...] > 0.0, delta, FAR)
    drive_all[...] = delta * act
    pair = small[:, rank:]
    columns = transposed(pair)
    reading = jnp.dot(pair, spread_ref[:, GROUP * states :], preferred_element_type=wide)
    state = carry[...]
    for group in range(length // GROUP):
        base = group * GROUP
        kept = []
        for t in range(base, base + GROUP):
            decay = jnp.exp2(step_all[t : t + 1, :] * coeff)
            state = decay * state + drive_all[t : t + 1, :] * columns[:states, t : t + 1]
            kept.append(state)
        kept_ref[base * states : (base + GROUP) * states, :] = jnp.concatenate(
            kept, axis=0
        ).astype(low)
    carry[...] = state
    for group in range(length // GROUP):
        here = slice(group * GROUP, (group + 1) * GROUP)
        block = kept_ref[group * GROUP * states : (group + 1) * GROUP * states, :]
        weights = jnp.where(chosen, reading[here], 0.0).astype(low)
        mixed_ref[here, :] = jnp.dot(weights, block, preferred_element_type=wide)
    mixed = mixed_ref[...] + skip_ref[...] * act
    mixed_ref[...] = mixed
    gated = (mixed * jax.nn.silu(gate)).astype(low)
    for j in range(parts):
        gated_ref[j, 0] = gated[j * quarter : (j + 1) * quarter]


def backward_body(
    order_ref,
    small_ref,
    pair_ref,
    dgated_ref,
    fresh_ref,
    mixed_ref,
    dpre_ref,
    kept_ref,
    before_ref,
    weight_ref,
    skip_ref,
    coeff_ref,
    spread_ref,
    partial_ref,
    dscan_ref,
    dgate_ref,
    delta_grad_ref,
    decay_ref,
    sums_ref,
    carry,
    step_all,
    drive_all,
    delta_all,
    dmix_all,
    lam_all,
    flow_all,
    lam_sum,
    flow_sum,
    cross_all,
    next_partial,
    next_dscan,
):
    turn = pl.program_id(0)

    @pl.when(turn == 0)
    def _():
        carry[...] = jnp.zeros_like(carry)
        delta_grad_ref[...] = jnp.zeros_like(delta_grad_ref)
        decay_ref[...] = jnp.zeros_like(decay_ref)
        sums_ref[...] = jnp.zeros_like(sums_ref)
        next_partial[...] = jnp.zeros_like(next_partial)
        next_dscan[...] = jnp.zeros_like(next_dscan)

    coeff = coeff_ref[...]
    states = coeff.shape[0]
    rank = weight_ref.shape[0]
    parts = small_ref.shape[0]
    length = mixed_ref.shape[0]
    quarter = length // parts
    spread = spread_ref[...]
    chosen = own_block(states)
    across = (((1,), (1,)), ((), ()))
    down = (((0,), (0,)), ((), ()))
    part = order_ref[order_ref.shape[0] - 1]
    small = jnp.concatenate([small_ref[part ^ j, 0] for j in range(parts)], axis=0)
    act = jnp.concatenate([pair_ref[j, 0, 0] for j in range(parts)], axis=0).astype(wide)
    gate = jnp.concatenate([pair_ref[j, 1, 0] for j in range(parts)], axis=0).astype(wide)
    dgated = jnp.concatenate([dgated_ref[j, 0] for j in range(parts)], axis=0).astype(wide)
    dpre = dpre_ref[...]
    delta = jax.nn.softplus(dpre)
    dmix = dgated * jax.nn.silu(gate)
    dgate = (dgated * mixed_ref[...] * silu_slope(gate)).astype(low)
    for j in range(parts):
        dgate_ref[j, 0] = dgate[j * quarter : (j + 1) * quarter]
    step_all[...] = jnp.where(fresh_ref[...] > 0.0, delta, FAR)
    drive_all[...] = delta * act
    delta_all[...] = delta
    dmix_all[...] = dmix
    pair = small[:, rank:]
    columns = transposed(pair)
    entering = jnp.dot(pair, spread[:, : GROUP * states], preferred_element_type=wide)
    first = jnp.where(turn == pl.num_programs(0) - 1, 0.0, before_ref[...].astype(wide))
    pulled = carry[...]
    summed = decay_ref[...]
    for group in range(length // GROUP - 1, -1, -1):
        base = group * GROUP
        lams = [None] * GROUP
        flows = [None] * GROUP
        rows = slice(base * states, (base + GROUP) * states)
        block = kept_ref[rows, :].astype(wide)
        if group:
            edge = kept_ref[(base - 1) * states : base * states, :].astype(wide)
        else:
            edge = first
        for i in range(GROUP - 1, -1, -1):
            t = base + i
            lam = columns[states:, t : t + 1] * dmix_all[t : t + 1, :] + pulled
            pulled = jnp.exp2(step_all[t : t + 1, :] * coeff) * lam
            flow = pulled * (block[(i - 1) * states : i * states] if i else edge)
            summed = summed + flow * delta_all[t : t + 1, :]
            lams[i] = lam
            flows[i] = flow * coeff
        lam_all[rows, :] = jnp.concatenate(lams, axis=0).astype(low)
        flow_all[rows, :] = jnp.concatenate(flows, axis=0).astype(low)
    carry[...] = pulled
    decay_ref[...] = summed
    ones = jnp.where(chosen, 1.0, 0.0).astype(low)
    for group in range(length // GROUP):
        here = slice(group * GROUP, (group + 1) * GROUP)
        rows = slice(group * GROUP * states, (group + 1) * GROUP * states)
        lam_block = lam_all[rows, :]
        weights = jnp.where(chosen, entering[here], 0.0).astype(low)
        lam_sum[here, :] = jnp.dot(weights, lam_block, preferred_element_type=wide)
        flow_sum[here, :] = jnp.dot(ones, flow_all[rows, :], preferred_element_type=wide)
        cross = lax.dot_general(
            drive_all[here, :].astype(low), lam_block, across, preferred_element_type=wide
        )
        cross_all[here, : GROUP * states] = jnp.where(chosen, cross, 0.0).astype(low)
        cross = lax.dot_general(
            dmix_all[here, :].astype(low), kept_ref[rows, :], across, preferred_element_type=wide
        )
        cross_all[here, GROUP * states :] = jnp.where(chosen, cross, 0.0).astype(low)
    dpair = lax.dot_general(cross_all[...], spread, across, preferred_element_type=wide)
    scale = 1.0 / math.log2(math.e)
    found = lam_sum[...]
    ddelta = flow_sum[...] * scale + found * act
    ddpre = (ddelta * jax.nn.sigmoid(dpre)).astype(low)
    delta_grad_ref[...] += lax.dot_general(
        small[:, :rank], ddpre, down, preferred_element_type=wide
    )
    dlow = lax.dot_general(ddpre, weight_ref[...], across, preferred_element_type=wide)
    dscan = (found * delta + dmix * skip_ref[...]).astype(low)
    sums_ref[0:1, :] += jnp.sum(ddpre.astype(wide), axis=0, keepdims=True)
    sums_ref[1:2, :] += jnp.sum(dmix * act, axis=0, keepdims=True)
    for value, store, after, span in (
        (dlow.astype(low), partial_ref, next_partial, slice(0, rank)),
        (dpair.astype(low), partial_ref, next_partial, slice(rank, rank + 2 * states)),
        (dscan, dscan_ref, next_dscan, slice(0, dscan.shape[1])),
    ):
        longer = jnp.concatenate([value, after[:, span]], axis=0)
        for j in range(parts):
            store[j, 0, :, span] = longer[j * quarter : (j + 1) * quarter + TAIL]
        after[:, span] = value[:TAIL]


def forward_scan(order, small, pair, fresh, weight, bias, skip, coeff, spread):
    parts, _, blocks, quarter, width = pair.shape
    states = coeff.shape[0]
    chunk = parts * quarter
    tokens = blocks * chunk

    def whole(values):
        return pl.BlockSpec(values.shape, lambda t, order: (0, 0))

    row = pl.BlockSpec((chunk, width), lambda t, order: (t, 0))
    return pl.pallas_call(
        forward_body,
        grid_spec=pltpu.PrefetchScalarGridSpec(
            num_scalar_prefetch=1,
            grid=(blocks,),
            in_specs=[
                pl.BlockSpec((parts, 1, quarter, small.shape[-1]), lambda t, order: (0, t, 0, 0)),
                pl.BlockSpec(
                    (parts, 2, 1, quarter, width), lambda t, order: (0, 0, order[t], 0, 0)
                ),
                pl.BlockSpec((chunk, 1), lambda t, order: (t, 0)),
            ]
            + [whole(v) for v in (weight, bias, skip, coeff, spread)],
            out_specs=[
                pl.BlockSpec((chunk * states, width), lambda t, order: (t, 0)),
                row,
                pl.BlockSpec((parts, 1, quarter, width), lambda t, order: (0, order[t], 0, 0)),
                row,
            ],
            scratch_shapes=[
                pltpu.VMEM((states, width), wide),
                pltpu.VMEM((chunk, width), wide),
                pltpu.VMEM((chunk, width), wide),
            ],
        ),
        out_shape=[
            jax.ShapeDtypeStruct((tokens * states, width), low),
            jax.ShapeDtypeStruct((tokens, width), wide),
            jax.ShapeDtypeStruct((parts, blocks, quarter, width), low),
            jax.ShapeDtypeStruct((tokens, width), wide),
        ],
        compiler_params=pltpu.CompilerParams(vmem_limit_bytes=32 * 1024 * 1024),
        name="forward_scan",
    )(order, small, pair, fresh, weight, bias, skip, coeff, spread)


def backward_scan(
    order, small, pair, dgated, fresh, mixed, dpre, kept, weight, skip, coeff, spread
):
    parts, _, blocks, quarter, width = pair.shape
    states = coeff.shape[0]
    rank = weight.shape[0]
    chunk = parts * quarter
    last = blocks - 1

    def whole(shape):
        return pl.BlockSpec(shape, lambda t, order: (0, 0))

    def cut(rows, columns):
        return pl.BlockSpec((parts, 1, rows, columns), lambda t, order: (0, last - t, 0, 0))

    def turned(rows, columns):
        return pl.BlockSpec(
            (parts, 1, rows, columns), lambda t, order: (0, order[last - t], 0, 0)
        )

    row = pl.BlockSpec((chunk, width), lambda t, order: (last - t, 0))
    return pl.pallas_call(
        backward_body,
        grid_spec=pltpu.PrefetchScalarGridSpec(
            num_scalar_prefetch=1,
            grid=(blocks,),
            in_specs=[
                cut(quarter, small.shape[-1]),
                pl.BlockSpec(
                    (parts, 2, 1, quarter, width),
                    lambda t, order: (0, 0, order[last - t], 0, 0),
                ),
                turned(quarter, width),
                pl.BlockSpec((chunk, 1), lambda t, order: (last - t, 0)),
                row,
                row,
                pl.BlockSpec((chunk * states, width), lambda t, order: (last - t, 0)),
                pl.BlockSpec(
                    (states, width),
                    lambda t, order: (jnp.maximum((last - t) * chunk - 1, 0), 0),
                ),
            ]
            + [whole(v.shape) for v in (weight, skip, coeff, spread)],
            out_specs=[
                cut(quarter + TAIL, small.shape[-1]),
                turned(quarter + TAIL, width),
                turned(quarter, width),
                whole((rank, width)),
                whole((states, width)),
                whole((8, width)),
            ],
            scratch_shapes=[pltpu.VMEM((states, width), wide)]
            + [pltpu.VMEM((chunk, width), wide)] * 4
            + [pltpu.VMEM((chunk * states, width), low)] * 2
            + [pltpu.VMEM((chunk, width), wide)] * 2
            + [
                pltpu.VMEM((chunk, 2 * GROUP * states), low),
                pltpu.VMEM((TAIL, small.shape[-1]), low),
                pltpu.VMEM((TAIL, width), low),
            ],
        ),
        out_shape=[
            jax.ShapeDtypeStruct((parts, blocks, quarter + TAIL, small.shape[-1]), low),
            jax.ShapeDtypeStruct((parts, blocks, quarter + TAIL, width), low),
            jax.ShapeDtypeStruct((parts, blocks, quarter, width), low),
            jax.ShapeDtypeStruct((rank, width), wide),
            jax.ShapeDtypeStruct((states, width), wide),
            jax.ShapeDtypeStruct((8, width), wide),
        ],
        compiler_params=pltpu.CompilerParams(vmem_limit_bytes=32 * 1024 * 1024),
        name="backward_scan",
    )(order, small, pair, dgated, fresh, mixed, dpre, kept, kept, weight, skip, coeff, spread)


def interleave_body(order_ref, inner_ref, gate_ref, out_ref):
    out_ref[:, 0, :] = inner_ref[0].astype(wide)
    out_ref[:, 1, :] = gate_ref[0].astype(wide)


def interleave(order, inner, gate):
    parts, rows, width = inner.shape
    block = min(256, rows)
    steps = rows // block
    spec = pl.BlockSpec((1, block, width), lambda p, t, order: (order[p], t, 0))
    return pl.pallas_call(
        interleave_body,
        grid_spec=pltpu.PrefetchScalarGridSpec(
            num_scalar_prefetch=1,
            grid=(parts, steps),
            in_specs=[spec, spec],
            out_specs=pl.BlockSpec(
                (block, 2, width), lambda p, t, order: (p * steps + t, 0, 0)
            ),
        ),
        out_shape=jax.ShapeDtypeStruct((parts * rows, 2, width), wide),
        compiler_params=pltpu.CompilerParams(vmem_limit_bytes=32 * 1024 * 1024),
        name="interleave",
    )(order, inner, gate)


def widen_body(order_ref, value_ref, out_ref):
    out_ref[...] = value_ref[0].astype(wide)


def add_body(order_ref, value_ref, base_ref, out_ref):
    out_ref[...] = base_ref[...] + value_ref[0].astype(wide)


def placed(order, values, base=None):
    parts, rows, width = values.shape
    flat = pl.BlockSpec((rows, width), lambda p, order: (p, 0))
    return pl.pallas_call(
        widen_body if base is None else add_body,
        grid_spec=pltpu.PrefetchScalarGridSpec(
            num_scalar_prefetch=1,
            grid=(parts,),
            in_specs=[pl.BlockSpec((1, rows, width), lambda p, order: (order[p], 0, 0))]
            + ([] if base is None else [flat]),
            out_specs=flat,
        ),
        out_shape=jax.ShapeDtypeStruct((parts * rows, width), wide),
        compiler_params=pltpu.CompilerParams(vmem_limit_bytes=32 * 1024 * 1024),
        name="placed",
    )(order, values, *(() if base is None else (base,)))


class Moves:
    def __init__(self, n_chan, n_state):
        self.n_chan = n_chan
        self.n_state = n_state
        self.near = (n_chan, n_state) == (8, 4)
        self.chan = lax.axis_index("chan")
        self.part = lax.axis_index("state")
        self.z = self.chan // 2
        self.y = self.chan % 2
        places = jnp.arange(n_chan, dtype=jnp.int32)
        if self.near:
            planes = lax.rem(self.z + 4 - places % 4, 4)
            self.blocks = planes * 2 + lax.rem(self.y + places // 4, 2)
            hops = lax.rem(self.z + 4 - places // 2, 4)
            self.order = lax.rem(self.y + places, 2) * 4 + hops
        else:
            self.blocks = places
            self.order = places

    def over_y(self, values):
        return lax.ppermute(values, "chan", [(i, i ^ 1) for i in range(8)])

    def over_z(self, values, hops):
        return lax.ppermute(values, "chan", [(i, (i + 2 * hops) % 8) for i in range(8)])

    def over_state(self, values, bits):
        return lax.ppermute(values, "state", [(i, i ^ bits) for i in range(4)])

    def swap_state(self, values):
        return lax.all_to_all(values, "state", 0, 0, tiled=True)

    def pair(self, bit, own, other):
        return jnp.stack([jnp.where(bit == 0, own, other), jnp.where(bit == 0, other, own)])

    def in_order(self, pieces):
        own, core, across, slant = pieces
        bit = self.part % 2
        near = self.pair(bit, own, core)
        far = self.pair(bit, across, slant)
        return self.pair(self.part // 2, near, far).reshape((4,) + own.shape)

    def pieces_state(self, values):
        core = self.over_state(values, 1)
        across = self.over_state(values, 2)
        return values, core, across, self.over_state(across, 1)

    def gather_state(self, values):
        if not self.near:
            return lax.all_gather(values, "state", axis=0)
        return self.in_order(self.pieces_state(values))

    def gather_near(self, values):
        if not self.near:
            found = lax.all_gather(values, "state", axis=0)
            return jnp.stack(
                [
                    lax.dynamic_index_in_dim(found, self.part ^ k, 0, keepdims=False)
                    for k in range(self.n_state)
                ]
            )
        return jnp.stack(self.pieces_state(values))

    def trade_state(self, values):
        if not self.near:
            return self.swap_state(values)
        chosen = [
            lax.dynamic_index_in_dim(values, self.part ^ k, 0, keepdims=False) for k in range(4)
        ]
        moved = [chosen[0]] + [self.over_state(chosen[k], k) for k in (1, 2, 3)]
        return self.in_order(moved)

    def pieces_chan(self, values):
        own = self.over_y(values)
        along = [self.over_z(values, hops) for hops in (1, 2, 3)]
        own, along[0] = tied(own, along[0])
        return [values] + along + [own] + [self.over_y(piece) for piece in along]

    def gather_chan(self, values):
        if not self.near:
            return lax.all_gather(values, "chan", axis=0)
        return jnp.stack(self.pieces_chan(values))

    def gather_rows(self, values, cut):
        if not self.near:
            found = lax.all_gather(values, "chan", axis=0)
            return found[:, :cut].reshape(-1, values.shape[1]), found[:, cut:]
        pieces = self.pieces_chan(values)
        first = jnp.concatenate([piece[:cut] for piece in pieces], axis=0)
        return first, jnp.stack([piece[cut:] for piece in pieces])

    def in_axis_order(self, values):
        if not self.near:
            return values
        return jnp.stack(
            [
                lax.dynamic_index_in_dim(values, self.order[k], 0, keepdims=False)
                for k in range(self.n_chan)
            ]
        )

    def gather_small(self, values):
        if not self.near:
            return lax.all_gather(values, "chan", axis=0)
        copies = jnp.broadcast_to(values[None], (self.n_chan,) + values.shape)
        return lax.all_to_all(copies, "chan", 0, 0, tiled=True)

    def sum_small(self, parts):
        moved = lax.all_to_all(parts, "chan", 0, 0, tiled=True)
        return jnp.sum(moved.astype(wide), axis=0)

    def joined_planes(self, kept, sent):
        return kept + self.over_y(sent).astype(wide)

    def summed_planes(self, joined):
        total = joined[0]
        for hops in (1, 2, 3):
            total = total + self.over_z(joined[4 - hops].astype(low), hops).astype(wide)
        return total

    def sum_planes(self, kept, sent):
        return self.summed_planes(self.joined_planes(kept, sent))

    def sum_chan(self, parts):
        if not self.near:
            return self.sum_small(parts.astype(low))
        return self.sum_planes(parts[:4], parts[4:].astype(low))

    def sum_row(self, values):
        if not self.near:
            return lax.psum(values, "chan")
        both = values + self.over_y(values)
        total = both
        for hops in (1, 2, 3):
            total = total + self.over_z(both, hops)
        return total

    def sum_state(self, parts):
        if not self.near:
            moved = lax.all_to_all(parts, "state", 0, 0, tiled=True)
            return jnp.sum(moved.astype(wide), axis=0).astype(low)
        cut = parts.reshape((2, 2) + parts.shape[1:])
        core = self.part % 2
        sent = lax.dynamic_index_in_dim(cut, 1 - core, 1, keepdims=False)
        kept = lax.dynamic_index_in_dim(cut, core, 1, keepdims=False)
        chip = (kept.astype(wide) + self.over_state(sent, 1).astype(wide)).astype(low)
        side = self.part // 2
        sent = lax.dynamic_index_in_dim(chip, 1 - side, 0, keepdims=False)
        kept = lax.dynamic_index_in_dim(chip, side, 0, keepdims=False)
        return (kept.astype(wide) + self.over_state(sent, 2).astype(wide)).astype(low)

    def total_state(self, values):
        rows, columns = values.shape
        parts = values.reshape(self.n_state, rows // self.n_state, columns)
        return self.gather_state(self.sum_state(parts)).reshape(rows, columns)


def tied(*values):
    return lax.optimization_barrier(values)


def shards(
    n_chan,
    n_state,
    hidden_in,
    norm_gain,
    in_weight,
    conv_kernel,
    conv_offset,
    select_rank,
    select_entry,
    select_read,
    delta_weight,
    step_bias,
    decay_log,
    skip_weight,
    out_weight,
    lengths,
    pad_mask,
    cotangent,
):
    rows_dev, width = hidden_in.shape
    tokens = pad_mask.shape[0]
    chans = in_weight.shape[2]
    taps = conv_kernel.shape[0]
    rank = select_rank.shape[1]
    per_state = select_entry.shape[1]
    states = per_state * n_state
    small = rank + 2 * states
    quarter = rows_dev // n_state
    own = chans // n_state
    rows_q = n_chan * quarter
    part = lax.axis_index("state")
    contract_rows = (((0,), (0,)), ((), ()))
    contract_cols = (((1,), (1,)), ((), ()))
    moves = Moves(n_chan, n_state)
    blocks = moves.blocks
    order = jnp.concatenate([moves.order, part[None]]).astype(jnp.int32)

    def mine(values, axis=0):
        return lax.dynamic_slice_in_dim(values, part * own, own, axis)

    def split_own(values):
        cut = values.reshape(values.shape[:-1] + (n_state, own))
        return jnp.moveaxis(cut, -2, 0)

    def join_own(values):
        moved = jnp.moveaxis(values, 0, -2)
        return moved.reshape(moved.shape[:-2] + (chans,))

    def chosen_rows(chooser, values):
        flat = values.reshape(values.shape[0], -1)
        found = jnp.dot(chooser, flat, precision=lax.Precision.HIGHEST)
        return found.reshape(values.shape)

    start = part * quarter
    hidden_q = lax.dynamic_slice_in_dim(hidden_in, start, quarter, 0)
    ahead = lax.rem(start + rows_dev - HALO, rows_dev)
    behind = lax.rem(start + quarter, rows_dev)
    local = jnp.concatenate(
        [
            hidden_q,
            lax.dynamic_slice_in_dim(hidden_in, ahead, HALO, 0),
            lax.dynamic_slice_in_dim(hidden_in, behind, HALO, 0),
        ],
        axis=0,
    )
    inv_all = lax.rsqrt(jnp.mean(local * local, axis=1, keepdims=True) + epsilon)
    scaled_all = local * inv_all
    normed_all = (scaled_all * norm_gain[None, :]).astype(low)
    inv_rms = inv_all[:quarter]
    scaled = scaled_all[:quarter]
    normed_q, normed_side = moves.gather_rows(normed_all, quarter)
    cot_q = lax.dynamic_slice_in_dim(cotangent, start, quarter, 0).astype(low)
    grad_q = lax.all_gather(cot_q, "chan", axis=0)

    place = positions(lengths, tokens)
    flags = [pad_mask.astype(wide)]
    flags += [(place >= lag).astype(wide) for lag in range(1, taps)]
    flags = jnp.stack(flags)
    padded = jnp.pad(flags, ((0, 0), (HALO, HALO + rows_dev)))
    span = quarter + 2 * HALO
    flags_win = lax.dynamic_slice_in_dim(padded, start, n_chan * rows_dev, 1)
    flags_win = flags_win.reshape(taps, n_chan, rows_dev)[:, :, :span]
    chooser = (blocks[:, None] == jnp.arange(n_chan)[None, :]).astype(wide)
    flags_win = jnp.einsum("kb,fbr->fkr", chooser, flags_win)
    mask_win = flags_win[0][:, :, None]
    valid_win = flags_win[1:]
    one_before = (blocks[:, None] - 1 == blocks[None, :]).astype(wide)
    one_after = (blocks[:, None] + 1 == blocks[None, :]).astype(wide)
    itself = jnp.eye(n_chan, dtype=wide)
    one_before = jnp.where(part == 0, one_before, itself)
    one_after = jnp.where(part == n_state - 1, one_after, itself)

    def valid_at(lag, first, count):
        if lag == 0:
            return 1.0
        return valid_win[lag - 1][:, first : first + count, None]

    columns = jnp.concatenate([select_entry, select_read], axis=1)
    columns = moves.gather_state(columns).reshape(n_state, chans, 2, per_state)
    columns = jnp.transpose(columns, (1, 2, 0, 3)).reshape(chans, 2 * states)
    select = jnp.concatenate([select_rank, columns], axis=1)
    decay_own = moves.swap_state(jnp.swapaxes(decay_log.reshape(per_state, n_state, own), 0, 1))
    coeff = -jnp.exp(decay_own.reshape(states, own))

    in_flat = lax.optimization_barrier(in_weight.reshape(width, 2 * chans))
    both = jnp.dot(normed_q, in_flat, preferred_element_type=wide)
    both = both.reshape(n_chan, quarter, 2 * chans)
    gate_q = both[:, :, chans:].astype(low)
    sides = jnp.dot(
        normed_side.reshape(-1, width), in_flat[:, :chans], preferred_element_type=wide
    ).reshape(n_chan, 2 * HALO, chans)
    before = chosen_rows(one_before, sides[:, :HALO])
    after = chosen_rows(one_after, sides[:, HALO:])
    inner_win = jnp.concatenate([before, both[:, :, :chans], after], axis=1) * mask_win

    reach = quarter + HALO
    conv_win = conv_offset
    for index in range(taps):
        lag = taps - 1 - index
        shifted = inner_win[:, HALO - lag : HALO - lag + reach]
        conv_win = conv_win + conv_kernel[index] * shifted * valid_at(lag, HALO, reach)
    act_win = jax.nn.silu(conv_win[:, :quarter]) * mask_win[:, HALO : HALO + quarter]
    act_win = act_win.astype(low)
    act_q = act_win.reshape(rows_q, chans)

    partial = jnp.dot(act_q, select, preferred_element_type=wide)
    summed = moves.sum_chan(partial.reshape(n_chan, quarter, small)).astype(low)
    sent = jnp.stack([split_own(act_win), split_own(gate_q)], axis=1)
    channels = moves.swap_state(sent)
    summed, channels = tied(summed, channels)
    picked = moves.gather_near(moves.gather_small(summed))

    if moves.near:
        grad_q = jnp.concatenate(
            [lax.dynamic_index_in_dim(grad_q, blocks[k], 0, keepdims=False) for k in range(8)],
            axis=0,
        )
    grad_q = grad_q.reshape(rows_q, width)
    dgated_q = lax.dot_general(grad_q, out_weight, contract_cols, preferred_element_type=wide)
    dgated_q = dgated_q.astype(low).reshape(n_chan, quarter, chans)
    dgated = moves.swap_state(split_own(dgated_q))
    picked, dgated = tied(picked, dgated)

    weight_own = mine(delta_weight, 1)
    bias_own = mine(step_bias)[None, :]
    skip_own = mine(skip_weight)[None, :]
    fresh = (place > 0).astype(wide)[:, None]
    spread = spreading(states)
    coeff_two = coeff * math.log2(math.e)
    kept, mixed, gated, dpre = forward_scan(
        order, picked, channels, fresh, weight_own, bias_own, skip_own, coeff_two, spread
    )

    gated_q = join_own(moves.trade_state(gated)).reshape(rows_q, chans)
    partial, dscan, dgate, delta_grad_own, decay_total, sums = backward_scan(
        order,
        picked,
        channels,
        dgated,
        fresh,
        mixed,
        dpre,
        kept,
        weight_own,
        skip_own,
        coeff_two,
        spread,
    )
    decay_grad_own = coeff * decay_total
    partial, gated_q = tied(partial, gated_q)
    partial = moves.sum_state(partial)

    branch = jnp.dot(gated_q, out_weight, preferred_element_type=wide)
    out_part = lax.dot_general(gated_q, grad_q, contract_rows, preferred_element_type=wide)
    packed = jnp.concatenate([delta_grad_own, decay_grad_own, sums], axis=0)
    partial, branch, out_part, packed, dscan, dgate = tied(
        partial, branch.astype(low), out_part.astype(low), packed, dscan, dgate
    )
    dsmall = moves.gather_chan(moves.sum_small(partial).astype(low))[:, :reach]
    dscan_win = join_own(moves.trade_state(dscan))[:, :reach].astype(wide)
    dgate_q = join_own(moves.trade_state(dgate)).reshape(rows_q, chans)
    gate_part = lax.dot_general(normed_q, dgate_q, contract_rows, preferred_element_type=wide)
    branch = lax.psum_scatter(
        moves.in_axis_order(branch.reshape(n_chan, quarter, width)).reshape(rows_q, width),
        "chan",
        scatter_dimension=0,
        tiled=True,
    )
    out_grad = moves.total_state(out_part).astype(wide)
    dsmall, dscan_win, dgate_q, gate_part = tied(
        dsmall, dscan_win, dgate_q, gate_part.astype(low)
    )

    dact = dscan_win + lax.dot_general(
        dsmall.reshape(-1, small), select, contract_cols, preferred_element_type=wide
    ).reshape(n_chan, reach, chans)
    dconv = dact * mask_win[:, HALO:] * silu_slope(conv_win)
    dinner = jnp.zeros((n_chan, quarter, chans), wide)
    kernel_rows = []
    for index in range(taps):
        lag = taps - 1 - index
        masked = dconv * valid_at(lag, HALO, reach)
        shifted = inner_win[:, HALO - lag : HALO - lag + quarter]
        kernel_rows.append(jnp.sum(masked[:, :quarter] * shifted, axis=(0, 1)))
        dinner = dinner + masked[:, lag : lag + quarter] * conv_kernel[index]
    kernel_rows.append(jnp.sum(dconv[:, :quarter], axis=(0, 1)))
    dinner = (dinner * mask_win[:, HALO : HALO + quarter]).astype(low).reshape(rows_q, chans)
    dboth = jnp.concatenate([dinner, dgate_q], axis=1)

    def backed(rows, weight):
        return lax.dot_general(rows, weight, contract_cols, preferred_element_type=wide)

    if moves.near:
        half = width // 2
        joined = []
        gains = []
        for columns in (slice(0, half), slice(half, width)):
            gain = jnp.zeros((half,), wide)
            halves = []
            for rows in (slice(rows_q // 2, rows_q), slice(0, rows_q // 2)):
                piece = backed(dboth[rows], in_flat[columns])
                gain = gain + jnp.sum(piece * normed_q[rows, columns].astype(wide), axis=0)
                halves.append(piece.reshape(4, quarter, half))
            joined.append(moves.joined_planes(halves[1], halves[0].astype(low)))
            gains.append(gain)
        joined[0], gains[0], gains[1], dinner = tied(joined[0], gains[0], gains[1], dinner)
        dnormed = jnp.concatenate([moves.summed_planes(v) for v in joined], axis=1)
        gain_part = jnp.concatenate(gains)
    else:
        dnormed = backed(dboth, in_flat)
        gain_part = jnp.sum(dnormed * normed_q.astype(wide), axis=0)
        dnormed = moves.sum_chan(dnormed.reshape(n_chan, quarter, width))
    gain_part = moves.sum_row(gain_part)[None]
    dscaled = dnormed * norm_gain[None, :]
    change = inv_rms * (dscaled - scaled * jnp.mean(dscaled * scaled, axis=1, keepdims=True))
    change = moves.gather_state(jnp.concatenate([change, gain_part], axis=0).astype(low))
    input_grad = cotangent + change[:, :quarter].reshape(rows_dev, width)
    gain_grad = jnp.sum(change[:, quarter].astype(wide), axis=0) / norm_gain

    result = hidden_in + moves.gather_state(branch).reshape(rows_dev, width)
    inner_part = lax.dot_general(normed_q, dinner, contract_rows, preferred_element_type=wide)
    gate_grad = moves.total_state(gate_part)
    in_grad = interleave(
        jnp.arange(n_state, dtype=jnp.int32),
        moves.total_state(inner_part.astype(low)).reshape(n_state, -1, chans),
        gate_grad.reshape(n_state, -1, chans),
    )

    dsmall_q = dsmall[:, :quarter].reshape(rows_q, small)
    select_grad = lax.dot_general(dsmall_q, act_q, contract_rows, preferred_element_type=wide)
    rest = moves.gather_near(jnp.concatenate([select_grad, jnp.stack(kernel_rows)], axis=0))
    rest = jnp.sum(rest, axis=0)
    rank_grad = rest[:rank].T
    first = rank + part * per_state
    entry_grad = lax.dynamic_slice_in_dim(rest, first, per_state, 0).T
    read_grad = lax.dynamic_slice_in_dim(rest, first + states, per_state, 0).T
    kernel_grad = rest[small : small + taps]
    offset_grad = rest[small + taps]
    packed = jnp.swapaxes(moves.gather_state(packed), 0, 1).reshape(-1, chans)
    delta_grad = packed[:rank]
    decay_grad = lax.dynamic_slice_in_dim(packed, rank + part * per_state, per_state, 0)
    bias_grad = packed[rank + states]
    skip_grad = packed[rank + states + 1]
    return (
        result,
        input_grad,
        gain_grad,
        in_grad,
        kernel_grad,
        offset_grad,
        rank_grad,
        entry_grad,
        read_grad,
        delta_grad,
        bias_grad,
        decay_grad,
        skip_grad,
        out_grad,
    )


def near_shards(
    n_chan,
    n_state,
    hidden_in,
    norm_gain,
    in_weight,
    conv_kernel,
    conv_offset,
    select_rank,
    select_entry,
    select_read,
    delta_weight,
    step_bias,
    decay_log,
    skip_weight,
    out_weight,
    lengths,
    pad_mask,
    cotangent,
):
    rows_dev, width = hidden_in.shape
    tokens = pad_mask.shape[0]
    chans = in_weight.shape[2]
    taps = conv_kernel.shape[0]
    rank = select_rank.shape[1]
    per_state = select_entry.shape[1]
    states = per_state * n_state
    small = rank + 2 * states
    quarter = rows_dev // n_state
    own = chans // n_state
    rows_q = n_chan * quarter
    part = lax.axis_index("state")
    contract_rows = (((0,), (0,)), ((), ()))
    contract_cols = (((1,), (1,)), ((), ()))
    moves = Moves(n_chan, n_state)
    blocks = moves.blocks
    order = jnp.concatenate([moves.order, part[None]]).astype(jnp.int32)

    def mine(values, axis=0):
        return lax.dynamic_slice_in_dim(values, part * own, own, axis)

    def split_own(values):
        cut = values.reshape(values.shape[:-1] + (n_state, own))
        return jnp.moveaxis(cut, -2, 0)

    def join_own(values):
        moved = jnp.moveaxis(values, 0, -2)
        return moved.reshape(moved.shape[:-2] + (chans,))

    def chosen_rows(chooser, values):
        flat = values.reshape(values.shape[0], -1)
        found = jnp.dot(chooser, flat, precision=lax.Precision.HIGHEST)
        return found.reshape(values.shape)

    start = part * quarter
    hidden_q = lax.dynamic_slice_in_dim(hidden_in, start, quarter, 0)
    ahead = lax.rem(start + rows_dev - HALO, rows_dev)
    behind = lax.rem(start + quarter, rows_dev)
    local = jnp.concatenate(
        [
            hidden_q,
            lax.dynamic_slice_in_dim(hidden_in, ahead, HALO, 0),
            lax.dynamic_slice_in_dim(hidden_in, behind, HALO, 0),
        ],
        axis=0,
    )
    inv_all = lax.rsqrt(jnp.mean(local * local, axis=1, keepdims=True) + epsilon)
    scaled_all = local * inv_all
    normed_all = (scaled_all * norm_gain[None, :]).astype(low)
    inv_rms = inv_all[:quarter]
    scaled = scaled_all[:quarter]
    cot_q = lax.dynamic_slice_in_dim(cotangent, start, quarter, 0).astype(low)
    ranks = part ^ jnp.arange(n_state, dtype=jnp.int32)

    def picks(values):
        return [
            lax.dynamic_index_in_dim(values, part ^ k, 0, keepdims=False) for k in range(4)
        ]

    def trades(values):
        return [values[0]] + [moves.over_state(values[k], k) for k in (1, 2, 3)]

    def core_halves(values):
        cut = values.reshape((2, 2) + values.shape[1:])
        core = part % 2
        return (
            lax.dynamic_index_in_dim(cut, 1 - core, 1, keepdims=False),
            lax.dynamic_index_in_dim(cut, core, 1, keepdims=False),
        )

    def chip_halves(values):
        side = part // 2
        return (
            lax.dynamic_index_in_dim(values, 1 - side, 0, keepdims=False),
            lax.dynamic_index_in_dim(values, side, 0, keepdims=False),
        )

    def added(kept, came):
        return (kept.astype(wide) + came.astype(wide)).astype(low)

    columns = jnp.concatenate([select_entry, select_read], axis=1)
    decay_cut = jnp.swapaxes(decay_log.reshape(per_state, n_state, own), 0, 1)
    across = moves.over_y(normed_all)
    along = [moves.over_z(normed_all, hops) for hops in (1, 2, 3)]
    columns_core = moves.over_state(columns, 1)
    columns_chip = moves.over_state(columns, 2)
    decay_own = moves.swap_state(decay_cut)
    in_flat = in_weight.reshape(width, 2 * chans)
    across, along[0], along[1], along[2], columns_core, columns_chip, decay_own, in_flat, cot_q = tied(
        across, *along, columns_core, columns_chip, decay_own, in_flat, cot_q
    )
    over = [moves.over_y(piece) for piece in along]
    grads = [cot_q] + [moves.over_z(cot_q, hops) for hops in (1, 2, 3)]
    columns_slant = moves.over_state(columns_chip, 1)
    over[0], over[1], over[2], grads[1], grads[2], grads[3], columns_slant = tied(
        *over, *grads[1:], columns_slant
    )
    pieces = [normed_all] + along + [across] + over
    normed_q = jnp.concatenate([piece[:quarter] for piece in pieces], axis=0)
    normed_side = jnp.stack([piece[quarter:] for piece in pieces])
    grads = grads + [moves.over_y(piece) for piece in grads]

    place = positions(lengths, tokens)
    flags = [pad_mask.astype(wide)]
    flags += [(place >= lag).astype(wide) for lag in range(1, taps)]
    flags = jnp.stack(flags)
    padded = jnp.pad(flags, ((0, 0), (HALO, HALO + rows_dev)))
    span = quarter + 2 * HALO
    flags_win = lax.dynamic_slice_in_dim(padded, start, n_chan * rows_dev, 1)
    flags_win = flags_win.reshape(taps, n_chan, rows_dev)[:, :, :span]
    chooser = (blocks[:, None] == jnp.arange(n_chan)[None, :]).astype(wide)
    flags_win = jnp.einsum("kb,fbr->fkr", chooser, flags_win)
    mask_win = flags_win[0][:, :, None]
    valid_win = flags_win[1:]
    one_before = (blocks[:, None] - 1 == blocks[None, :]).astype(wide)
    one_after = (blocks[:, None] + 1 == blocks[None, :]).astype(wide)
    itself = jnp.eye(n_chan, dtype=wide)
    one_before = jnp.where(part == 0, one_before, itself)
    one_after = jnp.where(part == n_state - 1, one_after, itself)

    def valid_at(lag, first, count):
        if lag == 0:
            return 1.0
        return valid_win[lag - 1][:, first : first + count, None]

    columns = moves.in_order((columns, columns_core, columns_chip, columns_slant))
    columns = columns.reshape(n_state, chans, 2, per_state)
    columns = jnp.transpose(columns, (1, 2, 0, 3)).reshape(chans, 2 * states)
    select = jnp.concatenate([select_rank, columns], axis=1)
    coeff = -jnp.exp(decay_own.reshape(states, own))

    both = jnp.dot(normed_q, in_flat, preferred_element_type=wide)
    both = both.reshape(n_chan, quarter, 2 * chans)
    gate_q = both[:, :, chans:].astype(low)
    sides = jnp.dot(
        normed_side.reshape(-1, width), in_flat[:, :chans], preferred_element_type=wide
    ).reshape(n_chan, 2 * HALO, chans)
    before = chosen_rows(one_before, sides[:, :HALO])
    after = chosen_rows(one_after, sides[:, HALO:])
    inner_win = jnp.concatenate([before, both[:, :, :chans], after], axis=1) * mask_win

    reach = quarter + HALO
    conv_win = conv_offset
    for index in range(taps):
        lag = taps - 1 - index
        shifted = inner_win[:, HALO - lag : HALO - lag + reach]
        conv_win = conv_win + conv_kernel[index] * shifted * valid_at(lag, HALO, reach)
    act_win = jax.nn.silu(conv_win[:, :quarter]) * mask_win[:, HALO : HALO + quarter]
    act_win = act_win.astype(low)
    act_q = act_win.reshape(rows_q, chans)

    sent = jnp.stack([split_own(act_win), split_own(gate_q)], axis=1)
    channels = moves.swap_state(sent)
    partial = jnp.dot(act_q, select, preferred_element_type=wide)
    partial = partial.reshape(n_chan, quarter, small)
    partial = moves.joined_planes(partial[:4], partial[4:].astype(low))
    summed = moves.summed_planes(partial).astype(low)
    summed, channels, grads[4], grads[5], grads[6], grads[7] = tied(summed, channels, *grads[4:])
    grad_q = jnp.concatenate(grads, axis=0)
    dgated_q = lax.dot_general(grad_q, out_weight, contract_cols, preferred_element_type=wide)
    dgated_q = split_own(dgated_q.astype(low).reshape(n_chan, quarter, chans))
    picked = moves.gather_small(summed)
    picked, dgated_q = tied(picked, dgated_q)
    picked = moves.gather_near(picked)
    dgated = moves.swap_state(dgated_q)
    picked, dgated = tied(picked, dgated)

    weight_own = mine(delta_weight, 1)
    bias_own = mine(step_bias)[None, :]
    skip_own = mine(skip_weight)[None, :]
    fresh = (place > 0).astype(wide)[:, None]
    spread = spreading(states)
    coeff_two = coeff * math.log2(math.e)
    kept, mixed, gated, dpre = forward_scan(
        order, picked, channels, fresh, weight_own, bias_own, skip_own, coeff_two, spread
    )

    gated = trades(picks(gated))
    partial, dscan, dgate, delta_grad_own, decay_total, sums = backward_scan(
        order,
        picked,
        channels,
        dgated,
        fresh,
        mixed,
        dpre,
        kept,
        weight_own,
        skip_own,
        coeff_two,
        spread,
    )
    decay_grad_own = coeff * decay_total
    packed = jnp.concatenate([delta_grad_own, decay_grad_own, sums], axis=0)
    partial, packed, dscan, dgate, *gated = tied(partial, packed, dscan, dgate, *gated)
    gated_q = join_own(moves.in_order(gated)).reshape(rows_q, chans)

    sent, kept = core_halves(partial)
    came = moves.over_state(sent, 1)
    out_part = lax.dot_general(gated_q, grad_q, contract_rows, preferred_element_type=wide)
    out_part = out_part.astype(low).reshape(n_state, own, width)
    branch = jnp.dot(gated_q, out_weight, preferred_element_type=wide).astype(low)
    branch = moves.in_axis_order(branch.reshape(n_chan, quarter, width)).reshape(rows_q, width)
    came, out_part, branch = tied(came, out_part, branch)
    branch = lax.psum_scatter(branch, "chan", scatter_dimension=0, tiled=True)
    sent, kept = chip_halves(added(kept, came))
    came = moves.over_state(sent, 2)
    sent, out_kept = core_halves(out_part)
    out_came = moves.over_state(sent, 1)
    packed_core = moves.over_state(packed, 1)
    packed_chip = moves.over_state(packed, 2)
    came, out_came, packed_core, packed_chip, dscan, dgate = tied(
        came, out_came, packed_core, packed_chip, dscan, dgate
    )
    partial = added(kept, came)
    out_part = added(out_kept, out_came)
    packed_slant = moves.over_state(packed_chip, 1)
    dscan = trades(picks(dscan))
    dgate = trades(picks(dgate))
    partial = moves.sum_small(partial).astype(low)
    partial, packed_slant, out_part, *both = tied(partial, packed_slant, out_part, *dscan, *dgate)
    dscan = both[:4]
    dgate_q = join_own(moves.in_order(both[4:])).reshape(rows_q, chans)
    dscan_win = join_own(moves.in_order(dscan))[:, :reach].astype(wide)
    along = [moves.over_z(partial, hops) for hops in (1, 2, 3)]
    across = moves.over_y(partial)
    sent, out_kept = chip_halves(out_part)
    out_came = moves.over_state(sent, 2)
    gate_part = lax.dot_general(normed_q, dgate_q, contract_rows, preferred_element_type=wide)
    gain = jnp.sum(gate_part * in_flat[:, chans:].astype(wide), axis=1)
    gate_part = gate_part.astype(low).reshape(n_state, -1, chans)
    across, along[0], along[1], along[2], gate_part, gain = tied(across, *along, gate_part, gain)
    over = [moves.over_y(piece) for piece in along]
    over[0], over[1], over[2], out_came, gate_part = tied(*over, out_came, gate_part)
    dsmall = jnp.stack([partial] + along + [across] + over)[:, :reach]
    out_part = added(out_kept, out_came)
    out_core = moves.over_state(out_part, 1)
    out_chip = moves.over_state(out_part, 2)
    sent, gate_kept = core_halves(gate_part)
    gate_came = moves.over_state(sent, 1)

    dact = dscan_win + lax.dot_general(
        dsmall.reshape(-1, small), select, contract_cols, preferred_element_type=wide
    ).reshape(n_chan, reach, chans)
    dconv = dact * mask_win[:, HALO:] * silu_slope(conv_win)
    dinner = jnp.zeros((n_chan, quarter, chans), wide)
    kernel_rows = []
    for index in range(taps):
        lag = taps - 1 - index
        masked = dconv * valid_at(lag, HALO, reach)
        shifted = inner_win[:, HALO - lag : HALO - lag + quarter]
        kernel_rows.append(jnp.sum(masked[:, :quarter] * shifted, axis=(0, 1)))
        dinner = dinner + masked[:, lag : lag + quarter] * conv_kernel[index]
    kernel_rows.append(jnp.sum(dconv[:, :quarter], axis=(0, 1)))
    dinner = (dinner * mask_win[:, HALO : HALO + quarter]).astype(low).reshape(rows_q, chans)
    dboth = jnp.concatenate([dinner, dgate_q], axis=1)

    def backed(rows, weight):
        return lax.dot_general(rows, weight, contract_cols, preferred_element_type=wide)

    half = width // 2
    first, second = slice(0, half), slice(half, width)
    other, same = slice(rows_q // 2, rows_q), slice(0, rows_q // 2)

    def plane(rows, columns):
        return backed(dboth[rows], in_flat[columns]).reshape(4, quarter, half)

    first_came = moves.over_y(plane(other, first).astype(low))
    second_came = moves.over_y(plane(other, second).astype(low))
    first_kept = plane(same, first)
    second_kept = plane(same, second)
    inner_part = lax.dot_general(normed_q, dinner, contract_rows, preferred_element_type=wide)
    gain = gain + jnp.sum(inner_part * in_flat[:, :chans].astype(wide), axis=1)
    inner_part = inner_part.astype(low).reshape(n_state, -1, chans)
    dsmall_q = dsmall[:, :quarter].reshape(rows_q, small)
    select_grad = lax.dot_general(dsmall_q, act_q, contract_rows, preferred_element_type=wide)
    rest = jnp.concatenate([select_grad, jnp.stack(kernel_rows)], axis=0)
    gate_part = added(gate_kept, gate_came)
    sent, gate_kept = chip_halves(gate_part)
    gate_came = moves.over_state(sent, 2)
    first_came, gate_came, out_core, out_chip, inner_part, gain, rest = tied(
        first_came, gate_came, out_core, out_chip, inner_part, gain, rest
    )

    joined = first_kept + first_came.astype(wide)
    first_sum = joined[0]
    first_along = [moves.over_z(joined[4 - hops].astype(low), hops) for hops in (1, 2, 3)]
    out_slant = moves.over_state(out_chip, 1)
    sent, inner_kept = core_halves(inner_part)
    inner_came = moves.over_state(sent, 1)
    gate_part = added(gate_kept, gate_came)
    gate_core = moves.over_state(gate_part, 1)
    gate_chip = moves.over_state(gate_part, 2)
    gain_came = moves.over_state(gain, 1)
    rest_core = moves.over_state(rest, 1)
    second_came, inner_came, gain_came, out_slant, rest_core = tied(
        second_came, inner_came, gain_came, out_slant, rest_core
    )

    joined = second_kept + second_came.astype(wide)
    second_sum = joined[0]
    second_along = [moves.over_z(joined[4 - hops].astype(low), hops) for hops in (1, 2, 3)]
    inner_part = added(inner_kept, inner_came)
    sent, inner_kept = chip_halves(inner_part)
    inner_came = moves.over_state(sent, 2)
    gain = gain + gain_came
    gain_came = moves.over_state(gain, 2)
    rest = rest + rest_core
    rest_chip = moves.over_state(rest, 2)
    out_grad = placed(ranks, jnp.stack([out_part, out_core, out_chip, out_slant]))
    tie = tied(
        *first_along, *second_along, inner_came, gate_core, gate_chip, gain_came, rest_chip, branch
    )
    first_along, second_along = tie[:3], tie[3:6]
    inner_came, gate_core, gate_chip, gain_came, rest_chip, branch = tie[6:]

    for piece in first_along:
        first_sum = first_sum + piece.astype(wide)
    for piece in second_along:
        second_sum = second_sum + piece.astype(wide)
    dnormed = jnp.concatenate([first_sum, second_sum], axis=1)
    dscaled = dnormed * norm_gain[None, :]
    change = inv_rms * (dscaled - scaled * jnp.mean(dscaled * scaled, axis=1, keepdims=True))
    change = change.astype(low)
    change_chip = moves.over_state(change, 2)
    change_core = moves.over_state(change, 1)
    inner_part = added(inner_kept, inner_came)
    inner_chip = moves.over_state(inner_part, 2)
    inner_core = moves.over_state(inner_part, 1)
    branch_chip = moves.over_state(branch, 2)
    branch_core = moves.over_state(branch, 1)
    gate_slant = moves.over_state(gate_chip, 1)
    gain = gain + gain_came
    gain_came = moves.over_y(gain)
    tie = tied(
        change_chip, change_core, inner_chip, inner_core, branch_chip, branch_core, gate_slant, gain_came
    )
    change_chip, change_core, inner_chip, inner_core, branch_chip, branch_core = tie[:6]
    gate_slant, gain_came = tie[6:]
    gain = gain + gain_came
    gains = [moves.over_z(gain, hops) for hops in (1, 2, 3)]
    change_slant = moves.over_state(change_chip, 1)
    inner_slant = moves.over_state(inner_chip, 1)
    branch_slant = moves.over_state(branch_chip, 1)
    input_grad = placed(
        ranks, jnp.stack([change, change_core, change_chip, change_slant]), cotangent
    )
    result = placed(ranks, jnp.stack([branch, branch_core, branch_chip, branch_slant]), hidden_in)
    gain_grad = (gain + gains[0] + gains[1] + gains[2]) / norm_gain
    in_grad = interleave(
        ranks,
        jnp.stack([inner_part, inner_core, inner_chip, inner_slant]),
        jnp.stack([gate_part, gate_core, gate_chip, gate_slant]),
    )

    rest = rest + rest_chip
    rank_grad = rest[:rank].T
    first = rank + part * per_state
    entry_grad = lax.dynamic_slice_in_dim(rest, first, per_state, 0).T
    read_grad = lax.dynamic_slice_in_dim(rest, first + states, per_state, 0).T
    kernel_grad = rest[small : small + taps]
    offset_grad = rest[small + taps]
    packed = moves.in_order((packed, packed_core, packed_chip, packed_slant))
    packed = jnp.swapaxes(packed, 0, 1).reshape(-1, chans)
    delta_grad = packed[:rank]
    decay_grad = lax.dynamic_slice_in_dim(packed, rank + part * per_state, per_state, 0)
    bias_grad = packed[rank + states]
    skip_grad = packed[rank + states + 1]
    return (
        result,
        input_grad,
        gain_grad,
        in_grad,
        kernel_grad,
        offset_grad,
        rank_grad,
        entry_grad,
        read_grad,
        delta_grad,
        bias_grad,
        decay_grad,
        skip_grad,
        out_grad,
    )


def solution(mesh):
    sizes = dict(mesh.shape)
    program = near_shards if (sizes["chan"], sizes["state"]) == (8, 4) else shards
    return jax.shard_map(
        functools.partial(program, sizes["chan"], sizes["state"]),
        mesh=mesh,
        in_specs=(
            P("chan", None),
            P(),
            P(None, None, "chan"),
            P(None, "chan"),
            P("chan"),
            P("chan", None),
            P("chan", "state"),
            P("chan", "state"),
            P(None, "chan"),
            P("chan"),
            P("state", "chan"),
            P("chan"),
            P("chan", None),
            P(),
            P(),
            P("chan", None),
        ),
        out_specs=(
            P("chan", None),
            P("chan", None),
            P(),
            P(None, None, "chan"),
            P(None, "chan"),
            P("chan"),
            P("chan", None),
            P("chan", "state"),
            P("chan", "state"),
            P(None, "chan"),
            P("chan"),
            P("state", "chan"),
            P("chan"),
            P("chan", None),
        ),
        check_vma=False,
    )
```

```python
import functools
import math

import jax
import jax.numpy as jnp
from jax import lax
from jax.experimental import pallas as pl
from jax.experimental.pallas import tpu as pltpu
from jax.sharding import PartitionSpec as P

epsilon = 1e-05
GROUP = 16
HALO = 4
TAIL = 16
FAR = 1e30
wide = jnp.float32
low = jnp.bfloat16


def spent(microseconds):
    moved = int(microseconds * 3.6e6)
    return pl.CostEstimate(flops=0, bytes_accessed=moved, transcendentals=0)


def in_hbm(values):
    return pltpu.with_memory_space_constraint(values, pltpu.HBM)


def positions(lengths, tokens_all):
    ends = jnp.cumsum(lengths)
    begins = ends - lengths
    places = jnp.arange(tokens_all, dtype=jnp.int32)
    opening = jnp.max(jnp.where(begins[:, None] <= places[None, :], begins[:, None], 0), axis=0)
    return places - opening


def silu_slope(values):
    logistic = jax.nn.sigmoid(values)
    return logistic * (1.0 + values * (1.0 - logistic))


def own_block(states):
    row = lax.broadcasted_iota(jnp.int32, (GROUP, GROUP * states), 0)
    col = lax.broadcasted_iota(jnp.int32, (GROUP, GROUP * states), 1)
    return jnp.logical_and(col >= row * states, col < (row + 1) * states)


def spreading(states):
    eye = jnp.eye(states, dtype=low)
    tiled = jnp.tile(eye, (1, GROUP))
    nothing = jnp.zeros_like(tiled)
    return jnp.concatenate(
        [
            jnp.concatenate([tiled, nothing], axis=1),
            jnp.concatenate([nothing, tiled], axis=1),
        ],
        axis=0,
    )


def transposed(values):
    count = values.shape[1]
    row = lax.broadcasted_iota(jnp.int32, (count, count), 0)
    col = lax.broadcasted_iota(jnp.int32, (count, count), 1)
    eye = jnp.where(row == col, 1.0, 0.0).astype(low)
    return lax.dot_general(eye, values, (((1,), (1,)), ((), ())), preferred_element_type=wide)


def forward_body(
    parts,
    order_ref,
    *refs,
):
    small_refs, dgated_refs, refs = refs[:parts], refs[parts : 2 * parts], refs[2 * parts :]
    forward_steps(order_ref, small_refs, dgated_refs, *refs)


def forward_steps(
    order_ref,
    small_refs,
    dgated_refs,
    pair_ref,
    fresh_ref,
    weight_ref,
    bias_ref,
    skip_ref,
    coeff_ref,
    spread_ref,
    kept_ref,
    dpre_ref,
    *rest,
):
    parts = len(small_refs)
    gated_ref, carry, step_all, drive_all, mixed_all, small_all, dgated_all = rest

    @pl.when(pl.program_id(0) == 0)
    def _():
        carry[...] = jnp.zeros_like(carry)

    coeff = coeff_ref[...]
    states = coeff.shape[0]
    rank = weight_ref.shape[0]
    length = dpre_ref.shape[0]
    quarter = length // parts
    chosen = own_block(states)
    part = order_ref[order_ref.shape[0] - 1]
    for j in range(parts):
        small_all[j] = small_refs[j][0]
    small = jnp.concatenate([small_all[part ^ j] for j in range(parts)], axis=0)
    act = jnp.concatenate([pair_ref[j, 0, 0] for j in range(parts)], axis=0).astype(wide)
    gate = jnp.concatenate([pair_ref[j, 1, 0] for j in range(parts)], axis=0).astype(wide)
    dpre = jnp.dot(small[:, :rank], weight_ref[...], preferred_element_type=wide) + bias_ref[...]
    dpre_ref[...] = dpre
    delta = jax.nn.softplus(dpre)
    step_all[...] = jnp.where(fresh_ref[...] > 0.0, delta, FAR)
    drive_all[...] = delta * act
    pair = small[:, rank:]
    columns = transposed(pair)
    reading = jnp.dot(pair, spread_ref[:, GROUP * states :], preferred_element_type=wide)
    state = carry[...]
    for group in range(length // GROUP):
        base = group * GROUP
        kept = []
        for t in range(base, base + GROUP):
            decay = jnp.exp2(step_all[t : t + 1, :] * coeff)
            state = decay * state + drive_all[t : t + 1, :] * columns[:states, t : t + 1]
            kept.append(state)
        kept_ref[base * states : (base + GROUP) * states, :] = jnp.concatenate(
            kept, axis=0
        ).astype(low)
    carry[...] = state
    for group in range(length // GROUP):
        here = slice(group * GROUP, (group + 1) * GROUP)
        block = kept_ref[group * GROUP * states : (group + 1) * GROUP * states, :]
        weights = jnp.where(chosen, reading[here], 0.0).astype(low)
        mixed_all[here, :] = jnp.dot(weights, block, preferred_element_type=wide)
    mixed = mixed_all[...] + skip_ref[...] * act
    for j in range(parts):
        dgated_all[j] = dgated_refs[j][0]
    dgated = jnp.concatenate([dgated_all[part ^ j] for j in range(parts)], axis=0).astype(wide)
    gated = (mixed * jax.nn.silu(gate)).astype(low)
    dgate = (dgated * mixed * silu_slope(gate)).astype(low)
    for j in range(parts):
        gated_ref[j, 0, 0] = gated[j * quarter : (j + 1) * quarter]
        gated_ref[j, 1, 0] = dgate[j * quarter : (j + 1) * quarter]


def backward_body(
    parts,
    order_ref,
    *refs,
):
    small_refs, dgated_refs, refs = refs[:parts], refs[parts : 2 * parts], refs[2 * parts :]
    backward_steps(order_ref, small_refs, dgated_refs, *refs)


def backward_steps(
    order_ref,
    small_refs,
    dgated_refs,
    pair_ref,
    fresh_ref,
    dpre_ref,
    kept_ref,
    before_ref,
    weight_ref,
    skip_ref,
    coeff_ref,
    spread_ref,
    *rest,
):
    parts = len(small_refs)
    own_ref, other_ref, dscan_ref = rest[:3]
    rest = rest[3:]
    (delta_grad_ref, decay_ref, sums_ref) = rest[:3]
    (carry, step_all, drive_all, delta_all, dmix_all, lam_all, flow_all) = rest[3:10]
    (lam_sum, flow_sum, cross_all, next_partial, next_dscan, small_all) = rest[10:16]
    (partial_all, dgated_all) = rest[16:]
    turn = pl.program_id(0)

    @pl.when(turn == 0)
    def _():
        carry[...] = jnp.zeros_like(carry)
        delta_grad_ref[...] = jnp.zeros_like(delta_grad_ref)
        decay_ref[...] = jnp.zeros_like(decay_ref)
        sums_ref[...] = jnp.zeros_like(sums_ref)
        next_partial[...] = jnp.zeros_like(next_partial)
        next_dscan[...] = jnp.zeros_like(next_dscan)

    coeff = coeff_ref[...]
    states = coeff.shape[0]
    rank = weight_ref.shape[0]
    length = dpre_ref.shape[0]
    quarter = length // parts
    spread = spread_ref[...]
    chosen = own_block(states)
    across = (((1,), (1,)), ((), ()))
    down = (((0,), (0,)), ((), ()))
    part = order_ref[order_ref.shape[0] - 1]
    for j in range(parts):
        small_all[j] = small_refs[j][0]
    small = jnp.concatenate([small_all[part ^ j] for j in range(parts)], axis=0)
    act = jnp.concatenate([pair_ref[j, 0, 0] for j in range(parts)], axis=0).astype(wide)
    gate = jnp.concatenate([pair_ref[j, 1, 0] for j in range(parts)], axis=0).astype(wide)
    for j in range(parts):
        dgated_all[j] = dgated_refs[j][0]
    dgated = jnp.concatenate([dgated_all[part ^ j] for j in range(parts)], axis=0).astype(wide)
    dpre = dpre_ref[...]
    delta = jax.nn.softplus(dpre)
    dmix = dgated * jax.nn.silu(gate)
    step_all[...] = jnp.where(fresh_ref[...] > 0.0, delta, FAR)
    drive_all[...] = delta * act
    delta_all[...] = delta
    dmix_all[...] = dmix
    pair = small[:, rank:]
    columns = transposed(pair)
    entering = jnp.dot(pair, spread[:, : GROUP * states], preferred_element_type=wide)
    first = jnp.where(turn == pl.num_programs(0) - 1, 0.0, before_ref[...].astype(wide))
    pulled = carry[...]
    summed = decay_ref[...]
    for group in range(length // GROUP - 1, -1, -1):
        base = group * GROUP
        lams = [None] * GROUP
        flows = [None] * GROUP
        rows = slice(base * states, (base + GROUP) * states)
        block = kept_ref[rows, :].astype(wide)
        if group:
            edge = kept_ref[(base - 1) * states : base * states, :].astype(wide)
        else:
            edge = first
        for i in range(GROUP - 1, -1, -1):
            t = base + i
            lam = columns[states:, t : t + 1] * dmix_all[t : t + 1, :] + pulled
            pulled = jnp.exp2(step_all[t : t + 1, :] * coeff) * lam
            flow = pulled * (block[(i - 1) * states : i * states] if i else edge)
            summed = summed + flow * delta_all[t : t + 1, :]
            lams[i] = lam
            flows[i] = flow * coeff
        lam_all[rows, :] = jnp.concatenate(lams, axis=0).astype(low)
        flow_all[rows, :] = jnp.concatenate(flows, axis=0).astype(low)
    carry[...] = pulled
    decay_ref[...] = summed
    ones = jnp.where(chosen, 1.0, 0.0).astype(low)
    for group in range(length // GROUP):
        here = slice(group * GROUP, (group + 1) * GROUP)
        rows = slice(group * GROUP * states, (group + 1) * GROUP * states)
        lam_block = lam_all[rows, :]
        weights = jnp.where(chosen, entering[here], 0.0).astype(low)
        lam_sum[here, :] = jnp.dot(weights, lam_block, preferred_element_type=wide)
        flow_sum[here, :] = jnp.dot(ones, flow_all[rows, :], preferred_element_type=wide)
        cross = lax.dot_general(
            drive_all[here, :].astype(low), lam_block, across, preferred_element_type=wide
        )
        cross_all[here, : GROUP * states] = jnp.where(chosen, cross, 0.0).astype(low)
        cross = lax.dot_general(
            dmix_all[here, :].astype(low), kept_ref[rows, :], across, preferred_element_type=wide
        )
        cross_all[here, GROUP * states :] = jnp.where(chosen, cross, 0.0).astype(low)
    dpair = lax.dot_general(cross_all[...], spread, across, preferred_element_type=wide)
    scale = 1.0 / math.log2(math.e)
    found = lam_sum[...]
    ddelta = flow_sum[...] * scale + found * act
    ddpre = (ddelta * jax.nn.sigmoid(dpre)).astype(low)
    delta_grad_ref[...] += lax.dot_general(
        small[:, :rank], ddpre, down, preferred_element_type=wide
    )
    dlow = lax.dot_general(ddpre, weight_ref[...], across, preferred_element_type=wide)
    dscan = (found * delta + dmix * skip_ref[...]).astype(low)
    sums_ref[0:1, :] += jnp.sum(ddpre.astype(wide), axis=0, keepdims=True)
    sums_ref[1:2, :] += jnp.sum(dmix * act, axis=0, keepdims=True)
    for value, store, after, span in (
        (dlow.astype(low), partial_all, next_partial, slice(0, rank)),
        (dpair.astype(low), partial_all, next_partial, slice(rank, rank + 2 * states)),
        (dscan, dscan_ref, next_dscan, slice(0, dscan.shape[1])),
    ):
        longer = jnp.concatenate([value, after[:, span]], axis=0)
        for j in range(parts):
            window = longer[j * quarter : (j + 1) * quarter + TAIL]
            if store is dscan_ref:
                store[j, 0] = window
            else:
                store[j, :, span] = window
        after[:, span] = value[:TAIL]
    for k in range(parts):
        (other_ref if k % 2 else own_ref)[k // 2, 0] = partial_all[part ^ k]


def forward_scan(order, small, pair, dgated, fresh, weight, bias, skip, coeff, spread):
    parts, _, blocks, quarter, width = pair.shape
    states = coeff.shape[0]
    columns = small[0].shape[-1]
    chunk = parts * quarter
    tokens = blocks * chunk

    def whole(values):
        return pl.BlockSpec(values.shape, lambda t, order: (0, 0))

    row = pl.BlockSpec((chunk, width), lambda t, order: (t, 0))
    return pl.pallas_call(
        functools.partial(forward_body, parts),
        grid_spec=pltpu.PrefetchScalarGridSpec(
            num_scalar_prefetch=1,
            grid=(blocks,),
            in_specs=[
                pl.BlockSpec((1, quarter, columns), lambda t, order: (order[blocks + t], 0, 0))
                for _ in range(parts)
            ]
            + [
                pl.BlockSpec((1, quarter, width), lambda t, order: (order[t], 0, 0))
                for _ in range(parts)
            ]
            + [
                pl.BlockSpec(
                    (parts, 2, 1, quarter, width), lambda t, order: (0, 0, order[t], 0, 0)
                ),
                pl.BlockSpec((chunk, 1), lambda t, order: (t, 0)),
            ]
            + [whole(v) for v in (weight, bias, skip, coeff, spread)],
            out_specs=[
                pl.BlockSpec((chunk * states, width), lambda t, order: (t, 0)),
                row,
                pl.BlockSpec(
                    (parts, 2, 1, quarter, width), lambda t, order: (0, 0, order[t], 0, 0)
                ),
            ],
            scratch_shapes=[
                pltpu.VMEM((states, width), wide),
                pltpu.VMEM((chunk, width), wide),
                pltpu.VMEM((chunk, width), wide),
                pltpu.VMEM((chunk, width), wide),
                pltpu.VMEM((parts, quarter, columns), low),
                pltpu.VMEM((parts, quarter, width), low),
            ],
        ),
        out_shape=[
            pltpu.HBM((tokens * states, width), low),
            pltpu.HBM((tokens, width), wide),
            pltpu.HBM((parts, 2, blocks, quarter, width), low),
        ],
        compiler_params=pltpu.CompilerParams(vmem_limit_bytes=16 * 1024 * 1024),
        cost_estimate=spent(14),
        name="forward_scan",
    )(order, *map(in_hbm, (*small, *dgated, pair, fresh, weight, bias, skip, coeff, spread)))


def backward_scan(
    order, small, pair, dgated, fresh, dpre, kept, weight, skip, coeff, spread
):
    parts, _, blocks, quarter, width = pair.shape
    states = coeff.shape[0]
    rank = weight.shape[0]
    columns = small[0].shape[-1]
    chunk = parts * quarter
    last = blocks - 1

    def whole(shape):
        return pl.BlockSpec(shape, lambda t, order: (0, 0))

    row = pl.BlockSpec((chunk, width), lambda t, order: (last - t, 0))
    return pl.pallas_call(
        functools.partial(backward_body, parts),
        grid_spec=pltpu.PrefetchScalarGridSpec(
            num_scalar_prefetch=1,
            grid=(blocks,),
            in_specs=[
                pl.BlockSpec(
                    (1, quarter, columns), lambda t, order: (order[blocks + last - t], 0, 0)
                )
                for _ in range(parts)
            ]
            + [
                pl.BlockSpec((1, quarter, width), lambda t, order: (order[last - t], 0, 0))
                for _ in range(parts)
            ]
            + [
                pl.BlockSpec(
                    (parts, 2, 1, quarter, width),
                    lambda t, order: (0, 0, order[last - t], 0, 0),
                ),
                pl.BlockSpec((chunk, 1), lambda t, order: (last - t, 0)),
                row,
                pl.BlockSpec((chunk * states, width), lambda t, order: (last - t, 0)),
                pl.BlockSpec(
                    (states, width),
                    lambda t, order: (jnp.maximum((last - t) * chunk - 1, 0), 0),
                ),
            ]
            + [whole(v.shape) for v in (weight, skip, coeff, spread)],
            out_specs=[
                pl.BlockSpec(
                    (parts // 2, 1, quarter + TAIL, columns),
                    lambda t, order: (0, order[blocks + last - t], 0, 0),
                )
                for _ in range(2)
            ]
            + [
                pl.BlockSpec(
                    (parts, 1, quarter + TAIL, width),
                    lambda t, order: (0, order[last - t], 0, 0),
                ),
                whole((rank, width)),
                whole((states, width)),
                whole((8, width)),
            ],
            scratch_shapes=[pltpu.VMEM((states, width), wide)]
            + [pltpu.VMEM((chunk, width), wide)] * 4
            + [pltpu.VMEM((chunk * states, width), low)] * 2
            + [pltpu.VMEM((chunk, width), wide)] * 2
            + [
                pltpu.VMEM((chunk, 2 * GROUP * states), low),
                pltpu.VMEM((TAIL, columns), low),
                pltpu.VMEM((TAIL, width), low),
                pltpu.VMEM((parts, quarter, columns), low),
                pltpu.VMEM((parts, quarter + TAIL, columns), low),
                pltpu.VMEM((parts, quarter, width), low),
            ],
        ),
        out_shape=[
            pltpu.HBM((parts // 2, blocks, quarter + TAIL, columns), low)
            for _ in range(2)
        ]
        + [
            pltpu.HBM((parts, blocks, quarter + TAIL, width), low),
            jax.ShapeDtypeStruct((rank, width), wide),
            jax.ShapeDtypeStruct((states, width), wide),
            jax.ShapeDtypeStruct((8, width), wide),
        ],
        compiler_params=pltpu.CompilerParams(vmem_limit_bytes=16 * 1024 * 1024),
        cost_estimate=spent(24),
        name="backward_scan",
    )(
        order,
        *map(
            in_hbm, (*small, *dgated, pair, fresh, dpre, kept, kept, weight, skip, coeff, spread)
        ),
    )


def interleave_body(inner_ref, gate_ref, out_ref):
    out_ref[:, 0, :] = inner_ref[...].astype(wide)
    out_ref[:, 1, :] = gate_ref[...].astype(wide)


def interleave(inner, gate):
    rows, width = inner.shape
    block = 256
    spec = pl.BlockSpec((block, width), lambda t: (t, 0))
    return pl.pallas_call(
        interleave_body,
        grid=(rows // block,),
        in_specs=[spec, spec],
        out_specs=pl.BlockSpec((block, 2, width), lambda t: (t, 0, 0)),
        out_shape=jax.ShapeDtypeStruct((rows, 2, width), wide),
        compiler_params=pltpu.CompilerParams(vmem_limit_bytes=16 * 1024 * 1024),
        cost_estimate=spent(5),
        name="interleave",
    )(inner, gate)


def placed_body(parts, order_ref, *refs):
    values, out_ref = refs[:parts], refs[-1]
    place = order_ref[pl.program_id(0)]
    for k in range(parts):

        @pl.when(place == k)
        def _(k=k):
            value = values[k][...].astype(wide)
            out_ref[...] = refs[parts][...] + value if len(refs) > parts + 1 else value


def placed(order, values, base=None):
    parts = len(values)
    rows, width = values[0].shape
    flat = pl.BlockSpec((rows, width), lambda p, order: (p, 0))
    return pl.pallas_call(
        functools.partial(placed_body, parts),
        grid_spec=pltpu.PrefetchScalarGridSpec(
            num_scalar_prefetch=1,
            grid=(parts,),
            in_specs=[pl.BlockSpec((rows, width), lambda p, order: (0, 0))] * parts
            + ([] if base is None else [flat]),
            out_specs=flat,
        ),
        out_shape=jax.ShapeDtypeStruct((parts * rows, width), wide),
        compiler_params=pltpu.CompilerParams(vmem_limit_bytes=24 * 1024 * 1024),
        cost_estimate=spent(2.5),
        name="placed",
    )(order, *values, *(() if base is None else (base,)))


def project_body(
    place_ref,
    *refs,
):
    pieces, refs = refs[:8], refs[8:]
    (weight_ref, flags_ref, taps_ref, offset_ref, select_ref) = refs[:5]
    (normed_ref, inner_ref, channels_ref, kept_ref, sent_ref) = refs[5:10]
    (sides, edges, window, total, acts) = refs[10:]
    turn = pl.program_id(0)
    quarter = channels_ref.shape[3]
    width = channels_ref.shape[4]
    halves = weight_ref.shape[1] // width
    taps = taps_ref.shape[0]
    inner_turns = pl.num_programs(0) // 2
    count = len(pieces)

    @pl.when(turn == 0)
    def _():
        for k in range(count):
            piece = pieces[k][...]
            normed_ref[k * quarter : (k + 1) * quarter, :] = piece[:quarter]
            sides[k * 8 : (k + 1) * 8, :] = piece[quarter:].astype(wide)
        edges[...] = jnp.zeros_like(edges)
        total[...] = jnp.zeros_like(total)

    main = jnp.dot(normed_ref[...], weight_ref[...], preferred_element_type=wide)

    @pl.when(turn < inner_turns)
    def _():
        edges[: count * 8, :] = jnp.dot(
            sides[...].astype(low), weight_ref[...], preferred_element_type=wide
        )
        for k in range(count):
            before = pl.multiple_of(place_ref[k] * 8, 8)
            after = pl.multiple_of(place_ref[count + k] * 8, 8)
            flags = flags_ref[k]
            window[0:8, :] = edges[pl.ds(before, 8), :]
            window[8 : 8 + quarter, :] = main[k * quarter : (k + 1) * quarter]
            window[8 + quarter : 16 + quarter, :] = edges[pl.ds(after, 8), :]
            masked = window[...] * flags[:, 0:1]
            window[...] = masked
            inner_ref[k] = masked
            conv = offset_ref[...] + taps_ref[taps - 1 : taps, :] * masked[8 : 8 + quarter]
            for lag in range(1, taps):
                shifted = window[8 - lag : 8 - lag + quarter, :]
                valid = flags[8 : 8 + quarter, lag : lag + 1]
                conv = conv + taps_ref[taps - 1 - lag : taps - lag, :] * shifted * valid
            act = (jax.nn.silu(conv) * flags[8 : 8 + quarter, 0:1]).astype(low)
            acts[k * quarter : (k + 1) * quarter, :] = act
            for h in range(halves):
                channels_ref[h, 0, k] = act[:, h * width : (h + 1) * width]
        total[...] += jnp.dot(acts[...], select_ref[...], preferred_element_type=wide)

    @pl.when(turn >= inner_turns)
    def _():
        gate = main.astype(low)
        for k in range(count):
            for h in range(halves):
                channels_ref[h, 0, k] = gate[
                    k * quarter : (k + 1) * quarter, h * width : (h + 1) * width
                ]

    @pl.when(turn == pl.num_programs(0) - 1)
    def _():
        for k in range(count // 2):
            plane = place_ref[2 * count + k]
            kept_ref[plane] = total[k * quarter : (k + 1) * quarter, :]
            other = k + count // 2
            sent_ref[plane] = total[other * quarter : (other + 1) * quarter, :].astype(low)


def project(places, pieces, weight, flags, taps, offset, select, parts):
    count = len(pieces)
    rows, depth = pieces[0].shape
    quarter = rows - 8
    chans = weight.shape[1] // 2
    width = chans // parts
    tile = 2 * width
    turns = 2 * chans // tile
    half = turns // 2
    small = select.shape[1]

    def whole(shape):
        return pl.BlockSpec(shape, lambda t, place: (0,) * len(shape))

    def inner(t):
        return jnp.minimum(t, half - 1)

    return pl.pallas_call(
        project_body,
        grid_spec=pltpu.PrefetchScalarGridSpec(
            num_scalar_prefetch=1,
            grid=(turns,),
            in_specs=[whole(pieces[0].shape) for _ in pieces]
            + [
                pl.BlockSpec((depth, tile), lambda t, place: (0, t)),
                whole(flags.shape),
                pl.BlockSpec((taps.shape[0], tile), lambda t, place: (0, inner(t))),
                pl.BlockSpec((1, tile), lambda t, place: (0, inner(t))),
                pl.BlockSpec((tile, small), lambda t, place: (inner(t), 0)),
            ],
            out_specs=[
                whole((count * quarter, depth)),
                pl.BlockSpec((count, quarter + 16, tile), lambda t, place: (0, 0, inner(t))),
                pl.BlockSpec(
                    (2, 1, count, quarter, width),
                    lambda t, place: (t % half, t // half, 0, 0, 0),
                ),
                whole((count // 2, quarter, small)),
                whole((count // 2, quarter, small)),
            ],
            scratch_shapes=[
                pltpu.VMEM((count * 8, depth), wide),
                pltpu.VMEM((count * 8 + 8, tile), wide),
                pltpu.VMEM((quarter + 16, tile), wide),
                pltpu.VMEM((count * quarter, small), wide),
                pltpu.VMEM((count * quarter, tile), low),
            ],
        ),
        out_shape=[
            pltpu.HBM((count * quarter, depth), low),
            pltpu.HBM((count, quarter + 16, chans), wide),
            jax.ShapeDtypeStruct((parts, 2, count, quarter, width), low),
            jax.ShapeDtypeStruct((count // 2, quarter, small), wide),
            jax.ShapeDtypeStruct((count // 2, quarter, small), low),
        ],
        compiler_params=pltpu.CompilerParams(vmem_limit_bytes=28 * 1024 * 1024),
        cost_estimate=spent(8),
        name="project",
    )(places, *map(in_hbm, (*pieces, weight, flags, taps, offset, select)))


def pull_body(order_ref, rows_ref, weight_ref, kept_ref, *refs):
    out_refs, found_ref = refs[:-1], refs[-1]
    count = rows_ref.shape[0]
    quarter = rows_ref.shape[1]
    width = out_refs[0].shape[2]
    turn = pl.program_id(0)
    bit = order_ref[count] & 1

    @pl.when(turn == 0)
    def _():
        for k in range(count):
            kept_ref[k * quarter : (k + 1) * quarter, :] = rows_ref[order_ref[k]]

    found_ref[...] = lax.dot_general(
        kept_ref[...], weight_ref[...], (((1,), (1,)), ((), ())), preferred_element_type=wide
    ).astype(low)
    for p in range(len(out_refs)):

        @pl.when(turn == p // 2)
        def _(p=p):
            here = pl.ds(pl.multiple_of((bit ^ (p % 2)) * width, width), width)
            for k in range(count):
                out_refs[p][k] = found_ref[k * quarter : (k + 1) * quarter, here]


def pull(order, rows, weight, parts):
    count, quarter, depth = rows.shape
    width = weight.shape[0] // parts
    piece = pl.BlockSpec((count, quarter, width), lambda t, order: (0, 0, 0))
    return pl.pallas_call(
        pull_body,
        grid_spec=pltpu.PrefetchScalarGridSpec(
            num_scalar_prefetch=1,
            grid=(parts // 2,),
            in_specs=[
                pl.BlockSpec((count, quarter, depth), lambda t, order: (0, 0, 0)),
                pl.BlockSpec((2 * width, depth), lambda t, order: ((order[count] // 2) ^ t, 0)),
            ],
            out_specs=[pl.BlockSpec((count * quarter, depth), lambda t, order: (0, 0))]
            + [piece] * parts,
            scratch_shapes=[pltpu.VMEM((count * quarter, 2 * width), low)],
        ),
        out_shape=[pltpu.HBM((count * quarter, depth), low)]
        + [pltpu.HBM((count, quarter, width), low)] * parts,
        compiler_params=pltpu.CompilerParams(vmem_limit_bytes=20 * 1024 * 1024),
        cost_estimate=spent(6),
        name="pull",
    )(order, in_hbm(rows), in_hbm(weight))


def emit_body(order_ref, *refs):
    pieces_ref, refs = refs[0], refs[1:]
    parts = pieces_ref.shape[0]
    (weight_ref, rows_ref, kept_ref, first_ref, second_ref, own_ref, other_ref) = refs[:7]
    (dgate_ref, gated, product) = refs[7:]
    turn = pl.program_id(0)
    half = pl.num_programs(0) // 2
    count, quarter, width = pieces_ref.shape[2:]

    @pl.when(pl.program_id(0) == 0)
    def _():
        for p in range(parts):
            here = slice(p * width, (p + 1) * width)
            for k in range(count):
                rows = slice(k * quarter, (k + 1) * quarter)
                gated[rows, here] = pieces_ref[p, 0, k]
                dgate_ref[rows, here] = pieces_ref[p, 1, k]

    values = gated[...]
    branch = jnp.dot(values, weight_ref[...], preferred_element_type=wide).astype(low)
    for k in range(count // 2):
        kept_ref[k] = branch[k * quarter : (k + 1) * quarter]
    other = branch[count // 2 * quarter :].reshape(count // 2, quarter, branch.shape[1])

    @pl.when(turn < half)
    def _():
        first_ref[...] = other

    @pl.when(turn >= half)
    def _():
        second_ref[...] = other

    product[...] = lax.dot_general(
        values, rows_ref[...], (((0,), (0,)), ((), ())), preferred_element_type=wide
    ).astype(low)
    part = order_ref[count]
    for p in range(parts):
        here = pl.ds(pl.multiple_of((part ^ p) * width, width), width)
        (other_ref if p % 2 else own_ref)[p // 2] = product[here, :]


def emit(order, pieces, weight, rows):
    parts, _, count, quarter, width = pieces.shape
    depth = weight.shape[1]
    tile = 512
    half = depth // tile // 2
    chans = parts * width
    tall = count * quarter
    return pl.pallas_call(
        emit_body,
        grid_spec=pltpu.PrefetchScalarGridSpec(
            num_scalar_prefetch=1,
            grid=(depth // tile,),
            in_specs=[
                pl.BlockSpec(pieces.shape, lambda t, order: (0, 0, 0, 0, 0)),
                pl.BlockSpec((chans, tile), lambda t, order: (0, t)),
                pl.BlockSpec((tall, tile), lambda t, order: (0, t)),
            ],
            out_specs=[
                pl.BlockSpec((count // 2, quarter, tile), lambda t, order: (0, 0, t)),
                pl.BlockSpec(
                    (count // 2, quarter, tile), lambda t, order: (0, 0, jnp.minimum(t, half - 1))
                ),
                pl.BlockSpec(
                    (count // 2, quarter, tile), lambda t, order: (0, 0, jnp.maximum(t - half, 0))
                ),
                pl.BlockSpec((parts // 2, width, tile), lambda t, order: (0, 0, t)),
                pl.BlockSpec((parts // 2, width, tile), lambda t, order: (0, 0, t)),
                pl.BlockSpec((tall, chans), lambda t, order: (0, 0)),
            ],
            scratch_shapes=[pltpu.VMEM((tall, chans), low), pltpu.VMEM((chans, tile), low)],
        ),
        out_shape=[
            pltpu.HBM((count // 2, quarter, depth), low),
            pltpu.HBM((count // 2, quarter, depth // 2), low),
            pltpu.HBM((count // 2, quarter, depth // 2), low),
            pltpu.HBM((parts // 2, width, depth), low),
            pltpu.HBM((parts // 2, width, depth), low),
            pltpu.HBM((tall, chans), low),
        ],
        compiler_params=pltpu.CompilerParams(vmem_limit_bytes=20 * 1024 * 1024),
        cost_estimate=spent(6),
        name="emit",
    )(order, in_hbm(pieces), in_hbm(weight), in_hbm(rows))


def turn_body(order_ref, *refs):
    count = 8
    smalls, refs = refs[:2], refs[2:]
    (dscan_ref, select_ref, inner_ref, flags_ref, taps_ref, offset_ref, dgate_ref) = refs[:7]
    (dboth_ref, grad_ref, rows_ref) = refs[7:10]
    (small_all, shifted, acts) = refs[10:]
    rank = grad_ref.shape[1]
    parts = pl.num_programs(0) // 2
    turn = pl.program_id(0)
    span = inner_ref.shape[1]
    quarter = span - 16
    reach = quarter + 8
    taps = taps_ref.shape[0]

    @pl.when(turn == 0)
    def _():
        for k in range(count):
            plane = order_ref[k] // 2
            small_all[k * span : (k + 1) * span, :] = smalls[k // (count // 2)][plane]

    @pl.when(turn < parts)
    def _():
        whole = lax.dot_general(
            small_all[...],
            select_ref[...],
            (((1,), (1,)), ((), ())),
            preferred_element_type=wide,
        )
        found = dscan_ref[0]
        sums = [0.0] * (taps + 1)
        for k in range(count):
            flags = flags_ref[k, 8 : 8 + reach, :]
            mask = flags[:, 0:1]
            conv = offset_ref[...]
            for lag in range(taps):
                term = taps_ref[taps - 1 - lag : taps - lag, :] * inner_ref[
                    k, 8 - lag : 8 - lag + reach, :
                ]
                conv = conv + (term * flags[:, lag : lag + 1] if lag else term)
            sig = jax.nn.sigmoid(conv)
            act = conv * sig * mask
            acts[k * quarter : (k + 1) * quarter, :] = act[:quarter].astype(low)
            dact = found[k, :reach].astype(wide) + whole[k * span : k * span + reach]
            dconv = dact * mask * (sig * (1.0 + conv * (1.0 - sig)))
            dinner = 0.0
            for lag in range(taps):
                masked = dconv * flags[:, lag : lag + 1] if lag else dconv
                sums[taps - 1 - lag] += jnp.sum(
                    masked[:quarter] * inner_ref[k, 8 - lag : 8 - lag + quarter, :],
                    axis=0,
                    keepdims=True,
                )
                if lag:
                    shifted[lag, :reach, :] = masked
                    masked = shifted[lag, lag : lag + quarter, :]
                else:
                    sums[taps] += jnp.sum(masked[:quarter], axis=0, keepdims=True)
                    masked = masked[:quarter]
                dinner = dinner + masked * taps_ref[taps - 1 - lag : taps - lag, :]
            dboth_ref[k * quarter : (k + 1) * quarter, :] = (dinner * mask[:quarter]).astype(low)
        for index, value in enumerate(sums):
            rows_ref[index : index + 1, :] = value
        mains = jnp.concatenate(
            [small_all[k * span : k * span + quarter, :] for k in range(count)], axis=0
        )
        grad_ref[...] = lax.dot_general(
            acts[...], mains[:, :rank], (((0,), (0,)), ((), ())), preferred_element_type=wide
        ).astype(low)
        rows_ref[8:, :] = lax.dot_general(
            mains[:, rank:], acts[...], (((0,), (0,)), ((), ())), preferred_element_type=wide
        )

    @pl.when(turn >= parts)
    def _():
        dboth_ref[...] = dgate_ref[...]


def turn_back(order, smalls, dscan, select, inner, flags, taps, offset, dgate, rank):
    parts, count, span, _ = dscan.shape
    small = smalls[0].shape[-1]
    chans = select.shape[0]
    width = chans // parts
    quarter = span - 16

    def whole(shape):
        return pl.BlockSpec(shape, lambda t, order: (0,) * len(shape))

    def early(t):
        return jnp.minimum(t, parts - 1)

    return pl.pallas_call(
        turn_body,
        grid_spec=pltpu.PrefetchScalarGridSpec(
            num_scalar_prefetch=1,
            grid=(2 * parts,),
            in_specs=[whole(v.shape) for v in smalls]
            + [
                pl.BlockSpec((1, count, span, width), lambda t, order: (early(t), 0, 0, 0)),
                pl.BlockSpec((width, small), lambda t, order: (early(t), 0)),
                pl.BlockSpec((count, span, width), lambda t, order: (0, 0, early(t))),
                whole(flags.shape),
                pl.BlockSpec((taps.shape[0], width), lambda t, order: (0, early(t))),
                pl.BlockSpec((1, width), lambda t, order: (0, early(t))),
                pl.BlockSpec(
                    (count * quarter, width), lambda t, order: (0, jnp.maximum(t - parts, 0))
                ),
            ],
            out_specs=[
                pl.BlockSpec((count * quarter, width), lambda t, order: (0, t)),
                pl.BlockSpec((width, rank), lambda t, order: (early(t), 0)),
                pl.BlockSpec((small - rank + 8, width), lambda t, order: (0, early(t))),
            ],
            scratch_shapes=[
                pltpu.VMEM((count * span, small), low),
                pltpu.VMEM((taps.shape[0], span, width), wide),
                pltpu.VMEM((count * quarter, width), low),
            ],
        ),
        out_shape=[
            jax.ShapeDtypeStruct((count * quarter, 2 * chans), low),
            pltpu.HBM((chans, rank), low),
            jax.ShapeDtypeStruct((small - rank + 8, chans), wide),
        ],
        compiler_params=pltpu.CompilerParams(vmem_limit_bytes=20 * 1024 * 1024),
        cost_estimate=spent(5.5),
        name="turn_back",
    )(
        order,
        *smalls,
        dscan,
        select,
        inner,
        flags,
        taps,
        offset,
        dgate,
    )


class Moves:
    def __init__(self, n_chan, n_state):
        self.n_chan = n_chan
        self.n_state = n_state
        self.near = (n_chan, n_state) == (8, 4)
        self.chan = lax.axis_index("chan").astype(jnp.uint32)
        self.part = lax.axis_index("state").astype(jnp.uint32)
        self.z = self.chan // 2
        self.y = self.chan % 2
        places = jnp.arange(n_chan, dtype=jnp.uint32)
        if self.near:
            planes = (self.z + 4 - places % 4) % 4
            self.blocks = planes * 2 + (self.y + places // 4) % 2
            hops = (self.z + 4 - places // 2) % 4
            self.order = (self.y + places) % 2 * 4 + hops
        else:
            self.blocks = places
            self.order = places

    def over_y(self, values):
        return lax.ppermute(values, "chan", [(i, i ^ 1) for i in range(8)])

    def over_z(self, values, hops):
        return lax.ppermute(values, "chan", [(i, (i + 2 * hops) % 8) for i in range(8)])

    def over_state(self, values, bits):
        return lax.ppermute(values, "state", [(i, i ^ bits) for i in range(4)])

    def swap_state(self, values):
        return lax.all_to_all(values, "state", 0, 0, tiled=True)

    def pair(self, bit, own, other):
        return jnp.stack([jnp.where(bit == 0, own, other), jnp.where(bit == 0, other, own)])

    def in_order(self, pieces):
        own, core, across, slant = pieces
        bit = self.part % 2
        near = self.pair(bit, own, core)
        far = self.pair(bit, across, slant)
        return self.pair(self.part // 2, near, far).reshape((4,) + own.shape)

    def pieces_state(self, values):
        core = self.over_state(values, 1)
        across = self.over_state(values, 2)
        return values, core, across, self.over_state(across, 1)

    def gather_state(self, values):
        if not self.near:
            return lax.all_gather(values, "state", axis=0)
        return self.in_order(self.pieces_state(values))

    def gather_near(self, values):
        if not self.near:
            found = lax.all_gather(values, "state", axis=0)
            return [
                lax.dynamic_index_in_dim(found, self.part ^ k, 0, keepdims=False)
                for k in range(self.n_state)
            ]
        return list(self.pieces_state(values))

    def trade_state(self, values):
        if not self.near:
            return self.swap_state(values)
        chosen = [
            lax.dynamic_index_in_dim(values, self.part ^ k, 0, keepdims=False) for k in range(4)
        ]
        moved = [chosen[0]] + [self.over_state(chosen[k], k) for k in (1, 2, 3)]
        return self.in_order(moved)

    def pieces_chan(self, values):
        own = self.over_y(values)
        along = [self.over_z(values, hops) for hops in (1, 2, 3)]
        own, along[0] = tied(own, along[0])
        return [values] + along + [own] + [self.over_y(piece) for piece in along]

    def gather_chan(self, values):
        if not self.near:
            return lax.all_gather(values, "chan", axis=0)
        return jnp.stack(self.pieces_chan(values))

    def gather_rows(self, values, cut):
        if not self.near:
            found = lax.all_gather(values, "chan", axis=0)
            return found[:, :cut].reshape(-1, values.shape[1]), found[:, cut:]
        pieces = self.pieces_chan(values)
        first = jnp.concatenate([piece[:cut] for piece in pieces], axis=0)
        return first, jnp.stack([piece[cut:] for piece in pieces])

    def in_axis_order(self, values):
        if not self.near:
            return values
        return jnp.stack(
            [
                lax.dynamic_index_in_dim(values, self.order[k], 0, keepdims=False)
                for k in range(self.n_chan)
            ]
        )

    def gather_small(self, values):
        if not self.near:
            return lax.all_gather(values, "chan", axis=0)
        copies = jnp.broadcast_to(values[None], (self.n_chan,) + values.shape)
        return lax.all_to_all(copies, "chan", 0, 0, tiled=True)

    def sum_small(self, parts):
        moved = lax.all_to_all(parts, "chan", 0, 0, tiled=True)
        return jnp.sum(moved.astype(wide), axis=0)

    def joined_planes(self, kept, sent):
        return kept + self.over_y(sent).astype(wide)

    def summed_planes(self, joined):
        total = joined[0]
        for hops in (1, 2, 3):
            total = total + self.over_z(joined[4 - hops].astype(low), hops).astype(wide)
        return total

    def sum_planes(self, kept, sent):
        return self.summed_planes(self.joined_planes(kept, sent))

    def sum_chan(self, parts):
        if not self.near:
            return self.sum_small(parts.astype(low))
        return self.sum_planes(parts[:4], parts[4:].astype(low))

    def sum_row(self, values):
        if not self.near:
            return lax.psum(values, "chan")
        both = values + self.over_y(values)
        total = both
        for hops in (1, 2, 3):
            total = total + self.over_z(both, hops)
        return total

    def sum_state(self, parts):
        if not self.near:
            moved = lax.all_to_all(parts, "state", 0, 0, tiled=True)
            return jnp.sum(moved.astype(wide), axis=0).astype(low)
        cut = parts.reshape((2, 2) + parts.shape[1:])
        core = self.part % 2
        sent = lax.dynamic_index_in_dim(cut, 1 - core, 1, keepdims=False)
        kept = lax.dynamic_index_in_dim(cut, core, 1, keepdims=False)
        chip = (kept.astype(wide) + self.over_state(sent, 1).astype(wide)).astype(low)
        side = self.part // 2
        sent = lax.dynamic_index_in_dim(chip, 1 - side, 0, keepdims=False)
        kept = lax.dynamic_index_in_dim(chip, side, 0, keepdims=False)
        return (kept.astype(wide) + self.over_state(sent, 2).astype(wide)).astype(low)

    def total_state(self, values):
        rows, columns = values.shape
        parts = values.reshape(self.n_state, rows // self.n_state, columns)
        return self.gather_state(self.sum_state(parts)).reshape(rows, columns)


def tied(*values):
    return lax.optimization_barrier(values)


def after(values, *others):
    token = lax.optimization_barrier((lax.create_token(), others))[0]
    return lax.optimization_barrier((token, values))[1]


def shards(
    n_chan,
    n_state,
    hidden_in,
    norm_gain,
    in_weight,
    conv_kernel,
    conv_offset,
    select_rank,
    select_entry,
    select_read,
    delta_weight,
    step_bias,
    decay_log,
    skip_weight,
    out_weight,
    lengths,
    pad_mask,
    cotangent,
):
    rows_dev, width = hidden_in.shape
    tokens = pad_mask.shape[0]
    chans = in_weight.shape[2]
    taps = conv_kernel.shape[0]
    rank = select_rank.shape[1]
    per_state = select_entry.shape[1]
    states = per_state * n_state
    small = rank + 2 * states
    quarter = rows_dev // n_state
    own = chans // n_state
    rows_q = n_chan * quarter
    part = lax.axis_index("state").astype(jnp.uint32)
    contract_rows = (((0,), (0,)), ((), ()))
    contract_cols = (((1,), (1,)), ((), ()))
    moves = Moves(n_chan, n_state)
    blocks = moves.blocks
    order = jnp.concatenate([moves.order, moves.order, part[None]]).astype(jnp.int32)

    def mine(values, axis=0):
        return lax.dynamic_slice_in_dim(values, part * own, own, axis)

    def in_axis(pieces):
        stacked = jnp.stack(pieces)
        return jnp.stack(
            [
                lax.dynamic_index_in_dim(stacked, part ^ j, 0, keepdims=False)
                for j in range(n_state)
            ]
        )

    def split_own(values):
        cut = values.reshape(values.shape[:-1] + (n_state, own))
        return jnp.moveaxis(cut, -2, 0)

    def join_own(values):
        moved = jnp.moveaxis(values, 0, -2)
        return moved.reshape(moved.shape[:-2] + (chans,))

    def chosen_rows(chooser, values):
        flat = values.reshape(values.shape[0], -1)
        found = jnp.dot(chooser, flat, precision=lax.Precision.HIGHEST)
        return found.reshape(values.shape)

    start = part * quarter
    hidden_q = lax.dynamic_slice_in_dim(hidden_in, start, quarter, 0)
    ahead = (start + (rows_dev - HALO)) % rows_dev
    behind = (start + quarter) % rows_dev
    local = jnp.concatenate(
        [
            hidden_q,
            lax.dynamic_slice_in_dim(hidden_in, ahead, HALO, 0),
            lax.dynamic_slice_in_dim(hidden_in, behind, HALO, 0),
        ],
        axis=0,
    )
    inv_all = lax.rsqrt(jnp.mean(local * local, axis=1, keepdims=True) + epsilon)
    scaled_all = local * inv_all
    normed_all = (scaled_all * norm_gain[None, :]).astype(low)
    inv_rms = inv_all[:quarter]
    scaled = scaled_all[:quarter]
    normed_q, normed_side = moves.gather_rows(normed_all, quarter)
    cot_q = lax.dynamic_slice_in_dim(cotangent, start, quarter, 0).astype(low)
    grad_q = lax.all_gather(cot_q, "chan", axis=0)

    place = positions(lengths, tokens)
    flags = [pad_mask.astype(wide)]
    flags += [(place >= lag).astype(wide) for lag in range(1, taps)]
    flags = jnp.stack(flags)
    padded = jnp.pad(flags, ((0, 0), (HALO, HALO + rows_dev)))
    span = quarter + 2 * HALO
    flags_win = lax.dynamic_slice_in_dim(padded, start, n_chan * rows_dev, 1)
    flags_win = flags_win.reshape(taps, n_chan, rows_dev)[:, :, :span]
    chooser = (blocks[:, None] == jnp.arange(n_chan)[None, :]).astype(wide)
    flags_win = jnp.einsum("kb,fbr->fkr", chooser, flags_win)
    mask_win = flags_win[0][:, :, None]
    valid_win = flags_win[1:]
    one_before = (blocks[:, None] - 1 == blocks[None, :]).astype(wide)
    one_after = (blocks[:, None] + 1 == blocks[None, :]).astype(wide)
    itself = jnp.eye(n_chan, dtype=wide)
    one_before = jnp.where(part == 0, one_before, itself)
    one_after = jnp.where(part == n_state - 1, one_after, itself)

    def valid_at(lag, first, count):
        if lag == 0:
            return 1.0
        return valid_win[lag - 1][:, first : first + count, None]

    columns = jnp.concatenate([select_entry, select_read], axis=1)
    columns = moves.gather_state(columns).reshape(n_state, chans, 2, per_state)
    columns = jnp.transpose(columns, (1, 2, 0, 3)).reshape(chans, 2 * states)
    select = jnp.concatenate([select_rank, columns], axis=1)
    decay_own = moves.swap_state(jnp.swapaxes(decay_log.reshape(per_state, n_state, own), 0, 1))
    coeff = -jnp.exp(decay_own.reshape(states, own))

    in_flat = lax.optimization_barrier(in_weight.reshape(width, 2 * chans))
    both = jnp.dot(normed_q, in_flat, preferred_element_type=wide)
    both = both.reshape(n_chan, quarter, 2 * chans)
    gate_q = both[:, :, chans:].astype(low)
    sides = jnp.dot(
        normed_side.reshape(-1, width), in_flat[:, :chans], preferred_element_type=wide
    ).reshape(n_chan, 2 * HALO, chans)
    before = chosen_rows(one_before, sides[:, :HALO])
    after = chosen_rows(one_after, sides[:, HALO:])
    inner_win = jnp.concatenate([before, both[:, :, :chans], after], axis=1) * mask_win

    reach = quarter + HALO
    conv_win = conv_offset
    for index in range(taps):
        lag = taps - 1 - index
        shifted = inner_win[:, HALO - lag : HALO - lag + reach]
        conv_win = conv_win + conv_kernel[index] * shifted * valid_at(lag, HALO, reach)
    act_win = jax.nn.silu(conv_win[:, :quarter]) * mask_win[:, HALO : HALO + quarter]
    act_win = act_win.astype(low)
    act_q = act_win.reshape(rows_q, chans)

    partial = jnp.dot(act_q, select, preferred_element_type=wide)
    summed = moves.sum_chan(partial.reshape(n_chan, quarter, small)).astype(low)
    sent = jnp.stack([split_own(act_win), split_own(gate_q)], axis=1)
    channels = moves.swap_state(sent)
    summed, channels = tied(summed, channels)
    picked = moves.gather_near(moves.gather_small(summed))

    if moves.near:
        grad_q = jnp.concatenate(
            [lax.dynamic_index_in_dim(grad_q, blocks[k], 0, keepdims=False) for k in range(8)],
            axis=0,
        )
    grad_q = grad_q.reshape(rows_q, width)
    dgated_q = lax.dot_general(grad_q, out_weight, contract_cols, preferred_element_type=wide)
    dgated_q = dgated_q.astype(low).reshape(n_chan, quarter, chans)
    dgated = list(in_axis(list(moves.swap_state(split_own(dgated_q)))))

    weight_own = mine(delta_weight, 1)
    bias_own = mine(step_bias)[None, :]
    skip_own = mine(skip_weight)[None, :]
    fresh = (place > 0).astype(wide)[:, None]
    spread = spreading(states)
    coeff_two = coeff * math.log2(math.e)
    kept, dpre, gated = forward_scan(
        order, picked, channels, dgated, fresh, weight_own, bias_own, skip_own, coeff_two, spread
    )

    gated = moves.swap_state(gated)
    gated_q = join_own(gated[:, 0]).reshape(rows_q, chans)
    dgate_q = join_own(gated[:, 1]).reshape(rows_q, chans)
    own_sums, other_sums, dscan, delta_grad_own, decay_total, sums = backward_scan(
        order,
        picked,
        channels,
        dgated,
        fresh,
        dpre,
        kept,
        weight_own,
        skip_own,
        coeff_two,
        spread,
    )
    partial = [(other_sums if k % 2 else own_sums)[k // 2] for k in range(n_state)]
    partial = in_axis(partial)
    decay_grad_own = coeff * decay_total
    partial, gated_q = tied(partial, gated_q)
    partial = moves.sum_state(partial)

    branch = jnp.dot(gated_q, out_weight, preferred_element_type=wide)
    out_part = lax.dot_general(gated_q, grad_q, contract_rows, preferred_element_type=wide)
    packed = jnp.concatenate([delta_grad_own, decay_grad_own, sums], axis=0)
    partial, branch, out_part, packed, dscan = tied(
        partial, branch.astype(low), out_part.astype(low), packed, dscan
    )
    dsmall = moves.gather_chan(moves.sum_small(partial).astype(low))[:, :reach]
    dscan_win = join_own(moves.swap_state(dscan))[:, :reach].astype(wide)
    gate_part = lax.dot_general(normed_q, dgate_q, contract_rows, preferred_element_type=wide)
    branch = lax.psum_scatter(
        moves.in_axis_order(branch.reshape(n_chan, quarter, width)).reshape(rows_q, width),
        "chan",
        scatter_dimension=0,
        tiled=True,
    )
    out_grad = moves.total_state(out_part).astype(wide)
    dsmall, dscan_win, dgate_q, gate_part = tied(
        dsmall, dscan_win, dgate_q, gate_part.astype(low)
    )

    dact = dscan_win + lax.dot_general(
        dsmall.reshape(-1, small), select, contract_cols, preferred_element_type=wide
    ).reshape(n_chan, reach, chans)
    dconv = dact * mask_win[:, HALO:] * silu_slope(conv_win)
    dinner = jnp.zeros((n_chan, quarter, chans), wide)
    kernel_rows = []
    for index in range(taps):
        lag = taps - 1 - index
        masked = dconv * valid_at(lag, HALO, reach)
        shifted = inner_win[:, HALO - lag : HALO - lag + quarter]
        kernel_rows.append(jnp.sum(masked[:, :quarter] * shifted, axis=(0, 1)))
        dinner = dinner + masked[:, lag : lag + quarter] * conv_kernel[index]
    kernel_rows.append(jnp.sum(dconv[:, :quarter], axis=(0, 1)))
    dinner = (dinner * mask_win[:, HALO : HALO + quarter]).astype(low).reshape(rows_q, chans)
    dboth = jnp.concatenate([dinner, dgate_q], axis=1)

    def backed(rows, weight):
        return lax.dot_general(rows, weight, contract_cols, preferred_element_type=wide)

    if moves.near:
        half = width // 2
        joined = []
        gains = []
        for columns in (slice(0, half), slice(half, width)):
            gain = jnp.zeros((half,), wide)
            halves = []
            for rows in (slice(rows_q // 2, rows_q), slice(0, rows_q // 2)):
                piece = backed(dboth[rows], in_flat[columns])
                gain = gain + jnp.sum(piece * normed_q[rows, columns].astype(wide), axis=0)
                halves.append(piece.reshape(4, quarter, half))
            joined.append(moves.joined_planes(halves[1], halves[0].astype(low)))
            gains.append(gain)
        joined[0], gains[0], gains[1], dinner = tied(joined[0], gains[0], gains[1], dinner)
        dnormed = jnp.concatenate([moves.summed_planes(v) for v in joined], axis=1)
        gain_part = jnp.concatenate(gains)
    else:
        dnormed = backed(dboth, in_flat)
        gain_part = jnp.sum(dnormed * normed_q.astype(wide), axis=0)
        dnormed = moves.sum_chan(dnormed.reshape(n_chan, quarter, width))
    gain_part = moves.sum_row(gain_part)[None]
    dscaled = dnormed * norm_gain[None, :]
    change = inv_rms * (dscaled - scaled * jnp.mean(dscaled * scaled, axis=1, keepdims=True))
    change = moves.gather_state(jnp.concatenate([change, gain_part], axis=0).astype(low))
    input_grad = cotangent + change[:, :quarter].reshape(rows_dev, width)
    gain_grad = jnp.sum(change[:, quarter].astype(wide), axis=0) / norm_gain

    result = hidden_in + moves.gather_state(branch).reshape(rows_dev, width)
    inner_part = lax.dot_general(normed_q, dinner, contract_rows, preferred_element_type=wide)
    gate_grad = moves.total_state(gate_part)
    in_grad = interleave(moves.total_state(inner_part.astype(low)), gate_grad)

    dsmall_q = dsmall[:, :quarter].reshape(rows_q, small)
    select_grad = lax.dot_general(dsmall_q, act_q, contract_rows, preferred_element_type=wide)
    rest = moves.gather_near(jnp.concatenate([select_grad, jnp.stack(kernel_rows)], axis=0))
    rest = sum(rest)
    rank_grad = rest[:rank].T
    first = rank + part * per_state
    entry_grad = lax.dynamic_slice_in_dim(rest, first, per_state, 0).T
    read_grad = lax.dynamic_slice_in_dim(rest, first + states, per_state, 0).T
    kernel_grad = rest[small : small + taps]
    offset_grad = rest[small + taps]
    packed = jnp.swapaxes(moves.gather_state(packed), 0, 1).reshape(-1, chans)
    delta_grad = packed[:rank]
    decay_grad = lax.dynamic_slice_in_dim(packed, rank + part * per_state, per_state, 0)
    bias_grad = packed[rank + states]
    skip_grad = packed[rank + states + 1]
    return (
        result,
        input_grad,
        gain_grad,
        in_grad,
        kernel_grad,
        offset_grad,
        rank_grad,
        entry_grad,
        read_grad,
        delta_grad,
        bias_grad,
        decay_grad,
        skip_grad,
        out_grad,
    )


def near_shards(
    n_chan,
    n_state,
    hidden_in,
    norm_gain,
    in_weight,
    conv_kernel,
    conv_offset,
    select_rank,
    select_entry,
    select_read,
    delta_weight,
    step_bias,
    decay_log,
    skip_weight,
    out_weight,
    lengths,
    pad_mask,
    cotangent,
):
    rows_dev, width = hidden_in.shape
    tokens = pad_mask.shape[0]
    chans = in_weight.shape[2]
    taps = conv_kernel.shape[0]
    rank = select_rank.shape[1]
    per_state = select_entry.shape[1]
    states = per_state * n_state
    small = rank + 2 * states
    quarter = rows_dev // n_state
    own = chans // n_state
    rows_q = n_chan * quarter
    part = lax.axis_index("state").astype(jnp.uint32)
    contract_rows = (((0,), (0,)), ((), ()))
    contract_cols = (((1,), (1,)), ((), ()))
    moves = Moves(n_chan, n_state)
    blocks = moves.blocks
    planes = jnp.arange(4, dtype=jnp.uint32)
    small_order = jnp.stack([(moves.y ^ u) * 4 + planes for u in (0, 1)], axis=1).reshape(-1)
    order = jnp.concatenate([moves.order, small_order, part[None]]).astype(jnp.int32)
    places = jnp.concatenate([blocks, part[None]]).astype(jnp.int32)
    blocks = blocks.astype(jnp.int32)

    def mine(values, axis=0):
        return lax.dynamic_slice_in_dim(values, part * own, own, axis)

    start = part * quarter
    hidden_q = lax.dynamic_slice_in_dim(hidden_in, start, quarter, 0)
    ahead = (start + (rows_dev - HALO)) % rows_dev
    behind = (start + quarter) % rows_dev
    local = jnp.concatenate(
        [
            hidden_q,
            lax.dynamic_slice_in_dim(hidden_in, behind, HALO, 0),
            lax.dynamic_slice_in_dim(hidden_in, ahead, HALO, 0),
        ],
        axis=0,
    )
    inv_all = lax.rsqrt(jnp.mean(local * local, axis=1, keepdims=True) + epsilon)
    scaled_all = local * inv_all
    normed_all = (scaled_all * norm_gain[None, :]).astype(low)
    inv_rms = inv_all[:quarter]
    scaled = scaled_all[:quarter]
    cot_q = lax.dynamic_slice_in_dim(cotangent, start, quarter, 0).astype(low)
    ranks = (part ^ jnp.arange(n_state, dtype=jnp.uint32)).astype(jnp.int32)

    def trades(values):
        return [values[0]] + [moves.over_state(values[k], k) for k in (1, 2, 3)]

    def core_halves(values):
        cut = values.reshape((2, 2) + values.shape[1:])
        core = part % 2
        return (
            lax.dynamic_index_in_dim(cut, 1 - core, 1, keepdims=False),
            lax.dynamic_index_in_dim(cut, core, 1, keepdims=False),
        )

    def chip_halves(values):
        side = part // 2
        return (
            lax.dynamic_index_in_dim(values, 1 - side, 0, keepdims=False),
            lax.dynamic_index_in_dim(values, side, 0, keepdims=False),
        )

    def total_of(own_part, others):
        total = own_part.astype(wide)
        for piece in others:
            total = total + piece.astype(wide)
        return total.astype(low)

    def added(kept, came):
        return (kept.astype(wide) + came.astype(wide)).astype(low)

    columns = jnp.concatenate([select_entry, select_read], axis=1)
    decay_cut = jnp.swapaxes(decay_log.reshape(per_state, n_state, own), 0, 1)
    across = moves.over_y(normed_all)
    along = [moves.over_z(normed_all, hops) for hops in (1, 2, 3)]
    columns_core = moves.over_state(columns, 1)
    columns_chip = moves.over_state(columns, 2)
    decay_own = moves.swap_state(decay_cut)
    in_flat = in_weight.reshape(width, 2 * chans)
    across, along[0], along[1], along[2], columns_core, columns_chip, decay_own, in_flat, cot_q = tied(
        across, *along, columns_core, columns_chip, decay_own, in_flat, cot_q
    )
    grads = lax.all_gather(cot_q, "chan", axis=0)
    over = [moves.over_y(piece) for piece in along]
    columns_slant = moves.over_state(columns_chip, 1)
    over[0], over[1], over[2], columns_slant = tied(*over, columns_slant)
    pieces = [normed_all] + along + [across] + over

    place = positions(lengths, tokens)
    flags = [pad_mask.astype(wide)]
    flags += [(place >= lag).astype(wide) for lag in range(1, taps)]
    flags = jnp.stack(flags)
    padded = jnp.pad(flags, ((0, 0), (8, 8 + rows_dev)))
    span = quarter + 16
    flags_win = lax.dynamic_slice_in_dim(padded, start, n_chan * rows_dev, 1)
    flags_win = flags_win.reshape(taps, n_chan, rows_dev)[:, :, :span]
    chooser = (blocks[:, None] == jnp.arange(n_chan)[None, :]).astype(wide)
    flags_rows = jnp.einsum("kb,fbr->krf", chooser, flags_win)
    itself = jnp.arange(n_chan, dtype=jnp.int32)
    nearby = blocks[:, None] - blocks[None, :]
    one_before = jnp.where(blocks > 0, jnp.argmax(nearby == 1, axis=1), n_chan)
    one_after = jnp.where(blocks < n_chan - 1, jnp.argmax(nearby == -1, axis=1), n_chan)
    one_before = jnp.where(part == 0, one_before, itself)
    one_after = jnp.where(part == n_state - 1, one_after, itself)
    neighbours = jnp.concatenate([one_before, one_after, blocks[:4] // 2]).astype(jnp.int32)

    columns = moves.in_order((columns, columns_core, columns_chip, columns_slant))
    columns = columns.reshape(n_state, chans, 2, per_state)
    columns = jnp.transpose(columns, (1, 2, 0, 3)).reshape(chans, 2 * states)
    select = jnp.concatenate([select_rank, columns], axis=1)
    coeff = -jnp.exp(decay_own.reshape(states, own))

    normed_q, inner_all, sent, kept, other = project(
        neighbours, pieces, in_flat, flags_rows, conv_kernel, conv_offset[None, :], select, n_state
    )
    reach = quarter + HALO
    channels = moves.swap_state(sent)
    came = moves.over_y(other)
    joined = added(kept, came)
    along = [moves.over_z(joined, hops) for hops in (1, 2, 3)]
    grad_q, *dgated = pull(places, grads, out_weight, n_state)
    along[0], along[1], along[2], *dgated = tied(*along, *dgated)
    summed = total_of(joined, along)
    came = moves.over_y(summed)
    dgated = trades(dgated)
    picked = moves.gather_near(jnp.concatenate([summed, came], axis=0))
    tie = tied(*picked, *dgated, channels)
    picked, dgated, channels = tie[:4], tie[4:8], tie[8]

    weight_own = mine(delta_weight, 1)
    bias_own = mine(step_bias)[None, :]
    skip_own = mine(skip_weight)[None, :]
    fresh = (place > 0).astype(wide)[:, None]
    spread = spreading(states)
    coeff_two = coeff * math.log2(math.e)
    kept, dpre, gated = forward_scan(
        order,
        picked,
        channels,
        dgated,
        fresh,
        weight_own,
        bias_own,
        skip_own,
        coeff_two,
        spread,
    )
    gated = moves.swap_state(gated)
    own_sums, other_sums, dscan, delta_grad_own, decay_total, sums = backward_scan(
        order,
        picked,
        channels,
        dgated,
        fresh,
        dpre,
        kept,
        weight_own,
        skip_own,
        coeff_two,
        spread,
    )
    decay_grad_own = coeff * decay_total
    packed = jnp.concatenate([delta_grad_own, decay_grad_own, sums], axis=0).astype(low)
    own_sums, other_sums, packed, gated, dscan = tied(
        own_sums, other_sums, packed, gated, dscan
    )

    half = width // 2
    first, second = slice(0, half), slice(half, width)
    came = moves.over_state(other_sums, 1)
    branch_kept, sent, second_branch, out_kept, out_sent, dgate_q = emit(
        places, gated, out_weight, grad_q
    )
    came, sent, second_branch, out_sent, dgate_q = tied(
        came, sent, second_branch, out_sent, dgate_q
    )

    chip = added(own_sums, came)
    came = moves.over_state(chip[1], 2)
    branch_came = moves.over_y(sent)
    gate_part = lax.dot_general(normed_q, dgate_q, contract_rows, preferred_element_type=wide)
    gain = jnp.sum(gate_part * in_flat[:, chans:].astype(wide), axis=1)
    gate_part = lax.psum_scatter(gate_part.astype(low), "state", scatter_dimension=0, tiled=True)
    out_came = moves.over_state(out_sent, 1)
    came, gain, out_came = tied(came, gain, out_came)

    joined = added(chip[0], came)
    came = moves.over_y(joined[4:])
    dscan = moves.swap_state(dscan)
    out_part = added(out_kept, out_came)
    out_came = moves.over_state(out_part[1], 2)
    packed_core = moves.over_state(packed, 1)
    came, second_branch, packed_core, branch_came = tied(
        came, second_branch, packed_core, branch_came
    )

    joined = added(joined[:4], came)
    along = [moves.over_z(joined, hops) for hops in (1, 2, 3)]
    second_came = moves.over_y(second_branch)
    along[0], along[1], along[2], second_came, out_came = tied(*along, second_came, out_came)

    partial = total_of(joined, along)
    came = moves.over_y(partial)
    branch_came = jnp.concatenate([branch_came, second_came], axis=2)
    branch = added(branch_kept, branch_came)
    branches = [moves.over_z(branch[4 - hops], hops) for hops in (1, 2, 3)]
    out_part = added(out_part[0], out_came)
    out_chip = moves.over_state(out_part, 2)
    came, partial, dscan, gate_part = tied(came, partial, dscan, gate_part)
    gate_grad = lax.all_gather(gate_part, "state", axis=0, tiled=True)

    dboth, rank_part, rows_part = turn_back(
        places,
        (partial, came),
        dscan,
        select,
        inner_all,
        flags_rows,
        conv_kernel,
        conv_offset[None, :],
        dgate_q,
        rank,
    )

    def backed(rows, weight):
        return lax.dot_general(rows, weight, contract_cols, preferred_element_type=wide)

    edge = width * 11 // 16
    left, right = slice(0, edge), slice(edge, width)
    other, same = slice(rows_q // 2, rows_q), slice(0, rows_q // 2)
    left_sent = backed(dboth[other], in_flat[left]).astype(low).reshape(4, quarter, edge)
    right_all = backed(dboth, in_flat[right]).reshape(2, 4, quarter, width - edge)
    right_sent = [right_all[:, 4 - hops].astype(low) for hops in (1, 2, 3)]
    out_core = moves.over_state(out_part, 1)
    out_slant = moves.over_state(out_chip, 1)
    packed_chip = moves.over_state(packed, 2)
    tie = tied(
        left_sent, dboth, rank_part, out_core, out_slant, packed_chip, *right_sent, *branches
    )
    left_sent, dboth, rank_part, out_core, out_slant, packed_chip = tie[:6]
    right_sent, branches = tie[6:9], tie[9:]

    left_came = moves.over_y(left_sent)
    right_along = [moves.over_z(right_sent[hops - 1], hops) for hops in (1, 2, 3)]
    rank_core = moves.over_state(rank_part, 1)
    left_kept = backed(dboth[same], in_flat[left]).reshape(4, quarter, edge)
    inner_part = lax.dot_general(
        normed_q,
        after(dboth, right_along[0])[:, :chans],
        contract_rows,
        preferred_element_type=wide,
    )
    gain = gain + jnp.sum(inner_part * in_flat[:, :chans].astype(wide), axis=1)
    gain = jnp.concatenate([rows_part, gain.reshape(-1, chans)], axis=0)
    branch = total_of(branch[0], branches)
    tie = tied(
        left_came,
        left_kept,
        inner_part.astype(low),
        gain,
        branch,
        gate_grad,
        rank_core,
        *right_along,
    )
    left_came, left_kept, inner_part, gain, branch, gate_grad, rank_core = tie[:7]
    right_along = tie[7:]
    inner_part = lax.psum_scatter(inner_part, "state", scatter_dimension=0, tiled=True)

    joined = left_kept + left_came.astype(wide)
    left_sum = joined[0]
    left_along = [moves.over_z(joined[4 - hops].astype(low), hops) for hops in (1, 2, 3)]
    right_sum = right_all[:, 0]
    for piece in right_along:
        right_sum = right_sum + piece.astype(wide)
    right_came = moves.over_y(right_sum[1].astype(low))
    gain_came = moves.over_state(gain, 1)
    out_grad = placed(ranks, (out_part, out_core, out_chip, out_slant))
    packed_slant = moves.over_state(packed_chip, 1)
    tie = tied(right_came, gain_came, out_grad, packed_slant, *left_along)
    right_came, gain_came, out_grad, packed_slant = tie[:4]
    left_along = tie[4:]

    for piece in left_along:
        left_sum = left_sum + piece.astype(wide)
    right_sum = right_sum[0] + right_came.astype(wide)
    dnormed = jnp.concatenate([left_sum, right_sum], axis=1)
    dscaled = dnormed * norm_gain[None, :]
    change = inv_rms * (dscaled - scaled * jnp.mean(dscaled * scaled, axis=1, keepdims=True))
    change = change.astype(low)
    change_chip = moves.over_state(change, 2)
    change_core = moves.over_state(change, 1)
    gain = gain + gain_came
    gain_came = moves.over_state(gain, 2)
    rank_sum = added(rank_part, rank_core)
    rank_chip = moves.over_state(rank_sum, 2)
    packed = moves.in_order((packed, packed_core, packed_chip, packed_slant))
    packed = jnp.swapaxes(packed, 0, 1).reshape(-1, chans).astype(wide)
    packs = (
        packed[:rank],
        packed[rank + states],
        lax.dynamic_slice_in_dim(packed, rank + part * per_state, per_state, 0),
        packed[rank + states + 1],
    )
    tie = tied(change_chip, change_core, gain_came, rank_chip, inner_part, *packs)
    change_chip, change_core, gain_came, rank_chip, inner_part = tie[:5]
    packs = tie[5:]
    inner_grad = lax.all_gather(inner_part, "state", axis=0, tiled=True)

    change_slant = moves.over_state(change_chip, 1)
    branch_chip = moves.over_state(branch, 2)
    branch_core = moves.over_state(branch, 1)
    gain = gain + gain_came
    gain_came = moves.over_y(gain[8 + 2 * states :].reshape(width))
    rank_grad = rank_sum.astype(wide) + rank_chip.astype(wide)
    place_at = 8 + part * per_state
    smalls = (
        gain[:taps],
        gain[taps],
        rank_grad,
        lax.dynamic_slice_in_dim(gain, place_at, per_state, 0).T,
        lax.dynamic_slice_in_dim(gain, place_at + states, per_state, 0).T,
        *packs,
    )
    tie = tied(change_slant, branch_chip, branch_core, gain_came, gain, *smalls)
    change_slant, branch_chip, branch_core, gain_came, gain = tie[:5]
    smalls = tie[5:]

    branch_slant = moves.over_state(branch_chip, 1)
    gain = gain[8 + 2 * states :].reshape(width) + gain_came
    gains = [gain] + [moves.over_z(gain, hops) for hops in (1, 2, 3)]
    input_grad = placed(ranks, (change, change_core, change_chip, change_slant), cotangent)
    result = placed(ranks, (branch, branch_core, branch_chip, branch_slant), hidden_in)
    gains = jnp.stack(gains)
    gain_grad = 0.0
    for plane_at in range(4):
        gain_grad = gain_grad + lax.dynamic_index_in_dim(
            gains, (moves.z + 4 - plane_at) % 4, 0, keepdims=False
        )
    gain_grad = gain_grad / norm_gain
    in_grad = interleave(inner_grad, gate_grad)
    return (result, input_grad, gain_grad, in_grad, *smalls, out_grad)


def solution(mesh):
    sizes = dict(mesh.shape)
    program = near_shards if (sizes["chan"], sizes["state"]) == (8, 4) else shards
    return jax.shard_map(
        functools.partial(program, sizes["chan"], sizes["state"]),
        mesh=mesh,
        in_specs=(
            P("chan", None),
            P(),
            P(None, None, "chan"),
            P(None, "chan"),
            P("chan"),
            P("chan", None),
            P("chan", "state"),
            P("chan", "state"),
            P(None, "chan"),
            P("chan"),
            P("state", "chan"),
            P("chan"),
            P("chan", None),
            P(),
            P(),
            P("chan", None),
        ),
        out_specs=(
            P("chan", None),
            P("chan", None),
            P(),
            P(None, None, "chan"),
            P(None, "chan"),
            P("chan"),
            P("chan", None),
            P("chan", "state"),
            P("chan", "state"),
            P(None, "chan"),
            P("chan"),
            P("state", "chan"),
            P("chan"),
            P("chan", None),
        ),
        check_vma=False,
    )
```

```python
import functools
import math

import jax
import jax.numpy as jnp
from jax import lax
from jax.experimental import pallas as pl
from jax.experimental.pallas import tpu as pltpu
from jax.sharding import PartitionSpec as P

epsilon = 1e-05
GROUP = 16
HALO = 4
TAIL = 16
FAR = 1e30
wide = jnp.float32
low = jnp.bfloat16


def spent(microseconds):
    moved = int(microseconds * 3.6e6)
    return pl.CostEstimate(flops=0, bytes_accessed=moved, transcendentals=0)


def in_hbm(values):
    return pltpu.with_memory_space_constraint(values, pltpu.HBM)


def positions(lengths, tokens_all):
    ends = jnp.cumsum(lengths)
    begins = ends - lengths
    places = jnp.arange(tokens_all, dtype=jnp.int32)
    opening = jnp.max(jnp.where(begins[:, None] <= places[None, :], begins[:, None], 0), axis=0)
    return places - opening


def delayed(values, amount):
    if amount == 0:
        return values
    padding = jnp.zeros((amount,) + values.shape[1:], values.dtype)
    return jnp.concatenate([padding, values[: values.shape[0] - amount]], axis=0)


def advanced(values, amount):
    if amount == 0:
        return values
    padding = jnp.zeros((amount,) + values.shape[1:], values.dtype)
    return jnp.concatenate([values[amount:], padding], axis=0)


def silu_slope(values):
    logistic = jax.nn.sigmoid(values)
    return logistic * (1.0 + values * (1.0 - logistic))


def linear_scan(decays, drive):
    total_rows = decays.shape[0]
    blocks = total_rows // 16
    factors = jnp.swapaxes(decays.reshape((blocks, 16) + decays.shape[1:]), 0, 1)
    sources = jnp.swapaxes(drive.reshape((blocks, 16) + drive.shape[1:]), 0, 1)

    def advance(totals, item):
        state_now, product_now = totals
        factor_now, source_now = item
        state_now = factor_now * state_now + source_now
        product_now = factor_now * product_now
        return ((state_now, product_now), (state_now, product_now))

    initial = (jnp.zeros(factors.shape[1:], jnp.float32), jnp.ones(factors.shape[1:], jnp.float32))
    final_pair, (local_states, products) = lax.scan(advance, initial, (factors, sources))

    def combine(early, later):
        return (early[0] * later[0], later[0] * early[1] + later[1])

    joined_factor, joined_state = lax.associative_scan(
        combine, (products[-1], local_states[-1]), axis=0
    )
    entering = jnp.concatenate([jnp.zeros_like(joined_state[:1]), joined_state[:-1]], axis=0)
    states = local_states + products * entering[None]
    return jnp.swapaxes(states, 0, 1).reshape(decays.shape)


def shards(
    hidden_in,
    norm_gain,
    in_weight,
    conv_kernel,
    conv_offset,
    select_rank,
    select_entry,
    select_read,
    delta_weight,
    step_bias,
    decay_log,
    skip_weight,
    out_weight,
    lengths,
    pad_mask,
    cotangent,
):
    rows_dev, width = hidden_in.shape
    tokens_all = pad_mask.shape[0]
    chans = in_weight.shape[2]
    kernel_len = conv_kernel.shape[0]
    per_state = select_entry.shape[1]
    contract_rows = (((0,), (0,)), ((), ()))
    contract_cols = (((1,), (1,)), ((), ()))
    place = positions(lengths, tokens_all)
    fresh = (place > 0).astype(jnp.float32)
    maskf = pad_mask.astype(jnp.float32)[:, None]
    square = jnp.mean(hidden_in * hidden_in, axis=1, keepdims=True)
    inv_rms = lax.rsqrt(square + epsilon)
    scaled = hidden_in * inv_rms
    normed = (scaled * norm_gain[None, :]).astype(jnp.bfloat16)
    in_flat = in_weight.reshape(width, 2 * chans)
    both = jnp.dot(
        lax.all_gather(normed, "chan", axis=0, tiled=True),
        in_flat,
        preferred_element_type=jnp.float32,
    )
    inner = both[:, :chans] * maskf
    gate_in = both[:, chans:]
    valids = []
    shifted = []
    conv = jnp.zeros((tokens_all, chans), jnp.float32) + conv_offset[None, :]
    for index in range(kernel_len):
        lag = kernel_len - 1 - index
        valids.append((place >= lag).astype(jnp.float32)[:, None])
        shifted.append(delayed(inner, lag))
        conv = conv + conv_kernel[index][None, :] * shifted[index] * valids[index]
    act = (jax.nn.silu(conv) * maskf).astype(jnp.bfloat16)
    act_wide = act.astype(jnp.float32)
    pair_map = jnp.concatenate([select_entry, select_read], axis=1)
    rank_part = jnp.dot(act, select_rank, preferred_element_type=jnp.float32)
    pair_part = jnp.dot(act, pair_map, preferred_element_type=jnp.float32)
    raw_sum, pair_sum = lax.psum((rank_part, pair_part), "chan")
    entry = pair_sum[:, :per_state]
    readout = pair_sum[:, per_state:]
    lowrank = raw_sum.astype(jnp.bfloat16)
    dpre = jnp.dot(lowrank, delta_weight, preferred_element_type=jnp.float32) + step_bias[None, :]
    delta = jax.nn.softplus(dpre)
    coeff = -jnp.exp(decay_log)
    decays = jnp.exp(delta[:, None, :] * coeff[None]) * fresh[:, None, None]
    drive = (delta * act_wide)[:, None, :] * entry[:, :, None]
    states = linear_scan(decays, drive)
    scan_part = jnp.sum(readout[:, :, None] * states, axis=1)
    scanned = lax.psum(scan_part, "state")
    mixed = scanned + skip_weight[None, :] * act_wide
    gate_act = jax.nn.silu(gate_in)
    gated = (mixed * gate_act).astype(jnp.bfloat16)
    gated_rows = gated
    branch = lax.psum_scatter(
        jnp.dot(gated_rows, out_weight, preferred_element_type=jnp.float32),
        "chan",
        scatter_dimension=0,
        tiled=True,
    )
    result = hidden_in + branch
    grad_low = cotangent.astype(jnp.bfloat16)
    pieces = lax.all_gather(grad_low, "chan", axis=0, tiled=True)
    gated_rows = gated
    product = lax.dot_general(pieces, out_weight, contract_cols, preferred_element_type=jnp.float32)
    outw_acc = lax.dot_general(
        gated_rows, pieces, contract_rows, preferred_element_type=jnp.float32
    )
    dmix = product * gate_act
    dgate = product * mixed * silu_slope(gate_in)
    skip_grad = jnp.sum(dmix * act_wide, axis=0)
    emitted = readout[:, :, None] * dmix[:, None, :]
    following = jnp.concatenate([decays[1:], jnp.zeros_like(decays[:1])], axis=0)
    adjoint = jnp.flip(linear_scan(jnp.flip(following, 0), jnp.flip(emitted, 0)), 0)
    earlier = jnp.concatenate([jnp.zeros_like(states[:1]), states[:-1]], axis=0)
    flow = adjoint * earlier * decays
    dread_part = jnp.sum(states * dmix[:, None, :], axis=2)
    dentry_part = jnp.sum(adjoint * (delta * act_wide)[:, None, :], axis=2)
    ddelta_part = jnp.sum(
        flow * coeff[None] + adjoint * entry[:, :, None] * act_wide[:, None, :], axis=1
    )
    decay_grad = coeff * jnp.sum(flow * delta[:, None, :], axis=0)
    dact_scan = jnp.sum(adjoint * entry[:, :, None], axis=1) * delta
    dentry_sum, dread_sum = lax.psum((dentry_part, dread_part), "chan")
    dpair = jnp.concatenate(
        [dentry_sum.astype(jnp.bfloat16), dread_sum.astype(jnp.bfloat16)], axis=1
    )
    pair_grad = lax.dot_general(act, dpair, contract_rows, preferred_element_type=jnp.float32)
    entry_grad = pair_grad[:, :per_state]
    read_grad = pair_grad[:, per_state:]
    dact_pair = lax.dot_general(dpair, pair_map, contract_cols, preferred_element_type=jnp.float32)
    dact_state, ddelta = lax.psum((dact_scan + dact_pair, ddelta_part), "state")
    ddpre = (ddelta * jax.nn.sigmoid(dpre)).astype(jnp.bfloat16)
    bias_grad = jnp.sum(ddpre.astype(jnp.float32), axis=0)
    delta_grad = lax.dot_general(lowrank, ddpre, contract_rows, preferred_element_type=jnp.float32)
    dlow_part = lax.dot_general(
        ddpre, delta_weight, contract_cols, preferred_element_type=jnp.float32
    )
    dlow = lax.psum(dlow_part, "chan").astype(jnp.bfloat16)
    rank_grad = lax.dot_general(act, dlow, contract_rows, preferred_element_type=jnp.float32)
    dact = (
        dact_state
        + dmix * skip_weight[None, :]
        + lax.dot_general(dlow, select_rank, contract_cols, preferred_element_type=jnp.float32)
    )
    dconv = dact * maskf * silu_slope(conv)
    offset_grad = jnp.sum(dconv, axis=0)
    kernel_rows = []
    dinner = jnp.zeros((tokens_all, chans), jnp.float32)
    for index in range(kernel_len):
        lag = kernel_len - 1 - index
        masked = dconv * valids[index]
        kernel_rows.append(jnp.sum(masked * shifted[index], axis=0))
        dinner = dinner + advanced(masked * conv_kernel[index][None, :], lag)
    kernel_grad = jnp.stack(kernel_rows, axis=0)
    dboth = jnp.concatenate([dinner * maskf, dgate], axis=1).astype(jnp.bfloat16)
    chosen = dboth
    in_flat_grad = lax.dot_general(
        lax.all_gather(normed, "chan", axis=0, tiled=True),
        chosen,
        contract_rows,
        preferred_element_type=jnp.float32,
    )
    in_grad = in_flat_grad.reshape(width, 2, chans)
    chosen = dboth
    dnormed = lax.psum_scatter(
        lax.dot_general(chosen, in_flat, contract_cols, preferred_element_type=jnp.float32),
        "chan",
        scatter_dimension=0,
        tiled=True,
    )
    gain_part = jnp.sum(dnormed * scaled, axis=0)
    gain_grad = lax.psum(gain_part, "chan")
    dscaled = dnormed * norm_gain[None, :]
    input_grad = cotangent + inv_rms * (
        dscaled - scaled * jnp.mean(dscaled * scaled, axis=1, keepdims=True)
    )
    return (
        result,
        input_grad,
        gain_grad,
        in_grad,
        kernel_grad,
        offset_grad,
        rank_grad,
        entry_grad,
        read_grad,
        delta_grad,
        bias_grad,
        decay_grad,
        skip_grad,
        outw_acc,
    )


def own_block(states):
    row = lax.broadcasted_iota(jnp.int32, (GROUP, GROUP * states), 0)
    col = lax.broadcasted_iota(jnp.int32, (GROUP, GROUP * states), 1)
    return jnp.logical_and(col >= row * states, col < (row + 1) * states)


def spreading(states):
    eye = jnp.eye(states, dtype=low)
    tiled = jnp.tile(eye, (1, GROUP))
    nothing = jnp.zeros_like(tiled)
    return jnp.concatenate(
        [
            jnp.concatenate([tiled, nothing], axis=1),
            jnp.concatenate([nothing, tiled], axis=1),
        ],
        axis=0,
    )


def transposed(values):
    count = values.shape[1]
    row = lax.broadcasted_iota(jnp.int32, (count, count), 0)
    col = lax.broadcasted_iota(jnp.int32, (count, count), 1)
    eye = jnp.where(row == col, 1.0, 0.0).astype(low)
    return lax.dot_general(eye, values, (((1,), (1,)), ((), ())), preferred_element_type=wide)


def forward_body(parts, order_ref, *refs):
    sources, refs = refs[: 2 * parts + 2], refs[2 * parts + 2 :]
    params, (kept_hbm, dpre_hbm, gated_hbm), refs = refs[:5], refs[5:8], refs[8:]
    carry, step_all, drive_all, small_all, dgated_all, pair_all, fresh_all = refs[:7]
    kept_all, dpre_all, gated_all, came, left = refs[7:]
    blocks = small_all.shape[1]
    chunk = step_all.shape[0]
    states = carry.shape[0]

    def entering(turn):
        block = order_ref[turn]
        rows = pl.ds(pl.multiple_of(turn * chunk, chunk), chunk)
        found = []
        for k in range(parts):
            found.append((sources[k].at[order_ref[blocks + turn]], small_all.at[k, turn]))
            found.append((sources[parts + k].at[block], dgated_all.at[k, turn]))
        found.append((sources[2 * parts].at[:, :, block], pair_all.at[:, :, turn]))
        found.append((sources[2 * parts + 1].at[rows], fresh_all.at[rows]))
        return [
            pltpu.make_async_copy(a, b, came.at[turn, i]) for i, (a, b) in enumerate(found)
        ]

    def leaving(turn):
        rows = pl.ds(pl.multiple_of(turn * chunk, chunk), chunk)
        tall = pl.ds(pl.multiple_of(turn * (chunk * states), chunk * states), chunk * states)
        found = [
            (kept_all.at[tall], kept_hbm.at[tall]),
            (dpre_all.at[rows], dpre_hbm.at[rows]),
            (gated_all.at[:, :, turn], gated_hbm.at[:, :, order_ref[turn]]),
        ]
        return [
            pltpu.make_async_copy(a, b, left.at[turn, i]) for i, (a, b) in enumerate(found)
        ]

    @pl.loop(0, blocks)
    def _(turn):
        for copy in entering(turn):
            copy.start()

    carry[...] = jnp.zeros_like(carry)

    @pl.loop(0, blocks)
    def _(turn):
        for copy in entering(turn):
            copy.wait()
        forward_steps(
            turn,
            parts,
            order_ref,
            small_all,
            dgated_all,
            pair_all,
            fresh_all,
            *params,
            kept_all,
            dpre_all,
            gated_all,
            carry,
            step_all,
            drive_all,
        )
        for copy in leaving(turn):
            copy.start()

    @pl.loop(0, blocks)
    def _(turn):
        for copy in leaving(turn):
            copy.wait()


def forward_steps(
    turn,
    parts,
    order_ref,
    small_all,
    dgated_all,
    pair_ref,
    fresh_ref,
    weight_ref,
    bias_ref,
    skip_ref,
    coeff_ref,
    spread_ref,
    kept_ref,
    dpre_ref,
    gated_ref,
    carry,
    step_all,
    drive_all,
):
    coeff = coeff_ref[...]
    states = coeff.shape[0]
    chunk = step_all.shape[0]
    origin = pl.multiple_of(turn * (chunk * states), chunk * states)
    rank = weight_ref.shape[0]
    quarter = small_all.shape[2]
    chosen = own_block(states)
    part = order_ref[order_ref.shape[0] - 1]
    columns = [None] * parts
    reading = [None] * parts

    def before(j):
        rows = slice(j * quarter, (j + 1) * quarter)
        small = small_all[part ^ j, turn]
        dpre = (
            jnp.dot(small[:, :rank], weight_ref[...], preferred_element_type=wide) + bias_ref[...]
        )
        dpre_ref[pl.ds(turn * chunk + j * quarter, quarter), :] = dpre
        delta = jax.nn.softplus(dpre)
        step_all[rows, :] = jnp.where(fresh_ref[pl.ds(turn * chunk + j * quarter, quarter), :].astype(wide) > 0.0, delta, FAR)
        drive_all[rows, :] = delta * pair_ref[j, 0, turn].astype(wide)
        pair = small[:, rank:]
        columns[j] = transposed(pair)
        reading[j] = jnp.dot(
            pair, spread_ref[:, GROUP * states :], preferred_element_type=wide
        )

    def scan(j, state):
        for group in range(quarter // GROUP):
            base = j * quarter + group * GROUP
            kept = []
            for t in range(base, base + GROUP):
                here = t - j * quarter
                decay = jnp.exp2(step_all[t : t + 1, :] * coeff)
                entry = columns[j][:states, here : here + 1]
                state = decay * state + drive_all[t : t + 1, :] * entry
                kept.append(state)
            rows = pl.ds(origin + base * states, GROUP * states)
            kept_ref[rows, :] = jnp.concatenate(kept, axis=0).astype(low)
        return state

    def finish_part(j):
        found = []
        for group in range(quarter // GROUP):
            base = j * quarter + group * GROUP
            block = kept_ref[pl.ds(origin + base * states, GROUP * states), :]
            here = reading[j][group * GROUP : (group + 1) * GROUP]
            weights = jnp.where(chosen, here, 0.0).astype(low)
            found.append(jnp.dot(weights, block, preferred_element_type=wide))
        act = pair_ref[j, 0, turn].astype(wide)
        gate = pair_ref[j, 1, turn].astype(wide)
        mixed = jnp.concatenate(found, axis=0) + skip_ref[...] * act
        dgated = dgated_all[part ^ j, turn].astype(wide)
        gated_ref[j, 0, turn] = (mixed * jax.nn.silu(gate)).astype(low)
        gated_ref[j, 1, turn] = (dgated * mixed * silu_slope(gate)).astype(low)

    state = carry[...]
    before(0)
    for j in range(parts):
        if j + 1 < parts:
            before(j + 1)
        state = scan(j, state)
        if j:
            finish_part(j - 1)
    finish_part(parts - 1)
    carry[...] = state


def backward_body(parts, order_ref, *refs):
    sources, refs = refs[: 2 * parts + 4], refs[2 * parts + 4 :]
    params, (own_hbm, other_hbm, dscan_hbm), refs = refs[:4], refs[4:7], refs[7:]
    results, refs = refs[:3], refs[3:]
    scratch, refs = refs[:11], refs[11:]
    (small_all, dgated_all, pair_all, fresh_all, dpre_all, kept_all, edge_all) = refs[:7]
    (own_all, other_all, dscan_all, came, left) = refs[7:]
    blocks = small_all.shape[1]
    chunk = scratch[1].shape[0]
    states = scratch[0].shape[0]
    for ref in (scratch[0], *results, *scratch[8:10]):
        ref[...] = jnp.zeros_like(ref)

    def entering(turn):
        at = blocks - 1 - turn
        block = order_ref[at]
        rows = pl.ds(pl.multiple_of(at * chunk, chunk), chunk)
        tall = pl.ds(pl.multiple_of(at * (chunk * states), chunk * states), chunk * states)
        found = []
        for k in range(parts):
            found.append((sources[k].at[order_ref[blocks + at]], small_all.at[k, at]))
            found.append((sources[parts + k].at[block], dgated_all.at[k, at]))
        found.append((sources[2 * parts].at[:, :, block], pair_all.at[:, :, at]))
        for source, target, here in zip(
            sources[2 * parts + 1 :], (fresh_all, dpre_all, kept_all), (rows, rows, tall)
        ):
            found.append((source.at[here], target.at[here]))
        ahead = pl.multiple_of(jnp.maximum(at * (chunk * states) - states, 0), states)
        found.append((sources[-1].at[pl.ds(ahead, states)], edge_all.at[at]))
        return [
            pltpu.make_async_copy(a, b, came.at[turn, i]) for i, (a, b) in enumerate(found)
        ]

    def leaving(turn):
        at = blocks - 1 - turn
        block = order_ref[at]
        place = order_ref[blocks + at]
        found = [
            (own_all.at[:, at], own_hbm.at[:, place]),
            (other_all.at[:, at], other_hbm.at[:, place]),
            (dscan_all.at[:, at], dscan_hbm.at[:, block]),
        ]
        return [
            pltpu.make_async_copy(a, b, left.at[turn, i]) for i, (a, b) in enumerate(found)
        ]

    @pl.loop(0, blocks)
    def _(turn):
        for copy in entering(turn):
            copy.start()

    @pl.loop(0, blocks)
    def _(turn):
        for copy in entering(turn):
            copy.wait()
        backward_steps(
            turn,
            parts,
            blocks,
            order_ref,
            small_all,
            dgated_all,
            pair_all,
            fresh_all,
            dpre_all,
            kept_all,
            edge_all,
            *params,
            own_all,
            other_all,
            dscan_all,
            *results,
            *scratch,
        )
        for copy in leaving(turn):
            copy.start()

    @pl.loop(0, blocks)
    def _(turn):
        for copy in leaving(turn):
            copy.wait()


def backward_steps(
    turn,
    parts,
    blocks,
    order_ref,
    small_all,
    dgated_all,
    pair_ref,
    fresh_ref,
    dpre_ref,
    kept_ref,
    edge_ref,
    weight_ref,
    skip_ref,
    coeff_ref,
    spread_ref,
    own_ref,
    other_ref,
    dscan_ref,
    delta_grad_ref,
    decay_ref,
    sums_ref,
    carry,
    step_all,
    drive_all,
    delta_all,
    dmix_all,
    lam_all,
    flow_all,
    cross_all,
    next_partial,
    next_dscan,
    partial_all,
):
    coeff = coeff_ref[...]
    states = coeff.shape[0]
    rank = weight_ref.shape[0]
    quarter = small_all.shape[2]
    chosen = own_block(states)
    ones = jnp.where(chosen, 1.0, 0.0).astype(low)
    across = (((1,), (1,)), ((), ()))
    down = (((0,), (0,)), ((), ()))
    part = order_ref[order_ref.shape[0] - 1]
    chunk = step_all.shape[0]
    block_turn = blocks - 1 - turn
    origin = pl.multiple_of(block_turn * (chunk * states), chunk * states)
    first = jnp.where(block_turn == 0, 0.0, edge_ref[block_turn].astype(wide))
    columns = [None] * parts
    entering = [None] * parts
    after_partial = [next_partial[...]]
    after_dscan = [next_dscan[...]]

    def before(j):
        rows = slice(j * quarter, (j + 1) * quarter)
        small = small_all[part ^ j, block_turn]
        delta = jax.nn.softplus(dpre_ref[pl.ds(block_turn * chunk + j * quarter, quarter), :])
        act = pair_ref[j, 0, block_turn].astype(wide)
        gate = pair_ref[j, 1, block_turn].astype(wide)
        step_all[rows, :] = jnp.where(fresh_ref[pl.ds(block_turn * chunk + j * quarter, quarter), :].astype(wide) > 0.0, delta, FAR)
        drive_all[rows, :] = delta * act
        delta_all[rows, :] = delta
        dmix_all[rows, :] = dgated_all[part ^ j, block_turn].astype(wide) * jax.nn.silu(gate)
        pair = small[:, rank:]
        columns[j] = transposed(pair)
        entering[j] = jnp.dot(
            pair, spread_ref[:, : GROUP * states], preferred_element_type=wide
        )

    def scan(j, pulled, summed):
        for group in range(quarter // GROUP - 1, -1, -1):
            base = j * quarter + group * GROUP
            lams = [None] * GROUP
            flows = [None] * GROUP
            rows = slice(base * states, (base + GROUP) * states)
            block = kept_ref[pl.ds(origin + base * states, GROUP * states), :].astype(wide)
            if base:
                edge = kept_ref[pl.ds(origin + (base - 1) * states, states), :].astype(wide)
            else:
                edge = first
            for i in range(GROUP - 1, -1, -1):
                t = base + i
                here = t - j * quarter
                read = columns[j][states:, here : here + 1]
                lam = read * dmix_all[t : t + 1, :] + pulled
                pulled = jnp.exp2(step_all[t : t + 1, :] * coeff) * lam
                flow = pulled * (block[(i - 1) * states : i * states] if i else edge)
                summed = summed + flow * delta_all[t : t + 1, :]
                lams[i] = lam
                flows[i] = flow * coeff
            lam_all[rows, :] = jnp.concatenate(lams, axis=0).astype(low)
            flow_all[rows, :] = jnp.concatenate(flows, axis=0).astype(low)
        return pulled, summed

    def finish_part(j):
        part_rows = slice(j * quarter, (j + 1) * quarter)
        lam_found = []
        flow_found = []
        for group in range(quarter // GROUP):
            base = j * quarter + group * GROUP
            here = slice(base, base + GROUP)
            rows = slice(base * states, (base + GROUP) * states)
            lam_block = lam_all[rows, :]
            entry = entering[j][group * GROUP : (group + 1) * GROUP]
            weights = jnp.where(chosen, entry, 0.0).astype(low)
            lam_found.append(jnp.dot(weights, lam_block, preferred_element_type=wide))
            flow_found.append(jnp.dot(ones, flow_all[rows, :], preferred_element_type=wide))
            cross = lax.dot_general(
                drive_all[here, :].astype(low), lam_block, across, preferred_element_type=wide
            )
            cross_all[here, : GROUP * states] = jnp.where(chosen, cross, 0.0).astype(low)
            cross = lax.dot_general(
                dmix_all[here, :].astype(low),
                kept_ref[pl.ds(origin + base * states, GROUP * states), :],
                across,
                preferred_element_type=wide,
            )
            cross_all[here, GROUP * states :] = jnp.where(chosen, cross, 0.0).astype(low)
        dpair = lax.dot_general(
            cross_all[part_rows, :], spread_ref[...], across, preferred_element_type=wide
        ).astype(low)
        found = jnp.concatenate(lam_found, axis=0)
        act = pair_ref[j, 0, block_turn].astype(wide)
        delta = delta_all[part_rows, :]
        dmix = dmix_all[part_rows, :]
        ddelta = jnp.concatenate(flow_found, axis=0) * (1.0 / math.log2(math.e)) + found * act
        ddpre = (ddelta * jax.nn.sigmoid(dpre_ref[pl.ds(block_turn * chunk + j * quarter, quarter), :])).astype(low)
        small = small_all[part ^ j, block_turn]
        delta_grad_ref[...] += lax.dot_general(
            small[:, :rank], ddpre, down, preferred_element_type=wide
        )
        dlow = lax.dot_general(
            ddpre, weight_ref[...], across, preferred_element_type=wide
        ).astype(low)
        dscan = (found * delta + dmix * skip_ref[...]).astype(low)
        sums_ref[0:1, :] += jnp.sum(ddpre.astype(wide), axis=0, keepdims=True)
        sums_ref[1:2, :] += jnp.sum(dmix * act, axis=0, keepdims=True)
        after_rows = after_partial[0]
        partial_all[j, :quarter, :rank] = dlow
        partial_all[j, :quarter, rank:] = dpair
        partial_all[j, quarter:, :] = after_rows
        dscan_ref[j, block_turn, :quarter, :] = dscan
        dscan_ref[j, block_turn, quarter:, :] = after_dscan[0]
        after_partial[0] = jnp.concatenate([dlow[:TAIL], dpair[:TAIL]], axis=1)
        after_dscan[0] = dscan[:TAIL]

    pulled = carry[...]
    summed = decay_ref[...]
    before(parts - 1)
    for j in range(parts - 1, -1, -1):
        if j:
            before(j - 1)
        pulled, summed = scan(j, pulled, summed)
        if j + 1 < parts:
            finish_part(j + 1)
    finish_part(0)
    carry[...] = pulled
    decay_ref[...] = summed
    next_partial[...] = after_partial[0]
    next_dscan[...] = after_dscan[0]
    for k in range(parts):
        (other_ref if k % 2 else own_ref)[k // 2, block_turn] = partial_all[part ^ k]


def forward_scan(order, small, pair, dgated, fresh, weight, bias, skip, coeff, spread):
    parts, _, blocks, quarter, width = pair.shape
    states = coeff.shape[0]
    columns = small[0].shape[-1]
    chunk = parts * quarter
    tokens = blocks * chunk
    streamed = (*small, *dgated, pair, fresh)
    params = (weight, bias, skip, coeff, spread)
    apart = pl.BlockSpec(memory_space=pl.ANY)
    kept = (tokens * states, width)
    gated = (parts, 2, blocks, quarter, width)
    return pl.pallas_call(
        functools.partial(forward_body, parts),
        grid_spec=pltpu.PrefetchScalarGridSpec(
            num_scalar_prefetch=1,
            grid=(1,),
            in_specs=[apart] * len(streamed)
            + [pl.BlockSpec(v.shape, lambda t, order: (0, 0)) for v in params],
            out_specs=[apart] * 3,
            scratch_shapes=[
                pltpu.VMEM((states, width), wide),
                pltpu.VMEM((chunk, width), wide),
                pltpu.VMEM((chunk, width), wide),
                pltpu.VMEM((parts, blocks, quarter, columns), low),
                pltpu.VMEM((parts, blocks, quarter, width), low),
                pltpu.VMEM(gated, low),
                pltpu.VMEM((tokens, width), low),
                pltpu.VMEM(kept, low),
                pltpu.VMEM((tokens, width), wide),
                pltpu.VMEM(gated, low),
                pltpu.SemaphoreType.DMA((blocks, len(streamed) + 1)),
                pltpu.SemaphoreType.DMA((blocks, 3)),
            ],
        ),
        out_shape=[
            pltpu.HBM(kept, low),
            pltpu.HBM((tokens, width), wide),
            pltpu.HBM(gated, low),
        ],
        compiler_params=pltpu.CompilerParams(vmem_limit_bytes=28 * 1024 * 1024),
        cost_estimate=spent(12),
        name="forward_scan",
    )(order, *map(in_hbm, streamed), *params)


def backward_scan(
    order, small, pair, dgated, fresh, dpre, kept, weight, skip, coeff, spread
):
    parts, _, blocks, quarter, width = pair.shape
    states = coeff.shape[0]
    rank = weight.shape[0]
    columns = small[0].shape[-1]
    chunk = parts * quarter
    tokens = blocks * chunk
    streamed = (*small, *dgated, pair, fresh, dpre, kept)
    params = (weight, skip, coeff, spread)
    apart = pl.BlockSpec(memory_space=pl.ANY)
    sums = (parts // 2, blocks, quarter + TAIL, columns)
    dscan = (parts, blocks, quarter + TAIL, width)
    results = ((rank, width), (states, width), (8, width))
    return pl.pallas_call(
        functools.partial(backward_body, parts),
        grid_spec=pltpu.PrefetchScalarGridSpec(
            num_scalar_prefetch=1,
            grid=(1,),
            in_specs=[apart] * len(streamed)
            + [pl.BlockSpec(v.shape, lambda t, order: (0, 0)) for v in params],
            out_specs=[apart] * 3 + [pl.BlockSpec(v, lambda t, order: (0, 0)) for v in results],
            scratch_shapes=[pltpu.VMEM((states, width), wide)]
            + [pltpu.VMEM((chunk, width), wide)] * 4
            + [pltpu.VMEM((chunk * states, width), low)] * 2
            + [
                pltpu.VMEM((chunk, 2 * GROUP * states), low),
                pltpu.VMEM((TAIL, columns), low),
                pltpu.VMEM((TAIL, width), low),
                pltpu.VMEM((parts, quarter + TAIL, columns), low),
                pltpu.VMEM((parts, blocks, quarter, columns), low),
                pltpu.VMEM((parts, blocks, quarter, width), low),
                pltpu.VMEM(pair.shape, low),
                pltpu.VMEM((tokens, width), low),
                pltpu.VMEM((tokens, width), wide),
                pltpu.VMEM((tokens * states, width), low),
                pltpu.VMEM((blocks, states, width), low),
                pltpu.VMEM(sums, low),
                pltpu.VMEM(sums, low),
                pltpu.VMEM(dscan, low),
                pltpu.SemaphoreType.DMA((blocks, len(streamed) + 1)),
                pltpu.SemaphoreType.DMA((blocks, 3)),
            ],
        ),
        out_shape=[pltpu.HBM(sums, low), pltpu.HBM(sums, low), pltpu.HBM(dscan, low)]
        + [jax.ShapeDtypeStruct(v, wide) for v in results],
        compiler_params=pltpu.CompilerParams(vmem_limit_bytes=28 * 1024 * 1024),
        cost_estimate=spent(19),
        name="backward_scan",
    )(order, *map(in_hbm, streamed), *params)


def interleave_body(inner_ref, gate_ref, out_ref):
    out_ref[:, 0, :] = inner_ref[...].astype(wide)
    out_ref[:, 1, :] = gate_ref[...].astype(wide)


def interleave(inner, gate):
    rows, width = inner.shape
    block = 256
    spec = pl.BlockSpec((block, width), lambda t: (t, 0))
    return pl.pallas_call(
        interleave_body,
        grid=(rows // block,),
        in_specs=[spec, spec],
        out_specs=pl.BlockSpec((block, 2, width), lambda t: (t, 0, 0)),
        out_shape=jax.ShapeDtypeStruct((rows, 2, width), wide),
        compiler_params=pltpu.CompilerParams(vmem_limit_bytes=16 * 1024 * 1024),
        cost_estimate=spent(5),
        name="interleave",
    )(inner, gate)


def placed_body(parts, order_ref, *refs):
    values, out_ref = refs[:parts], refs[-1]
    place = order_ref[pl.program_id(0)]
    for k in range(parts):

        @pl.when(place == k)
        def _(k=k):
            value = values[k][...].astype(wide)
            out_ref[...] = refs[parts][...] + value if len(refs) > parts + 1 else value


def placed(order, values, base=None):
    parts = len(values)
    rows, width = values[0].shape
    flat = pl.BlockSpec((rows, width), lambda p, order: (p, 0))
    return pl.pallas_call(
        functools.partial(placed_body, parts),
        grid_spec=pltpu.PrefetchScalarGridSpec(
            num_scalar_prefetch=1,
            grid=(parts,),
            in_specs=[pl.BlockSpec((rows, width), lambda p, order: (0, 0))] * parts
            + ([] if base is None else [flat]),
            out_specs=flat,
        ),
        out_shape=jax.ShapeDtypeStruct((parts * rows, width), wide),
        compiler_params=pltpu.CompilerParams(vmem_limit_bytes=24 * 1024 * 1024),
        cost_estimate=spent(2.5),
        name="placed",
    )(order, *values, *(() if base is None else (base,)))


def project_body(
    place_ref,
    *refs,
):
    pieces, refs = refs[:8], refs[8:]
    (weight_ref, flags_ref, taps_ref, offset_ref, select_ref) = refs[:5]
    (normed_ref, inner_ref, channels_ref, kept_ref, sent_ref) = refs[5:10]
    (sides, edges, window, total, acts) = refs[10:]
    turn = pl.program_id(0)
    quarter = channels_ref.shape[3]
    width = channels_ref.shape[4]
    halves = weight_ref.shape[1] // width
    taps = taps_ref.shape[0]
    inner_turns = pl.num_programs(0) // 2
    count = len(pieces)

    @pl.when(turn == 0)
    def _():
        for k in range(count):
            piece = pieces[k][...]
            normed_ref[k * quarter : (k + 1) * quarter, :] = piece[:quarter]
            sides[k * 8 : (k + 1) * 8, :] = piece[quarter:].astype(wide)
        edges[...] = jnp.zeros_like(edges)
        total[...] = jnp.zeros_like(total)

    main = jnp.dot(normed_ref[...], weight_ref[...], preferred_element_type=wide)

    @pl.when(turn < inner_turns)
    def _():
        edges[: count * 8, :] = jnp.dot(
            sides[...].astype(low), weight_ref[...], preferred_element_type=wide
        )
        for k in range(count):
            before = pl.multiple_of(place_ref[k] * 8, 8)
            after = pl.multiple_of(place_ref[count + k] * 8, 8)
            flags = flags_ref[k]
            window[0:8, :] = edges[pl.ds(before, 8), :]
            window[8 : 8 + quarter, :] = main[k * quarter : (k + 1) * quarter]
            window[8 + quarter : 16 + quarter, :] = edges[pl.ds(after, 8), :]
            masked = window[...] * flags[:, 0:1]
            window[...] = masked
            inner_ref[k] = masked
            conv = offset_ref[...] + taps_ref[taps - 1 : taps, :] * masked[8 : 8 + quarter]
            for lag in range(1, taps):
                shifted = window[8 - lag : 8 - lag + quarter, :]
                valid = flags[8 : 8 + quarter, lag : lag + 1]
                conv = conv + taps_ref[taps - 1 - lag : taps - lag, :] * shifted * valid
            act = (jax.nn.silu(conv) * flags[8 : 8 + quarter, 0:1]).astype(low)
            acts[k * quarter : (k + 1) * quarter, :] = act
            for h in range(halves):
                channels_ref[h, 0, k] = act[:, h * width : (h + 1) * width]
        total[...] += jnp.dot(acts[...], select_ref[...], preferred_element_type=wide)

    @pl.when(turn >= inner_turns)
    def _():
        gate = main.astype(low)
        for k in range(count):
            for h in range(halves):
                channels_ref[h, 0, k] = gate[
                    k * quarter : (k + 1) * quarter, h * width : (h + 1) * width
                ]

    @pl.when(turn == pl.num_programs(0) - 1)
    def _():
        for k in range(count // 2):
            plane = place_ref[2 * count + k]
            kept_ref[plane] = total[k * quarter : (k + 1) * quarter, :]
            other = k + count // 2
            sent_ref[plane] = total[other * quarter : (other + 1) * quarter, :].astype(low)


def project(places, pieces, weight, flags, taps, offset, select, parts):
    count = len(pieces)
    rows, depth = pieces[0].shape
    quarter = rows - 8
    chans = weight.shape[1] // 2
    width = chans // parts
    tile = 2 * width
    turns = 2 * chans // tile
    half = turns // 2
    small = select.shape[1]

    def whole(shape):
        return pl.BlockSpec(shape, lambda t, place: (0,) * len(shape))

    def inner(t):
        return jnp.minimum(t, half - 1)

    return pl.pallas_call(
        project_body,
        grid_spec=pltpu.PrefetchScalarGridSpec(
            num_scalar_prefetch=1,
            grid=(turns,),
            in_specs=[whole(pieces[0].shape) for _ in pieces]
            + [
                pl.BlockSpec((depth, tile), lambda t, place: (0, t)),
                whole(flags.shape),
                pl.BlockSpec((taps.shape[0], tile), lambda t, place: (0, inner(t))),
                pl.BlockSpec((1, tile), lambda t, place: (0, inner(t))),
                pl.BlockSpec((tile, small), lambda t, place: (inner(t), 0)),
            ],
            out_specs=[
                whole((count * quarter, depth)),
                pl.BlockSpec((count, quarter + 16, tile), lambda t, place: (0, 0, inner(t))),
                pl.BlockSpec(
                    (2, 1, count, quarter, width),
                    lambda t, place: (t % half, t // half, 0, 0, 0),
                ),
                whole((count // 2, quarter, small)),
                whole((count // 2, quarter, small)),
            ],
            scratch_shapes=[
                pltpu.VMEM((count * 8, depth), wide),
                pltpu.VMEM((count * 8 + 8, tile), wide),
                pltpu.VMEM((quarter + 16, tile), wide),
                pltpu.VMEM((count * quarter, small), wide),
                pltpu.VMEM((count * quarter, tile), low),
            ],
        ),
        out_shape=[
            pltpu.HBM((count * quarter, depth), low),
            pltpu.HBM((count, quarter + 16, chans), wide),
            jax.ShapeDtypeStruct((parts, 2, count, quarter, width), low),
            jax.ShapeDtypeStruct((count // 2, quarter, small), wide),
            jax.ShapeDtypeStruct((count // 2, quarter, small), low),
        ],
        compiler_params=pltpu.CompilerParams(vmem_limit_bytes=28 * 1024 * 1024),
        cost_estimate=spent(8),
        name="project",
    )(places, *map(in_hbm, (*pieces, weight, flags, taps, offset, select)))


def pull_body(order_ref, rows_ref, weight_ref, kept_ref, *refs):
    out_refs, found_ref = refs[:-1], refs[-1]
    count = rows_ref.shape[0]
    quarter = rows_ref.shape[1]
    width = out_refs[0].shape[2]
    turn = pl.program_id(0)
    bit = order_ref[count] & 1

    @pl.when(turn == 0)
    def _():
        for k in range(count):
            kept_ref[k * quarter : (k + 1) * quarter, :] = rows_ref[order_ref[k]]

    found_ref[...] = lax.dot_general(
        kept_ref[...], weight_ref[...], (((1,), (1,)), ((), ())), preferred_element_type=wide
    ).astype(low)
    for p in range(len(out_refs)):

        @pl.when(turn == p // 2)
        def _(p=p):
            here = pl.ds(pl.multiple_of((bit ^ (p % 2)) * width, width), width)
            for k in range(count):
                out_refs[p][k] = found_ref[k * quarter : (k + 1) * quarter, here]


def pull(order, rows, weight, parts):
    count, quarter, depth = rows.shape
    width = weight.shape[0] // parts
    piece = pl.BlockSpec((count, quarter, width), lambda t, order: (0, 0, 0))
    return pl.pallas_call(
        pull_body,
        grid_spec=pltpu.PrefetchScalarGridSpec(
            num_scalar_prefetch=1,
            grid=(parts // 2,),
            in_specs=[
                pl.BlockSpec((count, quarter, depth), lambda t, order: (0, 0, 0)),
                pl.BlockSpec((2 * width, depth), lambda t, order: ((order[count] // 2) ^ t, 0)),
            ],
            out_specs=[pl.BlockSpec((count * quarter, depth), lambda t, order: (0, 0))]
            + [piece] * parts,
            scratch_shapes=[pltpu.VMEM((count * quarter, 2 * width), low)],
        ),
        out_shape=[pltpu.HBM((count * quarter, depth), low)]
        + [pltpu.HBM((count, quarter, width), low)] * parts,
        compiler_params=pltpu.CompilerParams(vmem_limit_bytes=20 * 1024 * 1024),
        cost_estimate=spent(6),
        name="pull",
    )(order, in_hbm(rows), in_hbm(weight))


def emit_body(order_ref, *refs):
    pieces_ref, refs = refs[0], refs[1:]
    parts = pieces_ref.shape[0]
    (weight_ref, rows_ref, kept_ref, first_ref, second_ref, own_ref, other_ref) = refs[:7]
    (dgate_ref, gated, product) = refs[7:]
    turn = pl.program_id(0)
    half = pl.num_programs(0) // 4
    count, quarter, width = pieces_ref.shape[2:]

    @pl.when(pl.program_id(0) == 0)
    def _():
        for p in range(parts):
            here = slice(p * width, (p + 1) * width)
            for k in range(count):
                rows = slice(k * quarter, (k + 1) * quarter)
                gated[rows, here] = pieces_ref[p, 0, k]
                dgate_ref[rows, here] = pieces_ref[p, 1, k]

    values = gated[...]
    branch = jnp.dot(values, weight_ref[...], preferred_element_type=wide).astype(low)
    for k in range(count // 2):
        kept_ref[k] = branch[k * quarter : (k + 1) * quarter]
    other = branch[count // 2 * quarter :].reshape(count // 2, quarter, branch.shape[1])

    @pl.when(turn < half)
    def _():
        first_ref[...] = other

    @pl.when(turn >= half)
    def _():
        second_ref[...] = other

    product[...] = lax.dot_general(
        values, rows_ref[...], (((0,), (0,)), ((), ())), preferred_element_type=wide
    ).astype(low)
    part = order_ref[count]
    for p in range(parts):
        here = pl.ds(pl.multiple_of((part ^ p) * width, width), width)
        (other_ref if p % 2 else own_ref)[p // 2] = product[here, :]


def emit(order, pieces, weight, rows):
    parts, _, count, quarter, width = pieces.shape
    depth = weight.shape[1]
    tile = 512
    half = depth // tile // 4
    chans = parts * width
    tall = count * quarter
    return pl.pallas_call(
        emit_body,
        grid_spec=pltpu.PrefetchScalarGridSpec(
            num_scalar_prefetch=1,
            grid=(depth // tile,),
            in_specs=[
                pl.BlockSpec(pieces.shape, lambda t, order: (0, 0, 0, 0, 0)),
                pl.BlockSpec((chans, tile), lambda t, order: (0, t)),
                pl.BlockSpec((tall, tile), lambda t, order: (0, t)),
            ],
            out_specs=[
                pl.BlockSpec((count // 2, quarter, tile), lambda t, order: (0, 0, t)),
                pl.BlockSpec(
                    (count // 2, quarter, tile), lambda t, order: (0, 0, jnp.minimum(t, half - 1))
                ),
                pl.BlockSpec(
                    (count // 2, quarter, tile), lambda t, order: (0, 0, jnp.maximum(t - half, 0))
                ),
                pl.BlockSpec((parts // 2, width, tile), lambda t, order: (0, 0, t)),
                pl.BlockSpec((parts // 2, width, tile), lambda t, order: (0, 0, t)),
                pl.BlockSpec((tall, chans), lambda t, order: (0, 0)),
            ],
            scratch_shapes=[pltpu.VMEM((tall, chans), low), pltpu.VMEM((chans, tile), low)],
        ),
        out_shape=[
            pltpu.HBM((count // 2, quarter, depth), low),
            pltpu.HBM((count // 2, quarter, half * tile), low),
            pltpu.HBM((count // 2, quarter, depth - half * tile), low),
            pltpu.HBM((parts // 2, width, depth), low),
            pltpu.HBM((parts // 2, width, depth), low),
            pltpu.HBM((tall, chans), low),
        ],
        compiler_params=pltpu.CompilerParams(vmem_limit_bytes=20 * 1024 * 1024),
        cost_estimate=spent(6),
        name="emit",
    )(order, in_hbm(pieces), in_hbm(weight), in_hbm(rows))


def turn_body(order_ref, *refs):
    count = 8
    smalls, refs = refs[:2], refs[2:]
    (dscan_ref, select_ref, inner_ref, flags_ref, taps_ref, offset_ref, dgate_ref) = refs[:7]
    (dboth_ref, grad_ref, rows_ref) = refs[7:10]
    (small_all, shifted, acts) = refs[10:]
    rank = grad_ref.shape[1]
    parts = pl.num_programs(0) // 2
    turn = pl.program_id(0)
    span = inner_ref.shape[1]
    quarter = span - 16
    reach = quarter + 8
    taps = taps_ref.shape[0]

    @pl.when(turn == 0)
    def _():
        for k in range(count):
            plane = order_ref[k] // 2
            small_all[k * span : (k + 1) * span, :] = smalls[k // (count // 2)][plane]

    @pl.when(turn < parts)
    def _():
        whole = lax.dot_general(
            small_all[...],
            select_ref[...],
            (((1,), (1,)), ((), ())),
            preferred_element_type=wide,
        )
        found = dscan_ref[0]
        sums = [0.0] * (taps + 1)
        for k in range(count):
            flags = flags_ref[k, 8 : 8 + reach, :]
            mask = flags[:, 0:1]
            conv = offset_ref[...]
            for lag in range(taps):
                term = taps_ref[taps - 1 - lag : taps - lag, :] * inner_ref[
                    k, 8 - lag : 8 - lag + reach, :
                ]
                conv = conv + (term * flags[:, lag : lag + 1] if lag else term)
            sig = jax.nn.sigmoid(conv)
            act = conv * sig * mask
            acts[k * quarter : (k + 1) * quarter, :] = act[:quarter].astype(low)
            dact = found[k, :reach].astype(wide) + whole[k * span : k * span + reach]
            dconv = dact * mask * (sig * (1.0 + conv * (1.0 - sig)))
            dinner = 0.0
            for lag in range(taps):
                masked = dconv * flags[:, lag : lag + 1] if lag else dconv
                sums[taps - 1 - lag] += jnp.sum(
                    masked[:quarter] * inner_ref[k, 8 - lag : 8 - lag + quarter, :],
                    axis=0,
                    keepdims=True,
                )
                if lag:
                    shifted[lag, :reach, :] = masked
                    masked = shifted[lag, lag : lag + quarter, :]
                else:
                    sums[taps] += jnp.sum(masked[:quarter], axis=0, keepdims=True)
                    masked = masked[:quarter]
                dinner = dinner + masked * taps_ref[taps - 1 - lag : taps - lag, :]
            dboth_ref[k * quarter : (k + 1) * quarter, :] = (dinner * mask[:quarter]).astype(low)
        for index, value in enumerate(sums):
            rows_ref[index : index + 1, :] = value
        mains = jnp.concatenate(
            [small_all[k * span : k * span + quarter, :] for k in range(count)], axis=0
        )
        grad_ref[...] = lax.dot_general(
            acts[...], mains[:, :rank], (((0,), (0,)), ((), ())), preferred_element_type=wide
        ).astype(low)
        rows_ref[8:, :] = lax.dot_general(
            mains[:, rank:], acts[...], (((0,), (0,)), ((), ())), preferred_element_type=wide
        )

    @pl.when(turn >= parts)
    def _():
        dboth_ref[...] = dgate_ref[...]


def turn_back(order, smalls, dscan, select, inner, flags, taps, offset, dgate, rank):
    parts, count, span, _ = dscan.shape
    small = smalls[0].shape[-1]
    chans = select.shape[0]
    width = chans // parts
    quarter = span - 16

    def whole(shape):
        return pl.BlockSpec(shape, lambda t, order: (0,) * len(shape))

    def early(t):
        return jnp.minimum(t, parts - 1)

    return pl.pallas_call(
        turn_body,
        grid_spec=pltpu.PrefetchScalarGridSpec(
            num_scalar_prefetch=1,
            grid=(2 * parts,),
            in_specs=[whole(v.shape) for v in smalls]
            + [
                pl.BlockSpec((1, count, span, width), lambda t, order: (early(t), 0, 0, 0)),
                pl.BlockSpec((width, small), lambda t, order: (early(t), 0)),
                pl.BlockSpec((count, span, width), lambda t, order: (0, 0, early(t))),
                whole(flags.shape),
                pl.BlockSpec((taps.shape[0], width), lambda t, order: (0, early(t))),
                pl.BlockSpec((1, width), lambda t, order: (0, early(t))),
                pl.BlockSpec(
                    (count * quarter, width), lambda t, order: (0, jnp.maximum(t - parts, 0))
                ),
            ],
            out_specs=[
                pl.BlockSpec((count * quarter, width), lambda t, order: (0, t)),
                pl.BlockSpec((width, rank), lambda t, order: (early(t), 0)),
                pl.BlockSpec((small - rank + 8, width), lambda t, order: (0, early(t))),
            ],
            scratch_shapes=[
                pltpu.VMEM((count * span, small), low),
                pltpu.VMEM((taps.shape[0], span, width), wide),
                pltpu.VMEM((count * quarter, width), low),
            ],
        ),
        out_shape=[
            jax.ShapeDtypeStruct((count * quarter, 2 * chans), low),
            pltpu.HBM((chans, rank), low),
            jax.ShapeDtypeStruct((small - rank + 8, chans), wide),
        ],
        compiler_params=pltpu.CompilerParams(vmem_limit_bytes=20 * 1024 * 1024),
        cost_estimate=spent(5.5),
        name="turn_back",
    )(
        order,
        *smalls,
        dscan,
        select,
        inner,
        flags,
        taps,
        offset,
        dgate,
    )


class Moves:
    def __init__(self):
        self.chan = lax.axis_index("chan").astype(jnp.uint32)
        self.part = lax.axis_index("state").astype(jnp.uint32)
        self.z = self.chan // 2
        self.y = self.chan % 2
        places = jnp.arange(8, dtype=jnp.uint32)
        planes = (self.z + 4 - places % 4) % 4
        self.blocks = planes * 2 + (self.y + places // 4) % 2
        hops = (self.z + 4 - places // 2) % 4
        self.order = (self.y + places) % 2 * 4 + hops

    def over_y(self, values):
        return lax.ppermute(values, "chan", [(i, i ^ 1) for i in range(8)])

    def over_z(self, values, hops):
        return lax.ppermute(values, "chan", [(i, (i + 2 * hops) % 8) for i in range(8)])

    def over_state(self, values, bits):
        return lax.ppermute(values, "state", [(i, i ^ bits) for i in range(4)])

    def swap_state(self, values):
        return lax.all_to_all(values, "state", 0, 0, tiled=True)

    def pair(self, bit, own, other):
        return jnp.stack([jnp.where(bit == 0, own, other), jnp.where(bit == 0, other, own)])

    def in_order(self, pieces):
        own, core, across, slant = pieces
        bit = self.part % 2
        near = self.pair(bit, own, core)
        far = self.pair(bit, across, slant)
        return self.pair(self.part // 2, near, far).reshape((4,) + own.shape)

    def pieces_state(self, values):
        core = self.over_state(values, 1)
        across = self.over_state(values, 2)
        return values, core, across, self.over_state(across, 1)


def tied(*values):
    return lax.optimization_barrier(values)


def after(values, *others):
    token = lax.optimization_barrier((lax.create_token(), others))[0]
    return lax.optimization_barrier((token, values))[1]


def near_shards(
    n_chan,
    n_state,
    hidden_in,
    norm_gain,
    in_weight,
    conv_kernel,
    conv_offset,
    select_rank,
    select_entry,
    select_read,
    delta_weight,
    step_bias,
    decay_log,
    skip_weight,
    out_weight,
    lengths,
    pad_mask,
    cotangent,
):
    rows_dev, width = hidden_in.shape
    tokens = pad_mask.shape[0]
    chans = in_weight.shape[2]
    taps = conv_kernel.shape[0]
    rank = select_rank.shape[1]
    per_state = select_entry.shape[1]
    states = per_state * n_state
    small = rank + 2 * states
    quarter = rows_dev // n_state
    own = chans // n_state
    rows_q = n_chan * quarter
    part = lax.axis_index("state").astype(jnp.uint32)
    contract_rows = (((0,), (0,)), ((), ()))
    contract_cols = (((1,), (1,)), ((), ()))
    moves = Moves()
    blocks = moves.blocks
    planes = jnp.arange(4, dtype=jnp.uint32)
    small_order = jnp.stack([(moves.y ^ u) * 4 + planes for u in (0, 1)], axis=1).reshape(-1)
    order = jnp.concatenate([moves.order, small_order, part[None]]).astype(jnp.int32)
    places = jnp.concatenate([blocks, part[None]]).astype(jnp.int32)
    blocks = blocks.astype(jnp.int32)

    def mine(values, axis=0):
        return lax.dynamic_slice_in_dim(values, part * own, own, axis)

    start = part * quarter
    hidden_q = lax.dynamic_slice_in_dim(hidden_in, start, quarter, 0)
    ahead = (start + (rows_dev - HALO)) % rows_dev
    behind = (start + quarter) % rows_dev
    local = jnp.concatenate(
        [
            hidden_q,
            lax.dynamic_slice_in_dim(hidden_in, behind, HALO, 0),
            lax.dynamic_slice_in_dim(hidden_in, ahead, HALO, 0),
        ],
        axis=0,
    )
    inv_all = lax.rsqrt(jnp.mean(local * local, axis=1, keepdims=True) + epsilon)
    scaled_all = local * inv_all
    normed_all = (scaled_all * norm_gain[None, :]).astype(low)
    inv_rms = inv_all[:quarter]
    scaled = scaled_all[:quarter]
    cot_q = lax.dynamic_slice_in_dim(cotangent, start, quarter, 0).astype(low)
    ranks = (part ^ jnp.arange(n_state, dtype=jnp.uint32)).astype(jnp.int32)

    def trades(values):
        return [values[0]] + [moves.over_state(values[k], k) for k in (1, 2, 3)]

    def core_halves(values):
        cut = values.reshape((2, 2) + values.shape[1:])
        core = part % 2
        return (
            lax.dynamic_index_in_dim(cut, 1 - core, 1, keepdims=False),
            lax.dynamic_index_in_dim(cut, core, 1, keepdims=False),
        )

    def chip_halves(values):
        side = part // 2
        return (
            lax.dynamic_index_in_dim(values, 1 - side, 0, keepdims=False),
            lax.dynamic_index_in_dim(values, side, 0, keepdims=False),
        )

    def total_of(own_part, others):
        total = own_part.astype(wide)
        for piece in others:
            total = total + piece.astype(wide)
        return total.astype(low)

    def added(kept, came):
        return (kept.astype(wide) + came.astype(wide)).astype(low)

    columns = jnp.concatenate([select_entry, select_read], axis=1)
    decay_cut = jnp.swapaxes(decay_log.reshape(per_state, n_state, own), 0, 1)
    across = moves.over_y(normed_all)
    along = [moves.over_z(normed_all, hops) for hops in (1, 2, 3)]
    columns_core = moves.over_state(columns, 1)
    columns_chip = moves.over_state(columns, 2)
    decay_own = moves.swap_state(decay_cut)
    in_flat = in_weight.reshape(width, 2 * chans)
    across, along[0], along[1], along[2], columns_core, columns_chip, decay_own, in_flat, cot_q = tied(
        across, *along, columns_core, columns_chip, decay_own, in_flat, cot_q
    )
    grads = lax.all_gather(cot_q, "chan", axis=0)
    over = [moves.over_y(piece) for piece in along]
    columns_slant = moves.over_state(columns_chip, 1)
    over[0], over[1], over[2], columns_slant = tied(*over, columns_slant)
    pieces = [normed_all] + along + [across] + over

    place = positions(lengths, tokens)
    flags = [pad_mask.astype(wide)]
    flags += [(place >= lag).astype(wide) for lag in range(1, taps)]
    flags = jnp.stack(flags)
    padded = jnp.pad(flags, ((0, 0), (8, 8 + rows_dev)))
    span = quarter + 16
    flags_win = lax.dynamic_slice_in_dim(padded, start, n_chan * rows_dev, 1)
    flags_win = flags_win.reshape(taps, n_chan, rows_dev)[:, :, :span]
    chooser = (blocks[:, None] == jnp.arange(n_chan)[None, :]).astype(wide)
    flags_rows = jnp.einsum("kb,fbr->krf", chooser, flags_win)
    itself = jnp.arange(n_chan, dtype=jnp.int32)
    nearby = blocks[:, None] - blocks[None, :]
    one_before = jnp.where(blocks > 0, jnp.argmax(nearby == 1, axis=1), n_chan)
    one_after = jnp.where(blocks < n_chan - 1, jnp.argmax(nearby == -1, axis=1), n_chan)
    one_before = jnp.where(part == 0, one_before, itself)
    one_after = jnp.where(part == n_state - 1, one_after, itself)
    neighbours = jnp.concatenate([one_before, one_after, blocks[:4] // 2]).astype(jnp.int32)

    columns = moves.in_order((columns, columns_core, columns_chip, columns_slant))
    columns = columns.reshape(n_state, chans, 2, per_state)
    columns = jnp.transpose(columns, (1, 2, 0, 3)).reshape(chans, 2 * states)
    select = jnp.concatenate([select_rank, columns], axis=1)
    coeff = -jnp.exp(decay_own.reshape(states, own))

    normed_q, inner_all, sent, kept, other = project(
        neighbours, pieces, in_flat, flags_rows, conv_kernel, conv_offset[None, :], select, n_state
    )
    reach = quarter + HALO
    channels = moves.swap_state(sent)
    came = moves.over_y(other)
    joined = added(kept, came)
    along = [moves.over_z(joined, hops) for hops in (1, 2, 3)]
    grad_q, *dgated = pull(places, grads, out_weight, n_state)
    along[0], along[1], along[2], *dgated = tied(*along, *dgated)
    summed = total_of(joined, along)
    came = moves.over_y(summed)
    dgated = trades(dgated)
    picked = moves.pieces_state(jnp.concatenate([summed, came], axis=0))
    tie = tied(*picked, *dgated, channels)
    picked, dgated, channels = tie[:4], tie[4:8], tie[8]

    weight_own = mine(delta_weight, 1)
    bias_own = mine(step_bias)[None, :]
    skip_own = mine(skip_weight)[None, :]
    fresh = jnp.broadcast_to((place > 0).astype(low)[:, None], (tokens, own))
    spread = spreading(states)
    coeff_two = coeff * math.log2(math.e)
    kept, dpre, gated = forward_scan(
        order,
        picked,
        channels,
        dgated,
        fresh,
        weight_own,
        bias_own,
        skip_own,
        coeff_two,
        spread,
    )
    gated = moves.swap_state(gated)
    own_sums, other_sums, dscan, delta_grad_own, decay_total, sums = backward_scan(
        order,
        picked,
        channels,
        dgated,
        fresh,
        dpre,
        kept,
        weight_own,
        skip_own,
        coeff_two,
        spread,
    )
    decay_grad_own = coeff * decay_total
    packed = jnp.concatenate([delta_grad_own, decay_grad_own, sums], axis=0).astype(low)
    own_sums, other_sums, packed, gated, dscan = tied(
        own_sums, other_sums, packed, gated, dscan
    )

    came = moves.over_state(other_sums, 1)
    branch_kept, sent, second_branch, out_kept, out_sent, dgate_q = emit(
        places, gated, out_weight, grad_q
    )
    came, sent, second_branch, out_sent, dgate_q = tied(
        came, sent, second_branch, out_sent, dgate_q
    )

    chip = added(own_sums, came)
    came = moves.over_state(chip[1], 2)
    branch_came = moves.over_y(sent)
    gate_part = lax.dot_general(normed_q, dgate_q, contract_rows, preferred_element_type=wide)
    gain = jnp.sum(gate_part * in_flat[:, chans:].astype(wide), axis=1)
    gate_part = lax.psum_scatter(gate_part.astype(low), "state", scatter_dimension=0, tiled=True)
    out_came = moves.over_state(out_sent, 1)
    came, gain, out_came = tied(came, gain, out_came)

    joined = added(chip[0], came)
    came = moves.over_y(joined[4:])
    dscan = moves.swap_state(dscan)
    out_part = added(out_kept, out_came)
    out_came = moves.over_state(out_part[1], 2)
    packed_core = moves.over_state(packed, 1)
    came, second_branch, packed_core, branch_came = tied(
        came, second_branch, packed_core, branch_came
    )

    joined = added(joined[:4], came)
    along = [moves.over_z(joined, hops) for hops in (1, 2, 3)]
    second_came = moves.over_y(second_branch)
    along[0], along[1], along[2], second_came, out_came = tied(*along, second_came, out_came)

    partial = total_of(joined, along)
    came = moves.over_y(partial)
    branch_came = jnp.concatenate([branch_came, second_came], axis=2)
    branch = added(branch_kept, branch_came)
    branches = [moves.over_z(branch[4 - hops], hops) for hops in (1, 2, 3)]
    out_part = added(out_part[0], out_came)
    out_chip = moves.over_state(out_part, 2)
    came, partial, dscan, gate_part = tied(came, partial, dscan, gate_part)
    gate_grad = lax.all_gather(gate_part, "state", axis=0, tiled=True)

    dboth, rank_part, rows_part = turn_back(
        places,
        (partial, came),
        dscan,
        select,
        inner_all,
        flags_rows,
        conv_kernel,
        conv_offset[None, :],
        dgate_q,
        rank,
    )

    def backed(rows, weight):
        return lax.dot_general(rows, weight, contract_cols, preferred_element_type=wide)

    edge = width * 11 // 16
    left, right = slice(0, edge), slice(edge, width)
    other, same = slice(rows_q // 2, rows_q), slice(0, rows_q // 2)
    left_sent = backed(dboth[other], in_flat[left]).astype(low).reshape(4, quarter, edge)
    right_all = backed(dboth, in_flat[right]).reshape(2, 4, quarter, width - edge)
    right_sent = [right_all[:, 4 - hops].astype(low) for hops in (1, 2, 3)]
    out_core = moves.over_state(out_part, 1)
    out_slant = moves.over_state(out_chip, 1)
    packed_chip = moves.over_state(packed, 2)
    tie = tied(
        left_sent, dboth, rank_part, out_core, out_slant, packed_chip, branches[0], *right_sent
    )
    left_sent, dboth, rank_part, out_core, out_slant, packed_chip, branches[0] = tie[:7]
    right_sent = tie[7:]

    left_came = moves.over_y(left_sent)
    right_along = [moves.over_z(right_sent[hops - 1], hops) for hops in (1, 2, 3)]
    rank_core = moves.over_state(rank_part, 1)
    left_kept = backed(dboth[same], in_flat[left]).reshape(4, quarter, edge)
    inner_part = lax.dot_general(
        normed_q,
        after(dboth, right_along[0])[:, :chans],
        contract_rows,
        preferred_element_type=wide,
    )
    gain = gain + jnp.sum(inner_part * in_flat[:, :chans].astype(wide), axis=1)
    gain = jnp.concatenate([rows_part, gain.reshape(-1, chans)], axis=0)
    branch = total_of(branch[0], branches)
    tie = tied(
        left_came,
        left_kept,
        inner_part.astype(low),
        gain,
        branch,
        gate_grad,
        rank_core,
        *right_along,
    )
    left_came, left_kept, inner_part, gain, branch, gate_grad, rank_core = tie[:7]
    right_along = tie[7:]
    inner_part = lax.psum_scatter(inner_part, "state", scatter_dimension=0, tiled=True)

    joined = left_kept + left_came.astype(wide)
    left_sum = joined[0]
    left_along = [moves.over_z(joined[4 - hops].astype(low), hops) for hops in (1, 2, 3)]
    right_sum = right_all[:, 0]
    for piece in right_along:
        right_sum = right_sum + piece.astype(wide)
    right_came = moves.over_y(right_sum[1].astype(low))
    gain_came = moves.over_state(gain, 1)
    out_grad = placed(ranks, (out_part, out_core, out_chip, out_slant))
    packed_slant = moves.over_state(packed_chip, 1)
    tie = tied(right_came, gain_came, out_grad, packed_slant, *left_along)
    right_came, gain_came, out_grad, packed_slant = tie[:4]
    left_along = tie[4:]

    for piece in left_along:
        left_sum = left_sum + piece.astype(wide)
    right_sum = right_sum[0] + right_came.astype(wide)
    dnormed = jnp.concatenate([left_sum, right_sum], axis=1)
    dscaled = dnormed * norm_gain[None, :]
    change = inv_rms * (dscaled - scaled * jnp.mean(dscaled * scaled, axis=1, keepdims=True))
    change = change.astype(low)
    change_chip = moves.over_state(change, 2)
    change_core = moves.over_state(change, 1)
    gain = gain + gain_came
    gain_came = moves.over_state(gain, 2)
    rank_sum = added(rank_part, rank_core)
    rank_chip = moves.over_state(rank_sum, 2)
    packed = moves.in_order((packed, packed_core, packed_chip, packed_slant))
    packed = jnp.swapaxes(packed, 0, 1).reshape(-1, chans).astype(wide)
    packs = (
        packed[:rank],
        packed[rank + states],
        lax.dynamic_slice_in_dim(packed, rank + part * per_state, per_state, 0),
        packed[rank + states + 1],
    )
    tie = tied(change_chip, change_core, gain_came, rank_chip, inner_part, *packs)
    change_chip, change_core, gain_came, rank_chip, inner_part = tie[:5]
    packs = tie[5:]
    inner_grad = lax.all_gather(inner_part, "state", axis=0, tiled=True)

    change_slant = moves.over_state(change_chip, 1)
    branch_chip = moves.over_state(branch, 2)
    branch_core = moves.over_state(branch, 1)
    gain = gain + gain_came
    gain_came = moves.over_y(gain[8 + 2 * states :].reshape(width))
    rank_grad = rank_sum.astype(wide) + rank_chip.astype(wide)
    place_at = 8 + part * per_state
    smalls = (
        gain[:taps],
        gain[taps],
        rank_grad,
        lax.dynamic_slice_in_dim(gain, place_at, per_state, 0).T,
        lax.dynamic_slice_in_dim(gain, place_at + states, per_state, 0).T,
        *packs,
    )
    tie = tied(change_slant, branch_chip, branch_core, gain_came, gain, *smalls)
    change_slant, branch_chip, branch_core, gain_came, gain = tie[:5]
    smalls = tie[5:]

    branch_slant = moves.over_state(branch_chip, 1)
    gain = gain[8 + 2 * states :].reshape(width) + gain_came
    gains = [gain] + [moves.over_z(gain, hops) for hops in (1, 2, 3)]
    input_grad = placed(ranks, (change, change_core, change_chip, change_slant), cotangent)
    result = placed(ranks, (branch, branch_core, branch_chip, branch_slant), hidden_in)
    gains = jnp.stack(gains)
    gain_grad = 0.0
    for plane_at in range(4):
        gain_grad = gain_grad + lax.dynamic_index_in_dim(
            gains, (moves.z + 4 - plane_at) % 4, 0, keepdims=False
        )
    gain_grad = gain_grad / norm_gain
    in_grad = interleave(inner_grad, gate_grad)
    return (result, input_grad, gain_grad, in_grad, *smalls, out_grad)


def solution(mesh):
    sizes = dict(mesh.shape)
    near = (sizes["chan"], sizes["state"]) == (8, 4)
    program = functools.partial(near_shards, 8, 4) if near else shards
    return jax.shard_map(
        program,
        mesh=mesh,
        in_specs=(
            P("chan", None),
            P(),
            P(None, None, "chan"),
            P(None, "chan"),
            P("chan"),
            P("chan", None),
            P("chan", "state"),
            P("chan", "state"),
            P(None, "chan"),
            P("chan"),
            P("state", "chan"),
            P("chan"),
            P("chan", None),
            P(),
            P(),
            P("chan", None),
        ),
        out_specs=(
            P("chan", None),
            P("chan", None),
            P(),
            P(None, None, "chan"),
            P(None, "chan"),
            P("chan"),
            P("chan", None),
            P("chan", "state"),
            P("chan", "state"),
            P(None, "chan"),
            P("chan"),
            P("state", "chan"),
            P("chan"),
            P("chan", None),
        ),
        check_vma=False,
    )
```

```python
import functools
import math

import jax
import jax.numpy as jnp
from jax import lax
from jax.experimental import pallas as pl
from jax.experimental.pallas import tpu as pltpu
from jax.sharding import PartitionSpec as P

epsilon = 1e-05
GROUP = 16
HALO = 4
TAIL = 16
FAR = 1e30
wide = jnp.float32
low = jnp.bfloat16


def spent(microseconds):
    moved = int(microseconds * 3.6e6)
    return pl.CostEstimate(flops=0, bytes_accessed=moved, transcendentals=0)


def in_hbm(values):
    return pltpu.with_memory_space_constraint(values, pltpu.HBM)


def positions(lengths, tokens_all):
    ends = jnp.cumsum(lengths)
    begins = ends - lengths
    places = jnp.arange(tokens_all, dtype=jnp.int32)
    opening = jnp.max(jnp.where(begins[:, None] <= places[None, :], begins[:, None], 0), axis=0)
    return places - opening


def delayed(values, amount):
    if amount == 0:
        return values
    padding = jnp.zeros((amount,) + values.shape[1:], values.dtype)
    return jnp.concatenate([padding, values[: values.shape[0] - amount]], axis=0)


def advanced(values, amount):
    if amount == 0:
        return values
    padding = jnp.zeros((amount,) + values.shape[1:], values.dtype)
    return jnp.concatenate([values[amount:], padding], axis=0)


def silu_slope(values):
    logistic = jax.nn.sigmoid(values)
    return logistic * (1.0 + values * (1.0 - logistic))


def linear_scan(decays, drive):
    total_rows = decays.shape[0]
    blocks = total_rows // 16
    factors = jnp.swapaxes(decays.reshape((blocks, 16) + decays.shape[1:]), 0, 1)
    sources = jnp.swapaxes(drive.reshape((blocks, 16) + drive.shape[1:]), 0, 1)

    def advance(totals, item):
        state_now, product_now = totals
        factor_now, source_now = item
        state_now = factor_now * state_now + source_now
        product_now = factor_now * product_now
        return ((state_now, product_now), (state_now, product_now))

    initial = (jnp.zeros(factors.shape[1:], jnp.float32), jnp.ones(factors.shape[1:], jnp.float32))
    final_pair, (local_states, products) = lax.scan(advance, initial, (factors, sources))

    def combine(early, later):
        return (early[0] * later[0], later[0] * early[1] + later[1])

    joined_factor, joined_state = lax.associative_scan(
        combine, (products[-1], local_states[-1]), axis=0
    )
    entering = jnp.concatenate([jnp.zeros_like(joined_state[:1]), joined_state[:-1]], axis=0)
    states = local_states + products * entering[None]
    return jnp.swapaxes(states, 0, 1).reshape(decays.shape)


def shards(
    hidden_in,
    norm_gain,
    in_weight,
    conv_kernel,
    conv_offset,
    select_rank,
    select_entry,
    select_read,
    delta_weight,
    step_bias,
    decay_log,
    skip_weight,
    out_weight,
    lengths,
    pad_mask,
    cotangent,
):
    rows_dev, width = hidden_in.shape
    tokens_all = pad_mask.shape[0]
    chans = in_weight.shape[2]
    kernel_len = conv_kernel.shape[0]
    per_state = select_entry.shape[1]
    contract_rows = (((0,), (0,)), ((), ()))
    contract_cols = (((1,), (1,)), ((), ()))
    place = positions(lengths, tokens_all)
    fresh = (place > 0).astype(jnp.float32)
    maskf = pad_mask.astype(jnp.float32)[:, None]
    square = jnp.mean(hidden_in * hidden_in, axis=1, keepdims=True)
    inv_rms = lax.rsqrt(square + epsilon)
    scaled = hidden_in * inv_rms
    normed = (scaled * norm_gain[None, :]).astype(jnp.bfloat16)
    in_flat = in_weight.reshape(width, 2 * chans)
    both = jnp.dot(
        lax.all_gather(normed, "chan", axis=0, tiled=True),
        in_flat,
        preferred_element_type=jnp.float32,
    )
    inner = both[:, :chans] * maskf
    gate_in = both[:, chans:]
    valids = []
    shifted = []
    conv = jnp.zeros((tokens_all, chans), jnp.float32) + conv_offset[None, :]
    for index in range(kernel_len):
        lag = kernel_len - 1 - index
        valids.append((place >= lag).astype(jnp.float32)[:, None])
        shifted.append(delayed(inner, lag))
        conv = conv + conv_kernel[index][None, :] * shifted[index] * valids[index]
    act = (jax.nn.silu(conv) * maskf).astype(jnp.bfloat16)
    act_wide = act.astype(jnp.float32)
    pair_map = jnp.concatenate([select_entry, select_read], axis=1)
    rank_part = jnp.dot(act, select_rank, preferred_element_type=jnp.float32)
    pair_part = jnp.dot(act, pair_map, preferred_element_type=jnp.float32)
    raw_sum, pair_sum = lax.psum((rank_part, pair_part), "chan")
    entry = pair_sum[:, :per_state]
    readout = pair_sum[:, per_state:]
    lowrank = raw_sum.astype(jnp.bfloat16)
    dpre = jnp.dot(lowrank, delta_weight, preferred_element_type=jnp.float32) + step_bias[None, :]
    delta = jax.nn.softplus(dpre)
    coeff = -jnp.exp(decay_log)
    decays = jnp.exp(delta[:, None, :] * coeff[None]) * fresh[:, None, None]
    drive = (delta * act_wide)[:, None, :] * entry[:, :, None]
    states = linear_scan(decays, drive)
    scan_part = jnp.sum(readout[:, :, None] * states, axis=1)
    scanned = lax.psum(scan_part, "state")
    mixed = scanned + skip_weight[None, :] * act_wide
    gate_act = jax.nn.silu(gate_in)
    gated = (mixed * gate_act).astype(jnp.bfloat16)
    gated_rows = gated
    branch = lax.psum_scatter(
        jnp.dot(gated_rows, out_weight, preferred_element_type=jnp.float32),
        "chan",
        scatter_dimension=0,
        tiled=True,
    )
    result = hidden_in + branch
    grad_low = cotangent.astype(jnp.bfloat16)
    pieces = lax.all_gather(grad_low, "chan", axis=0, tiled=True)
    gated_rows = gated
    product = lax.dot_general(pieces, out_weight, contract_cols, preferred_element_type=jnp.float32)
    outw_acc = lax.dot_general(
        gated_rows, pieces, contract_rows, preferred_element_type=jnp.float32
    )
    dmix = product * gate_act
    dgate = product * mixed * silu_slope(gate_in)
    skip_grad = jnp.sum(dmix * act_wide, axis=0)
    emitted = readout[:, :, None] * dmix[:, None, :]
    following = jnp.concatenate([decays[1:], jnp.zeros_like(decays[:1])], axis=0)
    adjoint = jnp.flip(linear_scan(jnp.flip(following, 0), jnp.flip(emitted, 0)), 0)
    earlier = jnp.concatenate([jnp.zeros_like(states[:1]), states[:-1]], axis=0)
    flow = adjoint * earlier * decays
    dread_part = jnp.sum(states * dmix[:, None, :], axis=2)
    dentry_part = jnp.sum(adjoint * (delta * act_wide)[:, None, :], axis=2)
    ddelta_part = jnp.sum(
        flow * coeff[None] + adjoint * entry[:, :, None] * act_wide[:, None, :], axis=1
    )
    decay_grad = coeff * jnp.sum(flow * delta[:, None, :], axis=0)
    dact_scan = jnp.sum(adjoint * entry[:, :, None], axis=1) * delta
    dentry_sum, dread_sum = lax.psum((dentry_part, dread_part), "chan")
    dpair = jnp.concatenate(
        [dentry_sum.astype(jnp.bfloat16), dread_sum.astype(jnp.bfloat16)], axis=1
    )
    pair_grad = lax.dot_general(act, dpair, contract_rows, preferred_element_type=jnp.float32)
    entry_grad = pair_grad[:, :per_state]
    read_grad = pair_grad[:, per_state:]
    dact_pair = lax.dot_general(dpair, pair_map, contract_cols, preferred_element_type=jnp.float32)
    dact_state, ddelta = lax.psum((dact_scan + dact_pair, ddelta_part), "state")
    ddpre = (ddelta * jax.nn.sigmoid(dpre)).astype(jnp.bfloat16)
    bias_grad = jnp.sum(ddpre.astype(jnp.float32), axis=0)
    delta_grad = lax.dot_general(lowrank, ddpre, contract_rows, preferred_element_type=jnp.float32)
    dlow_part = lax.dot_general(
        ddpre, delta_weight, contract_cols, preferred_element_type=jnp.float32
    )
    dlow = lax.psum(dlow_part, "chan").astype(jnp.bfloat16)
    rank_grad = lax.dot_general(act, dlow, contract_rows, preferred_element_type=jnp.float32)
    dact = (
        dact_state
        + dmix * skip_weight[None, :]
        + lax.dot_general(dlow, select_rank, contract_cols, preferred_element_type=jnp.float32)
    )
    dconv = dact * maskf * silu_slope(conv)
    offset_grad = jnp.sum(dconv, axis=0)
    kernel_rows = []
    dinner = jnp.zeros((tokens_all, chans), jnp.float32)
    for index in range(kernel_len):
        lag = kernel_len - 1 - index
        masked = dconv * valids[index]
        kernel_rows.append(jnp.sum(masked * shifted[index], axis=0))
        dinner = dinner + advanced(masked * conv_kernel[index][None, :], lag)
    kernel_grad = jnp.stack(kernel_rows, axis=0)
    dboth = jnp.concatenate([dinner * maskf, dgate], axis=1).astype(jnp.bfloat16)
    chosen = dboth
    in_flat_grad = lax.dot_general(
        lax.all_gather(normed, "chan", axis=0, tiled=True),
        chosen,
        contract_rows,
        preferred_element_type=jnp.float32,
    )
    in_grad = in_flat_grad.reshape(width, 2, chans)
    chosen = dboth
    dnormed = lax.psum_scatter(
        lax.dot_general(chosen, in_flat, contract_cols, preferred_element_type=jnp.float32),
        "chan",
        scatter_dimension=0,
        tiled=True,
    )
    gain_part = jnp.sum(dnormed * scaled, axis=0)
    gain_grad = lax.psum(gain_part, "chan")
    dscaled = dnormed * norm_gain[None, :]
    input_grad = cotangent + inv_rms * (
        dscaled - scaled * jnp.mean(dscaled * scaled, axis=1, keepdims=True)
    )
    return (
        result,
        input_grad,
        gain_grad,
        in_grad,
        kernel_grad,
        offset_grad,
        rank_grad,
        entry_grad,
        read_grad,
        delta_grad,
        bias_grad,
        decay_grad,
        skip_grad,
        outw_acc,
    )


def own_block(states):
    row = lax.broadcasted_iota(jnp.int32, (GROUP, GROUP * states), 0)
    col = lax.broadcasted_iota(jnp.int32, (GROUP, GROUP * states), 1)
    return jnp.logical_and(col >= row * states, col < (row + 1) * states)


def spreading(states):
    eye = jnp.eye(states, dtype=low)
    tiled = jnp.tile(eye, (1, GROUP))
    nothing = jnp.zeros_like(tiled)
    return jnp.concatenate(
        [
            jnp.concatenate([tiled, nothing], axis=1),
            jnp.concatenate([nothing, tiled], axis=1),
        ],
        axis=0,
    )


def transposed(values):
    count = values.shape[1]
    row = lax.broadcasted_iota(jnp.int32, (count, count), 0)
    col = lax.broadcasted_iota(jnp.int32, (count, count), 1)
    eye = jnp.where(row == col, 1.0, 0.0).astype(low)
    return lax.dot_general(eye, values, (((1,), (1,)), ((), ())), preferred_element_type=wide)


def forward_body(parts, order_ref, *refs):
    sources, refs = refs[: 2 * parts + 2], refs[2 * parts + 2 :]
    params, (kept_hbm, dpre_hbm, gated_hbm), refs = refs[:5], refs[5:8], refs[8:]
    carry, step_all, drive_all, small_all, dgated_all, pair_all, fresh_all = refs[:7]
    kept_all, dpre_all, gated_all, came, left = refs[7:]
    blocks = small_all.shape[1]
    chunk = step_all.shape[0]
    states = carry.shape[0]

    def entering(turn):
        block = order_ref[turn]
        rows = pl.ds(pl.multiple_of(turn * chunk, chunk), chunk)
        found = []
        for k in range(parts):
            found.append((sources[k].at[order_ref[blocks + turn]], small_all.at[k, turn]))
            found.append((sources[parts + k].at[block], dgated_all.at[k, turn]))
        found.append((sources[2 * parts].at[:, :, block], pair_all.at[:, :, turn]))
        found.append((sources[2 * parts + 1].at[rows], fresh_all.at[rows]))
        return [
            pltpu.make_async_copy(a, b, came.at[turn, i]) for i, (a, b) in enumerate(found)
        ]

    def leaving(turn):
        rows = pl.ds(pl.multiple_of(turn * chunk, chunk), chunk)
        tall = pl.ds(pl.multiple_of(turn * (chunk * states), chunk * states), chunk * states)
        found = [
            (kept_all.at[tall], kept_hbm.at[tall]),
            (dpre_all.at[rows], dpre_hbm.at[rows]),
            (gated_all.at[:, :, turn], gated_hbm.at[:, :, order_ref[turn]]),
        ]
        return [
            pltpu.make_async_copy(a, b, left.at[turn, i]) for i, (a, b) in enumerate(found)
        ]

    @pl.loop(0, blocks)
    def _(turn):
        for copy in entering(turn):
            copy.start()

    carry[...] = jnp.zeros_like(carry)

    @pl.loop(0, blocks)
    def _(turn):
        for copy in entering(turn):
            copy.wait()
        forward_steps(
            turn,
            parts,
            order_ref,
            small_all,
            dgated_all,
            pair_all,
            fresh_all,
            *params,
            kept_all,
            dpre_all,
            gated_all,
            carry,
            step_all,
            drive_all,
        )
        for copy in leaving(turn):
            copy.start()

    @pl.loop(0, blocks)
    def _(turn):
        for copy in leaving(turn):
            copy.wait()


def forward_steps(
    turn,
    parts,
    order_ref,
    small_all,
    dgated_all,
    pair_ref,
    fresh_ref,
    weight_ref,
    bias_ref,
    skip_ref,
    coeff_ref,
    spread_ref,
    kept_ref,
    dpre_ref,
    gated_ref,
    carry,
    step_all,
    drive_all,
):
    coeff = coeff_ref[...]
    states = coeff.shape[0]
    chunk = step_all.shape[0]
    origin = pl.multiple_of(turn * (chunk * states), chunk * states)
    rank = weight_ref.shape[0]
    quarter = small_all.shape[2]
    chosen = own_block(states)
    part = order_ref[order_ref.shape[0] - 1]
    columns = [None] * parts
    reading = [None] * parts

    def before(j):
        rows = slice(j * quarter, (j + 1) * quarter)
        small = small_all[part ^ j, turn]
        dpre = (
            jnp.dot(small[:, :rank], weight_ref[...], preferred_element_type=wide) + bias_ref[...]
        )
        dpre_ref[pl.ds(turn * chunk + j * quarter, quarter), :] = dpre
        delta = jax.nn.softplus(dpre)
        step_all[rows, :] = jnp.where(fresh_ref[pl.ds(turn * chunk + j * quarter, quarter), :].astype(wide) > 0.0, delta, FAR)
        drive_all[rows, :] = delta * pair_ref[j, 0, turn].astype(wide)
        pair = small[:, rank:]
        columns[j] = transposed(pair)
        reading[j] = jnp.dot(
            pair, spread_ref[:, GROUP * states :], preferred_element_type=wide
        )

    def scan(j, state):
        for group in range(quarter // GROUP):
            base = j * quarter + group * GROUP
            kept = []
            for t in range(base, base + GROUP):
                here = t - j * quarter
                decay = jnp.exp2(step_all[t : t + 1, :] * coeff)
                entry = columns[j][:states, here : here + 1]
                state = decay * state + drive_all[t : t + 1, :] * entry
                kept.append(state)
            rows = pl.ds(origin + base * states, GROUP * states)
            kept_ref[rows, :] = jnp.concatenate(kept, axis=0).astype(low)
        return state

    def finish_part(j):
        found = []
        for group in range(quarter // GROUP):
            base = j * quarter + group * GROUP
            block = kept_ref[pl.ds(origin + base * states, GROUP * states), :]
            here = reading[j][group * GROUP : (group + 1) * GROUP]
            weights = jnp.where(chosen, here, 0.0).astype(low)
            found.append(jnp.dot(weights, block, preferred_element_type=wide))
        act = pair_ref[j, 0, turn].astype(wide)
        gate = pair_ref[j, 1, turn].astype(wide)
        mixed = jnp.concatenate(found, axis=0) + skip_ref[...] * act
        dgated = dgated_all[part ^ j, turn].astype(wide)
        gated_ref[j, 0, turn] = (mixed * jax.nn.silu(gate)).astype(low)
        gated_ref[j, 1, turn] = (dgated * mixed * silu_slope(gate)).astype(low)

    state = carry[...]
    before(0)
    for j in range(parts):
        if j + 1 < parts:
            before(j + 1)
        state = scan(j, state)
        if j:
            finish_part(j - 1)
    finish_part(parts - 1)
    carry[...] = state


def backward_body(parts, order_ref, *refs):
    sources, refs = refs[: 2 * parts + 4], refs[2 * parts + 4 :]
    params, (own_hbm, other_hbm, dscan_hbm), refs = refs[:4], refs[4:7], refs[7:]
    results, refs = refs[:3], refs[3:]
    scratch, refs = refs[:11], refs[11:]
    (small_all, dgated_all, pair_all, fresh_all, dpre_all, kept_all, edge_all) = refs[:7]
    (own_all, other_all, dscan_all, came, left) = refs[7:]
    blocks = small_all.shape[1]
    chunk = scratch[1].shape[0]
    states = scratch[0].shape[0]
    for ref in (scratch[0], *results, *scratch[8:10]):
        ref[...] = jnp.zeros_like(ref)

    def entering(turn):
        at = blocks - 1 - turn
        block = order_ref[at]
        rows = pl.ds(pl.multiple_of(at * chunk, chunk), chunk)
        tall = pl.ds(pl.multiple_of(at * (chunk * states), chunk * states), chunk * states)
        found = []
        for k in range(parts):
            found.append((sources[k].at[order_ref[blocks + at]], small_all.at[k, at]))
            found.append((sources[parts + k].at[block], dgated_all.at[k, at]))
        found.append((sources[2 * parts].at[:, :, block], pair_all.at[:, :, at]))
        for source, target, here in zip(
            sources[2 * parts + 1 :], (fresh_all, dpre_all, kept_all), (rows, rows, tall)
        ):
            found.append((source.at[here], target.at[here]))
        ahead = pl.multiple_of(jnp.maximum(at * (chunk * states) - states, 0), states)
        found.append((sources[-1].at[pl.ds(ahead, states)], edge_all.at[at]))
        return [
            pltpu.make_async_copy(a, b, came.at[turn, i]) for i, (a, b) in enumerate(found)
        ]

    def leaving(turn):
        at = blocks - 1 - turn
        block = order_ref[at]
        place = order_ref[blocks + at]
        found = [
            (own_all.at[:, at], own_hbm.at[:, place]),
            (other_all.at[:, at], other_hbm.at[:, place]),
            (dscan_all.at[:, at], dscan_hbm.at[:, block]),
        ]
        return [
            pltpu.make_async_copy(a, b, left.at[turn, i]) for i, (a, b) in enumerate(found)
        ]

    @pl.loop(0, blocks)
    def _(turn):
        for copy in entering(turn):
            copy.start()

    @pl.loop(0, blocks)
    def _(turn):
        for copy in entering(turn):
            copy.wait()
        backward_steps(
            turn,
            parts,
            blocks,
            order_ref,
            small_all,
            dgated_all,
            pair_all,
            fresh_all,
            dpre_all,
            kept_all,
            edge_all,
            *params,
            own_all,
            other_all,
            dscan_all,
            *results,
            *scratch,
        )
        for copy in leaving(turn):
            copy.start()

    @pl.loop(0, blocks)
    def _(turn):
        for copy in leaving(turn):
            copy.wait()


def backward_steps(
    turn,
    parts,
    blocks,
    order_ref,
    small_all,
    dgated_all,
    pair_ref,
    fresh_ref,
    dpre_ref,
    kept_ref,
    edge_ref,
    weight_ref,
    skip_ref,
    coeff_ref,
    spread_ref,
    own_ref,
    other_ref,
    dscan_ref,
    delta_grad_ref,
    decay_ref,
    sums_ref,
    carry,
    step_all,
    drive_all,
    delta_all,
    dmix_all,
    lam_all,
    flow_all,
    cross_all,
    next_partial,
    next_dscan,
    partial_all,
):
    coeff = coeff_ref[...]
    states = coeff.shape[0]
    rank = weight_ref.shape[0]
    quarter = small_all.shape[2]
    chosen = own_block(states)
    ones = jnp.where(chosen, 1.0, 0.0).astype(low)
    across = (((1,), (1,)), ((), ()))
    down = (((0,), (0,)), ((), ()))
    part = order_ref[order_ref.shape[0] - 1]
    chunk = step_all.shape[0]
    block_turn = blocks - 1 - turn
    origin = pl.multiple_of(block_turn * (chunk * states), chunk * states)
    first = jnp.where(block_turn == 0, 0.0, edge_ref[block_turn].astype(wide))
    columns = [None] * parts
    entering = [None] * parts
    after_partial = [next_partial[...]]
    after_dscan = [next_dscan[...]]

    def before(j):
        rows = slice(j * quarter, (j + 1) * quarter)
        small = small_all[part ^ j, block_turn]
        delta = jax.nn.softplus(dpre_ref[pl.ds(block_turn * chunk + j * quarter, quarter), :])
        act = pair_ref[j, 0, block_turn].astype(wide)
        gate = pair_ref[j, 1, block_turn].astype(wide)
        step_all[rows, :] = jnp.where(fresh_ref[pl.ds(block_turn * chunk + j * quarter, quarter), :].astype(wide) > 0.0, delta, FAR)
        drive_all[rows, :] = delta * act
        delta_all[rows, :] = delta
        dmix_all[rows, :] = dgated_all[part ^ j, block_turn].astype(wide) * jax.nn.silu(gate)
        pair = small[:, rank:]
        columns[j] = transposed(pair)
        entering[j] = jnp.dot(
            pair, spread_ref[:, : GROUP * states], preferred_element_type=wide
        )

    def scan(j, pulled, summed):
        for group in range(quarter // GROUP - 1, -1, -1):
            base = j * quarter + group * GROUP
            lams = [None] * GROUP
            flows = [None] * GROUP
            rows = slice(base * states, (base + GROUP) * states)
            block = kept_ref[pl.ds(origin + base * states, GROUP * states), :].astype(wide)
            if base:
                edge = kept_ref[pl.ds(origin + (base - 1) * states, states), :].astype(wide)
            else:
                edge = first
            for i in range(GROUP - 1, -1, -1):
                t = base + i
                here = t - j * quarter
                read = columns[j][states:, here : here + 1]
                lam = read * dmix_all[t : t + 1, :] + pulled
                pulled = jnp.exp2(step_all[t : t + 1, :] * coeff) * lam
                flow = pulled * (block[(i - 1) * states : i * states] if i else edge)
                summed = summed + flow * delta_all[t : t + 1, :]
                lams[i] = lam
                flows[i] = flow * coeff
            lam_all[rows, :] = jnp.concatenate(lams, axis=0).astype(low)
            flow_all[rows, :] = jnp.concatenate(flows, axis=0).astype(low)
        return pulled, summed

    def finish_part(j):
        part_rows = slice(j * quarter, (j + 1) * quarter)
        lam_found = []
        flow_found = []
        for group in range(quarter // GROUP):
            base = j * quarter + group * GROUP
            here = slice(base, base + GROUP)
            rows = slice(base * states, (base + GROUP) * states)
            lam_block = lam_all[rows, :]
            entry = entering[j][group * GROUP : (group + 1) * GROUP]
            weights = jnp.where(chosen, entry, 0.0).astype(low)
            lam_found.append(jnp.dot(weights, lam_block, preferred_element_type=wide))
            flow_found.append(jnp.dot(ones, flow_all[rows, :], preferred_element_type=wide))
            cross = lax.dot_general(
                drive_all[here, :].astype(low), lam_block, across, preferred_element_type=wide
            )
            cross_all[here, : GROUP * states] = jnp.where(chosen, cross, 0.0).astype(low)
            cross = lax.dot_general(
                dmix_all[here, :].astype(low),
                kept_ref[pl.ds(origin + base * states, GROUP * states), :],
                across,
                preferred_element_type=wide,
            )
            cross_all[here, GROUP * states :] = jnp.where(chosen, cross, 0.0).astype(low)
        dpair = lax.dot_general(
            cross_all[part_rows, :], spread_ref[...], across, preferred_element_type=wide
        ).astype(low)
        found = jnp.concatenate(lam_found, axis=0)
        act = pair_ref[j, 0, block_turn].astype(wide)
        delta = delta_all[part_rows, :]
        dmix = dmix_all[part_rows, :]
        ddelta = jnp.concatenate(flow_found, axis=0) * (1.0 / math.log2(math.e)) + found * act
        ddpre = (ddelta * jax.nn.sigmoid(dpre_ref[pl.ds(block_turn * chunk + j * quarter, quarter), :])).astype(low)
        small = small_all[part ^ j, block_turn]
        delta_grad_ref[...] += lax.dot_general(
            small[:, :rank], ddpre, down, preferred_element_type=wide
        )
        dlow = lax.dot_general(
            ddpre, weight_ref[...], across, preferred_element_type=wide
        ).astype(low)
        dscan = (found * delta + dmix * skip_ref[...]).astype(low)
        sums_ref[0:1, :] += jnp.sum(ddpre.astype(wide), axis=0, keepdims=True)
        sums_ref[1:2, :] += jnp.sum(dmix * act, axis=0, keepdims=True)
        after_rows = after_partial[0]
        partial_all[j, :quarter, :rank] = dlow
        partial_all[j, :quarter, rank:] = dpair
        partial_all[j, quarter:, :] = after_rows
        dscan_ref[j, block_turn, :quarter, :] = dscan
        dscan_ref[j, block_turn, quarter:, :] = after_dscan[0]
        after_partial[0] = jnp.concatenate([dlow[:TAIL], dpair[:TAIL]], axis=1)
        after_dscan[0] = dscan[:TAIL]

    pulled = carry[...]
    summed = decay_ref[...]
    before(parts - 1)
    for j in range(parts - 1, -1, -1):
        if j:
            before(j - 1)
        pulled, summed = scan(j, pulled, summed)
        if j + 1 < parts:
            finish_part(j + 1)
    finish_part(0)
    carry[...] = pulled
    decay_ref[...] = summed
    next_partial[...] = after_partial[0]
    next_dscan[...] = after_dscan[0]
    for k in range(parts):
        (other_ref if k % 2 else own_ref)[k // 2, block_turn] = partial_all[part ^ k]


def forward_scan(order, small, pair, dgated, fresh, weight, bias, skip, coeff, spread):
    parts, _, blocks, quarter, width = pair.shape
    states = coeff.shape[0]
    columns = small[0].shape[-1]
    chunk = parts * quarter
    tokens = blocks * chunk
    streamed = (*small, *dgated, pair, fresh)
    params = (weight, bias, skip, coeff, spread)
    apart = pl.BlockSpec(memory_space=pl.ANY)
    kept = (tokens * states, width)
    gated = (parts, 2, blocks, quarter, width)
    return pl.pallas_call(
        functools.partial(forward_body, parts),
        grid_spec=pltpu.PrefetchScalarGridSpec(
            num_scalar_prefetch=1,
            grid=(1,),
            in_specs=[apart] * len(streamed)
            + [pl.BlockSpec(v.shape, lambda t, order: (0, 0)) for v in params],
            out_specs=[apart] * 3,
            scratch_shapes=[
                pltpu.VMEM((states, width), wide),
                pltpu.VMEM((chunk, width), wide),
                pltpu.VMEM((chunk, width), wide),
                pltpu.VMEM((parts, blocks, quarter, columns), low),
                pltpu.VMEM((parts, blocks, quarter, width), low),
                pltpu.VMEM(gated, low),
                pltpu.VMEM((tokens, width), low),
                pltpu.VMEM(kept, low),
                pltpu.VMEM((tokens, width), wide),
                pltpu.VMEM(gated, low),
                pltpu.SemaphoreType.DMA((blocks, len(streamed) + 1)),
                pltpu.SemaphoreType.DMA((blocks, 3)),
            ],
        ),
        out_shape=[
            pltpu.HBM(kept, low),
            pltpu.HBM((tokens, width), wide),
            pltpu.HBM(gated, low),
        ],
        compiler_params=pltpu.CompilerParams(vmem_limit_bytes=28 * 1024 * 1024),
        cost_estimate=spent(12),
        name="forward_scan",
    )(order, *map(in_hbm, streamed), *params)


def backward_scan(
    order, small, pair, dgated, fresh, dpre, kept, weight, skip, coeff, spread
):
    parts, _, blocks, quarter, width = pair.shape
    states = coeff.shape[0]
    rank = weight.shape[0]
    columns = small[0].shape[-1]
    chunk = parts * quarter
    tokens = blocks * chunk
    streamed = (*small, *dgated, pair, fresh, dpre, kept)
    params = (weight, skip, coeff, spread)
    apart = pl.BlockSpec(memory_space=pl.ANY)
    sums = (parts // 2, blocks, quarter + TAIL, columns)
    dscan = (parts, blocks, quarter + TAIL, width)
    results = ((rank, width), (states, width), (8, width))
    return pl.pallas_call(
        functools.partial(backward_body, parts),
        grid_spec=pltpu.PrefetchScalarGridSpec(
            num_scalar_prefetch=1,
            grid=(1,),
            in_specs=[apart] * len(streamed)
            + [pl.BlockSpec(v.shape, lambda t, order: (0, 0)) for v in params],
            out_specs=[apart] * 3 + [pl.BlockSpec(v, lambda t, order: (0, 0)) for v in results],
            scratch_shapes=[pltpu.VMEM((states, width), wide)]
            + [pltpu.VMEM((chunk, width), wide)] * 4
            + [pltpu.VMEM((chunk * states, width), low)] * 2
            + [
                pltpu.VMEM((chunk, 2 * GROUP * states), low),
                pltpu.VMEM((TAIL, columns), low),
                pltpu.VMEM((TAIL, width), low),
                pltpu.VMEM((parts, quarter + TAIL, columns), low),
                pltpu.VMEM((parts, blocks, quarter, columns), low),
                pltpu.VMEM((parts, blocks, quarter, width), low),
                pltpu.VMEM(pair.shape, low),
                pltpu.VMEM((tokens, width), low),
                pltpu.VMEM((tokens, width), wide),
                pltpu.VMEM((tokens * states, width), low),
                pltpu.VMEM((blocks, states, width), low),
                pltpu.VMEM(sums, low),
                pltpu.VMEM(sums, low),
                pltpu.VMEM(dscan, low),
                pltpu.SemaphoreType.DMA((blocks, len(streamed) + 1)),
                pltpu.SemaphoreType.DMA((blocks, 3)),
            ],
        ),
        out_shape=[pltpu.HBM(sums, low), pltpu.HBM(sums, low), pltpu.HBM(dscan, low)]
        + [jax.ShapeDtypeStruct(v, wide) for v in results],
        compiler_params=pltpu.CompilerParams(vmem_limit_bytes=28 * 1024 * 1024),
        cost_estimate=spent(19),
        name="backward_scan",
    )(order, *map(in_hbm, streamed), *params)


def interleave_body(parts, order_ref, *refs):
    values, out_ref = refs[: 2 * parts], refs[2 * parts]
    width, block = values[0].shape
    places = [lax.broadcasted_iota(jnp.int32, (block, block), axis) for axis in (0, 1)]
    same = jnp.where(places[0] == places[1], 1.0, 0.0).astype(low)
    for part in range(parts):

        @pl.when(order_ref[0] == part)
        def _(part=part):
            for half in range(2):
                for k in range(parts):
                    out_ref[:, half, (part ^ k) * width : ((part ^ k) + 1) * width] = (
                        lax.dot_general(
                            same,
                            values[half * parts + k][...],
                            (((1,), (1,)), ((), ())),
                            preferred_element_type=wide,
                        )
                    )


def interleave(order, inner, gate):
    parts = len(inner)
    width, depth = inner[0].shape
    block = 256
    return pl.pallas_call(
        functools.partial(interleave_body, parts),
        grid_spec=pltpu.PrefetchScalarGridSpec(
            num_scalar_prefetch=1,
            grid=(depth // block,),
            in_specs=[pl.BlockSpec((width, block), lambda t, order: (0, t))] * parts
            + [pl.BlockSpec((None, width, block), lambda t, order: (1, 0, t))] * parts,
            out_specs=pl.BlockSpec((block, 2, parts * width), lambda t, order: (t, 0, 0)),
        ),
        out_shape=jax.ShapeDtypeStruct((depth, 2, parts * width), wide),
        compiler_params=pltpu.CompilerParams(vmem_limit_bytes=16 * 1024 * 1024),
        cost_estimate=spent(5),
        name="interleave",
    )(order, *inner, *gate)


def placed_body(parts, order_ref, *refs):
    values, out_ref = refs[:parts], refs[-1]
    place = order_ref[pl.program_id(0)]
    for k in range(parts):

        @pl.when(place == k)
        def _(k=k):
            value = values[k][...].astype(wide)
            out_ref[...] = refs[parts][...] + value if len(refs) > parts + 1 else value


def placed(order, values, base=None):
    parts = len(values)
    rows, width = values[0].shape[-2:]
    flat = pl.BlockSpec((rows, width), lambda p, order: (p, 0))
    if values[0].ndim == 3:
        piece = pl.BlockSpec((None, rows, width), lambda p, order: (0, 0, 0))
    else:
        piece = pl.BlockSpec((rows, width), lambda p, order: (0, 0))
    return pl.pallas_call(
        functools.partial(placed_body, parts),
        grid_spec=pltpu.PrefetchScalarGridSpec(
            num_scalar_prefetch=1,
            grid=(parts,),
            in_specs=[piece] * parts
            + ([] if base is None else [flat]),
            out_specs=flat,
        ),
        out_shape=jax.ShapeDtypeStruct((parts * rows, width), wide),
        compiler_params=pltpu.CompilerParams(vmem_limit_bytes=24 * 1024 * 1024),
        cost_estimate=spent(2.5),
        name="placed",
    )(order, *values, *(() if base is None else (base,)))


def project_body(
    place_ref,
    *refs,
):
    pieces, refs = refs[:8], refs[8:]
    (weight_ref, flags_ref, taps_ref, offset_ref, select_ref) = refs[:5]
    (normed_ref, inner_ref, channels_ref, kept_ref, sent_ref) = refs[5:10]
    (sides, edges, window, total, acts) = refs[10:]
    turn = pl.program_id(0)
    quarter = channels_ref.shape[3]
    width = channels_ref.shape[4]
    halves = weight_ref.shape[1] // width
    taps = taps_ref.shape[0]
    inner_turns = pl.num_programs(0) // 2
    count = len(pieces)

    @pl.when(turn == 0)
    def _():
        for k in range(count):
            piece = pieces[k][...]
            normed_ref[k * quarter : (k + 1) * quarter, :] = piece[:quarter]
            sides[k * 8 : (k + 1) * 8, :] = piece[quarter:].astype(wide)
        edges[...] = jnp.zeros_like(edges)
        total[...] = jnp.zeros_like(total)

    main = jnp.dot(normed_ref[...], weight_ref[...], preferred_element_type=wide)

    @pl.when(turn < inner_turns)
    def _():
        edges[: count * 8, :] = jnp.dot(
            sides[...].astype(low), weight_ref[...], preferred_element_type=wide
        )
        for k in range(count):
            before = pl.multiple_of(place_ref[k] * 8, 8)
            after = pl.multiple_of(place_ref[count + k] * 8, 8)
            flags = flags_ref[k]
            window[0:8, :] = edges[pl.ds(before, 8), :]
            window[8 : 8 + quarter, :] = main[k * quarter : (k + 1) * quarter]
            window[8 + quarter : 16 + quarter, :] = edges[pl.ds(after, 8), :]
            masked = window[...] * flags[:, 0:1]
            window[...] = masked
            inner_ref[k] = masked
            conv = offset_ref[...] + taps_ref[taps - 1 : taps, :] * masked[8 : 8 + quarter]
            for lag in range(1, taps):
                shifted = window[8 - lag : 8 - lag + quarter, :]
                valid = flags[8 : 8 + quarter, lag : lag + 1]
                conv = conv + taps_ref[taps - 1 - lag : taps - lag, :] * shifted * valid
            act = (jax.nn.silu(conv) * flags[8 : 8 + quarter, 0:1]).astype(low)
            acts[k * quarter : (k + 1) * quarter, :] = act
            for h in range(halves):
                channels_ref[h, 0, k] = act[:, h * width : (h + 1) * width]
        total[...] += jnp.dot(acts[...], select_ref[...], preferred_element_type=wide)

    @pl.when(turn >= inner_turns)
    def _():
        gate = main.astype(low)
        for k in range(count):
            for h in range(halves):
                channels_ref[h, 0, k] = gate[
                    k * quarter : (k + 1) * quarter, h * width : (h + 1) * width
                ]

    @pl.when(turn == pl.num_programs(0) - 1)
    def _():
        for k in range(count // 2):
            plane = place_ref[2 * count + k]
            kept_ref[plane] = total[k * quarter : (k + 1) * quarter, :]
            other = k + count // 2
            sent_ref[plane] = total[other * quarter : (other + 1) * quarter, :].astype(low)


def project(places, pieces, weight, flags, taps, offset, select, parts):
    count = len(pieces)
    rows, depth = pieces[0].shape
    quarter = rows - 8
    chans = weight.shape[1] // 2
    width = chans // parts
    tile = 2 * width
    turns = 2 * chans // tile
    half = turns // 2
    small = select.shape[1]

    def whole(shape):
        return pl.BlockSpec(shape, lambda t, place: (0,) * len(shape))

    def inner(t):
        return jnp.minimum(t, half - 1)

    return pl.pallas_call(
        project_body,
        grid_spec=pltpu.PrefetchScalarGridSpec(
            num_scalar_prefetch=1,
            grid=(turns,),
            in_specs=[whole(pieces[0].shape) for _ in pieces]
            + [
                pl.BlockSpec((depth, tile), lambda t, place: (0, t)),
                whole(flags.shape),
                pl.BlockSpec((taps.shape[0], tile), lambda t, place: (0, inner(t))),
                pl.BlockSpec((1, tile), lambda t, place: (0, inner(t))),
                pl.BlockSpec((tile, small), lambda t, place: (inner(t), 0)),
            ],
            out_specs=[
                whole((count * quarter, depth)),
                pl.BlockSpec((count, quarter + 16, tile), lambda t, place: (0, 0, inner(t))),
                pl.BlockSpec(
                    (2, 1, count, quarter, width),
                    lambda t, place: (t % half, t // half, 0, 0, 0),
                ),
                whole((count // 2, quarter, small)),
                whole((count // 2, quarter, small)),
            ],
            scratch_shapes=[
                pltpu.VMEM((count * 8, depth), wide),
                pltpu.VMEM((count * 8 + 8, tile), wide),
                pltpu.VMEM((quarter + 16, tile), wide),
                pltpu.VMEM((count * quarter, small), wide),
                pltpu.VMEM((count * quarter, tile), low),
            ],
        ),
        out_shape=[
            pltpu.HBM((count * quarter, depth), low),
            pltpu.HBM((count, quarter + 16, chans), wide),
            jax.ShapeDtypeStruct((parts, 2, count, quarter, width), low),
            jax.ShapeDtypeStruct((count // 2, quarter, small), wide),
            jax.ShapeDtypeStruct((count // 2, quarter, small), low),
        ],
        compiler_params=pltpu.CompilerParams(vmem_limit_bytes=28 * 1024 * 1024),
        cost_estimate=spent(8),
        name="project",
    )(places, *map(in_hbm, (*pieces, weight, flags, taps, offset, select)))


def pull_body(order_ref, rows_ref, weight_ref, kept_ref, *refs):
    out_refs, found_ref = refs[:-1], refs[-1]
    count = rows_ref.shape[0]
    quarter = rows_ref.shape[1]
    width = out_refs[0].shape[2]
    turn = pl.program_id(0)
    bit = order_ref[count] & 1

    @pl.when(turn == 0)
    def _():
        for k in range(count):
            kept_ref[k * quarter : (k + 1) * quarter, :] = rows_ref[order_ref[k]]

    found_ref[...] = lax.dot_general(
        kept_ref[...], weight_ref[...], (((1,), (1,)), ((), ())), preferred_element_type=wide
    ).astype(low)
    for p in range(len(out_refs)):

        @pl.when(turn == p // 2)
        def _(p=p):
            here = pl.ds(pl.multiple_of((bit ^ (p % 2)) * width, width), width)
            for k in range(count):
                out_refs[p][k] = found_ref[k * quarter : (k + 1) * quarter, here]


def pull(order, rows, weight, parts):
    count, quarter, depth = rows.shape
    width = weight.shape[0] // parts
    piece = pl.BlockSpec((count, quarter, width), lambda t, order: (0, 0, 0))
    return pl.pallas_call(
        pull_body,
        grid_spec=pltpu.PrefetchScalarGridSpec(
            num_scalar_prefetch=1,
            grid=(parts // 2,),
            in_specs=[
                pl.BlockSpec((count, quarter, depth), lambda t, order: (0, 0, 0)),
                pl.BlockSpec((2 * width, depth), lambda t, order: ((order[count] // 2) ^ t, 0)),
            ],
            out_specs=[pl.BlockSpec((count * quarter, depth), lambda t, order: (0, 0))]
            + [piece] * parts,
            scratch_shapes=[pltpu.VMEM((count * quarter, 2 * width), low)],
        ),
        out_shape=[pltpu.HBM((count * quarter, depth), low)]
        + [pltpu.HBM((count, quarter, width), low)] * parts,
        compiler_params=pltpu.CompilerParams(vmem_limit_bytes=20 * 1024 * 1024),
        cost_estimate=spent(6),
        name="pull",
    )(order, in_hbm(rows), in_hbm(weight))


def spread_parts(part, product, own_ref, other_ref):
    parts = 2 * own_ref.shape[0]
    width = product.shape[0] // parts
    for p in range(parts):
        here = pl.ds(pl.multiple_of((part ^ p) * width, width), width)
        yield (other_ref if p % 2 else own_ref), p // 2, here


def emit_body(order_ref, *refs):
    pieces_ref, refs = refs[0], refs[1:]
    parts = pieces_ref.shape[0]
    (weight_ref, rows_ref, normed_ref, turned_ref) = refs[:4]
    (kept_ref, sent_ref, own_ref, other_ref, dgate_ref, gain_ref) = refs[4:10]
    (gated, product, second) = refs[10:]
    count, quarter, width = pieces_ref.shape[2:]

    @pl.when(pl.program_id(0) == 0)
    def _():
        for p in range(parts):
            here = slice(p * width, (p + 1) * width)
            for k in range(count):
                rows = slice(k * quarter, (k + 1) * quarter)
                gated[rows, here] = pieces_ref[p, 0, k]
                dgate_ref[rows, here] = pieces_ref[p, 1, k]

    values = gated[...]
    branch = jnp.dot(values, weight_ref[...], preferred_element_type=wide).astype(low)
    kept_ref[...] = branch[: count // 2 * quarter].reshape(kept_ref.shape)
    sent_ref[...] = branch[count // 2 * quarter :].reshape(sent_ref.shape)
    down = (((0,), (0,)), ((), ()))
    product[...] = lax.dot_general(
        values, rows_ref[...], down, preferred_element_type=wide
    ).astype(low)
    found = lax.dot_general(
        dgate_ref[...], normed_ref[...], down, preferred_element_type=wide
    )
    gain_ref[...] = jnp.sum(found * turned_ref[...].astype(wide), axis=0, keepdims=True)
    second[...] = found.astype(low)
    for ref, p, here in spread_parts(order_ref[count], product, own_ref, other_ref):
        ref[p, 0] = product[here, :]
        ref[p, 1] = second[here, :]


def emit(order, pieces, weight, rows, normed, turned):
    parts, _, count, quarter, width = pieces.shape
    depth = weight.shape[1]
    tile = 512
    chans = parts * width
    tall = count * quarter
    blocks = pl.BlockSpec((count // 2, quarter, tile), lambda t, order: (0, 0, t))
    grads = pl.BlockSpec((parts // 2, 2, width, tile), lambda t, order: (0, 0, 0, t))
    columns = pl.BlockSpec((tall, tile), lambda t, order: (0, t))
    return pl.pallas_call(
        emit_body,
        grid_spec=pltpu.PrefetchScalarGridSpec(
            num_scalar_prefetch=1,
            grid=(depth // tile,),
            in_specs=[
                pl.BlockSpec(pieces.shape, lambda t, order: (0, 0, 0, 0, 0)),
                pl.BlockSpec((chans, tile), lambda t, order: (0, t)),
                columns,
                columns,
                pl.BlockSpec((chans, tile), lambda t, order: (1, t)),
            ],
            out_specs=[
                blocks,
                blocks,
                grads,
                grads,
                pl.BlockSpec((tall, chans), lambda t, order: (0, 0)),
                pl.BlockSpec((1, tile), lambda t, order: (0, t)),
            ],
            scratch_shapes=[
                pltpu.VMEM((tall, chans), low),
                pltpu.VMEM((chans, tile), low),
                pltpu.VMEM((chans, tile), low),
            ],
        ),
        out_shape=[
            pltpu.HBM((count // 2, quarter, depth), low),
            pltpu.HBM((count // 2, quarter, depth), low),
            pltpu.HBM((parts // 2, 2, width, depth), low),
            pltpu.HBM((parts // 2, 2, width, depth), low),
            pltpu.HBM((tall, chans), low),
            jax.ShapeDtypeStruct((1, depth), wide),
        ],
        compiler_params=pltpu.CompilerParams(vmem_limit_bytes=24 * 1024 * 1024),
        cost_estimate=spent(6),
        name="emit",
    )(order, *map(in_hbm, (pieces, weight, rows, normed, turned)))


def weigh_body(order_ref, rows_ref, normed_ref, turned_ref, own_ref, other_ref, gain_ref, product):
    found = lax.dot_general(
        rows_ref[...], normed_ref[...], (((0,), (0,)), ((), ())), preferred_element_type=wide
    )
    gain_ref[...] = jnp.sum(found * turned_ref[...].astype(wide), axis=0, keepdims=True)
    product[...] = found.astype(low)
    for ref, p, here in spread_parts(order_ref[8], product, own_ref, other_ref):
        ref[p] = product[here, :]


def weigh(order, rows, normed, turned, parts):
    tall, depth = normed.shape
    chans = rows.shape[1] // 2
    width = chans // parts
    tile = 512
    grads = pl.BlockSpec((parts // 2, width, tile), lambda t, order: (0, 0, t))
    return pl.pallas_call(
        weigh_body,
        grid_spec=pltpu.PrefetchScalarGridSpec(
            num_scalar_prefetch=1,
            grid=(depth // tile,),
            in_specs=[
                pl.BlockSpec((tall, chans), lambda t, order: (0, 0)),
                pl.BlockSpec((tall, tile), lambda t, order: (0, t)),
                pl.BlockSpec((chans, tile), lambda t, order: (0, t)),
            ],
            out_specs=[grads, grads, pl.BlockSpec((1, tile), lambda t, order: (0, t))],
            scratch_shapes=[pltpu.VMEM((chans, tile), low)],
        ),
        out_shape=[
            pltpu.HBM((parts // 2, width, depth), low),
            pltpu.HBM((parts // 2, width, depth), low),
            jax.ShapeDtypeStruct((1, depth), wide),
        ],
        compiler_params=pltpu.CompilerParams(vmem_limit_bytes=16 * 1024 * 1024),
        cost_estimate=spent(4),
        name="weigh",
    )(order, rows, in_hbm(normed), in_hbm(turned))


def turn_body(order_ref, *refs):
    count = 8
    smalls, refs = refs[:2], refs[2:]
    (dscan_ref, select_ref, inner_ref, flags_ref, taps_ref, offset_ref, dgate_ref) = refs[:7]
    (dboth_ref, grad_ref, rows_ref) = refs[7:10]
    (small_all, shifted, acts) = refs[10:]
    rank = grad_ref.shape[1]
    parts = pl.num_programs(0) // 2
    turn = pl.program_id(0)
    span = inner_ref.shape[1]
    quarter = span - 16
    reach = quarter + 8
    taps = taps_ref.shape[0]

    @pl.when(turn == 0)
    def _():
        for k in range(count):
            plane = order_ref[k] // 2
            small_all[k * span : (k + 1) * span, :] = smalls[k // (count // 2)][plane]

    @pl.when(turn < parts)
    def _():
        whole = lax.dot_general(
            small_all[...],
            select_ref[...],
            (((1,), (1,)), ((), ())),
            preferred_element_type=wide,
        )
        found = dscan_ref[0]
        sums = [0.0] * (taps + 1)
        for k in range(count):
            flags = flags_ref[k, 8 : 8 + reach, :]
            mask = flags[:, 0:1]
            conv = offset_ref[...]
            for lag in range(taps):
                term = taps_ref[taps - 1 - lag : taps - lag, :] * inner_ref[
                    k, 8 - lag : 8 - lag + reach, :
                ]
                conv = conv + (term * flags[:, lag : lag + 1] if lag else term)
            sig = jax.nn.sigmoid(conv)
            act = conv * sig * mask
            acts[k * quarter : (k + 1) * quarter, :] = act[:quarter].astype(low)
            dact = found[k, :reach].astype(wide) + whole[k * span : k * span + reach]
            dconv = dact * mask * (sig * (1.0 + conv * (1.0 - sig)))
            dinner = 0.0
            for lag in range(taps):
                masked = dconv * flags[:, lag : lag + 1] if lag else dconv
                sums[taps - 1 - lag] += jnp.sum(
                    masked[:quarter] * inner_ref[k, 8 - lag : 8 - lag + quarter, :],
                    axis=0,
                    keepdims=True,
                )
                if lag:
                    shifted[lag, :reach, :] = masked
                    masked = shifted[lag, lag : lag + quarter, :]
                else:
                    sums[taps] += jnp.sum(masked[:quarter], axis=0, keepdims=True)
                    masked = masked[:quarter]
                dinner = dinner + masked * taps_ref[taps - 1 - lag : taps - lag, :]
            dboth_ref[k * quarter : (k + 1) * quarter, :] = (dinner * mask[:quarter]).astype(low)
        for index, value in enumerate(sums):
            rows_ref[index : index + 1, :] = value
        mains = jnp.concatenate(
            [small_all[k * span : k * span + quarter, :] for k in range(count)], axis=0
        )
        grad_ref[...] = lax.dot_general(
            acts[...], mains[:, :rank], (((0,), (0,)), ((), ())), preferred_element_type=wide
        ).astype(low)
        rows_ref[8:, :] = lax.dot_general(
            mains[:, rank:], acts[...], (((0,), (0,)), ((), ())), preferred_element_type=wide
        )

    @pl.when(turn >= parts)
    def _():
        dboth_ref[...] = dgate_ref[...]


def turn_back(order, smalls, dscan, select, inner, flags, taps, offset, dgate, rank):
    parts, count, span, _ = dscan.shape
    small = smalls[0].shape[-1]
    chans = select.shape[0]
    width = chans // parts
    quarter = span - 16

    def whole(shape):
        return pl.BlockSpec(shape, lambda t, order: (0,) * len(shape))

    def early(t):
        return jnp.minimum(t, parts - 1)

    return pl.pallas_call(
        turn_body,
        grid_spec=pltpu.PrefetchScalarGridSpec(
            num_scalar_prefetch=1,
            grid=(2 * parts,),
            in_specs=[whole(v.shape) for v in smalls]
            + [
                pl.BlockSpec((1, count, span, width), lambda t, order: (early(t), 0, 0, 0)),
                pl.BlockSpec((width, small), lambda t, order: (early(t), 0)),
                pl.BlockSpec((count, span, width), lambda t, order: (0, 0, early(t))),
                whole(flags.shape),
                pl.BlockSpec((taps.shape[0], width), lambda t, order: (0, early(t))),
                pl.BlockSpec((1, width), lambda t, order: (0, early(t))),
                pl.BlockSpec(
                    (count * quarter, width), lambda t, order: (0, jnp.maximum(t - parts, 0))
                ),
            ],
            out_specs=[
                pl.BlockSpec((count * quarter, width), lambda t, order: (0, t)),
                pl.BlockSpec((width, rank), lambda t, order: (early(t), 0)),
                pl.BlockSpec((small - rank + 8, width), lambda t, order: (0, early(t))),
            ],
            scratch_shapes=[
                pltpu.VMEM((count * span, small), low),
                pltpu.VMEM((taps.shape[0], span, width), wide),
                pltpu.VMEM((count * quarter, width), low),
            ],
        ),
        out_shape=[
            jax.ShapeDtypeStruct((count * quarter, 2 * chans), low),
            pltpu.HBM((chans, rank), low),
            jax.ShapeDtypeStruct((small - rank + 8, chans), wide),
        ],
        compiler_params=pltpu.CompilerParams(vmem_limit_bytes=20 * 1024 * 1024),
        cost_estimate=spent(5.5),
        name="turn_back",
    )(
        order,
        *smalls,
        dscan,
        select,
        inner,
        flags,
        taps,
        offset,
        dgate,
    )


class Moves:
    def __init__(self):
        self.chan = lax.axis_index("chan").astype(jnp.uint32)
        self.part = lax.axis_index("state").astype(jnp.uint32)
        self.z = self.chan // 2
        self.y = self.chan % 2
        places = jnp.arange(8, dtype=jnp.uint32)
        planes = (self.z + 4 - places % 4) % 4
        self.blocks = planes * 2 + (self.y + places // 4) % 2
        hops = (self.z + 4 - places // 2) % 4
        self.order = (self.y + places) % 2 * 4 + hops

    def over_y(self, values):
        return lax.ppermute(values, "chan", [(i, i ^ 1) for i in range(8)])

    def over_z(self, values, hops):
        return lax.ppermute(values, "chan", [(i, (i + 2 * hops) % 8) for i in range(8)])

    def over_state(self, values, bits):
        return lax.ppermute(values, "state", [(i, i ^ bits) for i in range(4)])

    def swap_state(self, values):
        return lax.all_to_all(values, "state", 0, 0, tiled=True)

    def pair(self, bit, own, other):
        return jnp.stack([jnp.where(bit == 0, own, other), jnp.where(bit == 0, other, own)])

    def in_order(self, pieces):
        own, core, across, slant = pieces
        bit = self.part % 2
        near = self.pair(bit, own, core)
        far = self.pair(bit, across, slant)
        return self.pair(self.part // 2, near, far).reshape((4,) + own.shape)

    def pieces_state(self, values):
        core = self.over_state(values, 1)
        across = self.over_state(values, 2)
        return values, core, across, self.over_state(across, 1)


def tied(*values):
    return lax.optimization_barrier(values)


def after(values, *others):
    token = lax.optimization_barrier((lax.create_token(), others))[0]
    return lax.optimization_barrier((token, values))[1]


def near_shards(
    n_chan,
    n_state,
    hidden_in,
    norm_gain,
    in_weight,
    conv_kernel,
    conv_offset,
    select_rank,
    select_entry,
    select_read,
    delta_weight,
    step_bias,
    decay_log,
    skip_weight,
    out_weight,
    lengths,
    pad_mask,
    cotangent,
):
    rows_dev, width = hidden_in.shape
    tokens = pad_mask.shape[0]
    chans = in_weight.shape[2]
    taps = conv_kernel.shape[0]
    rank = select_rank.shape[1]
    per_state = select_entry.shape[1]
    states = per_state * n_state
    small = rank + 2 * states
    quarter = rows_dev // n_state
    own = chans // n_state
    rows_q = n_chan * quarter
    part = lax.axis_index("state").astype(jnp.uint32)
    contract_rows = (((0,), (0,)), ((), ()))
    contract_cols = (((1,), (1,)), ((), ()))
    moves = Moves()
    blocks = moves.blocks
    planes = jnp.arange(4, dtype=jnp.uint32)
    small_order = jnp.stack([(moves.y ^ u) * 4 + planes for u in (0, 1)], axis=1).reshape(-1)
    order = jnp.concatenate([moves.order, small_order, part[None]]).astype(jnp.int32)
    places = jnp.concatenate([blocks, part[None]]).astype(jnp.int32)
    blocks = blocks.astype(jnp.int32)

    def mine(values, axis=0):
        return lax.dynamic_slice_in_dim(values, part * own, own, axis)

    start = part * quarter
    hidden_q = lax.dynamic_slice_in_dim(hidden_in, start, quarter, 0)
    ahead = (start + (rows_dev - HALO)) % rows_dev
    behind = (start + quarter) % rows_dev
    local = jnp.concatenate(
        [
            hidden_q,
            lax.dynamic_slice_in_dim(hidden_in, behind, HALO, 0),
            lax.dynamic_slice_in_dim(hidden_in, ahead, HALO, 0),
        ],
        axis=0,
    )
    inv_all = lax.rsqrt(jnp.mean(local * local, axis=1, keepdims=True) + epsilon)
    scaled_all = local * inv_all
    normed_all = (scaled_all * norm_gain[None, :]).astype(low)
    inv_rms = inv_all[:quarter]
    scaled = scaled_all[:quarter]
    cot_q = lax.dynamic_slice_in_dim(cotangent, start, quarter, 0).astype(low)
    ranks = (part ^ jnp.arange(n_state, dtype=jnp.uint32)).astype(jnp.int32)

    def trades(values):
        return [values[0]] + [moves.over_state(values[k], k) for k in (1, 2, 3)]

    def core_halves(values):
        cut = values.reshape((2, 2) + values.shape[1:])
        core = part % 2
        return (
            lax.dynamic_index_in_dim(cut, 1 - core, 1, keepdims=False),
            lax.dynamic_index_in_dim(cut, core, 1, keepdims=False),
        )

    def chip_halves(values):
        side = part // 2
        return (
            lax.dynamic_index_in_dim(values, 1 - side, 0, keepdims=False),
            lax.dynamic_index_in_dim(values, side, 0, keepdims=False),
        )

    def total_of(own_part, others):
        total = own_part.astype(wide)
        for piece in others:
            total = total + piece.astype(wide)
        return total.astype(low)

    def added(kept, came):
        return (kept.astype(wide) + came.astype(wide)).astype(low)

    columns = jnp.concatenate([select_entry, select_read], axis=1)
    decay_cut = jnp.swapaxes(decay_log.reshape(per_state, n_state, own), 0, 1)
    across = moves.over_y(normed_all)
    along = [moves.over_z(normed_all, hops) for hops in (1, 2, 3)]
    columns_core = moves.over_state(columns, 1)
    columns_chip = moves.over_state(columns, 2)
    decay_own = moves.swap_state(decay_cut)
    in_flat = in_weight.reshape(width, 2 * chans)
    tie = tied(across, *along, columns_core, columns_chip, decay_own, in_flat, cot_q)
    across, along, columns_core, columns_chip = tie[0], list(tie[1:4]), *tie[4:6]
    decay_own, in_flat, cot_q = tie[6:]
    grads = lax.all_gather(cot_q, "chan", axis=0)
    over = [moves.over_y(piece) for piece in along]
    columns_slant = moves.over_state(columns_chip, 1)
    turned = in_flat.T
    over[0], over[1], over[2], columns_slant, turned = tied(*over, columns_slant, turned)
    pieces = [normed_all] + along + [across] + over

    place = positions(lengths, tokens)
    flags = [pad_mask.astype(wide)]
    flags += [(place >= lag).astype(wide) for lag in range(1, taps)]
    flags = jnp.stack(flags)
    padded = jnp.pad(flags, ((0, 0), (8, 8 + rows_dev)))
    span = quarter + 16
    flags_win = lax.dynamic_slice_in_dim(padded, start, n_chan * rows_dev, 1)
    flags_win = flags_win.reshape(taps, n_chan, rows_dev)[:, :, :span]
    chooser = (blocks[:, None] == jnp.arange(n_chan)[None, :]).astype(wide)
    flags_rows = jnp.einsum("kb,fbr->krf", chooser, flags_win)
    itself = jnp.arange(n_chan, dtype=jnp.int32)
    nearby = blocks[:, None] - blocks[None, :]
    one_before = jnp.where(blocks > 0, jnp.argmax(nearby == 1, axis=1), n_chan)
    one_after = jnp.where(blocks < n_chan - 1, jnp.argmax(nearby == -1, axis=1), n_chan)
    one_before = jnp.where(part == 0, one_before, itself)
    one_after = jnp.where(part == n_state - 1, one_after, itself)
    neighbours = jnp.concatenate([one_before, one_after, blocks[:4] // 2]).astype(jnp.int32)

    columns = moves.in_order((columns, columns_core, columns_chip, columns_slant))
    columns = columns.reshape(n_state, chans, 2, per_state)
    columns = jnp.transpose(columns, (1, 2, 0, 3)).reshape(chans, 2 * states)
    select = jnp.concatenate([select_rank, columns], axis=1)
    coeff = -jnp.exp(decay_own.reshape(states, own))

    normed_q, inner_all, sent, kept, other = project(
        neighbours, pieces, in_flat, flags_rows, conv_kernel, conv_offset[None, :], select, n_state
    )
    reach = quarter + HALO
    channels = moves.swap_state(sent)
    came = moves.over_y(other)
    joined = added(kept, came)
    along = [moves.over_z(joined, hops) for hops in (1, 2, 3)]
    grad_q, *dgated = pull(places, grads, out_weight, n_state)
    along[0], along[1], along[2], *dgated = tied(*along, *dgated)
    summed = total_of(joined, along)
    came = moves.over_y(summed)
    dgated = trades(dgated)
    picked = moves.pieces_state(jnp.concatenate([summed, came], axis=0))
    tie = tied(*picked, *dgated, channels)
    picked, dgated, channels = tie[:4], tie[4:8], tie[8]

    weight_own = mine(delta_weight, 1)
    bias_own = mine(step_bias)[None, :]
    skip_own = mine(skip_weight)[None, :]
    fresh = jnp.broadcast_to((place > 0).astype(low)[:, None], (tokens, own))
    spread = spreading(states)
    coeff_two = coeff * math.log2(math.e)
    kept, dpre, gated = forward_scan(
        order,
        picked,
        channels,
        dgated,
        fresh,
        weight_own,
        bias_own,
        skip_own,
        coeff_two,
        spread,
    )
    gated = moves.swap_state(gated)
    own_sums, other_sums, dscan, delta_grad_own, decay_total, sums = backward_scan(
        order,
        picked,
        channels,
        dgated,
        fresh,
        dpre,
        kept,
        weight_own,
        skip_own,
        coeff_two,
        spread,
    )
    decay_grad_own = coeff * decay_total
    packed = jnp.concatenate([delta_grad_own, decay_grad_own, sums], axis=0).astype(low)

    own_sums, other_sums, packed, gated, dscan = tied(
        own_sums, other_sums, packed, gated, dscan
    )
    came = moves.over_state(other_sums, 1)
    dscan = moves.swap_state(dscan)
    came, own_sums, packed, gated = tied(came, own_sums, packed, gated)

    chip = added(own_sums, came)
    came = moves.over_state(chip[1], 2)
    branch_kept, sent, parts_kept, parts_sent, dgate_q, gain = emit(
        places, gated, out_weight, grad_q, normed_q, turned
    )
    came, sent, parts_sent = tied(came, sent, parts_sent)

    joined = added(chip[0], came)
    came = moves.over_y(joined[4:])
    parts_came = moves.over_state(parts_sent, 1)
    came, parts_came, sent = tied(came, parts_came, sent)

    joined = added(joined[:4], came)
    along = [moves.over_z(joined, hops) for hops in (1, 2, 3)]
    branch_came = moves.over_y(sent)
    parts_sum = added(parts_kept, parts_came)
    parts_came = moves.over_state(parts_sum[1], 2)
    along[0], along[1], along[2], branch_came, dscan = tied(*along, branch_came, dscan)

    partial = total_of(joined, along)
    came = moves.over_y(partial)
    branch = added(branch_kept, branch_came)
    branches = [moves.over_z(branch[4 - hops], hops) for hops in (1, 2, 3)]
    came, partial = tied(came, partial)

    dboth, rank_part, rows_part = turn_back(
        places,
        (partial, came),
        dscan,
        select,
        inner_all,
        flags_rows,
        conv_kernel,
        conv_offset[None, :],
        dgate_q,
        rank,
    )

    def backed(rows, weight):
        return lax.dot_general(rows, weight, contract_cols, preferred_element_type=wide)

    edge = width * 11 // 16
    left, right = slice(0, edge), slice(edge, width)
    other, same = slice(rows_q // 2, rows_q), slice(0, rows_q // 2)
    left_sent = backed(dboth[other], in_flat[left]).astype(low).reshape(4, quarter, edge)
    right_all = backed(dboth, in_flat[right]).reshape(2, 4, quarter, width - edge)
    right_sent = [right_all[:, 4 - hops].astype(low) for hops in (1, 2, 3)]
    inner_kept, inner_sent, inner_gain = weigh(places, dboth, normed_q, turned, n_state)
    inner_came = moves.over_state(inner_sent, 1)
    gain = (gain + inner_gain).reshape(-1, chans)
    gain = jnp.concatenate([rows_part, gain], axis=0)
    small = jnp.concatenate([packed, rank_part], axis=0)
    tie = tied(left_sent, dboth, small, parts_came, inner_came, gain, *branches, *right_sent)
    left_sent, dboth, small, parts_came, inner_came, gain = tie[:6]
    branches, right_sent = tie[6:9], tie[9:]

    left_came = moves.over_y(left_sent)
    right_along = [moves.over_z(right_sent[hops - 1], hops) for hops in (1, 2, 3)]
    parts_own = added(parts_sum[0], parts_came)
    parts_chip = moves.over_state(parts_own, 2)
    gain_came = moves.over_state(gain, 1)
    left_kept = backed(after(dboth, right_along[0])[same], in_flat[left])
    left_kept = left_kept.reshape(4, quarter, edge)
    branch = total_of(branch[0], branches)
    tie = tied(left_came, left_kept, gain, gain_came, branch, parts_chip, *right_along)
    left_came, left_kept, gain, gain_came, branch, parts_chip = tie[:6]
    right_along = tie[6:]

    joined = left_kept + left_came.astype(wide)
    left_sum = joined[0]
    left_along = [moves.over_z(joined[4 - hops].astype(low), hops) for hops in (1, 2, 3)]
    right_sum = right_all[:, 0]
    for piece in right_along:
        right_sum = right_sum + piece.astype(wide)
    right_came = moves.over_y(right_sum[1].astype(low))
    inner_sum = added(inner_kept, inner_came)
    inner_came = moves.over_state(inner_sum[1], 2)
    gain = gain + gain_came
    gain_came = moves.over_state(gain, 2)
    small_core = moves.over_state(small, 1)
    tie = tied(right_came, gain, gain_came, inner_came, small_core, *left_along)
    right_came, gain, gain_came, inner_came, small_core = tie[:5]
    left_along = tie[5:]

    for piece in left_along:
        left_sum = left_sum + piece.astype(wide)
    right_sum = right_sum[0] + right_came.astype(wide)
    dnormed = jnp.concatenate([left_sum, right_sum], axis=1)
    dscaled = dnormed * norm_gain[None, :]
    change = inv_rms * (dscaled - scaled * jnp.mean(dscaled * scaled, axis=1, keepdims=True))
    change = change.astype(low)
    change_chip = moves.over_state(change, 2)
    change_core = moves.over_state(change, 1)
    inner_own = added(inner_sum[0], inner_came)
    inner_chip = moves.over_state(inner_own, 2)
    gain = gain + gain_came
    gain_came = moves.over_y(gain[8 + 2 * states :].reshape(width))
    inner_core = moves.over_state(inner_own, 1)
    parts_core = moves.over_state(parts_own, 1)
    parts_slant = moves.over_state(parts_chip, 1)
    out_grad = placed(ranks, (parts_own, parts_core, parts_chip, parts_slant))
    place_at = 8 + part * per_state
    smalls = (
        gain[:taps],
        gain[taps],
        lax.dynamic_slice_in_dim(gain, place_at, per_state, 0).T,
        lax.dynamic_slice_in_dim(gain, place_at + states, per_state, 0).T,
    )
    tie = tied(
        change_chip,
        change_core,
        gain,
        gain_came,
        inner_chip,
        inner_core,
        parts_core,
        parts_slant,
        out_grad,
        *smalls,
    )
    change_chip, change_core, gain, gain_came, inner_chip, inner_core = tie[:6]
    parts_core, parts_slant, out_grad = tie[6:9]
    smalls = tie[9:]

    inner_slant = moves.over_state(inner_chip, 1)
    branch_chip = moves.over_state(branch, 2)
    branch_core = moves.over_state(branch, 1)
    change_slant = moves.over_state(change_chip, 1)
    fixed = packed.shape[0]
    rank_sum = added(small[fixed:], small_core[fixed:])
    small_sum = jnp.concatenate([small[:fixed], rank_sum], axis=0)
    small_chip = moves.over_state(small_sum, 2)
    gain = gain[8 + 2 * states :].reshape(width) + gain_came
    in_grad = interleave(
        ranks,
        (inner_own, inner_core, inner_chip, inner_slant),
        (parts_own, parts_core, parts_chip, parts_slant),
    )
    tie = tied(branch_chip, branch_core, change_slant, small_chip, gain, in_grad)
    branch_chip, branch_core, change_slant, small_chip, gain, in_grad = tie

    branch_slant = moves.over_state(branch_chip, 1)
    packed_slant = moves.over_state(small_chip[:fixed], 1)
    gains = [gain] + [moves.over_z(gain, hops) for hops in (1, 2, 3)]
    rank_grad = rank_sum.astype(wide) + small_chip[fixed:].astype(wide)
    packed = moves.in_order((packed, small_core[:fixed], small_chip[:fixed], packed_slant))
    packed = jnp.swapaxes(packed, 0, 1).reshape(-1, chans).astype(wide)
    smalls = (
        *smalls[:2],
        rank_grad,
        *smalls[2:],
        packed[:rank],
        packed[rank + states],
        lax.dynamic_slice_in_dim(packed, rank + part * per_state, per_state, 0),
        packed[rank + states + 1],
    )
    input_grad = placed(ranks, (change, change_core, change_chip, change_slant), cotangent)
    result = placed(ranks, (branch, branch_core, branch_chip, branch_slant), hidden_in)
    gains = jnp.stack(gains)
    gain_grad = 0.0
    for plane_at in range(4):
        gain_grad = gain_grad + lax.dynamic_index_in_dim(
            gains, (moves.z + 4 - plane_at) % 4, 0, keepdims=False
        )
    gain_grad = gain_grad / norm_gain
    return (result, input_grad, gain_grad, in_grad, *smalls, out_grad)


def solution(mesh):
    sizes = dict(mesh.shape)
    near = (sizes["chan"], sizes["state"]) == (8, 4)
    program = functools.partial(near_shards, 8, 4) if near else shards
    return jax.shard_map(
        program,
        mesh=mesh,
        in_specs=(
            P("chan", None),
            P(),
            P(None, None, "chan"),
            P(None, "chan"),
            P("chan"),
            P("chan", None),
            P("chan", "state"),
            P("chan", "state"),
            P(None, "chan"),
            P("chan"),
            P("state", "chan"),
            P("chan"),
            P("chan", None),
            P(),
            P(),
            P("chan", None),
        ),
        out_specs=(
            P("chan", None),
            P("chan", None),
            P(),
            P(None, None, "chan"),
            P(None, "chan"),
            P("chan"),
            P("chan", None),
            P("chan", "state"),
            P("chan", "state"),
            P(None, "chan"),
            P("chan"),
            P("state", "chan"),
            P("chan"),
            P("chan", None),
        ),
        check_vma=False,
    )
```

```python
import functools
import math

import jax
import jax.numpy as jnp
from jax import lax
from jax.experimental import pallas as pl
from jax.experimental.pallas import tpu as pltpu
from jax.sharding import PartitionSpec as P

epsilon = 1e-05
GROUP = 16
HALO = 4
TAIL = 16
FAR = 1e30
wide = jnp.float32
low = jnp.bfloat16


def spent(microseconds):
    moved = int(microseconds * 3.6e6)
    return pl.CostEstimate(flops=0, bytes_accessed=moved, transcendentals=0)


def in_hbm(values):
    return pltpu.with_memory_space_constraint(values, pltpu.HBM)


def positions(lengths, tokens_all):
    ends = jnp.cumsum(lengths)
    begins = ends - lengths
    places = jnp.arange(tokens_all, dtype=jnp.int32)
    opening = jnp.max(jnp.where(begins[:, None] <= places[None, :], begins[:, None], 0), axis=0)
    return places - opening


def delayed(values, amount):
    if amount == 0:
        return values
    padding = jnp.zeros((amount,) + values.shape[1:], values.dtype)
    return jnp.concatenate([padding, values[: values.shape[0] - amount]], axis=0)


def advanced(values, amount):
    if amount == 0:
        return values
    padding = jnp.zeros((amount,) + values.shape[1:], values.dtype)
    return jnp.concatenate([values[amount:], padding], axis=0)


def silu_slope(values):
    logistic = jax.nn.sigmoid(values)
    return logistic * (1.0 + values * (1.0 - logistic))


def linear_scan(decays, drive):
    total_rows = decays.shape[0]
    blocks = total_rows // 16
    factors = jnp.swapaxes(decays.reshape((blocks, 16) + decays.shape[1:]), 0, 1)
    sources = jnp.swapaxes(drive.reshape((blocks, 16) + drive.shape[1:]), 0, 1)

    def advance(totals, item):
        state_now, product_now = totals
        factor_now, source_now = item
        state_now = factor_now * state_now + source_now
        product_now = factor_now * product_now
        return ((state_now, product_now), (state_now, product_now))

    initial = (jnp.zeros(factors.shape[1:], jnp.float32), jnp.ones(factors.shape[1:], jnp.float32))
    final_pair, (local_states, products) = lax.scan(advance, initial, (factors, sources))

    def combine(early, later):
        return (early[0] * later[0], later[0] * early[1] + later[1])

    joined_factor, joined_state = lax.associative_scan(
        combine, (products[-1], local_states[-1]), axis=0
    )
    entering = jnp.concatenate([jnp.zeros_like(joined_state[:1]), joined_state[:-1]], axis=0)
    states = local_states + products * entering[None]
    return jnp.swapaxes(states, 0, 1).reshape(decays.shape)


def shards(
    hidden_in,
    norm_gain,
    in_weight,
    conv_kernel,
    conv_offset,
    select_rank,
    select_entry,
    select_read,
    delta_weight,
    step_bias,
    decay_log,
    skip_weight,
    out_weight,
    lengths,
    pad_mask,
    cotangent,
):
    rows_dev, width = hidden_in.shape
    tokens_all = pad_mask.shape[0]
    chans = in_weight.shape[2]
    kernel_len = conv_kernel.shape[0]
    per_state = select_entry.shape[1]
    contract_rows = (((0,), (0,)), ((), ()))
    contract_cols = (((1,), (1,)), ((), ()))
    place = positions(lengths, tokens_all)
    fresh = (place > 0).astype(jnp.float32)
    maskf = pad_mask.astype(jnp.float32)[:, None]
    square = jnp.mean(hidden_in * hidden_in, axis=1, keepdims=True)
    inv_rms = lax.rsqrt(square + epsilon)
    scaled = hidden_in * inv_rms
    normed = (scaled * norm_gain[None, :]).astype(jnp.bfloat16)
    in_flat = in_weight.reshape(width, 2 * chans)
    both = jnp.dot(
        lax.all_gather(normed, "chan", axis=0, tiled=True),
        in_flat,
        preferred_element_type=jnp.float32,
    )
    inner = both[:, :chans] * maskf
    gate_in = both[:, chans:]
    valids = []
    shifted = []
    conv = jnp.zeros((tokens_all, chans), jnp.float32) + conv_offset[None, :]
    for index in range(kernel_len):
        lag = kernel_len - 1 - index
        valids.append((place >= lag).astype(jnp.float32)[:, None])
        shifted.append(delayed(inner, lag))
        conv = conv + conv_kernel[index][None, :] * shifted[index] * valids[index]
    act = (jax.nn.silu(conv) * maskf).astype(jnp.bfloat16)
    act_wide = act.astype(jnp.float32)
    pair_map = jnp.concatenate([select_entry, select_read], axis=1)
    rank_part = jnp.dot(act, select_rank, preferred_element_type=jnp.float32)
    pair_part = jnp.dot(act, pair_map, preferred_element_type=jnp.float32)
    raw_sum, pair_sum = lax.psum((rank_part, pair_part), "chan")
    entry = pair_sum[:, :per_state]
    readout = pair_sum[:, per_state:]
    lowrank = raw_sum.astype(jnp.bfloat16)
    dpre = jnp.dot(lowrank, delta_weight, preferred_element_type=jnp.float32) + step_bias[None, :]
    delta = jax.nn.softplus(dpre)
    coeff = -jnp.exp(decay_log)
    decays = jnp.exp(delta[:, None, :] * coeff[None]) * fresh[:, None, None]
    drive = (delta * act_wide)[:, None, :] * entry[:, :, None]
    states = linear_scan(decays, drive)
    scan_part = jnp.sum(readout[:, :, None] * states, axis=1)
    scanned = lax.psum(scan_part, "state")
    mixed = scanned + skip_weight[None, :] * act_wide
    gate_act = jax.nn.silu(gate_in)
    gated = (mixed * gate_act).astype(jnp.bfloat16)
    gated_rows = gated
    branch = lax.psum_scatter(
        jnp.dot(gated_rows, out_weight, preferred_element_type=jnp.float32),
        "chan",
        scatter_dimension=0,
        tiled=True,
    )
    result = hidden_in + branch
    grad_low = cotangent.astype(jnp.bfloat16)
    pieces = lax.all_gather(grad_low, "chan", axis=0, tiled=True)
    gated_rows = gated
    product = lax.dot_general(pieces, out_weight, contract_cols, preferred_element_type=jnp.float32)
    outw_acc = lax.dot_general(
        gated_rows, pieces, contract_rows, preferred_element_type=jnp.float32
    )
    dmix = product * gate_act
    dgate = product * mixed * silu_slope(gate_in)
    skip_grad = jnp.sum(dmix * act_wide, axis=0)
    emitted = readout[:, :, None] * dmix[:, None, :]
    following = jnp.concatenate([decays[1:], jnp.zeros_like(decays[:1])], axis=0)
    adjoint = jnp.flip(linear_scan(jnp.flip(following, 0), jnp.flip(emitted, 0)), 0)
    earlier = jnp.concatenate([jnp.zeros_like(states[:1]), states[:-1]], axis=0)
    flow = adjoint * earlier * decays
    dread_part = jnp.sum(states * dmix[:, None, :], axis=2)
    dentry_part = jnp.sum(adjoint * (delta * act_wide)[:, None, :], axis=2)
    ddelta_part = jnp.sum(
        flow * coeff[None] + adjoint * entry[:, :, None] * act_wide[:, None, :], axis=1
    )
    decay_grad = coeff * jnp.sum(flow * delta[:, None, :], axis=0)
    dact_scan = jnp.sum(adjoint * entry[:, :, None], axis=1) * delta
    dentry_sum, dread_sum = lax.psum((dentry_part, dread_part), "chan")
    dpair = jnp.concatenate(
        [dentry_sum.astype(jnp.bfloat16), dread_sum.astype(jnp.bfloat16)], axis=1
    )
    pair_grad = lax.dot_general(act, dpair, contract_rows, preferred_element_type=jnp.float32)
    entry_grad = pair_grad[:, :per_state]
    read_grad = pair_grad[:, per_state:]
    dact_pair = lax.dot_general(dpair, pair_map, contract_cols, preferred_element_type=jnp.float32)
    dact_state, ddelta = lax.psum((dact_scan + dact_pair, ddelta_part), "state")
    ddpre = (ddelta * jax.nn.sigmoid(dpre)).astype(jnp.bfloat16)
    bias_grad = jnp.sum(ddpre.astype(jnp.float32), axis=0)
    delta_grad = lax.dot_general(lowrank, ddpre, contract_rows, preferred_element_type=jnp.float32)
    dlow_part = lax.dot_general(
        ddpre, delta_weight, contract_cols, preferred_element_type=jnp.float32
    )
    dlow = lax.psum(dlow_part, "chan").astype(jnp.bfloat16)
    rank_grad = lax.dot_general(act, dlow, contract_rows, preferred_element_type=jnp.float32)
    dact = (
        dact_state
        + dmix * skip_weight[None, :]
        + lax.dot_general(dlow, select_rank, contract_cols, preferred_element_type=jnp.float32)
    )
    dconv = dact * maskf * silu_slope(conv)
    offset_grad = jnp.sum(dconv, axis=0)
    kernel_rows = []
    dinner = jnp.zeros((tokens_all, chans), jnp.float32)
    for index in range(kernel_len):
        lag = kernel_len - 1 - index
        masked = dconv * valids[index]
        kernel_rows.append(jnp.sum(masked * shifted[index], axis=0))
        dinner = dinner + advanced(masked * conv_kernel[index][None, :], lag)
    kernel_grad = jnp.stack(kernel_rows, axis=0)
    dboth = jnp.concatenate([dinner * maskf, dgate], axis=1).astype(jnp.bfloat16)
    chosen = dboth
    in_flat_grad = lax.dot_general(
        lax.all_gather(normed, "chan", axis=0, tiled=True),
        chosen,
        contract_rows,
        preferred_element_type=jnp.float32,
    )
    in_grad = in_flat_grad.reshape(width, 2, chans)
    chosen = dboth
    dnormed = lax.psum_scatter(
        lax.dot_general(chosen, in_flat, contract_cols, preferred_element_type=jnp.float32),
        "chan",
        scatter_dimension=0,
        tiled=True,
    )
    gain_part = jnp.sum(dnormed * scaled, axis=0)
    gain_grad = lax.psum(gain_part, "chan")
    dscaled = dnormed * norm_gain[None, :]
    input_grad = cotangent + inv_rms * (
        dscaled - scaled * jnp.mean(dscaled * scaled, axis=1, keepdims=True)
    )
    return (
        result,
        input_grad,
        gain_grad,
        in_grad,
        kernel_grad,
        offset_grad,
        rank_grad,
        entry_grad,
        read_grad,
        delta_grad,
        bias_grad,
        decay_grad,
        skip_grad,
        outw_acc,
    )


def own_block(states):
    row = lax.broadcasted_iota(jnp.int32, (GROUP, GROUP * states), 0)
    col = lax.broadcasted_iota(jnp.int32, (GROUP, GROUP * states), 1)
    return jnp.logical_and(col >= row * states, col < (row + 1) * states)


def spreading(states):
    eye = jnp.eye(states, dtype=low)
    tiled = jnp.tile(eye, (1, GROUP))
    nothing = jnp.zeros_like(tiled)
    return jnp.concatenate(
        [
            jnp.concatenate([tiled, nothing], axis=1),
            jnp.concatenate([nothing, tiled], axis=1),
        ],
        axis=0,
    )


def transposed(values):
    count = values.shape[1]
    row = lax.broadcasted_iota(jnp.int32, (count, count), 0)
    col = lax.broadcasted_iota(jnp.int32, (count, count), 1)
    eye = jnp.where(row == col, 1.0, 0.0).astype(low)
    return lax.dot_general(eye, values, (((1,), (1,)), ((), ())), preferred_element_type=wide)


def forward_body(parts, order_ref, *refs):
    sources, refs = refs[: 2 * parts + 2], refs[2 * parts + 2 :]
    params, (kept_hbm, dpre_hbm, gated_hbm), refs = refs[:5], refs[5:8], refs[8:]
    carry, step_all, drive_all, small_all, dgated_all, pair_all, fresh_all = refs[:7]
    kept_all, dpre_all, gated_all, came, left = refs[7:]
    blocks = small_all.shape[1]
    chunk = step_all.shape[0]
    states = carry.shape[0]

    def entering(turn):
        block = order_ref[turn]
        rows = pl.ds(pl.multiple_of(turn * chunk, chunk), chunk)
        found = []
        for k in range(parts):
            found.append((sources[k].at[order_ref[blocks + turn]], small_all.at[k, turn]))
            found.append((sources[parts + k].at[block], dgated_all.at[k, turn]))
        found.append((sources[2 * parts].at[:, :, block], pair_all.at[:, :, turn]))
        found.append((sources[2 * parts + 1].at[rows], fresh_all.at[rows]))
        return [
            pltpu.make_async_copy(a, b, came.at[turn, i]) for i, (a, b) in enumerate(found)
        ]

    def leaving(turn):
        rows = pl.ds(pl.multiple_of(turn * chunk, chunk), chunk)
        tall = pl.ds(pl.multiple_of(turn * (chunk * states), chunk * states), chunk * states)
        found = [
            (kept_all.at[tall], kept_hbm.at[tall]),
            (dpre_all.at[rows], dpre_hbm.at[rows]),
            (gated_all.at[:, :, turn], gated_hbm.at[:, :, order_ref[turn]]),
        ]
        return [
            pltpu.make_async_copy(a, b, left.at[turn, i]) for i, (a, b) in enumerate(found)
        ]

    @pl.loop(0, blocks)
    def _(turn):
        for copy in entering(turn):
            copy.start()

    carry[...] = jnp.zeros_like(carry)

    @pl.loop(0, blocks)
    def _(turn):
        for copy in entering(turn):
            copy.wait()
        forward_steps(
            turn,
            parts,
            order_ref,
            small_all,
            dgated_all,
            pair_all,
            fresh_all,
            *params,
            kept_all,
            dpre_all,
            gated_all,
            carry,
            step_all,
            drive_all,
        )
        for copy in leaving(turn):
            copy.start()

    @pl.loop(0, blocks)
    def _(turn):
        for copy in leaving(turn):
            copy.wait()


def forward_steps(
    turn,
    parts,
    order_ref,
    small_all,
    dgated_all,
    pair_ref,
    fresh_ref,
    weight_ref,
    bias_ref,
    skip_ref,
    coeff_ref,
    spread_ref,
    kept_ref,
    dpre_ref,
    gated_ref,
    carry,
    step_all,
    drive_all,
):
    coeff = coeff_ref[...]
    states = coeff.shape[0]
    chunk = step_all.shape[0]
    origin = pl.multiple_of(turn * (chunk * states), chunk * states)
    rank = weight_ref.shape[0]
    quarter = small_all.shape[2]
    chosen = own_block(states)
    part = order_ref[order_ref.shape[0] - 1]
    columns = [None] * parts
    reading = [None] * parts

    def before(j):
        rows = slice(j * quarter, (j + 1) * quarter)
        small = small_all[part ^ j, turn]
        dpre = (
            jnp.dot(small[:, :rank], weight_ref[...], preferred_element_type=wide) + bias_ref[...]
        )
        dpre_ref[pl.ds(turn * chunk + j * quarter, quarter), :] = dpre
        delta = jax.nn.softplus(dpre)
        step_all[rows, :] = jnp.where(fresh_ref[pl.ds(turn * chunk + j * quarter, quarter), :].astype(wide) > 0.0, delta, FAR)
        drive_all[rows, :] = delta * pair_ref[j, 0, turn].astype(wide)
        pair = small[:, rank:]
        columns[j] = transposed(pair)
        reading[j] = jnp.dot(
            pair, spread_ref[:, GROUP * states :], preferred_element_type=wide
        )

    def scan(j, state):
        for group in range(quarter // GROUP):
            base = j * quarter + group * GROUP
            kept = []
            for t in range(base, base + GROUP):
                here = t - j * quarter
                decay = jnp.exp2(step_all[t : t + 1, :] * coeff)
                entry = columns[j][:states, here : here + 1]
                state = decay * state + drive_all[t : t + 1, :] * entry
                kept.append(state)
            rows = pl.ds(origin + base * states, GROUP * states)
            kept_ref[rows, :] = jnp.concatenate(kept, axis=0).astype(low)
        return state

    def finish_part(j):
        found = []
        for group in range(quarter // GROUP):
            base = j * quarter + group * GROUP
            block = kept_ref[pl.ds(origin + base * states, GROUP * states), :]
            here = reading[j][group * GROUP : (group + 1) * GROUP]
            weights = jnp.where(chosen, here, 0.0).astype(low)
            found.append(jnp.dot(weights, block, preferred_element_type=wide))
        act = pair_ref[j, 0, turn].astype(wide)
        gate = pair_ref[j, 1, turn].astype(wide)
        mixed = jnp.concatenate(found, axis=0) + skip_ref[...] * act
        dgated = dgated_all[part ^ j, turn].astype(wide)
        gated_ref[j, 0, turn] = (mixed * jax.nn.silu(gate)).astype(low)
        gated_ref[j, 1, turn] = (dgated * mixed * silu_slope(gate)).astype(low)

    state = carry[...]
    before(0)
    for j in range(parts):
        if j + 1 < parts:
            before(j + 1)
        state = scan(j, state)
        if j:
            finish_part(j - 1)
    finish_part(parts - 1)
    carry[...] = state


def backward_body(parts, order_ref, *refs):
    sources, refs = refs[: 2 * parts + 4], refs[2 * parts + 4 :]
    params, (own_hbm, other_hbm, dscan_hbm), refs = refs[:4], refs[4:7], refs[7:]
    results, refs = refs[:3], refs[3:]
    scratch, refs = refs[:11], refs[11:]
    (small_all, dgated_all, pair_all, fresh_all, dpre_all, kept_all, edge_all) = refs[:7]
    (own_all, other_all, dscan_all, came, left) = refs[7:]
    blocks = small_all.shape[1]
    chunk = scratch[1].shape[0]
    states = scratch[0].shape[0]
    for ref in (scratch[0], *results, *scratch[8:10]):
        ref[...] = jnp.zeros_like(ref)

    def entering(turn):
        at = blocks - 1 - turn
        block = order_ref[at]
        rows = pl.ds(pl.multiple_of(at * chunk, chunk), chunk)
        tall = pl.ds(pl.multiple_of(at * (chunk * states), chunk * states), chunk * states)
        found = []
        for k in range(parts):
            found.append((sources[k].at[order_ref[blocks + at]], small_all.at[k, at]))
            found.append((sources[parts + k].at[block], dgated_all.at[k, at]))
        found.append((sources[2 * parts].at[:, :, block], pair_all.at[:, :, at]))
        for source, target, here in zip(
            sources[2 * parts + 1 :], (fresh_all, dpre_all, kept_all), (rows, rows, tall)
        ):
            found.append((source.at[here], target.at[here]))
        ahead = pl.multiple_of(jnp.maximum(at * (chunk * states) - states, 0), states)
        found.append((sources[-1].at[pl.ds(ahead, states)], edge_all.at[at]))
        return [
            pltpu.make_async_copy(a, b, came.at[turn, i]) for i, (a, b) in enumerate(found)
        ]

    def leaving(turn):
        at = blocks - 1 - turn
        block = order_ref[at]
        place = order_ref[blocks + at]
        found = [
            (own_all.at[:, at], own_hbm.at[:, place]),
            (other_all.at[:, at], other_hbm.at[:, place]),
            (dscan_all.at[:, at], dscan_hbm.at[:, block]),
        ]
        return [
            pltpu.make_async_copy(a, b, left.at[turn, i]) for i, (a, b) in enumerate(found)
        ]

    @pl.loop(0, blocks)
    def _(turn):
        for copy in entering(turn):
            copy.start()

    @pl.loop(0, blocks)
    def _(turn):
        for copy in entering(turn):
            copy.wait()
        backward_steps(
            turn,
            parts,
            blocks,
            order_ref,
            small_all,
            dgated_all,
            pair_all,
            fresh_all,
            dpre_all,
            kept_all,
            edge_all,
            *params,
            own_all,
            other_all,
            dscan_all,
            *results,
            *scratch,
        )
        for copy in leaving(turn):
            copy.start()

    @pl.loop(0, blocks)
    def _(turn):
        for copy in leaving(turn):
            copy.wait()


def backward_steps(
    turn,
    parts,
    blocks,
    order_ref,
    small_all,
    dgated_all,
    pair_ref,
    fresh_ref,
    dpre_ref,
    kept_ref,
    edge_ref,
    weight_ref,
    skip_ref,
    coeff_ref,
    spread_ref,
    own_ref,
    other_ref,
    dscan_ref,
    delta_grad_ref,
    decay_ref,
    sums_ref,
    carry,
    step_all,
    drive_all,
    delta_all,
    dmix_all,
    lam_all,
    flow_all,
    cross_all,
    next_partial,
    next_dscan,
    partial_all,
):
    coeff = coeff_ref[...]
    states = coeff.shape[0]
    rank = weight_ref.shape[0]
    quarter = small_all.shape[2]
    chosen = own_block(states)
    ones = jnp.where(chosen, 1.0, 0.0).astype(low)
    across = (((1,), (1,)), ((), ()))
    down = (((0,), (0,)), ((), ()))
    part = order_ref[order_ref.shape[0] - 1]
    chunk = step_all.shape[0]
    block_turn = blocks - 1 - turn
    origin = pl.multiple_of(block_turn * (chunk * states), chunk * states)
    first = jnp.where(block_turn == 0, 0.0, edge_ref[block_turn].astype(wide))
    columns = [None] * parts
    entering = [None] * parts
    after_partial = [next_partial[...]]
    after_dscan = [next_dscan[...]]

    def before(j):
        rows = slice(j * quarter, (j + 1) * quarter)
        small = small_all[part ^ j, block_turn]
        delta = jax.nn.softplus(dpre_ref[pl.ds(block_turn * chunk + j * quarter, quarter), :])
        act = pair_ref[j, 0, block_turn].astype(wide)
        gate = pair_ref[j, 1, block_turn].astype(wide)
        step_all[rows, :] = jnp.where(fresh_ref[pl.ds(block_turn * chunk + j * quarter, quarter), :].astype(wide) > 0.0, delta, FAR)
        drive_all[rows, :] = delta * act
        delta_all[rows, :] = delta
        dmix_all[rows, :] = dgated_all[part ^ j, block_turn].astype(wide) * jax.nn.silu(gate)
        pair = small[:, rank:]
        columns[j] = transposed(pair)
        entering[j] = jnp.dot(
            pair, spread_ref[:, : GROUP * states], preferred_element_type=wide
        )

    def scan(j, pulled, summed):
        for group in range(quarter // GROUP - 1, -1, -1):
            base = j * quarter + group * GROUP
            lams = [None] * GROUP
            flows = [None] * GROUP
            rows = slice(base * states, (base + GROUP) * states)
            block = kept_ref[pl.ds(origin + base * states, GROUP * states), :].astype(wide)
            if base:
                edge = kept_ref[pl.ds(origin + (base - 1) * states, states), :].astype(wide)
            else:
                edge = first
            for i in range(GROUP - 1, -1, -1):
                t = base + i
                here = t - j * quarter
                read = columns[j][states:, here : here + 1]
                lam = read * dmix_all[t : t + 1, :] + pulled
                pulled = jnp.exp2(step_all[t : t + 1, :] * coeff) * lam
                flow = pulled * (block[(i - 1) * states : i * states] if i else edge)
                summed = summed + flow * delta_all[t : t + 1, :]
                lams[i] = lam
                flows[i] = flow * coeff
            lam_all[rows, :] = jnp.concatenate(lams, axis=0).astype(low)
            flow_all[rows, :] = jnp.concatenate(flows, axis=0).astype(low)
        return pulled, summed

    def finish_part(j):
        part_rows = slice(j * quarter, (j + 1) * quarter)
        lam_found = []
        flow_found = []
        for group in range(quarter // GROUP):
            base = j * quarter + group * GROUP
            here = slice(base, base + GROUP)
            rows = slice(base * states, (base + GROUP) * states)
            lam_block = lam_all[rows, :]
            entry = entering[j][group * GROUP : (group + 1) * GROUP]
            weights = jnp.where(chosen, entry, 0.0).astype(low)
            lam_found.append(jnp.dot(weights, lam_block, preferred_element_type=wide))
            flow_found.append(jnp.dot(ones, flow_all[rows, :], preferred_element_type=wide))
            cross = lax.dot_general(
                drive_all[here, :].astype(low), lam_block, across, preferred_element_type=wide
            )
            cross_all[here, : GROUP * states] = jnp.where(chosen, cross, 0.0).astype(low)
            cross = lax.dot_general(
                dmix_all[here, :].astype(low),
                kept_ref[pl.ds(origin + base * states, GROUP * states), :],
                across,
                preferred_element_type=wide,
            )
            cross_all[here, GROUP * states :] = jnp.where(chosen, cross, 0.0).astype(low)
        dpair = lax.dot_general(
            cross_all[part_rows, :], spread_ref[...], across, preferred_element_type=wide
        ).astype(low)
        found = jnp.concatenate(lam_found, axis=0)
        act = pair_ref[j, 0, block_turn].astype(wide)
        delta = delta_all[part_rows, :]
        dmix = dmix_all[part_rows, :]
        ddelta = jnp.concatenate(flow_found, axis=0) * (1.0 / math.log2(math.e)) + found * act
        ddpre = (ddelta * jax.nn.sigmoid(dpre_ref[pl.ds(block_turn * chunk + j * quarter, quarter), :])).astype(low)
        small = small_all[part ^ j, block_turn]
        delta_grad_ref[...] += lax.dot_general(
            small[:, :rank], ddpre, down, preferred_element_type=wide
        )
        dlow = lax.dot_general(
            ddpre, weight_ref[...], across, preferred_element_type=wide
        ).astype(low)
        dscan = (found * delta + dmix * skip_ref[...]).astype(low)
        sums_ref[0:1, :] += jnp.sum(ddpre.astype(wide), axis=0, keepdims=True)
        sums_ref[1:2, :] += jnp.sum(dmix * act, axis=0, keepdims=True)
        after_rows = after_partial[0]
        partial_all[j, :quarter, :rank] = dlow
        partial_all[j, :quarter, rank:] = dpair
        partial_all[j, quarter:, :] = after_rows
        dscan_ref[j, block_turn, :quarter, :] = dscan
        dscan_ref[j, block_turn, quarter:, :] = after_dscan[0]
        after_partial[0] = jnp.concatenate([dlow[:TAIL], dpair[:TAIL]], axis=1)
        after_dscan[0] = dscan[:TAIL]

    pulled = carry[...]
    summed = decay_ref[...]
    before(parts - 1)
    for j in range(parts - 1, -1, -1):
        if j:
            before(j - 1)
        pulled, summed = scan(j, pulled, summed)
        if j + 1 < parts:
            finish_part(j + 1)
    finish_part(0)
    carry[...] = pulled
    decay_ref[...] = summed
    next_partial[...] = after_partial[0]
    next_dscan[...] = after_dscan[0]
    for k in range(parts):
        (other_ref if k % 2 else own_ref)[k // 2, block_turn] = partial_all[part ^ k]


def forward_scan(order, small, pair, dgated, fresh, weight, bias, skip, coeff, spread):
    parts, _, blocks, quarter, width = pair.shape
    states = coeff.shape[0]
    columns = small[0].shape[-1]
    chunk = parts * quarter
    tokens = blocks * chunk
    streamed = (*small, *dgated, pair, fresh)
    params = (weight, bias, skip, coeff, spread)
    apart = pl.BlockSpec(memory_space=pl.ANY)
    kept = (tokens * states, width)
    gated = (parts, 2, blocks, quarter, width)
    return pl.pallas_call(
        functools.partial(forward_body, parts),
        grid_spec=pltpu.PrefetchScalarGridSpec(
            num_scalar_prefetch=1,
            grid=(1,),
            in_specs=[apart] * len(streamed)
            + [pl.BlockSpec(v.shape, lambda t, order: (0, 0)) for v in params],
            out_specs=[apart] * 3,
            scratch_shapes=[
                pltpu.VMEM((states, width), wide),
                pltpu.VMEM((chunk, width), wide),
                pltpu.VMEM((chunk, width), wide),
                pltpu.VMEM((parts, blocks, quarter, columns), low),
                pltpu.VMEM((parts, blocks, quarter, width), low),
                pltpu.VMEM(gated, low),
                pltpu.VMEM((tokens, width), low),
                pltpu.VMEM(kept, low),
                pltpu.VMEM((tokens, width), wide),
                pltpu.VMEM(gated, low),
                pltpu.SemaphoreType.DMA((blocks, len(streamed) + 1)),
                pltpu.SemaphoreType.DMA((blocks, 3)),
            ],
        ),
        out_shape=[
            pltpu.HBM(kept, low),
            pltpu.HBM((tokens, width), wide),
            pltpu.HBM(gated, low),
        ],
        compiler_params=pltpu.CompilerParams(vmem_limit_bytes=28 * 1024 * 1024),
        cost_estimate=spent(12),
        name="forward_scan",
    )(order, *map(in_hbm, streamed), *params)


def backward_scan(
    order, small, pair, dgated, fresh, dpre, kept, weight, skip, coeff, spread
):
    parts, _, blocks, quarter, width = pair.shape
    states = coeff.shape[0]
    rank = weight.shape[0]
    columns = small[0].shape[-1]
    chunk = parts * quarter
    tokens = blocks * chunk
    streamed = (*small, *dgated, pair, fresh, dpre, kept)
    params = (weight, skip, coeff, spread)
    apart = pl.BlockSpec(memory_space=pl.ANY)
    sums = (parts // 2, blocks, quarter + TAIL, columns)
    dscan = (parts, blocks, quarter + TAIL, width)
    results = ((rank, width), (states, width), (8, width))
    return pl.pallas_call(
        functools.partial(backward_body, parts),
        grid_spec=pltpu.PrefetchScalarGridSpec(
            num_scalar_prefetch=1,
            grid=(1,),
            in_specs=[apart] * len(streamed)
            + [pl.BlockSpec(v.shape, lambda t, order: (0, 0)) for v in params],
            out_specs=[apart] * 3 + [pl.BlockSpec(v, lambda t, order: (0, 0)) for v in results],
            scratch_shapes=[pltpu.VMEM((states, width), wide)]
            + [pltpu.VMEM((chunk, width), wide)] * 4
            + [pltpu.VMEM((chunk * states, width), low)] * 2
            + [
                pltpu.VMEM((chunk, 2 * GROUP * states), low),
                pltpu.VMEM((TAIL, columns), low),
                pltpu.VMEM((TAIL, width), low),
                pltpu.VMEM((parts, quarter + TAIL, columns), low),
                pltpu.VMEM((parts, blocks, quarter, columns), low),
                pltpu.VMEM((parts, blocks, quarter, width), low),
                pltpu.VMEM(pair.shape, low),
                pltpu.VMEM((tokens, width), low),
                pltpu.VMEM((tokens, width), wide),
                pltpu.VMEM((tokens * states, width), low),
                pltpu.VMEM((blocks, states, width), low),
                pltpu.VMEM(sums, low),
                pltpu.VMEM(sums, low),
                pltpu.VMEM(dscan, low),
                pltpu.SemaphoreType.DMA((blocks, len(streamed) + 1)),
                pltpu.SemaphoreType.DMA((blocks, 3)),
            ],
        ),
        out_shape=[pltpu.HBM(sums, low), pltpu.HBM(sums, low), pltpu.HBM(dscan, low)]
        + [jax.ShapeDtypeStruct(v, wide) for v in results],
        compiler_params=pltpu.CompilerParams(vmem_limit_bytes=28 * 1024 * 1024),
        cost_estimate=spent(19),
        name="backward_scan",
    )(order, *map(in_hbm, streamed), *params)


def interleave_body(parts, order_ref, *refs):
    values, out_ref = refs[: 2 * parts], refs[2 * parts]
    width, block = values[0].shape
    same = diagonal(block)
    for part in range(parts):

        @pl.when(order_ref[0] == part)
        def _(part=part):
            for half in range(2):
                for k in range(parts):
                    out_ref[:, half, (part ^ k) * width : ((part ^ k) + 1) * width] = (
                        lax.dot_general(
                            same,
                            values[half * parts + k][...],
                            (((1,), (1,)), ((), ())),
                            preferred_element_type=wide,
                        )
                    )


def interleave(order, inner, gate):
    parts = len(inner)
    width, depth = inner[0].shape
    block = 256
    return pl.pallas_call(
        functools.partial(interleave_body, parts),
        grid_spec=pltpu.PrefetchScalarGridSpec(
            num_scalar_prefetch=1,
            grid=(depth // block,),
            in_specs=[pl.BlockSpec((width, block), lambda t, order: (0, t))] * parts
            + [pl.BlockSpec((None, width, block), lambda t, order: (1, 0, t))] * parts,
            out_specs=pl.BlockSpec((block, 2, parts * width), lambda t, order: (t, 0, 0)),
        ),
        out_shape=jax.ShapeDtypeStruct((depth, 2, parts * width), wide),
        compiler_params=pltpu.CompilerParams(vmem_limit_bytes=16 * 1024 * 1024),
        cost_estimate=spent(5),
        name="interleave",
    )(order, *inner, *gate)


def placed_body(parts, order_ref, *refs):
    values, out_ref = refs[:parts], refs[-1]
    place = order_ref[pl.program_id(0)]
    for k in range(parts):

        @pl.when(place == k)
        def _(k=k):
            value = values[k][...].astype(wide)
            out_ref[...] = refs[parts][...] + value if len(refs) > parts + 1 else value


def placed(order, values, base=None):
    parts = len(values)
    rows, width = values[0].shape[-2:]
    flat = pl.BlockSpec((rows, width), lambda p, order: (p, 0))
    if values[0].ndim == 3:
        piece = pl.BlockSpec((None, rows, width), lambda p, order: (0, 0, 0))
    else:
        piece = pl.BlockSpec((rows, width), lambda p, order: (0, 0))
    return pl.pallas_call(
        functools.partial(placed_body, parts),
        grid_spec=pltpu.PrefetchScalarGridSpec(
            num_scalar_prefetch=1,
            grid=(parts,),
            in_specs=[piece] * parts
            + ([] if base is None else [flat]),
            out_specs=flat,
        ),
        out_shape=jax.ShapeDtypeStruct((parts * rows, width), wide),
        compiler_params=pltpu.CompilerParams(vmem_limit_bytes=24 * 1024 * 1024),
        cost_estimate=spent(2.5),
        name="placed",
    )(order, *values, *(() if base is None else (base,)))


def diagonal(size):
    places = [lax.broadcasted_iota(jnp.int32, (size, size), axis) for axis in (0, 1)]
    return jnp.where(places[0] == places[1], 1.0, 0.0).astype(low)


def project_body(
    place_ref,
    *refs,
):
    pieces, refs = refs[:8], refs[8:]
    (weight_ref, flags_ref, taps_ref, offset_ref, select_ref) = refs[:5]
    (normed_ref, inner_ref, channels_ref, kept_ref, sent_ref, turned_ref) = refs[5:11]
    (sides, edges, window, total, acts) = refs[11:]
    turn = pl.program_id(0)
    quarter = channels_ref.shape[3]
    width = channels_ref.shape[4]
    halves = weight_ref.shape[1] // width
    taps = taps_ref.shape[0]
    inner_turns = pl.num_programs(0) // 2
    count = len(pieces)

    @pl.when(turn == 0)
    def _():
        for k in range(count):
            piece = pieces[k][...]
            normed_ref[k * quarter : (k + 1) * quarter, :] = piece[:quarter]
            sides[k * 8 : (k + 1) * 8, :] = piece[quarter:].astype(wide)
        edges[...] = jnp.zeros_like(edges)
        total[...] = jnp.zeros_like(total)

    main = jnp.dot(normed_ref[...], weight_ref[...], preferred_element_type=wide)
    tile = weight_ref.shape[1]
    same = diagonal(tile)
    for k in range(weight_ref.shape[0] // tile):
        here = slice(k * tile, (k + 1) * tile)
        turned_ref[:, here] = lax.dot_general(
            same, weight_ref[here, :], (((1,), (1,)), ((), ())), preferred_element_type=wide
        ).astype(low)

    @pl.when(turn < inner_turns)
    def _():
        edges[: count * 8, :] = jnp.dot(
            sides[...].astype(low), weight_ref[...], preferred_element_type=wide
        )
        for k in range(count):
            before = pl.multiple_of(place_ref[k] * 8, 8)
            after = pl.multiple_of(place_ref[count + k] * 8, 8)
            flags = flags_ref[k]
            window[0:8, :] = edges[pl.ds(before, 8), :]
            window[8 : 8 + quarter, :] = main[k * quarter : (k + 1) * quarter]
            window[8 + quarter : 16 + quarter, :] = edges[pl.ds(after, 8), :]
            masked = window[...] * flags[:, 0:1]
            window[...] = masked
            inner_ref[k] = masked
            conv = offset_ref[...] + taps_ref[taps - 1 : taps, :] * masked[8 : 8 + quarter]
            for lag in range(1, taps):
                shifted = window[8 - lag : 8 - lag + quarter, :]
                valid = flags[8 : 8 + quarter, lag : lag + 1]
                conv = conv + taps_ref[taps - 1 - lag : taps - lag, :] * shifted * valid
            act = (jax.nn.silu(conv) * flags[8 : 8 + quarter, 0:1]).astype(low)
            acts[k * quarter : (k + 1) * quarter, :] = act
            for h in range(halves):
                channels_ref[h, 0, k] = act[:, h * width : (h + 1) * width]
        total[...] += jnp.dot(acts[...], select_ref[...], preferred_element_type=wide)

    @pl.when(turn >= inner_turns)
    def _():
        gate = main.astype(low)
        for k in range(count):
            for h in range(halves):
                channels_ref[h, 0, k] = gate[
                    k * quarter : (k + 1) * quarter, h * width : (h + 1) * width
                ]

    @pl.when(turn == pl.num_programs(0) - 1)
    def _():
        for k in range(count // 2):
            plane = place_ref[2 * count + k]
            kept_ref[plane] = total[k * quarter : (k + 1) * quarter, :]
            other = k + count // 2
            sent_ref[plane] = total[other * quarter : (other + 1) * quarter, :].astype(low)


def project(places, pieces, weight, flags, taps, offset, select, parts):
    count = len(pieces)
    rows, depth = pieces[0].shape
    quarter = rows - 8
    chans = weight.shape[1] // 2
    width = chans // parts
    tile = 2 * width
    turns = 2 * chans // tile
    half = turns // 2
    small = select.shape[1]

    def whole(shape):
        return pl.BlockSpec(shape, lambda t, place: (0,) * len(shape))

    def inner(t):
        return jnp.minimum(t, half - 1)

    return pl.pallas_call(
        project_body,
        grid_spec=pltpu.PrefetchScalarGridSpec(
            num_scalar_prefetch=1,
            grid=(turns,),
            in_specs=[whole(pieces[0].shape) for _ in pieces]
            + [
                pl.BlockSpec((depth, tile), lambda t, place: (0, t)),
                whole(flags.shape),
                pl.BlockSpec((taps.shape[0], tile), lambda t, place: (0, inner(t))),
                pl.BlockSpec((1, tile), lambda t, place: (0, inner(t))),
                pl.BlockSpec((tile, small), lambda t, place: (inner(t), 0)),
            ],
            out_specs=[
                whole((count * quarter, depth)),
                pl.BlockSpec((count, quarter + 16, tile), lambda t, place: (0, 0, inner(t))),
                pl.BlockSpec(
                    (2, 1, count, quarter, width),
                    lambda t, place: (t % half, t // half, 0, 0, 0),
                ),
                whole((count // 2, quarter, small)),
                whole((count // 2, quarter, small)),
                pl.BlockSpec((tile, depth), lambda t, place: (t, 0)),
            ],
            scratch_shapes=[
                pltpu.VMEM((count * 8, depth), wide),
                pltpu.VMEM((count * 8 + 8, tile), wide),
                pltpu.VMEM((quarter + 16, tile), wide),
                pltpu.VMEM((count * quarter, small), wide),
                pltpu.VMEM((count * quarter, tile), low),
            ],
        ),
        out_shape=[
            pltpu.HBM((count * quarter, depth), low),
            pltpu.HBM((count, quarter + 16, chans), wide),
            jax.ShapeDtypeStruct((parts, 2, count, quarter, width), low),
            jax.ShapeDtypeStruct((count // 2, quarter, small), wide),
            jax.ShapeDtypeStruct((count // 2, quarter, small), low),
            pltpu.HBM((2 * chans, depth), low),
        ],
        compiler_params=pltpu.CompilerParams(vmem_limit_bytes=28 * 1024 * 1024),
        cost_estimate=spent(8),
        name="project",
    )(places, *map(in_hbm, (*pieces, weight, flags, taps, offset, select)))


def pull_body(order_ref, rows_ref, weight_ref, kept_ref, *refs):
    out_refs, found_ref = refs[:-1], refs[-1]
    count = rows_ref.shape[0]
    quarter = rows_ref.shape[1]
    width = out_refs[0].shape[2]
    turn = pl.program_id(0)
    bit = order_ref[count] & 1

    @pl.when(turn == 0)
    def _():
        for k in range(count):
            kept_ref[k * quarter : (k + 1) * quarter, :] = rows_ref[order_ref[k]]

    found_ref[...] = lax.dot_general(
        kept_ref[...], weight_ref[...], (((1,), (1,)), ((), ())), preferred_element_type=wide
    ).astype(low)
    for p in range(len(out_refs)):

        @pl.when(turn == p // 2)
        def _(p=p):
            here = pl.ds(pl.multiple_of((bit ^ (p % 2)) * width, width), width)
            for k in range(count):
                out_refs[p][k] = found_ref[k * quarter : (k + 1) * quarter, here]


def pull(order, rows, weight, parts):
    count, quarter, depth = rows.shape
    width = weight.shape[0] // parts
    piece = pl.BlockSpec((count, quarter, width), lambda t, order: (0, 0, 0))
    return pl.pallas_call(
        pull_body,
        grid_spec=pltpu.PrefetchScalarGridSpec(
            num_scalar_prefetch=1,
            grid=(parts // 2,),
            in_specs=[
                pl.BlockSpec((count, quarter, depth), lambda t, order: (0, 0, 0)),
                pl.BlockSpec((2 * width, depth), lambda t, order: ((order[count] // 2) ^ t, 0)),
            ],
            out_specs=[pl.BlockSpec((count * quarter, depth), lambda t, order: (0, 0))]
            + [piece] * parts,
            scratch_shapes=[pltpu.VMEM((count * quarter, 2 * width), low)],
        ),
        out_shape=[pltpu.HBM((count * quarter, depth), low)]
        + [pltpu.HBM((count, quarter, width), low)] * parts,
        compiler_params=pltpu.CompilerParams(vmem_limit_bytes=20 * 1024 * 1024),
        cost_estimate=spent(6),
        name="pull",
    )(order, in_hbm(rows), in_hbm(weight))


def spread_parts(part, product, own_ref, other_ref):
    parts = 2 * own_ref.shape[0]
    width = product.shape[0] // parts
    for p in range(parts):
        here = pl.ds(pl.multiple_of((part ^ p) * width, width), width)
        yield (other_ref if p % 2 else own_ref), p // 2, here


def emit_body(order_ref, *refs):
    pieces_ref, refs = refs[0], refs[1:]
    parts = pieces_ref.shape[0]
    (weight_ref, rows_ref, normed_ref, turned_ref) = refs[:4]
    (kept_ref, sent_ref, own_ref, other_ref, dgate_ref, gain_ref) = refs[4:10]
    (gated, product, second) = refs[10:]
    count, quarter, width = pieces_ref.shape[2:]

    @pl.when(pl.program_id(0) == 0)
    def _():
        for p in range(parts):
            here = slice(p * width, (p + 1) * width)
            for k in range(count):
                rows = slice(k * quarter, (k + 1) * quarter)
                gated[rows, here] = pieces_ref[p, 0, k]
                dgate_ref[rows, here] = pieces_ref[p, 1, k]

    values = gated[...]
    branch = jnp.dot(values, weight_ref[...], preferred_element_type=wide).astype(low)
    kept_ref[...] = branch[: count // 2 * quarter].reshape(kept_ref.shape)
    sent_ref[...] = branch[count // 2 * quarter :].reshape(sent_ref.shape)
    down = (((0,), (0,)), ((), ()))
    product[...] = lax.dot_general(
        values, rows_ref[...], down, preferred_element_type=wide
    ).astype(low)
    found = lax.dot_general(
        dgate_ref[...], normed_ref[...], down, preferred_element_type=wide
    )
    gain_ref[...] = jnp.sum(found * turned_ref[...].astype(wide), axis=0, keepdims=True)
    second[...] = found.astype(low)
    for ref, p, here in spread_parts(order_ref[count], product, own_ref, other_ref):
        ref[p, 0] = product[here, :]
        ref[p, 1] = second[here, :]


def emit(order, pieces, weight, rows, normed, turned):
    parts, _, count, quarter, width = pieces.shape
    depth = weight.shape[1]
    tile = 512
    chans = parts * width
    tall = count * quarter
    blocks = pl.BlockSpec((count // 2, quarter, tile), lambda t, order: (0, 0, t))
    grads = pl.BlockSpec((parts // 2, 2, width, tile), lambda t, order: (0, 0, 0, t))
    columns = pl.BlockSpec((tall, tile), lambda t, order: (0, t))
    return pl.pallas_call(
        emit_body,
        grid_spec=pltpu.PrefetchScalarGridSpec(
            num_scalar_prefetch=1,
            grid=(depth // tile,),
            in_specs=[
                pl.BlockSpec(pieces.shape, lambda t, order: (0, 0, 0, 0, 0)),
                pl.BlockSpec((chans, tile), lambda t, order: (0, t)),
                columns,
                columns,
                pl.BlockSpec((chans, tile), lambda t, order: (1, t)),
            ],
            out_specs=[
                blocks,
                blocks,
                grads,
                grads,
                pl.BlockSpec((tall, chans), lambda t, order: (0, 0)),
                pl.BlockSpec((1, tile), lambda t, order: (0, t)),
            ],
            scratch_shapes=[
                pltpu.VMEM((tall, chans), low),
                pltpu.VMEM((chans, tile), low),
                pltpu.VMEM((chans, tile), low),
            ],
        ),
        out_shape=[
            pltpu.HBM((count // 2, quarter, depth), low),
            pltpu.HBM((count // 2, quarter, depth), low),
            pltpu.HBM((parts // 2, 2, width, depth), low),
            pltpu.HBM((parts // 2, 2, width, depth), low),
            pltpu.HBM((tall, chans), low),
            jax.ShapeDtypeStruct((1, depth), wide),
        ],
        compiler_params=pltpu.CompilerParams(vmem_limit_bytes=24 * 1024 * 1024),
        cost_estimate=spent(6),
        name="emit",
    )(order, *map(in_hbm, (pieces, weight, rows, normed, turned)))


def weigh_body(order_ref, rows_ref, normed_ref, turned_ref, own_ref, other_ref, gain_ref, product):
    found = lax.dot_general(
        rows_ref[...], normed_ref[...], (((0,), (0,)), ((), ())), preferred_element_type=wide
    )
    gain_ref[...] = jnp.sum(found * turned_ref[...].astype(wide), axis=0, keepdims=True)
    product[...] = found.astype(low)
    for ref, p, here in spread_parts(order_ref[8], product, own_ref, other_ref):
        ref[p] = product[here, :]


def weigh(order, rows, normed, turned, parts):
    tall, depth = normed.shape
    chans = rows.shape[1] // 2
    width = chans // parts
    tile = 512
    grads = pl.BlockSpec((parts // 2, width, tile), lambda t, order: (0, 0, t))
    return pl.pallas_call(
        weigh_body,
        grid_spec=pltpu.PrefetchScalarGridSpec(
            num_scalar_prefetch=1,
            grid=(depth // tile,),
            in_specs=[
                pl.BlockSpec((tall, chans), lambda t, order: (0, 0)),
                pl.BlockSpec((tall, tile), lambda t, order: (0, t)),
                pl.BlockSpec((chans, tile), lambda t, order: (0, t)),
            ],
            out_specs=[grads, grads, pl.BlockSpec((1, tile), lambda t, order: (0, t))],
            scratch_shapes=[pltpu.VMEM((chans, tile), low)],
        ),
        out_shape=[
            pltpu.HBM((parts // 2, width, depth), low),
            pltpu.HBM((parts // 2, width, depth), low),
            jax.ShapeDtypeStruct((1, depth), wide),
        ],
        compiler_params=pltpu.CompilerParams(vmem_limit_bytes=16 * 1024 * 1024),
        cost_estimate=spent(4),
        name="weigh",
    )(order, rows, in_hbm(normed), in_hbm(turned))


def turn_body(order_ref, *refs):
    count = 8
    smalls, refs = refs[:2], refs[2:]
    (dscan_ref, select_ref, inner_ref, flags_ref, taps_ref, offset_ref, dgate_ref) = refs[:7]
    (dboth_ref, grad_ref, rows_ref) = refs[7:10]
    (small_all, shifted, acts) = refs[10:]
    rank = grad_ref.shape[1]
    parts = pl.num_programs(0) // 2
    turn = pl.program_id(0)
    span = inner_ref.shape[1]
    quarter = span - 16
    reach = quarter + 8
    taps = taps_ref.shape[0]

    @pl.when(turn == 0)
    def _():
        for k in range(count):
            plane = order_ref[k] // 2
            small_all[k * span : (k + 1) * span, :] = smalls[k // (count // 2)][plane]

    @pl.when(turn < parts)
    def _():
        whole = lax.dot_general(
            small_all[...],
            select_ref[...],
            (((1,), (1,)), ((), ())),
            preferred_element_type=wide,
        )
        found = dscan_ref[0]
        sums = [0.0] * (taps + 1)
        for k in range(count):
            flags = flags_ref[k, 8 : 8 + reach, :]
            mask = flags[:, 0:1]
            conv = offset_ref[...]
            for lag in range(taps):
                term = taps_ref[taps - 1 - lag : taps - lag, :] * inner_ref[
                    k, 8 - lag : 8 - lag + reach, :
                ]
                conv = conv + (term * flags[:, lag : lag + 1] if lag else term)
            sig = jax.nn.sigmoid(conv)
            act = conv * sig * mask
            acts[k * quarter : (k + 1) * quarter, :] = act[:quarter].astype(low)
            dact = found[k, :reach].astype(wide) + whole[k * span : k * span + reach]
            dconv = dact * mask * (sig * (1.0 + conv * (1.0 - sig)))
            dinner = 0.0
            for lag in range(taps):
                masked = dconv * flags[:, lag : lag + 1] if lag else dconv
                sums[taps - 1 - lag] += jnp.sum(
                    masked[:quarter] * inner_ref[k, 8 - lag : 8 - lag + quarter, :],
                    axis=0,
                    keepdims=True,
                )
                if lag:
                    shifted[lag, :reach, :] = masked
                    masked = shifted[lag, lag : lag + quarter, :]
                else:
                    sums[taps] += jnp.sum(masked[:quarter], axis=0, keepdims=True)
                    masked = masked[:quarter]
                dinner = dinner + masked * taps_ref[taps - 1 - lag : taps - lag, :]
            dboth_ref[k * quarter : (k + 1) * quarter, :] = (dinner * mask[:quarter]).astype(low)
        for index, value in enumerate(sums):
            rows_ref[index : index + 1, :] = value
        mains = jnp.concatenate(
            [small_all[k * span : k * span + quarter, :] for k in range(count)], axis=0
        )
        grad_ref[...] = lax.dot_general(
            acts[...], mains[:, :rank], (((0,), (0,)), ((), ())), preferred_element_type=wide
        ).astype(low)
        rows_ref[8:, :] = lax.dot_general(
            mains[:, rank:], acts[...], (((0,), (0,)), ((), ())), preferred_element_type=wide
        )

    @pl.when(turn >= parts)
    def _():
        dboth_ref[...] = dgate_ref[...]


def turn_back(order, smalls, dscan, select, inner, flags, taps, offset, dgate, rank):
    parts, count, span, _ = dscan.shape
    small = smalls[0].shape[-1]
    chans = select.shape[0]
    width = chans // parts
    quarter = span - 16

    def whole(shape):
        return pl.BlockSpec(shape, lambda t, order: (0,) * len(shape))

    def early(t):
        return jnp.minimum(t, parts - 1)

    return pl.pallas_call(
        turn_body,
        grid_spec=pltpu.PrefetchScalarGridSpec(
            num_scalar_prefetch=1,
            grid=(2 * parts,),
            in_specs=[whole(v.shape) for v in smalls]
            + [
                pl.BlockSpec((1, count, span, width), lambda t, order: (early(t), 0, 0, 0)),
                pl.BlockSpec((width, small), lambda t, order: (early(t), 0)),
                pl.BlockSpec((count, span, width), lambda t, order: (0, 0, early(t))),
                whole(flags.shape),
                pl.BlockSpec((taps.shape[0], width), lambda t, order: (0, early(t))),
                pl.BlockSpec((1, width), lambda t, order: (0, early(t))),
                pl.BlockSpec(
                    (count * quarter, width), lambda t, order: (0, jnp.maximum(t - parts, 0))
                ),
            ],
            out_specs=[
                pl.BlockSpec((count * quarter, width), lambda t, order: (0, t)),
                pl.BlockSpec((width, rank), lambda t, order: (early(t), 0)),
                pl.BlockSpec((small - rank + 8, width), lambda t, order: (0, early(t))),
            ],
            scratch_shapes=[
                pltpu.VMEM((count * span, small), low),
                pltpu.VMEM((taps.shape[0], span, width), wide),
                pltpu.VMEM((count * quarter, width), low),
            ],
        ),
        out_shape=[
            jax.ShapeDtypeStruct((count * quarter, 2 * chans), low),
            pltpu.HBM((chans, rank), low),
            jax.ShapeDtypeStruct((small - rank + 8, chans), wide),
        ],
        compiler_params=pltpu.CompilerParams(vmem_limit_bytes=20 * 1024 * 1024),
        cost_estimate=spent(5.5),
        name="turn_back",
    )(
        order,
        *smalls,
        dscan,
        select,
        inner,
        flags,
        taps,
        offset,
        dgate,
    )


class Moves:
    def __init__(self):
        self.chan = lax.axis_index("chan").astype(jnp.uint32)
        self.part = lax.axis_index("state").astype(jnp.uint32)
        self.z = self.chan // 2
        self.y = self.chan % 2
        places = jnp.arange(8, dtype=jnp.uint32)
        planes = (self.z + 4 - places % 4) % 4
        self.blocks = planes * 2 + (self.y + places // 4) % 2
        hops = (self.z + 4 - places // 2) % 4
        self.order = (self.y + places) % 2 * 4 + hops

    def over_y(self, values):
        return lax.ppermute(values, "chan", [(i, i ^ 1) for i in range(8)])

    def over_z(self, values, hops):
        return lax.ppermute(values, "chan", [(i, (i + 2 * hops) % 8) for i in range(8)])

    def over_state(self, values, bits):
        return lax.ppermute(values, "state", [(i, i ^ bits) for i in range(4)])

    def swap_state(self, values):
        return lax.all_to_all(values, "state", 0, 0, tiled=True)

    def pair(self, bit, own, other):
        return jnp.stack([jnp.where(bit == 0, own, other), jnp.where(bit == 0, other, own)])

    def in_order(self, pieces):
        own, core, across, slant = pieces
        bit = self.part % 2
        near = self.pair(bit, own, core)
        far = self.pair(bit, across, slant)
        return self.pair(self.part // 2, near, far).reshape((4,) + own.shape)

    def pieces_state(self, values):
        core = self.over_state(values, 1)
        across = self.over_state(values, 2)
        return values, core, across, self.over_state(across, 1)


def tied(*values):
    return lax.optimization_barrier(values)


def after(values, *others):
    token = lax.optimization_barrier((lax.create_token(), others))[0]
    return lax.optimization_barrier((token, values))[1]


def near_shards(
    n_chan,
    n_state,
    hidden_in,
    norm_gain,
    in_weight,
    conv_kernel,
    conv_offset,
    select_rank,
    select_entry,
    select_read,
    delta_weight,
    step_bias,
    decay_log,
    skip_weight,
    out_weight,
    lengths,
    pad_mask,
    cotangent,
):
    rows_dev, width = hidden_in.shape
    tokens = pad_mask.shape[0]
    chans = in_weight.shape[2]
    taps = conv_kernel.shape[0]
    rank = select_rank.shape[1]
    per_state = select_entry.shape[1]
    states = per_state * n_state
    small = rank + 2 * states
    quarter = rows_dev // n_state
    own = chans // n_state
    rows_q = n_chan * quarter
    part = lax.axis_index("state").astype(jnp.uint32)
    contract_rows = (((0,), (0,)), ((), ()))
    contract_cols = (((1,), (1,)), ((), ()))
    moves = Moves()
    blocks = moves.blocks
    planes = jnp.arange(4, dtype=jnp.uint32)
    small_order = jnp.stack([(moves.y ^ u) * 4 + planes for u in (0, 1)], axis=1).reshape(-1)
    order = jnp.concatenate([moves.order, small_order, part[None]]).astype(jnp.int32)
    places = jnp.concatenate([blocks, part[None]]).astype(jnp.int32)
    blocks = blocks.astype(jnp.int32)

    def mine(values, axis=0):
        return lax.dynamic_slice_in_dim(values, part * own, own, axis)

    start = part * quarter
    hidden_q = lax.dynamic_slice_in_dim(hidden_in, start, quarter, 0)
    ahead = (start + (rows_dev - HALO)) % rows_dev
    behind = (start + quarter) % rows_dev
    local = jnp.concatenate(
        [
            hidden_q,
            lax.dynamic_slice_in_dim(hidden_in, behind, HALO, 0),
            lax.dynamic_slice_in_dim(hidden_in, ahead, HALO, 0),
        ],
        axis=0,
    )
    inv_all = lax.rsqrt(jnp.mean(local * local, axis=1, keepdims=True) + epsilon)
    scaled_all = local * inv_all
    normed_all = (scaled_all * norm_gain[None, :]).astype(low)
    inv_rms = inv_all[:quarter]
    scaled = scaled_all[:quarter]
    cot_q = lax.dynamic_slice_in_dim(cotangent, start, quarter, 0).astype(low)
    ranks = (part ^ jnp.arange(n_state, dtype=jnp.uint32)).astype(jnp.int32)

    def trades(values):
        return [values[0]] + [moves.over_state(values[k], k) for k in (1, 2, 3)]

    def core_halves(values):
        cut = values.reshape((2, 2) + values.shape[1:])
        core = part % 2
        return (
            lax.dynamic_index_in_dim(cut, 1 - core, 1, keepdims=False),
            lax.dynamic_index_in_dim(cut, core, 1, keepdims=False),
        )

    def chip_halves(values):
        side = part // 2
        return (
            lax.dynamic_index_in_dim(values, 1 - side, 0, keepdims=False),
            lax.dynamic_index_in_dim(values, side, 0, keepdims=False),
        )

    def total_of(own_part, others):
        total = own_part.astype(wide)
        for piece in others:
            total = total + piece.astype(wide)
        return total.astype(low)

    def added(kept, came):
        return (kept.astype(wide) + came.astype(wide)).astype(low)

    columns = jnp.concatenate([select_entry, select_read], axis=1)
    decay_cut = jnp.swapaxes(decay_log.reshape(per_state, n_state, own), 0, 1)
    across = moves.over_y(normed_all)
    along = [moves.over_z(normed_all, hops) for hops in (1, 2, 3)]
    columns_core = moves.over_state(columns, 1)
    columns_chip = moves.over_state(columns, 2)
    decay_own = moves.swap_state(decay_cut)
    in_flat = in_weight.reshape(width, 2 * chans)
    tie = tied(across, *along, columns_core, columns_chip, decay_own, in_flat, cot_q)
    across, along, columns_core, columns_chip = tie[0], list(tie[1:4]), *tie[4:6]
    decay_own, in_flat, cot_q = tie[6:]
    grads = lax.all_gather(cot_q, "chan", axis=0)
    over = [moves.over_y(piece) for piece in along]
    columns_slant = moves.over_state(columns_chip, 1)
    over[0], over[1], over[2], columns_slant = tied(*over, columns_slant)
    pieces = [normed_all] + along + [across] + over

    place = positions(lengths, tokens)
    flags = [pad_mask.astype(wide)]
    flags += [(place >= lag).astype(wide) for lag in range(1, taps)]
    flags = jnp.stack(flags)
    padded = jnp.pad(flags, ((0, 0), (8, 8 + rows_dev)))
    span = quarter + 16
    flags_win = lax.dynamic_slice_in_dim(padded, start, n_chan * rows_dev, 1)
    flags_win = flags_win.reshape(taps, n_chan, rows_dev)[:, :, :span]
    chooser = (blocks[:, None] == jnp.arange(n_chan)[None, :]).astype(wide)
    flags_rows = jnp.einsum("kb,fbr->krf", chooser, flags_win)
    itself = jnp.arange(n_chan, dtype=jnp.int32)
    nearby = blocks[:, None] - blocks[None, :]
    one_before = jnp.where(blocks > 0, jnp.argmax(nearby == 1, axis=1), n_chan)
    one_after = jnp.where(blocks < n_chan - 1, jnp.argmax(nearby == -1, axis=1), n_chan)
    one_before = jnp.where(part == 0, one_before, itself)
    one_after = jnp.where(part == n_state - 1, one_after, itself)
    neighbours = jnp.concatenate([one_before, one_after, blocks[:4] // 2]).astype(jnp.int32)

    columns = moves.in_order((columns, columns_core, columns_chip, columns_slant))
    columns = columns.reshape(n_state, chans, 2, per_state)
    columns = jnp.transpose(columns, (1, 2, 0, 3)).reshape(chans, 2 * states)
    select = jnp.concatenate([select_rank, columns], axis=1)
    coeff = -jnp.exp(decay_own.reshape(states, own))

    normed_q, inner_all, sent, kept, other, turned = project(
        neighbours, pieces, in_flat, flags_rows, conv_kernel, conv_offset[None, :], select, n_state
    )
    reach = quarter + HALO
    channels = moves.swap_state(sent)
    came = moves.over_y(other)
    joined = added(kept, came)
    along = [moves.over_z(joined, hops) for hops in (1, 2, 3)]
    grad_q, *dgated = pull(places, grads, out_weight, n_state)
    along[0], along[1], along[2], *dgated = tied(*along, *dgated)
    summed = total_of(joined, along)
    came = moves.over_y(summed)
    dgated = trades(dgated)
    picked = moves.pieces_state(jnp.concatenate([summed, came], axis=0))
    tie = tied(*picked, *dgated, channels)
    picked, dgated, channels = tie[:4], tie[4:8], tie[8]

    weight_own = mine(delta_weight, 1)
    bias_own = mine(step_bias)[None, :]
    skip_own = mine(skip_weight)[None, :]
    fresh = jnp.broadcast_to((place > 0).astype(low)[:, None], (tokens, own))
    spread = spreading(states)
    coeff_two = coeff * math.log2(math.e)
    kept, dpre, gated = forward_scan(
        order,
        picked,
        channels,
        dgated,
        fresh,
        weight_own,
        bias_own,
        skip_own,
        coeff_two,
        spread,
    )
    gated = moves.swap_state(gated)
    own_sums, other_sums, dscan, delta_grad_own, decay_total, sums = backward_scan(
        order,
        picked,
        channels,
        dgated,
        fresh,
        dpre,
        kept,
        weight_own,
        skip_own,
        coeff_two,
        spread,
    )
    decay_grad_own = coeff * decay_total
    packed = jnp.concatenate([delta_grad_own, decay_grad_own, sums], axis=0).astype(low)

    own_sums, other_sums, packed, gated, dscan = tied(
        own_sums, other_sums, packed, gated, dscan
    )
    came = moves.over_state(other_sums, 1)
    dscan = moves.swap_state(dscan)
    came, own_sums, packed, gated = tied(came, own_sums, packed, gated)

    chip = added(own_sums, came)
    came = moves.over_state(chip[1], 2)
    branch_kept, sent, parts_kept, parts_sent, dgate_q, gain = emit(
        places, gated, out_weight, grad_q, normed_q, turned
    )
    came, sent, parts_sent = tied(came, sent, parts_sent)

    joined = added(chip[0], came)
    came = moves.over_y(joined[4:])
    parts_came = moves.over_state(parts_sent, 1)
    came, parts_came, sent = tied(came, parts_came, sent)

    joined = added(joined[:4], came)
    along = [moves.over_z(joined, hops) for hops in (1, 2, 3)]
    branch_came = moves.over_y(sent)
    parts_sum = added(parts_kept, parts_came)
    parts_came = moves.over_state(parts_sum[1], 2)
    along[0], along[1], along[2], branch_came, dscan = tied(*along, branch_came, dscan)

    partial = total_of(joined, along)
    came = moves.over_y(partial)
    branch = added(branch_kept, branch_came)
    branches = [moves.over_z(branch[4 - hops], hops) for hops in (1, 2, 3)]
    came, partial, parts_came = tied(came, partial, parts_came)
    parts_own = added(parts_sum[0], parts_came)
    came, partial, parts_own = tied(came, partial, parts_own)
    parts_chip = moves.over_state(parts_own, 2)

    dboth, rank_part, rows_part = turn_back(
        places,
        (partial, came),
        dscan,
        select,
        inner_all,
        flags_rows,
        conv_kernel,
        conv_offset[None, :],
        dgate_q,
        rank,
    )

    def backed(rows, weight):
        return lax.dot_general(rows, weight, contract_cols, preferred_element_type=wide)

    edge = width * 11 // 16
    left, right = slice(0, edge), slice(edge, width)
    other, same = slice(rows_q // 2, rows_q), slice(0, rows_q // 2)
    left_sent = backed(dboth[other], in_flat[left]).astype(low).reshape(4, quarter, edge)
    right_all = backed(dboth, in_flat[right]).reshape(2, 4, quarter, width - edge)
    right_sent = [right_all[:, 4 - hops].astype(low) for hops in (1, 2, 3)]
    inner_kept, inner_sent, inner_gain = weigh(places, dboth, normed_q, turned, n_state)
    inner_came = moves.over_state(inner_sent, 1)
    gain = (gain + inner_gain).reshape(-1, chans)
    gain = jnp.concatenate([rows_part, gain], axis=0)
    small = jnp.concatenate([packed, rank_part], axis=0)
    tie = tied(left_sent, dboth, small, inner_came, gain, *branches, *right_sent)
    left_sent, dboth, small, inner_came, gain = tie[:5]
    branches, right_sent = tie[5:8], tie[8:]

    left_came = moves.over_y(left_sent)
    right_along = [moves.over_z(right_sent[hops - 1], hops) for hops in (1, 2, 3)]
    gain_came = moves.over_state(gain, 1)
    left_kept = backed(after(dboth, right_along[0])[same], in_flat[left])
    left_kept = left_kept.reshape(4, quarter, edge)
    branch = total_of(branch[0], branches)
    tie = tied(left_came, left_kept, gain, gain_came, branch, parts_chip, *right_along)
    left_came, left_kept, gain, gain_came, branch, parts_chip = tie[:6]
    right_along = tie[6:]

    joined = left_kept + left_came.astype(wide)
    left_sum = joined[0]
    left_along = [moves.over_z(joined[4 - hops].astype(low), hops) for hops in (1, 2, 3)]
    right_sum = right_all[:, 0]
    for piece in right_along:
        right_sum = right_sum + piece.astype(wide)
    right_came = moves.over_y(right_sum[1].astype(low))
    inner_sum = added(inner_kept, inner_came)
    inner_came = moves.over_state(inner_sum[1], 2)
    gain = gain + gain_came
    gain_came = moves.over_state(gain, 2)
    small_core = moves.over_state(small, 1)
    tie = tied(right_came, gain, gain_came, inner_came, small_core, *left_along)
    right_came, gain, gain_came, inner_came, small_core = tie[:5]
    left_along = tie[5:]

    for piece in left_along:
        left_sum = left_sum + piece.astype(wide)
    right_sum = right_sum[0] + right_came.astype(wide)
    dnormed = jnp.concatenate([left_sum, right_sum], axis=1)
    dscaled = dnormed * norm_gain[None, :]
    change = inv_rms * (dscaled - scaled * jnp.mean(dscaled * scaled, axis=1, keepdims=True))
    change = change.astype(low)
    change_chip = moves.over_state(change, 2)
    change_core = moves.over_state(change, 1)
    inner_own = added(inner_sum[0], inner_came)
    inner_chip = moves.over_state(inner_own, 2)
    gain = gain + gain_came
    gain_came = moves.over_y(gain[8 + 2 * states :].reshape(width))
    inner_core = moves.over_state(inner_own, 1)
    parts_core = moves.over_state(parts_own, 1)
    parts_slant = moves.over_state(parts_chip, 1)
    out_grad = placed(ranks, (parts_own, parts_core, parts_chip, parts_slant))
    place_at = 8 + part * per_state
    smalls = (
        gain[:taps],
        gain[taps],
        lax.dynamic_slice_in_dim(gain, place_at, per_state, 0).T,
        lax.dynamic_slice_in_dim(gain, place_at + states, per_state, 0).T,
    )
    tie = tied(
        change_chip,
        change_core,
        gain,
        gain_came,
        inner_chip,
        inner_core,
        parts_core,
        parts_slant,
        out_grad,
        *smalls,
    )
    change_chip, change_core, gain, gain_came, inner_chip, inner_core = tie[:6]
    parts_core, parts_slant, out_grad = tie[6:9]
    smalls = tie[9:]

    inner_slant = moves.over_state(inner_chip, 1)
    branch_chip = moves.over_state(branch, 2)
    branch_core = moves.over_state(branch, 1)
    change_slant = moves.over_state(change_chip, 1)
    fixed = packed.shape[0]
    rank_sum = added(small[fixed:], small_core[fixed:])
    small_sum = jnp.concatenate([small[:fixed], rank_sum], axis=0)
    small_chip = moves.over_state(small_sum, 2)
    gain = gain[8 + 2 * states :].reshape(width) + gain_came
    in_grad = interleave(
        ranks,
        (inner_own, inner_core, inner_chip, inner_slant),
        (parts_own, parts_core, parts_chip, parts_slant),
    )
    tie = tied(branch_chip, branch_core, change_slant, small_chip, gain, in_grad)
    branch_chip, branch_core, change_slant, small_chip, gain, in_grad = tie

    branch_slant = moves.over_state(branch_chip, 1)
    packed_slant = moves.over_state(small_chip[:fixed], 1)
    gains = [gain] + [moves.over_z(gain, hops) for hops in (1, 2, 3)]
    rank_grad = rank_sum.astype(wide) + small_chip[fixed:].astype(wide)
    packed = moves.in_order((packed, small_core[:fixed], small_chip[:fixed], packed_slant))
    packed = jnp.swapaxes(packed, 0, 1).reshape(-1, chans).astype(wide)
    smalls = (
        *smalls[:2],
        rank_grad,
        *smalls[2:],
        packed[:rank],
        packed[rank + states],
        lax.dynamic_slice_in_dim(packed, rank + part * per_state, per_state, 0),
        packed[rank + states + 1],
    )
    input_grad = placed(ranks, (change, change_core, change_chip, change_slant), cotangent)
    result = placed(ranks, (branch, branch_core, branch_chip, branch_slant), hidden_in)
    gains = jnp.stack(gains)
    gain_grad = 0.0
    for plane_at in range(4):
        gain_grad = gain_grad + lax.dynamic_index_in_dim(
            gains, (moves.z + 4 - plane_at) % 4, 0, keepdims=False
        )
    gain_grad = gain_grad / norm_gain
    return (result, input_grad, gain_grad, in_grad, *smalls, out_grad)


def solution(mesh):
    sizes = dict(mesh.shape)
    near = (sizes["chan"], sizes["state"]) == (8, 4)
    program = functools.partial(near_shards, 8, 4) if near else shards
    return jax.shard_map(
        program,
        mesh=mesh,
        in_specs=(
            P("chan", None),
            P(),
            P(None, None, "chan"),
            P(None, "chan"),
            P("chan"),
            P("chan", None),
            P("chan", "state"),
            P("chan", "state"),
            P(None, "chan"),
            P("chan"),
            P("state", "chan"),
            P("chan"),
            P("chan", None),
            P(),
            P(),
            P("chan", None),
        ),
        out_specs=(
            P("chan", None),
            P("chan", None),
            P(),
            P(None, None, "chan"),
            P(None, "chan"),
            P("chan"),
            P("chan", None),
            P("chan", "state"),
            P("chan", "state"),
            P(None, "chan"),
            P("chan"),
            P("state", "chan"),
            P("chan"),
            P("chan", None),
        ),
        check_vma=False,
    )
```

```python
import functools
import math

import jax
import jax.numpy as jnp
from jax import lax
from jax.experimental import pallas as pl
from jax.experimental.pallas import tpu as pltpu
from jax.sharding import PartitionSpec as P

epsilon = 1e-05
GROUP = 16
HALO = 4
TAIL = 16
FAR = 1e30
wide = jnp.float32
low = jnp.bfloat16


def spent(microseconds):
    moved = int(microseconds * 3.6e6)
    return pl.CostEstimate(flops=0, bytes_accessed=moved, transcendentals=0)


def in_hbm(values):
    return pltpu.with_memory_space_constraint(values, pltpu.HBM)


def positions(lengths, tokens_all):
    ends = jnp.cumsum(lengths)
    begins = ends - lengths
    places = jnp.arange(tokens_all, dtype=jnp.int32)
    opening = jnp.max(jnp.where(begins[:, None] <= places[None, :], begins[:, None], 0), axis=0)
    return places - opening


def delayed(values, amount):
    if amount == 0:
        return values
    padding = jnp.zeros((amount,) + values.shape[1:], values.dtype)
    return jnp.concatenate([padding, values[: values.shape[0] - amount]], axis=0)


def advanced(values, amount):
    if amount == 0:
        return values
    padding = jnp.zeros((amount,) + values.shape[1:], values.dtype)
    return jnp.concatenate([values[amount:], padding], axis=0)


def silu_slope(values):
    logistic = jax.nn.sigmoid(values)
    return logistic * (1.0 + values * (1.0 - logistic))


def linear_scan(decays, drive):
    total_rows = decays.shape[0]
    blocks = total_rows // 16
    factors = jnp.swapaxes(decays.reshape((blocks, 16) + decays.shape[1:]), 0, 1)
    sources = jnp.swapaxes(drive.reshape((blocks, 16) + drive.shape[1:]), 0, 1)

    def advance(totals, item):
        state_now, product_now = totals
        factor_now, source_now = item
        state_now = factor_now * state_now + source_now
        product_now = factor_now * product_now
        return ((state_now, product_now), (state_now, product_now))

    initial = (jnp.zeros(factors.shape[1:], jnp.float32), jnp.ones(factors.shape[1:], jnp.float32))
    final_pair, (local_states, products) = lax.scan(advance, initial, (factors, sources))

    def combine(early, later):
        return (early[0] * later[0], later[0] * early[1] + later[1])

    joined_factor, joined_state = lax.associative_scan(
        combine, (products[-1], local_states[-1]), axis=0
    )
    entering = jnp.concatenate([jnp.zeros_like(joined_state[:1]), joined_state[:-1]], axis=0)
    states = local_states + products * entering[None]
    return jnp.swapaxes(states, 0, 1).reshape(decays.shape)


def shards(
    hidden_in,
    norm_gain,
    in_weight,
    conv_kernel,
    conv_offset,
    select_rank,
    select_entry,
    select_read,
    delta_weight,
    step_bias,
    decay_log,
    skip_weight,
    out_weight,
    lengths,
    pad_mask,
    cotangent,
):
    rows_dev, width = hidden_in.shape
    tokens_all = pad_mask.shape[0]
    chans = in_weight.shape[2]
    kernel_len = conv_kernel.shape[0]
    per_state = select_entry.shape[1]
    contract_rows = (((0,), (0,)), ((), ()))
    contract_cols = (((1,), (1,)), ((), ()))
    place = positions(lengths, tokens_all)
    fresh = (place > 0).astype(jnp.float32)
    maskf = pad_mask.astype(jnp.float32)[:, None]
    square = jnp.mean(hidden_in * hidden_in, axis=1, keepdims=True)
    inv_rms = lax.rsqrt(square + epsilon)
    scaled = hidden_in * inv_rms
    normed = (scaled * norm_gain[None, :]).astype(jnp.bfloat16)
    in_flat = in_weight.reshape(width, 2 * chans)
    both = jnp.dot(
        lax.all_gather(normed, "chan", axis=0, tiled=True),
        in_flat,
        preferred_element_type=jnp.float32,
    )
    inner = both[:, :chans] * maskf
    gate_in = both[:, chans:]
    valids = []
    shifted = []
    conv = jnp.zeros((tokens_all, chans), jnp.float32) + conv_offset[None, :]
    for index in range(kernel_len):
        lag = kernel_len - 1 - index
        valids.append((place >= lag).astype(jnp.float32)[:, None])
        shifted.append(delayed(inner, lag))
        conv = conv + conv_kernel[index][None, :] * shifted[index] * valids[index]
    act = (jax.nn.silu(conv) * maskf).astype(jnp.bfloat16)
    act_wide = act.astype(jnp.float32)
    pair_map = jnp.concatenate([select_entry, select_read], axis=1)
    rank_part = jnp.dot(act, select_rank, preferred_element_type=jnp.float32)
    pair_part = jnp.dot(act, pair_map, preferred_element_type=jnp.float32)
    raw_sum, pair_sum = lax.psum((rank_part, pair_part), "chan")
    entry = pair_sum[:, :per_state]
    readout = pair_sum[:, per_state:]
    lowrank = raw_sum.astype(jnp.bfloat16)
    dpre = jnp.dot(lowrank, delta_weight, preferred_element_type=jnp.float32) + step_bias[None, :]
    delta = jax.nn.softplus(dpre)
    coeff = -jnp.exp(decay_log)
    decays = jnp.exp(delta[:, None, :] * coeff[None]) * fresh[:, None, None]
    drive = (delta * act_wide)[:, None, :] * entry[:, :, None]
    states = linear_scan(decays, drive)
    scan_part = jnp.sum(readout[:, :, None] * states, axis=1)
    scanned = lax.psum(scan_part, "state")
    mixed = scanned + skip_weight[None, :] * act_wide
    gate_act = jax.nn.silu(gate_in)
    gated = (mixed * gate_act).astype(jnp.bfloat16)
    gated_rows = gated
    branch = lax.psum_scatter(
        jnp.dot(gated_rows, out_weight, preferred_element_type=jnp.float32),
        "chan",
        scatter_dimension=0,
        tiled=True,
    )
    result = hidden_in + branch
    grad_low = cotangent.astype(jnp.bfloat16)
    pieces = lax.all_gather(grad_low, "chan", axis=0, tiled=True)
    gated_rows = gated
    product = lax.dot_general(pieces, out_weight, contract_cols, preferred_element_type=jnp.float32)
    outw_acc = lax.dot_general(
        gated_rows, pieces, contract_rows, preferred_element_type=jnp.float32
    )
    dmix = product * gate_act
    dgate = product * mixed * silu_slope(gate_in)
    skip_grad = jnp.sum(dmix * act_wide, axis=0)
    emitted = readout[:, :, None] * dmix[:, None, :]
    following = jnp.concatenate([decays[1:], jnp.zeros_like(decays[:1])], axis=0)
    adjoint = jnp.flip(linear_scan(jnp.flip(following, 0), jnp.flip(emitted, 0)), 0)
    earlier = jnp.concatenate([jnp.zeros_like(states[:1]), states[:-1]], axis=0)
    flow = adjoint * earlier * decays
    dread_part = jnp.sum(states * dmix[:, None, :], axis=2)
    dentry_part = jnp.sum(adjoint * (delta * act_wide)[:, None, :], axis=2)
    ddelta_part = jnp.sum(
        flow * coeff[None] + adjoint * entry[:, :, None] * act_wide[:, None, :], axis=1
    )
    decay_grad = coeff * jnp.sum(flow * delta[:, None, :], axis=0)
    dact_scan = jnp.sum(adjoint * entry[:, :, None], axis=1) * delta
    dentry_sum, dread_sum = lax.psum((dentry_part, dread_part), "chan")
    dpair = jnp.concatenate(
        [dentry_sum.astype(jnp.bfloat16), dread_sum.astype(jnp.bfloat16)], axis=1
    )
    pair_grad = lax.dot_general(act, dpair, contract_rows, preferred_element_type=jnp.float32)
    entry_grad = pair_grad[:, :per_state]
    read_grad = pair_grad[:, per_state:]
    dact_pair = lax.dot_general(dpair, pair_map, contract_cols, preferred_element_type=jnp.float32)
    dact_state, ddelta = lax.psum((dact_scan + dact_pair, ddelta_part), "state")
    ddpre = (ddelta * jax.nn.sigmoid(dpre)).astype(jnp.bfloat16)
    bias_grad = jnp.sum(ddpre.astype(jnp.float32), axis=0)
    delta_grad = lax.dot_general(lowrank, ddpre, contract_rows, preferred_element_type=jnp.float32)
    dlow_part = lax.dot_general(
        ddpre, delta_weight, contract_cols, preferred_element_type=jnp.float32
    )
    dlow = lax.psum(dlow_part, "chan").astype(jnp.bfloat16)
    rank_grad = lax.dot_general(act, dlow, contract_rows, preferred_element_type=jnp.float32)
    dact = (
        dact_state
        + dmix * skip_weight[None, :]
        + lax.dot_general(dlow, select_rank, contract_cols, preferred_element_type=jnp.float32)
    )
    dconv = dact * maskf * silu_slope(conv)
    offset_grad = jnp.sum(dconv, axis=0)
    kernel_rows = []
    dinner = jnp.zeros((tokens_all, chans), jnp.float32)
    for index in range(kernel_len):
        lag = kernel_len - 1 - index
        masked = dconv * valids[index]
        kernel_rows.append(jnp.sum(masked * shifted[index], axis=0))
        dinner = dinner + advanced(masked * conv_kernel[index][None, :], lag)
    kernel_grad = jnp.stack(kernel_rows, axis=0)
    dboth = jnp.concatenate([dinner * maskf, dgate], axis=1).astype(jnp.bfloat16)
    chosen = dboth
    in_flat_grad = lax.dot_general(
        lax.all_gather(normed, "chan", axis=0, tiled=True),
        chosen,
        contract_rows,
        preferred_element_type=jnp.float32,
    )
    in_grad = in_flat_grad.reshape(width, 2, chans)
    chosen = dboth
    dnormed = lax.psum_scatter(
        lax.dot_general(chosen, in_flat, contract_cols, preferred_element_type=jnp.float32),
        "chan",
        scatter_dimension=0,
        tiled=True,
    )
    gain_part = jnp.sum(dnormed * scaled, axis=0)
    gain_grad = lax.psum(gain_part, "chan")
    dscaled = dnormed * norm_gain[None, :]
    input_grad = cotangent + inv_rms * (
        dscaled - scaled * jnp.mean(dscaled * scaled, axis=1, keepdims=True)
    )
    return (
        result,
        input_grad,
        gain_grad,
        in_grad,
        kernel_grad,
        offset_grad,
        rank_grad,
        entry_grad,
        read_grad,
        delta_grad,
        bias_grad,
        decay_grad,
        skip_grad,
        outw_acc,
    )


def own_block(states):
    row = lax.broadcasted_iota(jnp.int32, (GROUP, GROUP * states), 0)
    col = lax.broadcasted_iota(jnp.int32, (GROUP, GROUP * states), 1)
    return jnp.logical_and(col >= row * states, col < (row + 1) * states)


def spreading(states):
    eye = jnp.eye(states, dtype=low)
    tiled = jnp.tile(eye, (1, GROUP))
    nothing = jnp.zeros_like(tiled)
    return jnp.concatenate(
        [
            jnp.concatenate([tiled, nothing], axis=1),
            jnp.concatenate([nothing, tiled], axis=1),
        ],
        axis=0,
    )


def transposed(values):
    count = values.shape[1]
    row = lax.broadcasted_iota(jnp.int32, (count, count), 0)
    col = lax.broadcasted_iota(jnp.int32, (count, count), 1)
    eye = jnp.where(row == col, 1.0, 0.0).astype(low)
    return lax.dot_general(eye, values, (((1,), (1,)), ((), ())), preferred_element_type=wide)


def forward_body(parts, order_ref, *refs):
    sources, refs = refs[: 2 * parts + 2], refs[2 * parts + 2 :]
    params, (kept_hbm, dpre_hbm, gated_hbm), refs = refs[:5], refs[5:8], refs[8:]
    carry, step_all, drive_all, small_all, dgated_all, pair_all, fresh_all = refs[:7]
    kept_all, dpre_all, gated_all, came, left = refs[7:]
    blocks = small_all.shape[1]
    chunk = step_all.shape[0]
    states = carry.shape[0]

    def entering(turn):
        block = order_ref[turn]
        rows = pl.ds(pl.multiple_of(turn * chunk, chunk), chunk)
        found = []
        for k in range(parts):
            found.append((sources[k].at[order_ref[blocks + turn]], small_all.at[k, turn]))
            found.append((sources[parts + k].at[block], dgated_all.at[k, turn]))
        found.append((sources[2 * parts].at[:, :, block], pair_all.at[:, :, turn]))
        found.append((sources[2 * parts + 1].at[rows], fresh_all.at[rows]))
        return [
            pltpu.make_async_copy(a, b, came.at[turn, i]) for i, (a, b) in enumerate(found)
        ]

    def leaving(turn):
        rows = pl.ds(pl.multiple_of(turn * chunk, chunk), chunk)
        tall = pl.ds(pl.multiple_of(turn * (chunk * states), chunk * states), chunk * states)
        found = [
            (kept_all.at[tall], kept_hbm.at[tall]),
            (dpre_all.at[rows], dpre_hbm.at[rows]),
            (gated_all.at[:, :, turn], gated_hbm.at[:, :, order_ref[turn]]),
        ]
        return [
            pltpu.make_async_copy(a, b, left.at[turn, i]) for i, (a, b) in enumerate(found)
        ]

    @pl.loop(0, blocks)
    def _(turn):
        for copy in entering(turn):
            copy.start()

    carry[...] = jnp.zeros_like(carry)

    @pl.loop(0, blocks)
    def _(turn):
        for copy in entering(turn):
            copy.wait()
        forward_steps(
            turn,
            parts,
            order_ref,
            small_all,
            dgated_all,
            pair_all,
            fresh_all,
            *params,
            kept_all,
            dpre_all,
            gated_all,
            carry,
            step_all,
            drive_all,
        )
        for copy in leaving(turn):
            copy.start()

    @pl.loop(0, blocks)
    def _(turn):
        for copy in leaving(turn):
            copy.wait()


def forward_steps(
    turn,
    parts,
    order_ref,
    small_all,
    dgated_all,
    pair_ref,
    fresh_ref,
    weight_ref,
    bias_ref,
    skip_ref,
    coeff_ref,
    spread_ref,
    kept_ref,
    dpre_ref,
    gated_ref,
    carry,
    step_all,
    drive_all,
):
    coeff = coeff_ref[...]
    states = coeff.shape[0]
    chunk = step_all.shape[0]
    origin = pl.multiple_of(turn * (chunk * states), chunk * states)
    rank = weight_ref.shape[0]
    quarter = small_all.shape[2]
    chosen = own_block(states)
    part = order_ref[order_ref.shape[0] - 1]
    columns = [None] * parts
    reading = [None] * parts

    def before(j):
        rows = slice(j * quarter, (j + 1) * quarter)
        small = small_all[part ^ j, turn]
        dpre = (
            jnp.dot(small[:, :rank], weight_ref[...], preferred_element_type=wide) + bias_ref[...]
        )
        dpre_ref[pl.ds(turn * chunk + j * quarter, quarter), :] = dpre
        delta = jax.nn.softplus(dpre)
        step_all[rows, :] = jnp.where(fresh_ref[pl.ds(turn * chunk + j * quarter, quarter), :].astype(wide) > 0.0, delta, FAR)
        drive_all[rows, :] = delta * pair_ref[j, 0, turn].astype(wide)
        pair = small[:, rank:]
        columns[j] = transposed(pair)
        reading[j] = jnp.dot(
            pair, spread_ref[:, GROUP * states :], preferred_element_type=wide
        )

    def scan(j, state):
        for group in range(quarter // GROUP):
            base = j * quarter + group * GROUP
            kept = []
            for t in range(base, base + GROUP):
                here = t - j * quarter
                decay = jnp.exp2(step_all[t : t + 1, :] * coeff)
                entry = columns[j][:states, here : here + 1]
                state = decay * state + drive_all[t : t + 1, :] * entry
                kept.append(state)
            rows = pl.ds(origin + base * states, GROUP * states)
            kept_ref[rows, :] = jnp.concatenate(kept, axis=0).astype(low)
        return state

    def finish_part(j):
        found = []
        for group in range(quarter // GROUP):
            base = j * quarter + group * GROUP
            block = kept_ref[pl.ds(origin + base * states, GROUP * states), :]
            here = reading[j][group * GROUP : (group + 1) * GROUP]
            weights = jnp.where(chosen, here, 0.0).astype(low)
            found.append(jnp.dot(weights, block, preferred_element_type=wide))
        act = pair_ref[j, 0, turn].astype(wide)
        gate = pair_ref[j, 1, turn].astype(wide)
        mixed = jnp.concatenate(found, axis=0) + skip_ref[...] * act
        dgated = dgated_all[part ^ j, turn].astype(wide)
        gated_ref[j, 0, turn] = (mixed * jax.nn.silu(gate)).astype(low)
        gated_ref[j, 1, turn] = (dgated * mixed * silu_slope(gate)).astype(low)

    state = carry[...]
    before(0)
    for j in range(parts):
        if j + 1 < parts:
            before(j + 1)
        state = scan(j, state)
        if j:
            finish_part(j - 1)
    finish_part(parts - 1)
    carry[...] = state


def backward_body(parts, order_ref, *refs):
    sources, refs = refs[: 2 * parts + 4], refs[2 * parts + 4 :]
    params, (own_hbm, other_hbm, dscan_hbm), refs = refs[:4], refs[4:7], refs[7:]
    results, refs = refs[:3], refs[3:]
    scratch, refs = refs[:11], refs[11:]
    (small_all, dgated_all, pair_all, fresh_all, dpre_all, kept_all, edge_all) = refs[:7]
    (own_all, other_all, dscan_all, came, left) = refs[7:]
    blocks = small_all.shape[1]
    chunk = scratch[1].shape[0]
    states = scratch[0].shape[0]
    for ref in (scratch[0], *results, *scratch[8:10]):
        ref[...] = jnp.zeros_like(ref)

    def entering(turn):
        at = blocks - 1 - turn
        block = order_ref[at]
        rows = pl.ds(pl.multiple_of(at * chunk, chunk), chunk)
        tall = pl.ds(pl.multiple_of(at * (chunk * states), chunk * states), chunk * states)
        found = []
        for k in range(parts):
            found.append((sources[k].at[order_ref[blocks + at]], small_all.at[k, at]))
            found.append((sources[parts + k].at[block], dgated_all.at[k, at]))
        found.append((sources[2 * parts].at[:, :, block], pair_all.at[:, :, at]))
        for source, target, here in zip(
            sources[2 * parts + 1 :], (fresh_all, dpre_all, kept_all), (rows, rows, tall)
        ):
            found.append((source.at[here], target.at[here]))
        ahead = pl.multiple_of(jnp.maximum(at * (chunk * states) - states, 0), states)
        found.append((sources[-1].at[pl.ds(ahead, states)], edge_all.at[at]))
        return [
            pltpu.make_async_copy(a, b, came.at[turn, i]) for i, (a, b) in enumerate(found)
        ]

    def leaving(turn):
        at = blocks - 1 - turn
        block = order_ref[at]
        place = order_ref[blocks + at]
        found = [
            (own_all.at[:, at], own_hbm.at[:, place]),
            (other_all.at[:, at], other_hbm.at[:, place]),
            (dscan_all.at[:, at], dscan_hbm.at[:, block]),
        ]
        return [
            pltpu.make_async_copy(a, b, left.at[turn, i]) for i, (a, b) in enumerate(found)
        ]

    @pl.loop(0, blocks)
    def _(turn):
        for copy in entering(turn):
            copy.start()

    @pl.loop(0, blocks)
    def _(turn):
        for copy in entering(turn):
            copy.wait()
        backward_steps(
            turn,
            parts,
            blocks,
            order_ref,
            small_all,
            dgated_all,
            pair_all,
            fresh_all,
            dpre_all,
            kept_all,
            edge_all,
            *params,
            own_all,
            other_all,
            dscan_all,
            *results,
            *scratch,
        )
        for copy in leaving(turn):
            copy.start()

    @pl.loop(0, blocks)
    def _(turn):
        for copy in leaving(turn):
            copy.wait()


def backward_steps(
    turn,
    parts,
    blocks,
    order_ref,
    small_all,
    dgated_all,
    pair_ref,
    fresh_ref,
    dpre_ref,
    kept_ref,
    edge_ref,
    weight_ref,
    skip_ref,
    coeff_ref,
    spread_ref,
    own_ref,
    other_ref,
    dscan_ref,
    delta_grad_ref,
    decay_ref,
    sums_ref,
    carry,
    step_all,
    drive_all,
    delta_all,
    dmix_all,
    lam_all,
    flow_all,
    cross_all,
    next_partial,
    next_dscan,
    partial_all,
):
    coeff = coeff_ref[...]
    states = coeff.shape[0]
    rank = weight_ref.shape[0]
    quarter = small_all.shape[2]
    chosen = own_block(states)
    ones = jnp.where(chosen, 1.0, 0.0).astype(low)
    across = (((1,), (1,)), ((), ()))
    down = (((0,), (0,)), ((), ()))
    part = order_ref[order_ref.shape[0] - 1]
    chunk = step_all.shape[0]
    block_turn = blocks - 1 - turn
    origin = pl.multiple_of(block_turn * (chunk * states), chunk * states)
    first = jnp.where(block_turn == 0, 0.0, edge_ref[block_turn].astype(wide))
    columns = [None] * parts
    entering = [None] * parts
    after_partial = [next_partial[...]]
    after_dscan = [next_dscan[...]]

    def before(j):
        rows = slice(j * quarter, (j + 1) * quarter)
        small = small_all[part ^ j, block_turn]
        delta = jax.nn.softplus(dpre_ref[pl.ds(block_turn * chunk + j * quarter, quarter), :])
        act = pair_ref[j, 0, block_turn].astype(wide)
        gate = pair_ref[j, 1, block_turn].astype(wide)
        step_all[rows, :] = jnp.where(fresh_ref[pl.ds(block_turn * chunk + j * quarter, quarter), :].astype(wide) > 0.0, delta, FAR)
        drive_all[rows, :] = delta * act
        delta_all[rows, :] = delta
        dmix_all[rows, :] = dgated_all[part ^ j, block_turn].astype(wide) * jax.nn.silu(gate)
        pair = small[:, rank:]
        columns[j] = transposed(pair)
        entering[j] = jnp.dot(
            pair, spread_ref[:, : GROUP * states], preferred_element_type=wide
        )

    def scan(j, pulled, summed):
        for group in range(quarter // GROUP - 1, -1, -1):
            base = j * quarter + group * GROUP
            lams = [None] * GROUP
            flows = [None] * GROUP
            rows = slice(base * states, (base + GROUP) * states)
            block = kept_ref[pl.ds(origin + base * states, GROUP * states), :].astype(wide)
            if base:
                edge = kept_ref[pl.ds(origin + (base - 1) * states, states), :].astype(wide)
            else:
                edge = first
            for i in range(GROUP - 1, -1, -1):
                t = base + i
                here = t - j * quarter
                read = columns[j][states:, here : here + 1]
                lam = read * dmix_all[t : t + 1, :] + pulled
                pulled = jnp.exp2(step_all[t : t + 1, :] * coeff) * lam
                flow = pulled * (block[(i - 1) * states : i * states] if i else edge)
                summed = summed + flow * delta_all[t : t + 1, :]
                lams[i] = lam
                flows[i] = flow * coeff
            lam_all[rows, :] = jnp.concatenate(lams, axis=0).astype(low)
            flow_all[rows, :] = jnp.concatenate(flows, axis=0).astype(low)
        return pulled, summed

    def finish_part(j):
        part_rows = slice(j * quarter, (j + 1) * quarter)
        lam_found = []
        flow_found = []
        for group in range(quarter // GROUP):
            base = j * quarter + group * GROUP
            here = slice(base, base + GROUP)
            rows = slice(base * states, (base + GROUP) * states)
            lam_block = lam_all[rows, :]
            entry = entering[j][group * GROUP : (group + 1) * GROUP]
            weights = jnp.where(chosen, entry, 0.0).astype(low)
            lam_found.append(jnp.dot(weights, lam_block, preferred_element_type=wide))
            flow_found.append(jnp.dot(ones, flow_all[rows, :], preferred_element_type=wide))
            cross = lax.dot_general(
                drive_all[here, :].astype(low), lam_block, across, preferred_element_type=wide
            )
            cross_all[here, : GROUP * states] = jnp.where(chosen, cross, 0.0).astype(low)
            cross = lax.dot_general(
                dmix_all[here, :].astype(low),
                kept_ref[pl.ds(origin + base * states, GROUP * states), :],
                across,
                preferred_element_type=wide,
            )
            cross_all[here, GROUP * states :] = jnp.where(chosen, cross, 0.0).astype(low)
        dpair = lax.dot_general(
            cross_all[part_rows, :], spread_ref[...], across, preferred_element_type=wide
        ).astype(low)
        found = jnp.concatenate(lam_found, axis=0)
        act = pair_ref[j, 0, block_turn].astype(wide)
        delta = delta_all[part_rows, :]
        dmix = dmix_all[part_rows, :]
        ddelta = jnp.concatenate(flow_found, axis=0) * (1.0 / math.log2(math.e)) + found * act
        ddpre = (ddelta * jax.nn.sigmoid(dpre_ref[pl.ds(block_turn * chunk + j * quarter, quarter), :])).astype(low)
        small = small_all[part ^ j, block_turn]
        delta_grad_ref[...] += lax.dot_general(
            small[:, :rank], ddpre, down, preferred_element_type=wide
        )
        dlow = lax.dot_general(
            ddpre, weight_ref[...], across, preferred_element_type=wide
        ).astype(low)
        dscan = (found * delta + dmix * skip_ref[...]).astype(low)
        sums_ref[0:1, :] += jnp.sum(ddpre.astype(wide), axis=0, keepdims=True)
        sums_ref[1:2, :] += jnp.sum(dmix * act, axis=0, keepdims=True)
        after_rows = after_partial[0]
        partial_all[j, :quarter, :rank] = dlow
        partial_all[j, :quarter, rank:] = dpair
        partial_all[j, quarter:, :] = after_rows
        dscan_ref[j, block_turn, :quarter, :] = dscan
        dscan_ref[j, block_turn, quarter:, :] = after_dscan[0]
        after_partial[0] = jnp.concatenate([dlow[:TAIL], dpair[:TAIL]], axis=1)
        after_dscan[0] = dscan[:TAIL]

    pulled = carry[...]
    summed = decay_ref[...]
    before(parts - 1)
    for j in range(parts - 1, -1, -1):
        if j:
            before(j - 1)
        pulled, summed = scan(j, pulled, summed)
        if j + 1 < parts:
            finish_part(j + 1)
    finish_part(0)
    carry[...] = pulled
    decay_ref[...] = summed
    next_partial[...] = after_partial[0]
    next_dscan[...] = after_dscan[0]
    for k in range(parts):
        (other_ref if k % 2 else own_ref)[k // 2, block_turn] = partial_all[part ^ k]


def forward_scan(order, small, pair, dgated, fresh, weight, bias, skip, coeff, spread):
    parts, _, blocks, quarter, width = pair.shape
    states = coeff.shape[0]
    columns = small[0].shape[-1]
    chunk = parts * quarter
    tokens = blocks * chunk
    streamed = (*small, *dgated, pair, fresh)
    params = (weight, bias, skip, coeff, spread)
    apart = pl.BlockSpec(memory_space=pl.ANY)
    kept = (tokens * states, width)
    gated = (parts, 2, blocks, quarter, width)
    return pl.pallas_call(
        functools.partial(forward_body, parts),
        grid_spec=pltpu.PrefetchScalarGridSpec(
            num_scalar_prefetch=1,
            grid=(1,),
            in_specs=[apart] * len(streamed)
            + [pl.BlockSpec(v.shape, lambda t, order: (0, 0)) for v in params],
            out_specs=[apart] * 3,
            scratch_shapes=[
                pltpu.VMEM((states, width), wide),
                pltpu.VMEM((chunk, width), wide),
                pltpu.VMEM((chunk, width), wide),
                pltpu.VMEM((parts, blocks, quarter, columns), low),
                pltpu.VMEM((parts, blocks, quarter, width), low),
                pltpu.VMEM(gated, low),
                pltpu.VMEM((tokens, width), low),
                pltpu.VMEM(kept, low),
                pltpu.VMEM((tokens, width), wide),
                pltpu.VMEM(gated, low),
                pltpu.SemaphoreType.DMA((blocks, len(streamed) + 1)),
                pltpu.SemaphoreType.DMA((blocks, 3)),
            ],
        ),
        out_shape=[
            pltpu.HBM(kept, low),
            pltpu.HBM((tokens, width), wide),
            pltpu.HBM(gated, low),
        ],
        compiler_params=pltpu.CompilerParams(vmem_limit_bytes=28 * 1024 * 1024),
        cost_estimate=spent(12),
        name="forward_scan",
    )(order, *map(in_hbm, streamed), *params)


def backward_scan(
    order, small, pair, dgated, fresh, dpre, kept, weight, skip, coeff, spread
):
    parts, _, blocks, quarter, width = pair.shape
    states = coeff.shape[0]
    rank = weight.shape[0]
    columns = small[0].shape[-1]
    chunk = parts * quarter
    tokens = blocks * chunk
    streamed = (*small, *dgated, pair, fresh, dpre, kept)
    params = (weight, skip, coeff, spread)
    apart = pl.BlockSpec(memory_space=pl.ANY)
    sums = (parts // 2, blocks, quarter + TAIL, columns)
    dscan = (parts, blocks, quarter + TAIL, width)
    results = ((rank, width), (states, width), (8, width))
    return pl.pallas_call(
        functools.partial(backward_body, parts),
        grid_spec=pltpu.PrefetchScalarGridSpec(
            num_scalar_prefetch=1,
            grid=(1,),
            in_specs=[apart] * len(streamed)
            + [pl.BlockSpec(v.shape, lambda t, order: (0, 0)) for v in params],
            out_specs=[apart] * 3 + [pl.BlockSpec(v, lambda t, order: (0, 0)) for v in results],
            scratch_shapes=[pltpu.VMEM((states, width), wide)]
            + [pltpu.VMEM((chunk, width), wide)] * 4
            + [pltpu.VMEM((chunk * states, width), low)] * 2
            + [
                pltpu.VMEM((chunk, 2 * GROUP * states), low),
                pltpu.VMEM((TAIL, columns), low),
                pltpu.VMEM((TAIL, width), low),
                pltpu.VMEM((parts, quarter + TAIL, columns), low),
                pltpu.VMEM((parts, blocks, quarter, columns), low),
                pltpu.VMEM((parts, blocks, quarter, width), low),
                pltpu.VMEM(pair.shape, low),
                pltpu.VMEM((tokens, width), low),
                pltpu.VMEM((tokens, width), wide),
                pltpu.VMEM((tokens * states, width), low),
                pltpu.VMEM((blocks, states, width), low),
                pltpu.VMEM(sums, low),
                pltpu.VMEM(sums, low),
                pltpu.VMEM(dscan, low),
                pltpu.SemaphoreType.DMA((blocks, len(streamed) + 1)),
                pltpu.SemaphoreType.DMA((blocks, 3)),
            ],
        ),
        out_shape=[pltpu.HBM(sums, low), pltpu.HBM(sums, low), pltpu.HBM(dscan, low)]
        + [jax.ShapeDtypeStruct(v, wide) for v in results],
        compiler_params=pltpu.CompilerParams(vmem_limit_bytes=28 * 1024 * 1024),
        cost_estimate=spent(19),
        name="backward_scan",
    )(order, *map(in_hbm, streamed), *params)


def interleave_body(parts, order_ref, *refs):
    values, out_ref = refs[: 2 * parts], refs[2 * parts]
    width, block = values[0].shape
    same = diagonal(block)
    for part in range(parts):

        @pl.when(order_ref[0] == part)
        def _(part=part):
            for half in range(2):
                for k in range(parts):
                    out_ref[:, half, (part ^ k) * width : ((part ^ k) + 1) * width] = (
                        lax.dot_general(
                            same,
                            values[half * parts + k][...],
                            (((1,), (1,)), ((), ())),
                            preferred_element_type=wide,
                        )
                    )


def interleave(order, inner, gate):
    parts = len(inner)
    width, depth = inner[0].shape
    block = 256
    return pl.pallas_call(
        functools.partial(interleave_body, parts),
        grid_spec=pltpu.PrefetchScalarGridSpec(
            num_scalar_prefetch=1,
            grid=(depth // block,),
            in_specs=[pl.BlockSpec((width, block), lambda t, order: (0, t))] * parts
            + [pl.BlockSpec((None, width, block), lambda t, order: (1, 0, t))] * parts,
            out_specs=pl.BlockSpec((block, 2, parts * width), lambda t, order: (t, 0, 0)),
        ),
        out_shape=jax.ShapeDtypeStruct((depth, 2, parts * width), wide),
        compiler_params=pltpu.CompilerParams(vmem_limit_bytes=16 * 1024 * 1024),
        cost_estimate=spent(5),
        name="interleave",
    )(order, *inner, *gate)


def placed_body(parts, order_ref, *refs):
    values, out_ref = refs[:parts], refs[-1]
    place = order_ref[pl.program_id(0)]
    for k in range(parts):

        @pl.when(place == k)
        def _(k=k):
            value = values[k][...].astype(wide)
            out_ref[...] = refs[parts][...] + value if len(refs) > parts + 1 else value


def placed(order, values, base=None):
    parts = len(values)
    rows, width = values[0].shape[-2:]
    flat = pl.BlockSpec((rows, width), lambda p, order: (p, 0))
    if values[0].ndim == 3:
        piece = pl.BlockSpec((None, rows, width), lambda p, order: (0, 0, 0))
    else:
        piece = pl.BlockSpec((rows, width), lambda p, order: (0, 0))
    return pl.pallas_call(
        functools.partial(placed_body, parts),
        grid_spec=pltpu.PrefetchScalarGridSpec(
            num_scalar_prefetch=1,
            grid=(parts,),
            in_specs=[piece] * parts
            + ([] if base is None else [flat]),
            out_specs=flat,
        ),
        out_shape=jax.ShapeDtypeStruct((parts * rows, width), wide),
        compiler_params=pltpu.CompilerParams(vmem_limit_bytes=24 * 1024 * 1024),
        cost_estimate=spent(2.5),
        name="placed",
    )(order, *values, *(() if base is None else (base,)))


def diagonal(size):
    places = [lax.broadcasted_iota(jnp.int32, (size, size), axis) for axis in (0, 1)]
    return jnp.where(places[0] == places[1], 1.0, 0.0).astype(low)


def project_body(
    place_ref,
    *refs,
):
    pieces, refs = refs[:8], refs[8:]
    (weight_ref, flags_ref, taps_ref, offset_ref, select_ref) = refs[:5]
    (normed_ref, inner_ref, channels_ref, kept_ref, sent_ref, turned_ref) = refs[5:11]
    (sides, edges, window, total, acts) = refs[11:]
    turn = pl.program_id(0)
    quarter = channels_ref.shape[3]
    width = channels_ref.shape[4]
    halves = weight_ref.shape[1] // width
    taps = taps_ref.shape[0]
    inner_turns = pl.num_programs(0) // 2
    count = len(pieces)

    @pl.when(turn == 0)
    def _():
        for k in range(count):
            piece = pieces[k][...]
            normed_ref[k * quarter : (k + 1) * quarter, :] = piece[:quarter]
            sides[k * 8 : (k + 1) * 8, :] = piece[quarter:].astype(wide)
        edges[...] = jnp.zeros_like(edges)
        total[...] = jnp.zeros_like(total)

    main = jnp.dot(normed_ref[...], weight_ref[...], preferred_element_type=wide)
    tile = weight_ref.shape[1]
    same = diagonal(tile)
    for k in range(weight_ref.shape[0] // tile):
        here = slice(k * tile, (k + 1) * tile)
        turned_ref[:, here] = lax.dot_general(
            same, weight_ref[here, :], (((1,), (1,)), ((), ())), preferred_element_type=wide
        ).astype(low)

    @pl.when(turn < inner_turns)
    def _():
        edges[: count * 8, :] = jnp.dot(
            sides[...].astype(low), weight_ref[...], preferred_element_type=wide
        )
        for k in range(count):
            before = pl.multiple_of(place_ref[k] * 8, 8)
            after = pl.multiple_of(place_ref[count + k] * 8, 8)
            flags = flags_ref[k]
            window[0:8, :] = edges[pl.ds(before, 8), :]
            window[8 : 8 + quarter, :] = main[k * quarter : (k + 1) * quarter]
            window[8 + quarter : 16 + quarter, :] = edges[pl.ds(after, 8), :]
            masked = window[...] * flags[:, 0:1]
            window[...] = masked
            inner_ref[k] = masked
            conv = offset_ref[...] + taps_ref[taps - 1 : taps, :] * masked[8 : 8 + quarter]
            for lag in range(1, taps):
                shifted = window[8 - lag : 8 - lag + quarter, :]
                valid = flags[8 : 8 + quarter, lag : lag + 1]
                conv = conv + taps_ref[taps - 1 - lag : taps - lag, :] * shifted * valid
            act = (jax.nn.silu(conv) * flags[8 : 8 + quarter, 0:1]).astype(low)
            acts[k * quarter : (k + 1) * quarter, :] = act
            for h in range(halves):
                channels_ref[h, 0, k] = act[:, h * width : (h + 1) * width]
        total[...] += jnp.dot(acts[...], select_ref[...], preferred_element_type=wide)

    @pl.when(turn >= inner_turns)
    def _():
        gate = main.astype(low)
        for k in range(count):
            for h in range(halves):
                channels_ref[h, 0, k] = gate[
                    k * quarter : (k + 1) * quarter, h * width : (h + 1) * width
                ]

    @pl.when(turn == pl.num_programs(0) - 1)
    def _():
        for k in range(count // 2):
            plane = place_ref[2 * count + k]
            kept_ref[plane] = total[k * quarter : (k + 1) * quarter, :]
            other = k + count // 2
            sent_ref[plane] = total[other * quarter : (other + 1) * quarter, :].astype(low)


def project(places, pieces, weight, flags, taps, offset, select, parts):
    count = len(pieces)
    rows, depth = pieces[0].shape
    quarter = rows - 8
    chans = weight.shape[1] // 2
    width = chans // parts
    tile = 2 * width
    turns = 2 * chans // tile
    half = turns // 2
    small = select.shape[1]

    def whole(shape):
        return pl.BlockSpec(shape, lambda t, place: (0,) * len(shape))

    def inner(t):
        return jnp.minimum(t, half - 1)

    return pl.pallas_call(
        project_body,
        grid_spec=pltpu.PrefetchScalarGridSpec(
            num_scalar_prefetch=1,
            grid=(turns,),
            in_specs=[whole(pieces[0].shape) for _ in pieces]
            + [
                pl.BlockSpec((depth, tile), lambda t, place: (0, t)),
                whole(flags.shape),
                pl.BlockSpec((taps.shape[0], tile), lambda t, place: (0, inner(t))),
                pl.BlockSpec((1, tile), lambda t, place: (0, inner(t))),
                pl.BlockSpec((tile, small), lambda t, place: (inner(t), 0)),
            ],
            out_specs=[
                whole((count * quarter, depth)),
                pl.BlockSpec((count, quarter + 16, tile), lambda t, place: (0, 0, inner(t))),
                pl.BlockSpec(
                    (2, 1, count, quarter, width),
                    lambda t, place: (t % half, t // half, 0, 0, 0),
                ),
                whole((count // 2, quarter, small)),
                whole((count // 2, quarter, small)),
                pl.BlockSpec((tile, depth), lambda t, place: (t, 0)),
            ],
            scratch_shapes=[
                pltpu.VMEM((count * 8, depth), wide),
                pltpu.VMEM((count * 8 + 8, tile), wide),
                pltpu.VMEM((quarter + 16, tile), wide),
                pltpu.VMEM((count * quarter, small), wide),
                pltpu.VMEM((count * quarter, tile), low),
            ],
        ),
        out_shape=[
            pltpu.HBM((count * quarter, depth), low),
            pltpu.HBM((count, quarter + 16, chans), wide),
            jax.ShapeDtypeStruct((parts, 2, count, quarter, width), low),
            jax.ShapeDtypeStruct((count // 2, quarter, small), wide),
            jax.ShapeDtypeStruct((count // 2, quarter, small), low),
            pltpu.HBM((2 * chans, depth), low),
        ],
        compiler_params=pltpu.CompilerParams(vmem_limit_bytes=28 * 1024 * 1024),
        cost_estimate=spent(8),
        name="project",
    )(places, *map(in_hbm, (*pieces, weight, flags, taps, offset, select)))


def pull_body(order_ref, rows_ref, weight_ref, kept_ref, *refs):
    out_refs, found_ref = refs[:-1], refs[-1]
    count = rows_ref.shape[0]
    quarter = rows_ref.shape[1]
    width = out_refs[0].shape[2]
    turn = pl.program_id(0)
    bit = order_ref[count] & 1

    @pl.when(turn == 0)
    def _():
        for k in range(count):
            kept_ref[k * quarter : (k + 1) * quarter, :] = rows_ref[order_ref[k]]

    found_ref[...] = lax.dot_general(
        kept_ref[...], weight_ref[...], (((1,), (1,)), ((), ())), preferred_element_type=wide
    ).astype(low)
    for p in range(len(out_refs)):

        @pl.when(turn == p // 2)
        def _(p=p):
            here = pl.ds(pl.multiple_of((bit ^ (p % 2)) * width, width), width)
            for k in range(count):
                out_refs[p][k] = found_ref[k * quarter : (k + 1) * quarter, here]


def pull(order, rows, weight, parts):
    count, quarter, depth = rows.shape
    width = weight.shape[0] // parts
    piece = pl.BlockSpec((count, quarter, width), lambda t, order: (0, 0, 0))
    return pl.pallas_call(
        pull_body,
        grid_spec=pltpu.PrefetchScalarGridSpec(
            num_scalar_prefetch=1,
            grid=(parts // 2,),
            in_specs=[
                pl.BlockSpec((count, quarter, depth), lambda t, order: (0, 0, 0)),
                pl.BlockSpec((2 * width, depth), lambda t, order: ((order[count] // 2) ^ t, 0)),
            ],
            out_specs=[pl.BlockSpec((count * quarter, depth), lambda t, order: (0, 0))]
            + [piece] * parts,
            scratch_shapes=[pltpu.VMEM((count * quarter, 2 * width), low)],
        ),
        out_shape=[pltpu.HBM((count * quarter, depth), low)]
        + [pltpu.HBM((count, quarter, width), low)] * parts,
        compiler_params=pltpu.CompilerParams(vmem_limit_bytes=20 * 1024 * 1024),
        cost_estimate=spent(6),
        name="pull",
    )(order, in_hbm(rows), in_hbm(weight))


def spread_parts(part, product, own_ref, other_ref):
    parts = 2 * own_ref.shape[0]
    width = product.shape[0] // parts
    for p in range(parts):
        here = pl.ds(pl.multiple_of((part ^ p) * width, width), width)
        yield (other_ref if p % 2 else own_ref), p // 2, here


def emit_body(order_ref, *refs):
    pieces_ref, refs = refs[0], refs[1:]
    parts = pieces_ref.shape[0]
    (weight_ref, rows_ref, normed_ref, turned_ref) = refs[:4]
    (kept_ref, sent_ref, own_ref, other_ref, dgate_ref, gain_ref) = refs[4:10]
    (gated, product, second) = refs[10:]
    count, quarter, width = pieces_ref.shape[2:]

    @pl.when(pl.program_id(0) == 0)
    def _():
        for p in range(parts):
            here = slice(p * width, (p + 1) * width)
            for k in range(count):
                rows = slice(k * quarter, (k + 1) * quarter)
                gated[rows, here] = pieces_ref[p, 0, k]
                dgate_ref[rows, here] = pieces_ref[p, 1, k]

    values = gated[...]
    branch = jnp.dot(values, weight_ref[...], preferred_element_type=wide).astype(low)
    kept_ref[...] = branch[: count // 2 * quarter].reshape(kept_ref.shape)
    sent_ref[...] = branch[count // 2 * quarter :].reshape(sent_ref.shape)
    down = (((0,), (0,)), ((), ()))
    product[...] = lax.dot_general(
        values, rows_ref[...], down, preferred_element_type=wide
    ).astype(low)
    found = lax.dot_general(
        dgate_ref[...], normed_ref[...], down, preferred_element_type=wide
    )
    gain_ref[...] = jnp.sum(found * turned_ref[...].astype(wide), axis=0, keepdims=True)
    second[...] = found.astype(low)
    for ref, p, here in spread_parts(order_ref[count], product, own_ref, other_ref):
        ref[p, 0] = product[here, :]
        ref[p, 1] = second[here, :]


def emit(order, pieces, weight, rows, normed, turned):
    parts, _, count, quarter, width = pieces.shape
    depth = weight.shape[1]
    tile = 512
    chans = parts * width
    tall = count * quarter
    blocks = pl.BlockSpec((count // 2, quarter, tile), lambda t, order: (0, 0, t))
    grads = pl.BlockSpec((parts // 2, 2, width, tile), lambda t, order: (0, 0, 0, t))
    columns = pl.BlockSpec((tall, tile), lambda t, order: (0, t))
    return pl.pallas_call(
        emit_body,
        grid_spec=pltpu.PrefetchScalarGridSpec(
            num_scalar_prefetch=1,
            grid=(depth // tile,),
            in_specs=[
                pl.BlockSpec(pieces.shape, lambda t, order: (0, 0, 0, 0, 0)),
                pl.BlockSpec((chans, tile), lambda t, order: (0, t)),
                columns,
                columns,
                pl.BlockSpec((chans, tile), lambda t, order: (1, t)),
            ],
            out_specs=[
                blocks,
                blocks,
                grads,
                grads,
                pl.BlockSpec((tall, chans), lambda t, order: (0, 0)),
                pl.BlockSpec((1, tile), lambda t, order: (0, t)),
            ],
            scratch_shapes=[
                pltpu.VMEM((tall, chans), low),
                pltpu.VMEM((chans, tile), low),
                pltpu.VMEM((chans, tile), low),
            ],
        ),
        out_shape=[
            pltpu.HBM((count // 2, quarter, depth), low),
            pltpu.HBM((count // 2, quarter, depth), low),
            pltpu.HBM((parts // 2, 2, width, depth), low),
            pltpu.HBM((parts // 2, 2, width, depth), low),
            pltpu.HBM((tall, chans), low),
            jax.ShapeDtypeStruct((1, depth), wide),
        ],
        compiler_params=pltpu.CompilerParams(vmem_limit_bytes=24 * 1024 * 1024),
        cost_estimate=spent(6),
        name="emit",
    )(order, *map(in_hbm, (pieces, weight, rows, normed, turned)))


def weigh_body(order_ref, rows_ref, normed_ref, turned_ref, own_ref, other_ref, gain_ref, product):
    found = lax.dot_general(
        rows_ref[...], normed_ref[...], (((0,), (0,)), ((), ())), preferred_element_type=wide
    )
    gain_ref[...] = jnp.sum(found * turned_ref[...].astype(wide), axis=0, keepdims=True)
    product[...] = found.astype(low)
    for ref, p, here in spread_parts(order_ref[8], product, own_ref, other_ref):
        ref[p] = product[here, :]


def weigh(order, rows, normed, turned, parts):
    tall, depth = normed.shape
    chans = rows.shape[1] // 2
    width = chans // parts
    tile = 512
    grads = pl.BlockSpec((parts // 2, width, tile), lambda t, order: (0, 0, t))
    return pl.pallas_call(
        weigh_body,
        grid_spec=pltpu.PrefetchScalarGridSpec(
            num_scalar_prefetch=1,
            grid=(depth // tile,),
            in_specs=[
                pl.BlockSpec((tall, chans), lambda t, order: (0, 0)),
                pl.BlockSpec((tall, tile), lambda t, order: (0, t)),
                pl.BlockSpec((chans, tile), lambda t, order: (0, t)),
            ],
            out_specs=[grads, grads, pl.BlockSpec((1, tile), lambda t, order: (0, t))],
            scratch_shapes=[pltpu.VMEM((chans, tile), low)],
        ),
        out_shape=[
            pltpu.HBM((parts // 2, width, depth), low),
            pltpu.HBM((parts // 2, width, depth), low),
            jax.ShapeDtypeStruct((1, depth), wide),
        ],
        compiler_params=pltpu.CompilerParams(vmem_limit_bytes=16 * 1024 * 1024),
        cost_estimate=spent(4),
        name="weigh",
    )(order, rows, in_hbm(normed), in_hbm(turned))


def turn_body(order_ref, *refs):
    count = 8
    smalls, refs = refs[:2], refs[2:]
    (dscan_ref, select_ref, inner_ref, flags_ref, taps_ref, offset_ref, dgate_ref) = refs[:7]
    (dboth_ref, grad_ref, rows_ref) = refs[7:10]
    (small_all, shifted, acts) = refs[10:]
    rank = grad_ref.shape[1]
    parts = pl.num_programs(0) // 2
    turn = pl.program_id(0)
    span = inner_ref.shape[1]
    quarter = span - 16
    reach = quarter + 8
    taps = taps_ref.shape[0]

    @pl.when(turn == 0)
    def _():
        for k in range(count):
            plane = order_ref[k] // 2
            small_all[k * span : (k + 1) * span, :] = smalls[k // (count // 2)][plane]

    @pl.when(turn < parts)
    def _():
        whole = lax.dot_general(
            small_all[...],
            select_ref[...],
            (((1,), (1,)), ((), ())),
            preferred_element_type=wide,
        )
        found = dscan_ref[0]
        sums = [0.0] * (taps + 1)
        for k in range(count):
            flags = flags_ref[k, 8 : 8 + reach, :]
            mask = flags[:, 0:1]
            conv = offset_ref[...]
            for lag in range(taps):
                term = taps_ref[taps - 1 - lag : taps - lag, :] * inner_ref[
                    k, 8 - lag : 8 - lag + reach, :
                ]
                conv = conv + (term * flags[:, lag : lag + 1] if lag else term)
            sig = jax.nn.sigmoid(conv)
            act = conv * sig * mask
            acts[k * quarter : (k + 1) * quarter, :] = act[:quarter].astype(low)
            dact = found[k, :reach].astype(wide) + whole[k * span : k * span + reach]
            dconv = dact * mask * (sig * (1.0 + conv * (1.0 - sig)))
            dinner = 0.0
            for lag in range(taps):
                masked = dconv * flags[:, lag : lag + 1] if lag else dconv
                sums[taps - 1 - lag] += jnp.sum(
                    masked[:quarter] * inner_ref[k, 8 - lag : 8 - lag + quarter, :],
                    axis=0,
                    keepdims=True,
                )
                if lag:
                    shifted[lag, :reach, :] = masked
                    masked = shifted[lag, lag : lag + quarter, :]
                else:
                    sums[taps] += jnp.sum(masked[:quarter], axis=0, keepdims=True)
                    masked = masked[:quarter]
                dinner = dinner + masked * taps_ref[taps - 1 - lag : taps - lag, :]
            dboth_ref[k * quarter : (k + 1) * quarter, :] = (dinner * mask[:quarter]).astype(low)
        for index, value in enumerate(sums):
            rows_ref[index : index + 1, :] = value
        mains = jnp.concatenate(
            [small_all[k * span : k * span + quarter, :] for k in range(count)], axis=0
        )
        grad_ref[...] = lax.dot_general(
            acts[...], mains[:, :rank], (((0,), (0,)), ((), ())), preferred_element_type=wide
        ).astype(low)
        rows_ref[8:, :] = lax.dot_general(
            mains[:, rank:], acts[...], (((0,), (0,)), ((), ())), preferred_element_type=wide
        )

    @pl.when(turn >= parts)
    def _():
        dboth_ref[...] = dgate_ref[...]


def turn_back(order, smalls, dscan, select, inner, flags, taps, offset, dgate, rank):
    parts, count, span, _ = dscan.shape
    small = smalls[0].shape[-1]
    chans = select.shape[0]
    width = chans // parts
    quarter = span - 16

    def whole(shape):
        return pl.BlockSpec(shape, lambda t, order: (0,) * len(shape))

    def early(t):
        return jnp.minimum(t, parts - 1)

    return pl.pallas_call(
        turn_body,
        grid_spec=pltpu.PrefetchScalarGridSpec(
            num_scalar_prefetch=1,
            grid=(2 * parts,),
            in_specs=[whole(v.shape) for v in smalls]
            + [
                pl.BlockSpec((1, count, span, width), lambda t, order: (early(t), 0, 0, 0)),
                pl.BlockSpec((width, small), lambda t, order: (early(t), 0)),
                pl.BlockSpec((count, span, width), lambda t, order: (0, 0, early(t))),
                whole(flags.shape),
                pl.BlockSpec((taps.shape[0], width), lambda t, order: (0, early(t))),
                pl.BlockSpec((1, width), lambda t, order: (0, early(t))),
                pl.BlockSpec(
                    (count * quarter, width), lambda t, order: (0, jnp.maximum(t - parts, 0))
                ),
            ],
            out_specs=[
                pl.BlockSpec((count * quarter, width), lambda t, order: (0, t)),
                pl.BlockSpec((width, rank), lambda t, order: (early(t), 0)),
                pl.BlockSpec((small - rank + 8, width), lambda t, order: (0, early(t))),
            ],
            scratch_shapes=[
                pltpu.VMEM((count * span, small), low),
                pltpu.VMEM((taps.shape[0], span, width), wide),
                pltpu.VMEM((count * quarter, width), low),
            ],
        ),
        out_shape=[
            jax.ShapeDtypeStruct((count * quarter, 2 * chans), low),
            pltpu.HBM((chans, rank), low),
            jax.ShapeDtypeStruct((small - rank + 8, chans), wide),
        ],
        compiler_params=pltpu.CompilerParams(vmem_limit_bytes=20 * 1024 * 1024),
        cost_estimate=spent(5.5),
        name="turn_back",
    )(
        order,
        *smalls,
        dscan,
        select,
        inner,
        flags,
        taps,
        offset,
        dgate,
    )


class Moves:
    def __init__(self):
        self.chan = lax.axis_index("chan").astype(jnp.uint32)
        self.part = lax.axis_index("state").astype(jnp.uint32)
        self.z = self.chan // 2
        self.y = self.chan % 2
        places = jnp.arange(8, dtype=jnp.uint32)
        planes = (self.z + 4 - places % 4) % 4
        self.blocks = planes * 2 + (self.y + places // 4) % 2
        hops = (self.z + 4 - places // 2) % 4
        self.order = (self.y + places) % 2 * 4 + hops

    def over_y(self, values):
        return lax.ppermute(values, "chan", [(i, i ^ 1) for i in range(8)])

    def over_z(self, values, hops):
        return lax.ppermute(values, "chan", [(i, (i + 2 * hops) % 8) for i in range(8)])

    def over_state(self, values, bits):
        return lax.ppermute(values, "state", [(i, i ^ bits) for i in range(4)])

    def swap_state(self, values):
        return lax.all_to_all(values, "state", 0, 0, tiled=True)

    def pair(self, bit, own, other):
        return jnp.stack([jnp.where(bit == 0, own, other), jnp.where(bit == 0, other, own)])

    def in_order(self, pieces):
        own, core, across, slant = pieces
        bit = self.part % 2
        near = self.pair(bit, own, core)
        far = self.pair(bit, across, slant)
        return self.pair(self.part // 2, near, far).reshape((4,) + own.shape)

    def pieces_state(self, values):
        core = self.over_state(values, 1)
        across = self.over_state(values, 2)
        return values, core, across, self.over_state(across, 1)


def tied(*values):
    return lax.optimization_barrier(values)


def after(values, *others):
    token = lax.optimization_barrier((lax.create_token(), others))[0]
    return lax.optimization_barrier((token, values))[1]


def near_shards(
    n_chan,
    n_state,
    hidden_in,
    norm_gain,
    in_weight,
    conv_kernel,
    conv_offset,
    select_rank,
    select_entry,
    select_read,
    delta_weight,
    step_bias,
    decay_log,
    skip_weight,
    out_weight,
    lengths,
    pad_mask,
    cotangent,
):
    rows_dev, width = hidden_in.shape
    tokens = pad_mask.shape[0]
    chans = in_weight.shape[2]
    taps = conv_kernel.shape[0]
    rank = select_rank.shape[1]
    per_state = select_entry.shape[1]
    states = per_state * n_state
    small = rank + 2 * states
    quarter = rows_dev // n_state
    own = chans // n_state
    rows_q = n_chan * quarter
    part = lax.axis_index("state").astype(jnp.uint32)
    contract_rows = (((0,), (0,)), ((), ()))
    contract_cols = (((1,), (1,)), ((), ()))
    moves = Moves()
    blocks = moves.blocks
    planes = jnp.arange(4, dtype=jnp.uint32)
    small_order = jnp.stack([(moves.y ^ u) * 4 + planes for u in (0, 1)], axis=1).reshape(-1)
    order = jnp.concatenate([moves.order, small_order, part[None]]).astype(jnp.int32)
    places = jnp.concatenate([blocks, part[None]]).astype(jnp.int32)
    blocks = blocks.astype(jnp.int32)

    def mine(values, axis=0):
        return lax.dynamic_slice_in_dim(values, part * own, own, axis)

    start = part * quarter
    hidden_q = lax.dynamic_slice_in_dim(hidden_in, start, quarter, 0)
    ahead = (start + (rows_dev - HALO)) % rows_dev
    behind = (start + quarter) % rows_dev
    local = jnp.concatenate(
        [
            hidden_q,
            lax.dynamic_slice_in_dim(hidden_in, behind, HALO, 0),
            lax.dynamic_slice_in_dim(hidden_in, ahead, HALO, 0),
        ],
        axis=0,
    )
    inv_all = lax.rsqrt(jnp.mean(local * local, axis=1, keepdims=True) + epsilon)
    scaled_all = local * inv_all
    normed_all = (scaled_all * norm_gain[None, :]).astype(low)
    inv_rms = inv_all[:quarter]
    scaled = scaled_all[:quarter]
    cot_q = lax.dynamic_slice_in_dim(cotangent, start, quarter, 0).astype(low)
    ranks = (part ^ jnp.arange(n_state, dtype=jnp.uint32)).astype(jnp.int32)

    def trades(values):
        return [values[0]] + [moves.over_state(values[k], k) for k in (1, 2, 3)]

    def core_halves(values):
        cut = values.reshape((2, 2) + values.shape[1:])
        core = part % 2
        return (
            lax.dynamic_index_in_dim(cut, 1 - core, 1, keepdims=False),
            lax.dynamic_index_in_dim(cut, core, 1, keepdims=False),
        )

    def chip_halves(values):
        side = part // 2
        return (
            lax.dynamic_index_in_dim(values, 1 - side, 0, keepdims=False),
            lax.dynamic_index_in_dim(values, side, 0, keepdims=False),
        )

    def total_of(own_part, others):
        total = own_part.astype(wide)
        for piece in others:
            total = total + piece.astype(wide)
        return total.astype(low)

    def added(kept, came):
        return (kept.astype(wide) + came.astype(wide)).astype(low)

    columns = jnp.concatenate([select_entry, select_read], axis=1)
    decay_cut = jnp.swapaxes(decay_log.reshape(per_state, n_state, own), 0, 1)
    across = moves.over_y(normed_all)
    along = [moves.over_z(normed_all, hops) for hops in (1, 2, 3)]
    columns_core = moves.over_state(columns, 1)
    columns_chip = moves.over_state(columns, 2)
    decay_own = moves.swap_state(decay_cut)
    in_flat = in_weight.reshape(width, 2 * chans)
    tie = tied(across, *along, columns_core, columns_chip, decay_own, in_flat, cot_q)
    across, along, columns_core, columns_chip = tie[0], list(tie[1:4]), *tie[4:6]
    decay_own, in_flat, cot_q = tie[6:]
    grads = lax.all_gather(cot_q, "chan", axis=0)
    over = [moves.over_y(piece) for piece in along]
    columns_slant = moves.over_state(columns_chip, 1)
    over[0], over[1], over[2], columns_slant = tied(*over, columns_slant)
    pieces = [normed_all] + along + [across] + over

    place = positions(lengths, tokens)
    flags = [pad_mask.astype(wide)]
    flags += [(place >= lag).astype(wide) for lag in range(1, taps)]
    flags = jnp.stack(flags)
    padded = jnp.pad(flags, ((0, 0), (8, 8 + rows_dev)))
    span = quarter + 16
    flags_win = lax.dynamic_slice_in_dim(padded, start, n_chan * rows_dev, 1)
    flags_win = flags_win.reshape(taps, n_chan, rows_dev)[:, :, :span]
    chooser = (blocks[:, None] == jnp.arange(n_chan)[None, :]).astype(wide)
    flags_rows = jnp.einsum("kb,fbr->krf", chooser, flags_win)
    itself = jnp.arange(n_chan, dtype=jnp.int32)
    nearby = blocks[:, None] - blocks[None, :]
    one_before = jnp.where(blocks > 0, jnp.argmax(nearby == 1, axis=1), n_chan)
    one_after = jnp.where(blocks < n_chan - 1, jnp.argmax(nearby == -1, axis=1), n_chan)
    one_before = jnp.where(part == 0, one_before, itself)
    one_after = jnp.where(part == n_state - 1, one_after, itself)
    neighbours = jnp.concatenate([one_before, one_after, blocks[:4] // 2]).astype(jnp.int32)

    columns = moves.in_order((columns, columns_core, columns_chip, columns_slant))
    columns = columns.reshape(n_state, chans, 2, per_state)
    columns = jnp.transpose(columns, (1, 2, 0, 3)).reshape(chans, 2 * states)
    select = jnp.concatenate([select_rank, columns], axis=1)
    coeff = -jnp.exp(decay_own.reshape(states, own))

    normed_q, inner_all, sent, kept, other, turned = project(
        neighbours, pieces, in_flat, flags_rows, conv_kernel, conv_offset[None, :], select, n_state
    )
    reach = quarter + HALO
    channels = moves.swap_state(sent)
    came = moves.over_y(other)
    joined = added(kept, came)
    along = [moves.over_z(joined, hops) for hops in (1, 2, 3)]
    grad_q, *dgated = pull(places, grads, out_weight, n_state)
    along[0], along[1], along[2], *dgated = tied(*along, *dgated)
    summed = total_of(joined, along)
    came = moves.over_y(summed)
    dgated = trades(dgated)
    picked = moves.pieces_state(jnp.concatenate([summed, came], axis=0))
    tie = tied(*picked, *dgated, channels)
    picked, dgated, channels = tie[:4], tie[4:8], tie[8]

    weight_own = mine(delta_weight, 1)
    bias_own = mine(step_bias)[None, :]
    skip_own = mine(skip_weight)[None, :]
    fresh = jnp.broadcast_to((place > 0).astype(low)[:, None], (tokens, own))
    spread = spreading(states)
    coeff_two = coeff * math.log2(math.e)
    kept, dpre, gated = forward_scan(
        order,
        picked,
        channels,
        dgated,
        fresh,
        weight_own,
        bias_own,
        skip_own,
        coeff_two,
        spread,
    )
    gated = moves.swap_state(gated)
    own_sums, other_sums, dscan, delta_grad_own, decay_total, sums = backward_scan(
        order,
        picked,
        channels,
        dgated,
        fresh,
        dpre,
        kept,
        weight_own,
        skip_own,
        coeff_two,
        spread,
    )
    decay_grad_own = coeff * decay_total
    packed = jnp.concatenate([delta_grad_own, decay_grad_own, sums], axis=0).astype(low)

    own_sums, other_sums, packed, gated, dscan = tied(
        own_sums, other_sums, packed, gated, dscan
    )
    came = moves.over_state(other_sums, 1)
    dscan = moves.swap_state(dscan)
    came, own_sums, packed, gated = tied(came, own_sums, packed, gated)

    chip = added(own_sums, came)
    came = moves.over_state(chip[1], 2)
    branch_kept, sent, parts_kept, parts_sent, dgate_q, gain = emit(
        places, gated, out_weight, grad_q, normed_q, turned
    )
    came, sent, parts_sent = tied(came, sent, parts_sent)

    joined = added(chip[0], came)
    came = moves.over_y(joined[4:])
    parts_came = moves.over_state(parts_sent, 1)
    came, parts_came, sent = tied(came, parts_came, sent)

    joined = added(joined[:4], came)
    along = [moves.over_z(joined, hops) for hops in (1, 2, 3)]
    branch_came = moves.over_y(sent)
    parts_sum = added(parts_kept, parts_came)
    parts_came = moves.over_state(parts_sum[1], 2)
    along[0], along[1], along[2], branch_came, dscan = tied(*along, branch_came, dscan)

    partial = total_of(joined, along)
    came = moves.over_y(partial)
    branch = added(branch_kept, branch_came)
    branches = [moves.over_z(branch[4 - hops], hops) for hops in (1, 2, 3)]
    came, partial, parts_came = tied(came, partial, parts_came)
    parts_own = added(parts_sum[0], parts_came)
    came, partial, parts_own = tied(came, partial, parts_own)
    parts_chip = moves.over_state(parts_own, 2)

    dboth, rank_part, rows_part = turn_back(
        places,
        (partial, came),
        dscan,
        select,
        inner_all,
        flags_rows,
        conv_kernel,
        conv_offset[None, :],
        dgate_q,
        rank,
    )

    def backed(rows, weight):
        return lax.dot_general(rows, weight, contract_cols, preferred_element_type=wide)

    edge = width * 5 // 8
    left, right = slice(0, edge), slice(edge, width)
    other, same = slice(rows_q // 2, rows_q), slice(0, rows_q // 2)
    left_sent = backed(dboth[other], in_flat[left]).astype(low).reshape(4, quarter, edge)
    right_all = backed(dboth, in_flat[right]).reshape(2, 4, quarter, width - edge)
    right_sent = [right_all[:, 4 - hops].astype(low) for hops in (1, 2, 3)]
    inner_kept, inner_sent, inner_gain = weigh(places, dboth, normed_q, turned, n_state)
    inner_came = moves.over_state(inner_sent, 1)
    gain = (gain + inner_gain).reshape(-1, chans)
    gain = jnp.concatenate([rows_part, gain], axis=0)
    small = jnp.concatenate([packed, rank_part], axis=0)
    tie = tied(left_sent, dboth, small, inner_came, gain, *branches, *right_sent)
    left_sent, dboth, small, inner_came, gain = tie[:5]
    branches, right_sent = tie[5:8], tie[8:]

    left_came = moves.over_y(left_sent)
    right_along = [moves.over_z(right_sent[hops - 1], hops) for hops in (1, 2, 3)]
    gain = gain + moves.over_state(gain, 1)
    gain_came = moves.over_state(gain, 2)
    left_kept = backed(after(dboth, right_along[0])[same], in_flat[left])
    left_kept = left_kept.reshape(4, quarter, edge)
    branch = total_of(branch[0], branches)
    tie = tied(left_came, left_kept, gain, gain_came, branch, parts_chip, *right_along)
    left_came, left_kept, gain, gain_came, branch, parts_chip = tie[:6]
    right_along = tie[6:]

    joined = left_kept + left_came.astype(wide)
    left_sum = joined[0]
    left_along = [moves.over_z(joined[4 - hops].astype(low), hops) for hops in (1, 2, 3)]
    right_sum = right_all[:, 0]
    for piece in right_along:
        right_sum = right_sum + piece.astype(wide)
    right_came = moves.over_y(right_sum[1].astype(low))
    inner_sum = added(inner_kept, inner_came)
    inner_came = moves.over_state(inner_sum[1], 2)
    small_core = moves.over_state(small, 1)
    tie = tied(right_came, inner_came, small_core, *left_along)
    right_came, inner_came, small_core = tie[:3]
    left_along = tie[3:]

    for piece in left_along:
        left_sum = left_sum + piece.astype(wide)
    right_sum = right_sum[0] + right_came.astype(wide)
    dnormed = jnp.concatenate([left_sum, right_sum], axis=1)
    dscaled = dnormed * norm_gain[None, :]
    change = inv_rms * (dscaled - scaled * jnp.mean(dscaled * scaled, axis=1, keepdims=True))
    change = change.astype(low)
    change_chip = moves.over_state(change, 2)
    change_core = moves.over_state(change, 1)
    inner_own = added(inner_sum[0], inner_came)
    inner_chip = moves.over_state(inner_own, 2)
    gain = gain + gain_came
    gain_came = moves.over_y(gain[8 + 2 * states :].reshape(width))
    inner_core = moves.over_state(inner_own, 1)
    parts_core = moves.over_state(parts_own, 1)
    parts_slant = moves.over_state(parts_chip, 1)
    out_grad = placed(ranks, (parts_own, parts_core, parts_chip, parts_slant))
    place_at = 8 + part * per_state
    smalls = (
        gain[:taps],
        gain[taps],
        lax.dynamic_slice_in_dim(gain, place_at, per_state, 0).T,
        lax.dynamic_slice_in_dim(gain, place_at + states, per_state, 0).T,
    )
    tie = tied(
        change_chip,
        change_core,
        gain,
        gain_came,
        inner_chip,
        inner_core,
        parts_core,
        parts_slant,
        out_grad,
        *smalls,
    )
    change_chip, change_core, gain, gain_came, inner_chip, inner_core = tie[:6]
    parts_core, parts_slant, out_grad = tie[6:9]
    smalls = tie[9:]

    inner_slant = moves.over_state(inner_chip, 1)
    branch_chip = moves.over_state(branch, 2)
    branch_core = moves.over_state(branch, 1)
    change_slant = moves.over_state(change_chip, 1)
    fixed = packed.shape[0]
    rank_sum = added(small[fixed:], small_core[fixed:])
    small_sum = jnp.concatenate([small[:fixed], rank_sum], axis=0)
    small_chip = moves.over_state(small_sum, 2)
    gain = gain[8 + 2 * states :].reshape(width) + gain_came
    in_grad = interleave(
        ranks,
        (inner_own, inner_core, inner_chip, inner_slant),
        (parts_own, parts_core, parts_chip, parts_slant),
    )
    tie = tied(branch_chip, branch_core, change_slant, small_chip, gain, in_grad)
    branch_chip, branch_core, change_slant, small_chip, gain, in_grad = tie

    branch_slant = moves.over_state(branch_chip, 1)
    packed_slant = moves.over_state(small_chip[:fixed], 1)
    gains = [gain] + [moves.over_z(gain, hops) for hops in (1, 2, 3)]
    rank_grad = rank_sum.astype(wide) + small_chip[fixed:].astype(wide)
    packed = moves.in_order((packed, small_core[:fixed], small_chip[:fixed], packed_slant))
    packed = jnp.swapaxes(packed, 0, 1).reshape(-1, chans).astype(wide)
    smalls = (
        *smalls[:2],
        rank_grad,
        *smalls[2:],
        packed[:rank],
        packed[rank + states],
        lax.dynamic_slice_in_dim(packed, rank + part * per_state, per_state, 0),
        packed[rank + states + 1],
    )
    input_grad = placed(ranks, (change, change_core, change_chip, change_slant), cotangent)
    result = placed(ranks, (branch, branch_core, branch_chip, branch_slant), hidden_in)
    gains = jnp.stack(gains)
    gain_grad = 0.0
    for plane_at in range(4):
        gain_grad = gain_grad + lax.dynamic_index_in_dim(
            gains, (moves.z + 4 - plane_at) % 4, 0, keepdims=False
        )
    gain_grad = gain_grad / norm_gain
    return (result, input_grad, gain_grad, in_grad, *smalls, out_grad)


def solution(mesh):
    sizes = dict(mesh.shape)
    near = (sizes["chan"], sizes["state"]) == (8, 4)
    program = functools.partial(near_shards, 8, 4) if near else shards
    return jax.shard_map(
        program,
        mesh=mesh,
        in_specs=(
            P("chan", None),
            P(),
            P(None, None, "chan"),
            P(None, "chan"),
            P("chan"),
            P("chan", None),
            P("chan", "state"),
            P("chan", "state"),
            P(None, "chan"),
            P("chan"),
            P("state", "chan"),
            P("chan"),
            P("chan", None),
            P(),
            P(),
            P("chan", None),
        ),
        out_specs=(
            P("chan", None),
            P("chan", None),
            P(),
            P(None, None, "chan"),
            P(None, "chan"),
            P("chan"),
            P("chan", None),
            P("chan", "state"),
            P("chan", "state"),
            P(None, "chan"),
            P("chan"),
            P("state", "chan"),
            P("chan"),
            P("chan", None),
        ),
        check_vma=False,
    )
```
